32 devices in a mesh: section: 4 (over y, x), dp: 8 (over z, core).
Axes of the slice: x: 2, y: 2, z: 4, core: 2. Of those that a mesh axis runs over, the one named last changes fastest.
Arguments:
- tokens: bfloat16 [2, 8, 128, 768], P(None, 'dp'), may hold values from -6 to 6
- cotangent: bfloat16 [2, 8, 128, 768], P(None, 'dp'), may hold values from -6 to 6
- lengths: int32 [2, 8], P(None, 'dp'), may hold values from 32 to 128, as said below
- routes: int32 [2, 8, 128], P(None, 'dp'), may hold values from 0 to 3, as said below
- slots: int32 [2, 8, 128], P(None, 'dp'), may hold values from 0 to 63, as said below
- norm_gain: bfloat16 [4, 768], P(None, ('section', 'dp')), may hold values from 0.25 to 1.75
- norm_bias: bfloat16 [4, 768], P(None, ('section', 'dp')), may hold values from -1.5 to 1.5
- attn_qkv: bfloat16 [2, 768, 2304], P(None, None, ('section', 'dp')), may hold values from -0.21875 to 0.21875
- attn_out: bfloat16 [2, 768, 768], P(None, None, ('section', 'dp')), may hold values from -1.75 to 1.75
- attn_out_bias: bfloat16 [2, 768], P(None, ('section', 'dp')), may hold values from -1.5 to 1.5
- ffn_up: bfloat16 [768, 3072], P(None, ('section', 'dp')), may hold values from -0.21875 to 0.21875
- ffn_up_bias: bfloat16 [3072], P(('section', 'dp')), may hold values from -2.5 to 2.5
- ffn_down: bfloat16 [3072, 768], P(None, ('section', 'dp')), may hold values from -0.109375 to 0.109375
- ffn_down_bias: bfloat16 [768], P(('section', 'dp')), may hold values from -1.5 to 1.5
- router: bfloat16 [768, 4], P(('section', 'dp')), may hold values from -0.15625 to 0.15625
- expert_up: bfloat16 [8, 768, 1536], P('dp', None, 'section'), may hold values from -0.21875 to 0.21875
- expert_down: bfloat16 [8, 1536, 768], P('dp', 'section'), may hold values from -0.21875 to 0.21875
Outputs:
- section_outputs: float32 [4, 2, 8, 128, 768], P('section', None, 'dp')
- section_grads: float32 [4, 2, 8, 128, 768], P('section', None, 'dp')
- grad_norm_gain: float32 [4, 768], P(None, ('section', 'dp'))
- grad_norm_bias: float32 [4, 768], P(None, ('section', 'dp'))
- grad_attn_qkv: float32 [2, 768, 2304], P(None, None, ('section', 'dp'))
- grad_attn_out: float32 [2, 768, 768], P(None, None, ('section', 'dp'))
- grad_attn_out_bias: float32 [2, 768], P(None, ('section', 'dp'))
- grad_ffn_up: float32 [768, 3072], P(None, ('section', 'dp'))
- grad_ffn_up_bias: float32 [3072], P(('section', 'dp'))
- grad_ffn_down: float32 [3072, 768], P(None, ('section', 'dp'))
- grad_ffn_down_bias: float32 [768], P(('section', 'dp'))
- grad_router: float32 [768, 4], P(('section', 'dp'))
- grad_expert_up: float32 [8, 768, 1536], P('dp', None, 'section')
- grad_expert_down: float32 [8, 1536, 768], P('dp', 'section')
The draws below stay inside these ranges and needn't reach their ends.
Inputs may be any that keep to these rules, and one draw needn't show every extreme that they name: `lengths`: in each micro-batch some sequence has length exactly 128. `routes`: no expert gets more than 64 tokens of one sequence in one micro-batch; in each micro-batch one expert gets exactly 64 tokens of every sequence. slots of the tokens of one sequence and micro-batch that go to the same expert are distinct.
All inputs are finite; a program needn't handle non-finite values.
Results may differ from the reference program's by a relative error of at most 0.019.
Values may be sent and summed in bfloat16 or wider, within the bound.
A program may use at most 320 MiB of HBM per device.

```python
import jax
import jax.numpy as jnp
from jax import lax

D = 768
FF = 3072
HEADS = 12
HEAD_DIM = 64
LEN = 128
MICRO = 2
BATCH = 8
EXPERTS = 4
CAP = 64


def routing_tables(key):
    full_expert = jax.random.randint(jax.random.fold_in(key, 101), (MICRO,), 0, EXPERTS)
    pool_key = jax.random.fold_in(key, 102)
    shuffle_key = jax.random.fold_in(key, 103)

    def one_block(flat_index):
        chosen = full_expert[flat_index // BATCH]
        slot_pool = jax.random.permutation(jax.random.fold_in(pool_key, flat_index), (EXPERTS - 1) * CAP)[:LEN - CAP]
        expert = (slot_pool // CAP).astype(jnp.int32)
        expert = expert + (expert >= chosen).astype(jnp.int32)
        slot_index = (slot_pool % CAP).astype(jnp.int32)
        experts_all = jnp.concatenate([jnp.zeros((CAP,), jnp.int32) + chosen, expert])
        slots_all = jnp.concatenate([jnp.arange(CAP, dtype=jnp.int32), slot_index])
        shuffle = jax.random.permutation(jax.random.fold_in(shuffle_key, flat_index), LEN)
        return (experts_all[shuffle], slots_all[shuffle])
    experts_flat, slots_flat = jax.vmap(one_block)(jnp.arange(MICRO * BATCH, dtype=jnp.int32))
    return (experts_flat.reshape(MICRO, BATCH, LEN), slots_flat.reshape(MICRO, BATCH, LEN))


def draw_routes(key, part):
    tables = routing_tables(key)
    return tables[0].astype(jnp.int32)


def draw_slots(key, part):
    tables = routing_tables(key)
    return tables[1].astype(jnp.int32)


def draw_lengths(key, part):
    key = jax.random.fold_in(key, 5)
    drawn_lengths = jax.random.randint(jax.random.fold_in(key, 1), (MICRO, BATCH), LEN // 4, LEN + 1)
    longest = jax.random.randint(jax.random.fold_in(key, 2), (MICRO, 1), 0, BATCH)
    return jnp.where(jnp.arange(BATCH)[None, :] == longest, LEN, drawn_lengths).astype(jnp.int32)


def shard_levels(stream_key, dims, cuts, low, high):
    def one(dim, blocks):
        steps = jax.random.uniform(jax.random.fold_in(jax.random.fold_in(stream_key, 6), dim), (blocks,), jnp.float32, low / len(cuts), high / len(cuts))
        return jnp.repeat(jnp.exp(steps), dims[dim] // blocks).reshape((-1,) + (1,) * (len(dims) - dim - 1))

    loudness = one(*cuts[0])
    for cut in cuts[1:]:
        loudness = loudness * one(*cut)
    return loudness


def scatter_about(stream_key, shape, width, limit, cuts=(), held_as=jnp.bfloat16):
    values = width * jax.random.normal(stream_key, shape, jnp.float32)
    if cuts:
        values = values * shard_levels(stream_key, shape, cuts, -0.22, 0.18)
    return jnp.clip(values, -limit, limit).astype(held_as)


def setup_inputs(seed: int = 0) -> dict:
    streams_of = jax.random.split(jax.random.key(seed), 18)
    tokens = scatter_about(streams_of[0], (MICRO, BATCH, LEN, D), 1.0, 6.0, ((1, 8),))
    cotangent = scatter_about(streams_of[1], (MICRO, BATCH, LEN, D), 1.0, 6.0, ((1, 8),))
    lengths = draw_lengths(jax.random.fold_in(streams_of[17], 71), 0)
    routes = draw_routes(jax.random.fold_in(streams_of[17], 71), 0)
    slots = draw_slots(jax.random.fold_in(streams_of[17], 71), 0)
    norm_gain = jnp.clip(1.0 + 0.15 * jax.random.normal(streams_of[5], (4, D), jnp.float32), 0.25, 1.75).astype(jnp.bfloat16)
    norm_bias = scatter_about(streams_of[6], (4, D), 0.3, 1.5, ((1, 32),))
    attn_qkv = scatter_about(streams_of[7], (2, D, 3 * D), D ** -0.5, 0.21875, ((2, 32),))
    attn_out = scatter_about(streams_of[8], (2, D, D), (D // 64) ** -0.5, 1.75, ((2, 32),))
    attn_out_bias = scatter_about(streams_of[9], (2, D), 0.3, 1.5, ((1, 32),))
    ffn_up = scatter_about(streams_of[10], (D, FF), D ** -0.5, 0.21875, ((1, 32),))
    ffn_up_bias = scatter_about(streams_of[11], (FF,), 0.5, 2.5, ((0, 32),))
    ffn_down = scatter_about(streams_of[12], (FF, D), FF ** -0.5, 0.109375, ((1, 32),))
    ffn_down_bias = scatter_about(streams_of[13], (D,), 0.3, 1.5, ((0, 32),))
    router = scatter_about(streams_of[14], (D, EXPERTS), (2 * D) ** -0.5, 0.15625, ((0, 32),))
    expert_up = scatter_about(streams_of[15], (2 * EXPERTS, D, FF // 2), D ** -0.5, 0.21875, ((0, 8), (2, 4)))
    expert_down = scatter_about(streams_of[16], (2 * EXPERTS, FF // 2, D), (FF // 4) ** -0.5, 0.21875, ((0, 8), (1, 4)))
    return {"tokens": tokens, "cotangent": cotangent, "lengths": lengths, "routes": routes, "slots": slots, "norm_gain": norm_gain, "norm_bias": norm_bias, "attn_qkv": attn_qkv, "attn_out": attn_out, "attn_out_bias": attn_out_bias, "ffn_up": ffn_up, "ffn_up_bias": ffn_up_bias, "ffn_down": ffn_down, "ffn_down_bias": ffn_down_bias, "router": router, "expert_up": expert_up, "expert_down": expert_down}


top_precision = lax.Precision.HIGHEST
eps_norm = 1e-05
masked_score = -1000000000.0

@jax.custom_vjp
def low(v):
    return lax.optimization_barrier(v.astype(jnp.bfloat16)).astype(jnp.float32)

@jax.custom_vjp
def low_back(v):
    return v

def low_keep(v):
    return (low(v), None)

def low_pass(kept, grad):
    return (grad,)

def back_keep(v):
    return (v, None)

def back_low(kept, grad):
    return (low(grad),)
low.defvjp(low_keep, low_pass)
low_back.defvjp(back_keep, back_low)

def layer_norm(values, gain_row, shift_row):
    center = values - lax.optimization_barrier(jnp.mean(values, axis=-1, keepdims=True))
    spread = lax.optimization_barrier(jnp.mean(center * center, axis=-1, keepdims=True))
    return center * lax.rsqrt(spread + eps_norm) * gain_row + shift_row

def gelu_exact(values):
    return jax.nn.gelu(values, approximate=False)

def attention_half(stream, length, gain_row, shift_row, w_qkv, w_out, b_out):
    normed = low(layer_norm(stream, gain_row, shift_row))
    packed = low_back(low(jnp.dot(normed, w_qkv, precision=top_precision)))
    packed = packed.reshape(LEN, 3, HEADS, HEAD_DIM)
    scores = jnp.einsum('qhd,khd->hqk', packed[:, 0], packed[:, 1], precision=top_precision) * HEAD_DIM ** (-0.5)
    scores = low_back(scores)
    position = jnp.arange(LEN)
    allowed = (position[None, :] <= position[:, None]) & (position[None, :] < length)
    scores = jnp.where(allowed[None], scores, masked_score)
    row_max = lax.optimization_barrier(jnp.max(scores, axis=-1, keepdims=True))
    exponent = jnp.exp(scores - row_max)
    probabilities = exponent / lax.optimization_barrier(jnp.sum(exponent, axis=-1, keepdims=True))
    context = jnp.einsum('hqk,khd->qhd', low(probabilities), packed[:, 2], precision=top_precision).reshape(LEN, D)
    context = low_back(low(context))
    return stream + low_back(jnp.dot(context, w_out, precision=top_precision) + b_out)

def ffn_half(stream, gain_row, shift_row, w_up, b_up, w_down, b_down):
    normed = low(layer_norm(stream, gain_row, shift_row))
    pre_act = low_back(jnp.dot(normed, w_up, precision=top_precision) + b_up)
    activated = low(gelu_exact(pre_act))
    return stream + low_back(jnp.dot(activated, w_down, precision=top_precision) + b_down)

def expert_block(item):
    rows_in, w_up, w_down = item
    pre_act = low_back(jnp.dot(rows_in, w_up, precision=top_precision))
    activated = low(gelu_exact(pre_act))
    return jnp.dot(activated, w_down, precision=top_precision)

def expert_half(stream, route_ids, slot_ids, gain_row, shift_row, w_router, e_up, e_down):
    full_up = jnp.transpose(e_up.reshape(EXPERTS, 2, D, FF // 2), (0, 2, 1, 3)).reshape(EXPERTS, D, FF)
    full_down = e_down.reshape(EXPERTS, FF, D)
    normed = low(layer_norm(stream, gain_row, shift_row))
    logits = low_back(jnp.einsum('bld,de->ble', normed, w_router, precision=top_precision))
    score = jnp.take_along_axis(logits, route_ids[..., None], axis=-1)[..., 0]
    gate_value = jax.nn.sigmoid(score)
    outgoing = low_back(normed)
    row_ids = (jnp.arange(BATCH).astype(jnp.int32)[:, None] * CAP + slot_ids).astype(jnp.int32)
    buffer_rows = jnp.zeros((EXPERTS, BATCH * CAP, D), jnp.float32).at[route_ids, row_ids].add(outgoing)
    results = lax.map(jax.checkpoint(expert_block), (buffer_rows, full_up, full_down))
    results = low_back(low(results))
    returned = results[route_ids, row_ids]
    return stream + gate_value[..., None] * returned

def reference(tokens, cotangent, lengths, routes, slots, norm_gain, norm_bias, attn_qkv, attn_out, attn_out_bias, ffn_up, ffn_up_bias, ffn_down, ffn_down_bias, router, expert_up, expert_down):
    params = tuple((item.astype(jnp.float32) for item in (norm_gain, norm_bias, attn_qkv, attn_out, attn_out_bias, ffn_up, ffn_up_bias, ffn_down, ffn_down_bias, router, expert_up, expert_down)))
    tokens_f = tokens.astype(jnp.float32)
    probes = jnp.zeros((3,) + tokens.shape, jnp.float32)

    def forward(stream_in, probe_set, gains, shifts, w_qkv, w_out, b_out, w_up, b_up, w_down, b_down, w_router, e_up, e_down):
        stacked = []
        for micro_index in range(MICRO):

            def dense_part(item):
                first_in, probe_one, probe_two, probe_three, length = item
                out_zero = attention_half(first_in, length, gains[0], shifts[0], w_qkv[0], w_out[0], b_out[0])
                second_in = low_back(low(out_zero)) + probe_one
                out_one = ffn_half(second_in, gains[1], shifts[1], w_up, b_up, w_down, b_down)
                third_in = low_back(low(out_one)) + probe_two
                out_two = attention_half(third_in, length, gains[2], shifts[2], w_qkv[1], w_out[1], b_out[1])
                fourth_in = low_back(low(out_two)) + probe_three
                return (out_zero, out_one, out_two, fourth_in)
            out_zero, out_one, out_two, fourth_in = lax.map(jax.checkpoint(dense_part), (stream_in[micro_index], probe_set[0, micro_index], probe_set[1, micro_index], probe_set[2, micro_index], lengths[micro_index]))
            out_three = expert_half(fourth_in, routes[micro_index], slots[micro_index], gains[3], shifts[3], w_router, e_up, e_down)
            stacked.append(jnp.stack([out_zero, out_one, out_two, out_three]))
        return jnp.stack(stacked, axis=1)
    result, pull_back = jax.vjp(forward, tokens_f, probes, *params)
    cot_full = jnp.zeros(result.shape, jnp.float32).at[3].set(cotangent.astype(jnp.float32))
    grads = pull_back(cot_full)
    section_grads = jnp.concatenate([grads[0][None], grads[1]], axis=0)
    return (result, section_grads, grads[2], grads[3], grads[4], grads[5], grads[6], grads[7], grads[8], grads[9], grads[10], grads[11], grads[12], grads[13])
```

```python
import functools
import types

import jax
import jax.numpy as jnp
from jax import lax
from jax.experimental import pallas as pl
from jax.experimental.pallas import tpu as pltpu
from jax.sharding import PartitionSpec as P

HEADS = 12
HEAD_DIM = 64
EPS = 1e-05
MASKED = -1000000000.0
MESH = pl.DeviceIdType.MESH
F32 = jnp.float32
BF16 = jnp.bfloat16
LANES = 128


def dot_as(left, right, left_dim, right_dim):
    return lax.dot_general(
        left, right, (((left_dim,), (right_dim,)), ((), ())), preferred_element_type=F32
    )


def mm(left, right):
    return dot_as(left, right, 1, 0)


def mm_nt(left, right):
    return dot_as(left, right, 1, 1)


def mm_tn(left, right):
    return dot_as(left, right, 0, 0)


def normalize(values):
    center = values - jnp.mean(values, axis=-1, keepdims=True)
    spread = jnp.mean(center * center, axis=-1, keepdims=True)
    inverse = lax.rsqrt(spread + EPS)
    return center * inverse, inverse


def gelu_parts(pre):
    half = 0.5 + 0.5 * lax.erf(pre * 0.7071067811865476)
    density = jnp.exp(-0.5 * pre * pre) * 0.3989422804014327
    return pre * half, half + pre * density


def layers_kernel(geo, *refs):
    g = geo
    (
        x0, cot, lens, place_row, place_col, gains, shifts, b_out, b_down, b_up, w_router, router_row,
        w_qkv, w_out, w_up, w_down, e_up, e_down,
        sec_out, sec_grad, small, g_bup, g_qkv, g_out, g_up, g_down, g_eup, g_edown,
        xs, gs, normed, wide, qkv, probs, ctx, act, dgelu, dpre, dqkv, part, got, mine, table, disp, dispc,
        rows, crow, grow, acte, dpree, keep_d, keep_y, snd_d, snd_y, rcv_d, rcv_y, out_d, out_y, back_d, back_y,
        scat_s, scat_r, gath_s, gath_r, disp_s, disp_r, pair_s, pair_r, back_s, back_r,
    ) = refs
    width = g.width
    sec = lax.axis_index("section")
    dev = lax.axis_index("dp")
    core = lax.rem(dev, 2)
    chip = lax.div(dev, 2)
    sib = dev + 1 - 2 * core
    span = g.micro * g.cap
    own = pl.ds(pl.multiple_of(sec * g.piece, g.piece), g.piece)

    def peer_section(offset):
        return lax.rem(sec + offset, g.sections)

    def peer_chip(offset):
        return lax.rem(chip + offset, g.chips)

    def piece_at(index):
        return pl.ds(pl.multiple_of(index * g.piece, g.piece), g.piece)

    def span_at(index):
        return pl.ds(pl.multiple_of(index * span, span), span)

    def remote(source, target, send, arrive, where):
        return pltpu.make_async_remote_copy(
            src_ref=source, dst_ref=target, send_sem=send, recv_sem=arrive, device_id=where, device_id_type=MESH
        )

    started = []

    def launch(copy):
        copy.start()
        started.append(copy)

    barrier = pltpu.get_barrier_semaphore()
    for offset in range(1, g.sections):
        pl.semaphore_signal(barrier, inc=1, device_id={"section": peer_section(offset)}, device_id_type=MESH)
    for offset in range(1, g.chips):
        pl.semaphore_signal(barrier, inc=1, device_id={"dp": 2 * peer_chip(offset) + core}, device_id_type=MESH)
    pl.semaphore_signal(barrier, inc=1, device_id={"dp": sib}, device_id_type=MESH)
    pl.semaphore_wait(barrier, g.sections - 1 + g.chips - 1 + 1)

    def scatter_copy(slot, offset):
        return remote(
            part.at[slot, piece_at(peer_section(offset))], got.at[slot, offset - 1],
            scat_s.at[slot, offset - 1], scat_r.at[slot, offset - 1], {"section": peer_section(offset)},
        )

    def scatter_start(slot, value):
        part[slot] = value.astype(BF16)
        mine[...] = value
        for offset in range(1, g.sections):
            launch(scatter_copy(slot, offset))

    def scatter_sum(slot):
        total = mine[own, :]
        for offset in range(1, g.sections):
            scatter_copy(slot, offset).wait_recv()
            total = total + got[slot, offset - 1].astype(F32)
        return total

    def gather_copy(buffer, slot, sem, source, offset):
        return remote(
            buffer.at[slot, piece_at(source)], buffer.at[slot, piece_at(source)],
            gath_s.at[sem, offset - 1], gath_r.at[sem, offset - 1], {"section": peer_section(offset)},
        )

    def gather_start(buffer, slot, sem):
        for offset in range(1, g.sections):
            launch(gather_copy(buffer, slot, sem, sec, offset))

    def gather_wait(buffer, slot, sem):
        for offset in range(1, g.sections):
            source = lax.rem(sec + g.sections - offset, g.sections)
            gather_copy(buffer, slot, sem, source, offset).wait_recv()

    def disp_copy(which, source, target, offset):
        at_chip = peer_chip(offset)
        return remote(
            source.at[span_at(at_chip)], target.at[core, span_at(chip)],
            disp_s.at[which, offset - 1], disp_r.at[which, offset - 1], {"dp": 2 * at_chip + core},
        )

    def disp_start(which, source, target):
        for offset in range(1, g.chips):
            launch(disp_copy(which, source, target, offset))
        target[core, span_at(chip), :] = source[span_at(chip), :]

    def pair_copy(which, source, target):
        return remote(source, target, pair_s.at[which], pair_r.at[which], {"dp": sib})

    def disp_wait(which, source, target):
        for offset in range(1, g.chips):
            disp_copy(which, source, target, offset).wait_recv()
        launch(pair_copy(which, target.at[core], target.at[core]))

    def back_copy(which, source, target, offset):
        at_chip = peer_chip(offset)
        return remote(
            source.at[span_at(at_chip)], target.at[span_at(chip)],
            back_s.at[which, offset - 1], back_r.at[which, offset - 1], {"dp": 2 * at_chip + core},
        )

    def back_start(which, source, target):
        for offset in range(1, g.chips):
            launch(back_copy(which, source, target, offset))
        target[span_at(chip), :] = source[span_at(chip), :]

    def back_wait(which, source, target):
        for offset in range(1, g.chips):
            back_copy(which, source, target, offset).wait_recv()

    def norm_into(source, target, index):
        @pl.loop(0, g.sections)
        def _(step):
            at = piece_at(step)
            unit, _ = normalize(source[at, :].astype(F32))
            target[at, :] = (unit * gains[index : index + 1, :] + shifts[index : index + 1, :]).astype(BF16)

    slot_ids = lax.broadcasted_iota(jnp.int32, table.shape, 0)
    table[...] = jnp.where(slot_ids == place_row[...], 1.0, 0.0).astype(BF16)
    dispc[...] = mm(table[...], cot[...]).astype(BF16)
    disp_start(0, dispc, crow)

    key_ids = lax.broadcasted_iota(jnp.int32, (g.seq, g.seq), 0)
    query_ids = lax.broadcasted_iota(jnp.int32, (g.seq, g.seq), 1)
    scale = HEAD_DIM**-0.5

    def head_slice(block, head):
        first = block * g.head_cols + head * HEAD_DIM
        return slice(first, first + HEAD_DIM)

    def token_slice(micro):
        return slice(micro * g.seq, (micro + 1) * g.seq)

    def attention_forward(layer, stream, slot):
        norm_into(stream, normed.at[2 * layer], 2 * layer)
        qkv[layer] = mm_nt(w_qkv[layer], normed[2 * layer]).astype(BF16)
        for micro in range(g.micro):
            allowed = (key_ids <= query_ids) & (key_ids < lens[micro : micro + 1, :])
            for head in range(g.heads):
                at = token_slice(micro)
                scores = mm_tn(qkv[layer, head_slice(1, head), at], qkv[layer, head_slice(0, head), at]) * scale
                scores = jnp.where(allowed, scores, MASKED)
                weight = jnp.exp(scores - jnp.max(scores, axis=0, keepdims=True))
                weight = weight / jnp.sum(weight, axis=0, keepdims=True)
                probs[layer, micro, head] = weight
                ctx[layer, head_slice(0, head), at] = mm(
                    qkv[layer, head_slice(2, head), at], weight.astype(BF16)
                ).astype(BF16)
        scatter_start(slot, mm_tn(ctx[layer], w_out[layer]))

    def finish_forward(section, bias, stream):
        total = scatter_sum(section) + bias + stream[own, :].astype(F32)
        xs[section, own, :] = total.astype(BF16)
        gather_start(xs, section, section)
        gather_wait(xs, section, section)

    attention_forward(0, x0, 0)
    finish_forward(0, b_out[0:1, :], x0)

    norm_into(xs.at[0], normed.at[1], 1)
    for block in range(g.hidden // g.block):
        at = slice(block * g.block, (block + 1) * g.block)
        pre = mm_nt(normed[1], w_up[at, :]) + b_up[:, at]
        value, slope = gelu_parts(pre)
        act[:, at] = value.astype(BF16)
        dgelu[:, at] = slope
    scatter_start(1, mm_nt(act[...], w_down[...]))
    finish_forward(1, b_down[...], xs.at[0])

    attention_forward(1, xs.at[1], 2)
    finish_forward(2, b_out[1:2, :], xs.at[1])

    norm_into(xs.at[2], wide.at[:, pl.ds(0, width)], 3)
    logits = mm(wide[:, :width], w_router[...])
    lane = lax.broadcasted_iota(jnp.int32, logits.shape, 1)
    chosen = (place_col[...] >= lane * span) & (place_col[...] < lane * span + span)
    score = jnp.sum(jnp.where(chosen, logits, 0.0), axis=-1, keepdims=True)
    gate = 1.0 / (1.0 + jnp.exp(-score))
    gate_high = gate.astype(BF16).astype(F32)
    lane = lax.broadcasted_iota(jnp.int32, (g.tokens, LANES), 1)
    pair = jnp.where(lane == 0, gate_high, jnp.where(lane == 1, gate - gate_high, 0.0))
    wide[:, width:] = pair.astype(BF16)
    disp[...] = mm(table[...], wide[...]).astype(BF16)
    disp_start(1, disp, rows)
    disp_wait(0, dispc, crow)
    disp_wait(1, disp, rows)

    small[...] = jnp.zeros_like(small)

    def expert_block(side, at, keep_first):
        row = rows[side, at, :width]
        tail = rows[side, at, width:].astype(F32)
        gate_row = tail[:, 0:1] + tail[:, 1:2]
        grad_row = (gate_row * crow[side, at, :].astype(F32)).astype(BF16)
        grow[side, at, :] = grad_row
        value, slope = gelu_parts(mm(row, e_up[...]))
        value = value.astype(BF16)
        acte[side, at, :] = value
        result = mm(value, e_down[...])
        total = jnp.sum(grad_row.astype(F32) * result, axis=-1, keepdims=True) * (1.0 - gate_row)
        inner = (slope * mm_nt(grad_row, e_down[...])).astype(BF16)
        dpree[side, at, :] = inner
        back = mm_nt(inner, e_up[...]) + total * router_row[...]
        small[12:13, :] += jnp.sum(row.astype(F32) * total, axis=0, keepdims=True)
        result = result * gate_row
        if keep_first:
            keep_d[at, :] = back
            keep_y[at, :] = result
        else:
            snd_d[at, :] = back.astype(BF16)
            snd_y[at, :] = result.astype(BF16)

    half_rows = g.chips * span

    @pl.loop(0, half_rows // g.block)
    def _(step):
        expert_block(core, pl.ds(pl.multiple_of(step * g.block, g.block), g.block), True)

    pair_copy(0, crow.at[1 - core], crow.at[1 - core]).wait_recv()
    pair_copy(1, rows.at[1 - core], rows.at[1 - core]).wait_recv()

    @pl.loop(0, half_rows // g.block)
    def _(step):
        expert_block(1 - core, pl.ds(pl.multiple_of(step * g.block, g.block), g.block), False)

    launch(pair_copy(2, snd_d, rcv_d))
    launch(pair_copy(3, snd_y, rcv_y))
    pair_copy(2, snd_d, rcv_d).wait_recv()
    out_d[...] = (keep_d[...] + rcv_d[...].astype(F32)).astype(BF16)
    back_start(0, out_d, back_d)
    pair_copy(3, snd_y, rcv_y).wait_recv()
    out_y[...] = (keep_y[...] + rcv_y[...].astype(F32)).astype(BF16)
    back_start(1, out_y, back_y)
    g_eup[...] = mm_tn(rows[0, :, :width], dpree[0]) + mm_tn(rows[1, :, :width], dpree[1])
    g_edown[...] = mm_tn(acte[0], grow[0]) + mm_tn(acte[1], grow[1])

    def finish_backward(section, slot, stream, above):
        grad = scatter_sum(slot)
        unit, inverse = normalize(stream[own, :].astype(F32))
        small[section : section + 1, :] = jnp.sum(grad * unit, axis=0, keepdims=True)
        small[4 + section : 5 + section, :] = jnp.sum(grad, axis=0, keepdims=True)
        grad = grad * gains[section : section + 1, :]
        shared = jnp.mean(grad, axis=-1, keepdims=True)
        along = jnp.mean(grad * unit, axis=-1, keepdims=True)
        grad = inverse * (grad - shared - unit * along) + above[own, :].astype(F32)
        gs[section, own, :] = grad.astype(BF16)
        gather_start(gs, section, 4 + section)
        gather_wait(gs, section, 4 + section)

    back_wait(0, out_d, back_d)
    scatter_start(3, mm_tn(table[...], back_d[...]))
    finish_backward(3, 3, xs.at[2], cot)

    def bias_row(index, section):
        small[index : index + 1, :] = jnp.sum(gs[section, own, :].astype(F32), axis=0, keepdims=True)

    def attention_backward(layer, section, slot):
        grad = gs[section + 1]
        dctx = mm_nt(w_out[layer], grad).astype(BF16)
        for micro in range(g.micro):
            for head in range(g.heads):
                at = token_slice(micro)
                weight = probs[layer, micro, head]
                low = weight.astype(BF16)
                dhead = dctx[head_slice(0, head), at]
                query = qkv[layer, head_slice(0, head), at]
                key = qkv[layer, head_slice(1, head), at]
                value = qkv[layer, head_slice(2, head), at]
                dprobs = mm_tn(value, dhead)
                delta = jnp.sum(weight * dprobs, axis=0, keepdims=True)
                dscores = (weight * (dprobs - delta)).astype(BF16)
                dqkv[head_slice(0, head), at] = (mm(key, dscores) * scale).astype(BF16)
                dqkv[head_slice(1, head), at] = (mm_nt(query, dscores) * scale).astype(BF16)
                dqkv[head_slice(2, head), at] = mm_nt(dhead, low).astype(BF16)
        scatter_start(slot, mm_tn(dqkv[...], w_qkv[layer]))
        g_out[layer] = mm(ctx[layer], grad)
        g_qkv[layer] = mm(dqkv[...], normed[2 * layer])
        bias_row(8 + layer, section + 1)

    attention_backward(1, 2, 4)
    finish_backward(2, 4, xs.at[1], gs.at[3])

    grad_one = gs[2]
    for block in range(g.hidden // g.block):
        at = slice(block * g.block, (block + 1) * g.block)
        dpre[:, at] = (dgelu[:, at] * mm(grad_one, w_down[:, at])).astype(BF16)
    scatter_start(5, mm(dpre[...], w_up[...]))
    g_down[...] = mm_tn(gs[2], act[...])
    g_up[...] = mm_tn(dpre[...], normed[1])
    g_bup[...] = jnp.broadcast_to(jnp.sum(dpre[...].astype(F32), axis=0, keepdims=True), g_bup.shape)
    bias_row(10, 2)
    finish_backward(1, 5, xs.at[0], gs.at[2])

    attention_backward(0, 0, 6)
    finish_backward(0, 6, x0, gs.at[1])

    back_wait(1, out_y, back_y)
    scatter_start(7, mm_tn(table[...], back_y[...]))
    xs[3, own, :] = (scatter_sum(7) + xs[2, own, :].astype(F32)).astype(BF16)
    gather_start(xs, 3, 3)
    gather_wait(xs, 3, 3)
    sec_out[...] = xs[sec].astype(F32)
    sec_grad[...] = gs[sec].astype(F32)
    for copy in started:
        copy.wait_send()


def run_layers(g, *operands):
    tokens, width, hidden = g.tokens, g.width, g.hidden
    slots = g.chips * g.micro * g.cap
    inner = operands[-1].shape[0]
    qkv_rows = 3 * g.head_cols
    shape = jax.ShapeDtypeStruct
    vmem = pltpu.VMEM
    dma = pltpu.SemaphoreType.DMA
    outs = (
        shape((tokens, width), F32), shape((tokens, width), F32), shape((16, width), F32), shape((8, hidden), F32),
        shape((2, qkv_rows, width), F32), shape((2, g.head_cols, width), F32), shape((hidden, width), F32),
        shape((width, hidden), F32), shape((width, inner), F32), shape((inner, width), F32),
    )
    scratch = [
        vmem((4, tokens, width), BF16),
        vmem((4, tokens, width), BF16),
        vmem((3, tokens, width), BF16),
        vmem((tokens, width + LANES), BF16),
        vmem((2, qkv_rows, tokens), BF16),
        vmem((2, g.micro, g.heads, g.seq, g.seq), F32),
        vmem((2, g.head_cols, tokens), BF16),
        vmem((tokens, hidden), BF16),
        vmem((tokens, hidden), F32),
        vmem((tokens, hidden), BF16),
        vmem((qkv_rows, tokens), BF16),
        vmem((8, tokens, width), BF16),
        vmem((8, g.sections - 1, g.piece, width), BF16),
        vmem((tokens, width), F32),
        vmem((slots, tokens), BF16),
        vmem((slots, width + LANES), BF16),
        vmem((slots, width), BF16),
        vmem((2, slots, width + LANES), BF16),
        vmem((2, slots, width), BF16),
        vmem((2, slots, width), BF16),
        vmem((2, slots, inner), BF16),
        vmem((2, slots, inner), BF16),
        vmem((slots, width), F32),
        vmem((slots, width), F32),
    ] + [vmem((slots, width), BF16)] * 8 + [
        dma((8, g.sections - 1)), dma((8, g.sections - 1)), dma((8, g.sections - 1)), dma((8, g.sections - 1)),
        dma((2, g.chips - 1)), dma((2, g.chips - 1)), dma((4,)), dma((4,)),
        dma((2, g.chips - 1)), dma((2, g.chips - 1)),
    ]
    whole = pl.BlockSpec(memory_space=pltpu.VMEM)
    return pl.pallas_call(
        functools.partial(layers_kernel, g),
        out_shape=outs,
        in_specs=[whole] * len(operands),
        out_specs=[whole] * len(outs),
        scratch_shapes=scratch,
        compiler_params=pltpu.CompilerParams(
            collective_id=0, has_side_effects=True, vmem_limit_bytes=62 * 1024 * 1024
        ),
    )(*operands)


BOTH = ("section", "dp")


def body(
    tokens, cotangent, lengths, routes, slots, norm_gain, norm_bias, attn_qkv, attn_out, attn_out_bias,
    ffn_up, ffn_up_bias, ffn_down, ffn_down_bias, router, expert_up, expert_down,
):
    sections, devices = lax.axis_size("section"), lax.axis_size("dp")
    sec, dev = lax.axis_index("section"), lax.axis_index("dp")
    micro, _, seq, width = tokens.shape
    experts = router.shape[1]
    head_cols = width // sections
    hidden = ffn_up.shape[1] * devices
    cap = 2 * seq // experts
    g = types.SimpleNamespace(
        sections=sections, chips=devices // 2, micro=micro, seq=seq, width=width, hidden=hidden, cap=cap,
        tokens=micro * seq, piece=micro * seq // sections, heads=head_cols // HEAD_DIM, head_cols=head_cols,
        block=256,
    )

    def every(array, axis):
        return lax.all_gather(array, BOTH, axis=axis, tiled=True)

    def part_of(array, axis, size):
        return lax.dynamic_slice_in_dim(array, sec * size, size, axis)

    gains = every(norm_gain, 1).astype(F32)
    shifts = every(norm_bias, 1).astype(F32)
    b_out = every(attn_out_bias, 1).astype(F32)
    b_down = every(ffn_down_bias, 0).astype(F32)[None]
    b_up = lax.all_gather(ffn_up_bias, "dp", axis=0, tiled=True).astype(F32)[None]
    full_router = every(router, 0)
    w_router = jnp.pad(full_router, ((0, 0), (0, LANES - experts)))
    router_row = lax.dynamic_slice_in_dim(full_router, dev // 2, 1, 1).astype(F32).T
    qkv_full = every(attn_qkv, 2).reshape(2, width, 3, width)
    w_qkv = part_of(qkv_full, 3, head_cols).transpose(0, 2, 3, 1).reshape(2, 3 * head_cols, width)
    w_out = part_of(every(attn_out, 2), 1, head_cols)
    w_up = lax.all_gather(ffn_up, "dp", axis=1, tiled=True).T
    w_down = part_of(every(ffn_down, 1), 0, hidden).T

    token_ids = jnp.arange(micro)[:, None] * cap
    place = (routes[:, 0] * (micro * cap) + token_ids + slots[:, 0]).reshape(micro * seq)
    lens = jnp.broadcast_to(lengths, (micro, seq))
    results = run_layers(
        g, tokens.reshape(micro * seq, width), cotangent.reshape(micro * seq, width), lens,
        place[None, :], place[:, None], gains, shifts, b_out, b_down, b_up, w_router, router_row,
        w_qkv, w_out, w_up, w_down, expert_up[0], expert_down[0],
    )
    sec_out, sec_grad, small, g_bup, g_qkv, g_out, g_up, g_down, g_eup, g_edown = results

    def embed(array, shape, axis, size):
        return lax.dynamic_update_slice_in_dim(jnp.zeros(shape, F32), array, sec * size, axis)

    def share(array, axis, over=BOTH):
        return lax.psum_scatter(array, over, scatter_dimension=axis, tiled=True)

    g_qkv = g_qkv.reshape(2, 3, head_cols, width).transpose(0, 3, 1, 2)
    g_qkv = embed(g_qkv, (2, width, 3, width), 3, head_cols).reshape(2, width, 3 * width)
    g_out = embed(g_out, (2, width, width), 1, head_cols)
    g_down = embed(g_down.T, (hidden * sections, width), 0, hidden)
    g_router = lax.dynamic_update_slice_in_dim(jnp.zeros((width, experts), F32), small[12][:, None], dev // 2, 1)
    out_shape = (1, micro, 1, seq, width)
    return (
        sec_out.reshape(out_shape),
        sec_grad.reshape(out_shape),
        share(small[0:4], 1),
        share(small[4:8], 1),
        share(g_qkv, 2),
        share(g_out, 2),
        share(small[8:10], 1),
        share(g_up.T, 1, "dp"),
        share(g_bup[0], 0, "dp"),
        share(g_down, 1),
        share(small[10], 0),
        share(g_router, 0),
        g_eup[None],
        g_edown[None],
    )


def solution(mesh):
    batch = P(None, "dp", None, None)
    table = P(None, "dp", None)
    in_specs = (
        batch, batch, P(None, "dp"), table, table,
        P(None, BOTH), P(None, BOTH), P(None, None, BOTH), P(None, None, BOTH), P(None, BOTH),
        P(None, BOTH), P(BOTH), P(None, BOTH), P(BOTH), P(BOTH, None),
        P("dp", None, "section"), P("dp", "section", None),
    )
    streams = P("section", None, "dp", None, None)
    out_specs = (
        streams, streams,
        P(None, BOTH), P(None, BOTH), P(None, None, BOTH), P(None, None, BOTH), P(None, BOTH),
        P(None, BOTH), P(BOTH), P(None, BOTH), P(BOTH), P(BOTH, None),
        P("dp", None, "section"), P("dp", "section", None),
    )
    return jax.shard_map(body, mesh=mesh, in_specs=in_specs, out_specs=out_specs, check_vma=False)
```

```python
import functools
import types

import jax
import jax.numpy as jnp
from jax import lax
from jax.experimental import pallas as pl
from jax.experimental.pallas import tpu as pltpu
from jax.sharding import PartitionSpec as P

HEADS = 12
HEAD_DIM = 64
EPS = 1e-05
MASKED = -1000000000.0
MESH = pl.DeviceIdType.MESH
F32 = jnp.float32
BF16 = jnp.bfloat16
LANES = 128


def dot_as(left, right, left_dim, right_dim):
    return lax.dot_general(
        left, right, (((left_dim,), (right_dim,)), ((), ())), preferred_element_type=F32
    )


def mm(left, right):
    return dot_as(left, right, 1, 0)


def mm_nt(left, right):
    return dot_as(left, right, 1, 1)


def mm_tn(left, right):
    return dot_as(left, right, 0, 0)


def normalize(values):
    center = values - jnp.mean(values, axis=-1, keepdims=True)
    spread = jnp.mean(center * center, axis=-1, keepdims=True)
    inverse = lax.rsqrt(spread + EPS)
    return center * inverse, inverse


def gelu_parts(pre):
    half = 0.5 + 0.5 * lax.erf(pre * 0.7071067811865476)
    density = jnp.exp(-0.5 * pre * pre) * 0.3989422804014327
    return pre * half, half + pre * density


TAIL = 8
GROUP = 32
FIRST_ROUTER = 11


def layers_kernel(g, names, *refs):
    r = types.SimpleNamespace(**dict(zip(names, refs, strict=True)))
    width, span, hidden = g.width, g.span, g.hidden
    sec = lax.axis_index("section")
    dev = lax.axis_index("dp")
    core = lax.rem(dev, 2)
    chip = lax.div(dev, 2)
    sib = dev + 1 - 2 * core
    slot_rows = g.chips * span

    def peer_section(offset):
        return lax.rem(sec + offset, g.sections)

    def peer_chip(offset):
        return lax.rem(chip + offset, g.chips)

    def rows_at(index, size):
        return pl.ds(pl.multiple_of(index * size, size), size)

    def piece_at(index):
        return rows_at(index, g.piece)

    own = piece_at(sec)

    def remote(source, target, send, arrive, where):
        return pltpu.make_async_remote_copy(
            src_ref=source, dst_ref=target, send_sem=send, recv_sem=arrive, device_id=where, device_id_type=MESH
        )

    started = []

    def launch(copy):
        copy.start()
        started.append(copy)
        return copy

    barrier = pltpu.get_barrier_semaphore()
    partners = [(a, b) for a in range(g.sections) for b in range(g.chips) if a + b and (g.direct or a * b == 0)]
    for section_offset, chip_offset in partners:
        where = {"section": peer_section(section_offset), "dp": 2 * peer_chip(chip_offset) + core}
        pl.semaphore_signal(barrier, inc=1, device_id=where, device_id_type=MESH)
    pl.semaphore_signal(barrier, inc=1, device_id={"dp": sib}, device_id_type=MESH)
    pl.semaphore_wait(barrier, len(partners) + 1)

    def scatter_copy(slot, offset):
        return remote(
            r.part.at[slot, piece_at(peer_section(offset))], r.got.at[slot, offset - 1],
            r.scat_s.at[slot, offset - 1], r.scat_r.at[slot, offset - 1], {"section": peer_section(offset)},
        )

    def scatter_start(slot, value):
        r.part[slot] = value.astype(BF16)
        r.mine[...] = value
        for offset in range(1, g.sections):
            launch(scatter_copy(slot, offset))

    def scatter_sum(slot):
        total = r.mine[own, :]
        for offset in range(1, g.sections):
            scatter_copy(slot, offset).wait_recv()
            total = total + r.got[slot, offset - 1].astype(F32)
        return total

    def gather_copy(buffer, slot, sem, source, offset):
        return remote(
            buffer.at[slot, piece_at(source)], buffer.at[slot, piece_at(source)],
            r.gath_s.at[sem, offset - 1], r.gath_r.at[sem, offset - 1], {"section": peer_section(offset)},
        )

    def gather_start(buffer, slot, sem):
        for offset in range(1, g.sections):
            launch(gather_copy(buffer, slot, sem, sec, offset))

    def gather_wait(buffer, slot, sem):
        for offset in range(1, g.sections):
            source = lax.rem(sec + g.sections - offset, g.sections)
            gather_copy(buffer, slot, sem, source, offset).wait_recv()

    def disp_copy(which, source, target, offset):
        at_chip = peer_chip(offset)
        return remote(
            source.at[rows_at(at_chip, span)], target.at[core, rows_at(chip, span)],
            r.disp_s.at[which, offset - 1], r.disp_r.at[which, offset - 1], {"dp": 2 * at_chip + core},
        )

    def disp_start(which, source, target):
        for offset in range(1, g.chips):
            launch(disp_copy(which, source, target, offset))
        target[core, rows_at(chip, span), :] = source[rows_at(chip, span), :]

    def pair_copy(which, source, target):
        return remote(source, target, r.pair_s.at[which], r.pair_r.at[which], {"dp": sib})

    def disp_wait(which, source, target):
        for offset in range(1, g.chips):
            disp_copy(which, source, target, offset).wait_recv()
        launch(pair_copy(which, target.at[core], target.at[core]))

    def back_copy(which, source, target, offset):
        at_chip = peer_chip(offset)
        return remote(
            source.at[rows_at(at_chip, span)], target.at[rows_at(chip, span)],
            r.back_s.at[which, offset - 1], r.back_r.at[which, offset - 1], {"dp": 2 * at_chip + core},
        )

    def back_start(which, source, target):
        for offset in range(1, g.chips):
            launch(back_copy(which, source, target, offset))
        target[rows_at(chip, span), :] = source[rows_at(chip, span), :]

    def back_wait(which, source, target):
        for offset in range(1, g.chips):
            back_copy(which, source, target, offset).wait_recv()

    fold = g.cols - TAIL
    half = width // 2
    waiting = {}

    def turn(at_dev, index):
        return lax.div(3 * at_dev + index, g.devices)

    def qkv_section(at_dev, index, section):
        return lax.rem(turn(at_dev, index) - section + g.sections, g.sections)

    def qkv_send(layer):
        for index in range(3):
            to = qkv_section(dev, index, sec)
            for offset in range(g.chips):
                at_chip = peer_chip(offset)
                copy = remote(
                    r.pq.at[layer, index], r.rq.at[layer, core, chip, index],
                    r.wq_s.at[layer, index, offset], r.wq_r.at[layer, index, offset],
                    {"section": to, "dp": 2 * at_chip + core},
                )
                if offset:
                    launch(copy)
                else:

                    @pl.when(to != sec)
                    def _(copy=copy):
                        copy.start()

                    @pl.when(to == sec)
                    def _(index=index):
                        r.rq[layer, core, chip, index] = r.pq[layer, index]

    def qkv_arrive(layer):
        for index in range(3):
            for offset in range(g.chips):
                at_chip = lax.rem(chip + g.chips - offset, g.chips)
                target = r.rq.at[layer, core, at_chip, index]
                origin = qkv_section(2 * at_chip + core, index, sec)
                copy = remote(
                    target, target, r.wq_s.at[layer, index, offset], r.wq_r.at[layer, index, offset],
                    {"section": origin, "dp": 2 * at_chip + core},
                )
                if offset:
                    copy.wait_recv()
                else:

                    @pl.when(origin != sec)
                    def _(copy=copy):
                        copy.wait_recv()
                        copy.wait_send()

        waiting["qkv", layer] = pair_copy(4 + layer, r.rq.at[layer, core], r.rq.at[layer, core])
        waiting["qkv", layer].start()

    def settle(key, target):
        waiting[key].wait_send()
        pair_copy(waiting_slot[key], target, target).wait_recv()

    waiting_slot = {("qkv", 0): 4, ("qkv", 1): 5, "out": 6, "up": 7, "down": 8}

    def many_send(source, target, send, arrive):
        for section_offset in range(g.sections):
            for offset in range(g.chips):
                to, at_chip = peer_section(section_offset), peer_chip(offset)
                if section_offset + offset:
                    launch(remote(
                        source.at[to], target.at[core, chip, sec], send.at[section_offset, offset],
                        arrive.at[section_offset, offset], {"section": to, "dp": 2 * at_chip + core},
                    ))
        target[core, chip, sec] = source[sec]

    def many_arrive(target, send, arrive, key):
        for section_offset in range(g.sections):
            for offset in range(g.chips):
                origin = lax.rem(sec + g.sections - section_offset, g.sections)
                at_chip = lax.rem(chip + g.chips - offset, g.chips)
                if section_offset + offset:
                    place = target.at[core, at_chip, origin]
                    remote(
                        place, place, send.at[section_offset, offset], arrive.at[section_offset, offset],
                        {"section": origin, "dp": 2 * at_chip + core},
                    ).wait_recv()
        waiting[key] = pair_copy(waiting_slot[key], target.at[core], target.at[core])
        waiting[key].start()

    def up_copy(offset, at_chip, place):
        return remote(
            r.pu, r.ru.at[core, place], r.wu_s.at[offset - 1], r.wu_r.at[offset - 1], {"dp": 2 * at_chip + core}
        )

    def up_send():
        for offset in range(1, g.chips):
            launch(up_copy(offset, peer_chip(offset), chip))
        r.ru[core, chip] = r.pu[...]

    def up_arrive():
        for offset in range(1, g.chips):
            at_chip = lax.rem(chip + g.chips - offset, g.chips)
            up_copy(offset, at_chip, at_chip).wait_recv()
        waiting["up"] = pair_copy(7, r.ru.at[core], r.ru.at[core])
        waiting["up"].start()

    def unfold_wide(target, first, piece):
        target[first : first + fold, 0:width] = piece[:, 0:width]
        target[first + fold : first + g.cols, 0:half] = piece[0:TAIL, width:]
        target[first + fold : first + g.cols, half:width] = piece[TAIL:, width:]

    def fold_wide(source, first):
        tail = source[first + fold : first + g.cols, 0:width]
        tail = jnp.concatenate([tail[:, :half], tail[:, half:]], axis=0)
        return jnp.concatenate([source[first : first + fold, 0:width], tail], axis=1).astype(BF16)

    part_cols = g.head_cols // 2
    tail_lane = g.head_cols + 2 * GROUP

    def unfold_out(layer):
        for at_core in range(2):
            for at_chip in range(g.chips):
                for at_sec in range(g.sections):
                    piece = r.ro[at_core, at_chip, at_sec, layer].astype(F32)
                    first = (at_sec * g.devices + 2 * at_chip + at_core) * g.cols
                    last = slice(first + fold, first + g.cols)
                    r.tmp[first : first + fold, 0:tail_lane] = piece[:, 0:tail_lane]
                    r.tmp[last, 0:part_cols] = piece[0:TAIL, tail_lane : tail_lane + part_cols]
                    r.tmp[last, part_cols : 2 * part_cols] = piece[TAIL:, tail_lane : tail_lane + part_cols]
                    r.tmp[last, g.head_cols : g.head_cols + GROUP] = piece[0:TAIL, g.head_cols + GROUP : tail_lane]
        flipped = r.tmp[:, 0:tail_lane].T
        r.w_out[layer] = flipped[: g.head_cols].astype(BF16)
        if layer == 0:
            r.prm[...] = flipped[g.head_cols : g.head_cols + GROUP]
            r.w_router[...] = r.tmp[:, tail_lane - LANES : tail_lane].astype(BF16)

    def fold_out(layer):
        for at_core in range(2):
            for at_chip in range(g.chips):
                for at_sec in range(g.sections):
                    first = (at_sec * g.devices + 2 * at_chip + at_core) * g.cols
                    top = r.tmp[first : first + fold, 0 : g.head_cols + GROUP]
                    last = r.tmp[first + fold : first + g.cols, 0 : g.head_cols + GROUP]
                    small = jnp.concatenate([last[:, g.head_cols :], last[:, g.head_cols :]], axis=0)
                    tail = jnp.concatenate([last[:, :part_cols], last[:, part_cols : 2 * part_cols]], axis=0)
                    empty = jnp.zeros((fold, g.out_lanes - tail_lane - part_cols), F32)
                    r.ro[at_core, at_chip, at_sec, layer] = jnp.concatenate(
                        [top, small, tail, empty], axis=1
                    ).astype(BF16)

    def chunk_places():
        for at_core in range(2):
            for at_chip in range(g.chips):
                for index in range(3):
                    first = (3 * (2 * at_chip + at_core) + index) * g.cols
                    yield at_core, at_chip, index, first

    def unfold_qkv(layer):
        for at_core, at_chip, index, first in chunk_places():
            unfold_wide(r.tmp, first, r.rq[layer, at_core, at_chip, index].astype(F32))
        r.w_qkv[layer] = r.tmp[0 : 3 * g.head_cols, 0:width].astype(BF16)

    def unfold_down():
        for at_core in range(2):
            for at_chip in range(g.chips):
                for at_sec in range(g.sections):
                    first = (at_sec * g.devices + 2 * at_chip + at_core) * g.cols
                    unfold_wide(r.tmp, first, r.rd[at_core, at_chip, at_sec].astype(F32))
        r.w_down[...] = r.tmp[...].astype(BF16)

    def grad_pair(slot, buffer, landing):
        copy = pair_copy(slot, buffer.at[1 - core], landing)
        launch(copy)

    def grad_merge(slot, buffer, landing):
        pair_copy(slot, buffer.at[1 - core], landing).wait_recv()
        for at_chip in range(g.chips):
            total = buffer[core, at_chip].astype(F32) + landing[at_chip].astype(F32)
            buffer[core, at_chip] = total.astype(BF16)

    def grad_qkv_send(layer):
        grad_merge(9 + layer, r.rq.at[layer], r.hq.at[layer])
        for index in range(3):
            for offset in range(g.chips):
                at_chip = peer_chip(offset)
                to = qkv_section(2 * at_chip + core, index, sec)
                copy = remote(
                    r.rq.at[layer, core, at_chip, index], r.aq.at[layer, chip, index],
                    r.gq_s.at[layer, index, offset], r.gq_r.at[layer, index, offset],
                    {"section": to, "dp": 2 * at_chip + core},
                )
                if offset:
                    launch(copy)
                else:

                    @pl.when(to != sec)
                    def _(copy=copy):
                        copy.start()

                    @pl.when(to == sec)
                    def _(index=index):
                        r.aq[layer, chip, index] = r.rq[layer, core, chip, index]

    def grad_qkv_finish(layer):
        for index in range(3):
            for offset in range(g.chips):
                at_chip = lax.rem(chip + g.chips - offset, g.chips)
                origin = qkv_section(dev, index, sec)
                place = r.aq.at[layer, at_chip, index]
                copy = remote(
                    place, place, r.gq_s.at[layer, index, offset], r.gq_r.at[layer, index, offset],
                    {"section": origin, "dp": 2 * at_chip + core},
                )
                if offset:
                    copy.wait_recv()
                else:

                    @pl.when(origin != sec)
                    def _(copy=copy):
                        copy.wait_recv()
                        copy.wait_send()

            total = r.aq[layer, 0, index].astype(F32)
            for at_chip in range(1, g.chips):
                total = total + r.aq[layer, at_chip, index].astype(F32)
            unfold_wide(r.o_qkv.at[layer, index], 0, total)

    def grad_many_send(slot, buffer, landing, target, send, arrive):
        grad_merge(slot, buffer, landing)
        for section_offset in range(g.sections):
            for offset in range(g.chips):
                to, at_chip = peer_section(section_offset), peer_chip(offset)
                if section_offset + offset:
                    launch(remote(
                        buffer.at[core, at_chip, to], target.at[chip, sec], send.at[section_offset, offset],
                        arrive.at[section_offset, offset], {"section": to, "dp": 2 * at_chip + core},
                    ))
        target[chip, sec] = buffer[core, chip, sec]

    def grad_many_arrive(target, send, arrive):
        for section_offset in range(g.sections):
            for offset in range(g.chips):
                origin = lax.rem(sec + g.sections - section_offset, g.sections)
                at_chip = lax.rem(chip + g.chips - offset, g.chips)
                if section_offset + offset:
                    place = target.at[at_chip, origin]
                    remote(
                        place, place, send.at[section_offset, offset], arrive.at[section_offset, offset],
                        {"section": origin, "dp": 2 * at_chip + core},
                    ).wait_recv()

    def grad_up_copy(offset, at_chip, place):
        return remote(
            r.ru.at[core, at_chip], r.au.at[place], r.gu_s.at[offset - 1], r.gu_r.at[offset - 1],
            {"dp": 2 * at_chip + core},
        )

    def grad_up_send():
        grad_merge(13, r.ru, r.hu)
        for offset in range(1, g.chips):
            launch(grad_up_copy(offset, peer_chip(offset), chip))
        r.au[chip] = r.ru[core, chip]

    def norm_into(source, target, index):
        @pl.loop(0, g.sections)
        def _(step):
            at = piece_at(step)
            unit, _ = normalize(source[at, :].astype(F32))
            target[at, :] = (unit * r.prm[index : index + 1, :] + r.prm[4 + index : 5 + index, :]).astype(BF16)

    if g.direct:
        many_send(r.po, r.ro, r.wo_s, r.wo_r)
        qkv_send(0)
    slot_ids = lax.broadcasted_iota(jnp.int32, r.table.shape, 0)
    r.table[...] = jnp.where(slot_ids == r.place_row[...], 1.0, 0.0).astype(BF16)
    r.dispc[...] = mm(r.table[...], r.cot[...]).astype(BF16)
    r.small[...] = jnp.zeros_like(r.small)
    if g.direct:
        many_arrive(r.ro, r.wo_s, r.wo_r, "out")
        qkv_arrive(0)
        up_send()
        many_send(r.pd, r.rd, r.wd_s, r.wd_r)
        qkv_send(1)
        settle("out", r.ro.at[1 - core])
        unfold_out(0)
        settle(("qkv", 0), r.rq.at[0, 1 - core])
        unfold_qkv(0)

    key_ids = lax.broadcasted_iota(jnp.int32, (g.seq, g.seq), 0)
    query_ids = lax.broadcasted_iota(jnp.int32, (g.seq, g.seq), 1)
    scale = HEAD_DIM**-0.5

    def block_of(index):
        return lax.rem(index + sec, 3) if g.direct else index

    def head_slice(head):
        return slice(head * HEAD_DIM, (head + 1) * HEAD_DIM)

    def token_slice(micro):
        return slice(micro * g.seq, (micro + 1) * g.seq)

    def attention_forward(layer, stream, slot):
        norm_into(stream, r.normed.at[2 * layer], 2 * layer)
        packed = mm_nt(r.w_qkv[layer], r.normed[2 * layer]).astype(BF16)
        r.qkv[layer] = packed.reshape(3, g.head_cols, g.tokens)
        for micro in range(g.micro):
            allowed = (key_ids <= query_ids) & (key_ids < r.lens[micro : micro + 1, :])
            for head in range(g.heads):
                at = token_slice(micro)
                key = r.qkv[layer, block_of(1), head_slice(head), at]
                scores = mm_tn(key, r.qkv[layer, block_of(0), head_slice(head), at]) * scale
                scores = jnp.where(allowed, scores, MASKED)
                weight = jnp.exp(scores - jnp.max(scores, axis=0, keepdims=True))
                weight = weight / jnp.sum(weight, axis=0, keepdims=True)
                r.probs[layer, micro, head] = weight
                value = r.qkv[layer, block_of(2), head_slice(head), at]
                r.ctx[layer, head_slice(head), at] = mm(value, weight.astype(BF16)).astype(BF16)
        scatter_start(slot, mm_tn(r.ctx[layer], r.w_out[layer]))

    def finish_forward(section, bias, stream):
        total = scatter_sum(section) + bias + stream[own, :].astype(F32)
        r.xs[section, own, :] = total.astype(BF16)
        gather_start(r.xs, section, section)

    attention_forward(0, r.x0, 0)
    if g.direct:
        unfold_out(1)
    finish_forward(0, r.prm[8:9, :], r.x0)
    if g.direct:
        up_arrive()
        settle("up", r.ru.at[1 - core])
        r.b_up[...] = r.ru[:, :, :, width:].reshape(hidden, LANES).astype(F32).T[0:8, :]
    gather_wait(r.xs, 0, 0)

    def up_rows(at):
        if g.direct:
            return r.ru[:, :, :, :width].reshape(hidden, width)[at]
        return r.w_up[at, :]

    norm_into(r.xs.at[0], r.normed.at[1], 1)
    for block in range(hidden // g.block):
        at = slice(block * g.block, (block + 1) * g.block)
        pre = mm_nt(r.normed[1], up_rows(at)) + r.b_up[0:1, at]
        value, slope = gelu_parts(pre)
        r.act[:, at] = value.astype(BF16)
        r.dgelu[:, at] = slope
    if g.direct:
        many_arrive(r.rd, r.wd_s, r.wd_r, "down")
        settle("down", r.rd.at[1 - core])
        unfold_down()
    scatter_start(1, mm_nt(r.act[...], r.w_down[...]))
    if g.direct:
        qkv_arrive(1)
    finish_forward(1, r.prm[10:11, :], r.xs.at[0])
    if g.direct:
        settle(("qkv", 1), r.rq.at[1, 1 - core])
        unfold_qkv(1)
    gather_wait(r.xs, 1, 1)

    attention_forward(1, r.xs.at[1], 2)
    disp_start(0, r.dispc, r.crow)
    finish_forward(2, r.prm[9:10, :], r.xs.at[1])
    gather_wait(r.xs, 2, 2)

    wide = r.wide
    norm_into(r.xs.at[2], wide.at[:, pl.ds(0, width)], 3)
    logits = mm(wide[:, :width], r.w_router[...])
    lane = lax.broadcasted_iota(jnp.int32, logits.shape, 1) - g.router_lane
    chosen = (r.place_col[...] >= lane * span) & (r.place_col[...] < lane * span + span)
    score = jnp.sum(jnp.where(chosen, logits, 0.0), axis=-1, keepdims=True)
    gate = 1.0 / (1.0 + jnp.exp(-score))
    gate_high = gate.astype(BF16).astype(F32)
    lane = lax.broadcasted_iota(jnp.int32, (g.tokens, LANES), 1)
    pair = jnp.where(lane == 0, gate_high, jnp.where(lane == 1, gate - gate_high, 0.0))
    wide[:, width:] = pair.astype(BF16)
    r.disp[...] = mm(r.table[...], wide[...]).astype(BF16)
    disp_start(1, r.disp, r.rows)
    disp_wait(0, r.dispc, r.crow)
    disp_wait(1, r.disp, r.rows)

    own_router = FIRST_ROUTER + chip
    router_row = r.prm[pl.ds(own_router, 1), :]

    def expert_block(side, at, keep_first):
        row = r.rows[side, at, :width]
        tail = r.rows[side, at, width:].astype(F32)
        gate_row = tail[:, 0:1] + tail[:, 1:2]
        grad_row = (gate_row * r.crow[side, at, :].astype(F32)).astype(BF16)
        r.grow[side, at, :] = grad_row
        value, slope = gelu_parts(mm(row, r.e_up[...]))
        value = value.astype(BF16)
        r.acte[side, at, :] = value
        result = mm(value, r.e_down[...])
        total = jnp.sum(grad_row.astype(F32) * result, axis=-1, keepdims=True) * (1.0 - gate_row)
        inner = (slope * mm_nt(grad_row, r.e_down[...])).astype(BF16)
        r.dpree[side, at, :] = inner
        back = mm_nt(inner, r.e_up[...]) + total * router_row
        r.small[pl.ds(own_router, 1), :] += jnp.sum(row.astype(F32) * total, axis=0, keepdims=True)
        result = result * gate_row
        if keep_first:
            r.keep_d[at, :] = back
            r.keep_y[at, :] = result
        else:
            r.snd_d[at, :] = back.astype(BF16)
            r.snd_y[at, :] = result.astype(BF16)

    @pl.loop(0, slot_rows // g.block)
    def _(step):
        expert_block(core, rows_at(step, g.block), True)

    pair_copy(0, r.crow.at[1 - core], r.crow.at[1 - core]).wait_recv()
    pair_copy(1, r.rows.at[1 - core], r.rows.at[1 - core]).wait_recv()

    @pl.loop(0, slot_rows // g.block)
    def _(step):
        expert_block(1 - core, rows_at(step, g.block), False)

    launch(pair_copy(2, r.snd_d, r.rcv_d))
    launch(pair_copy(3, r.snd_y, r.rcv_y))
    pair_copy(2, r.snd_d, r.rcv_d).wait_recv()
    r.out_d[...] = (r.keep_d[...] + r.rcv_d[...].astype(F32)).astype(BF16)
    back_start(0, r.out_d, r.back_d)
    pair_copy(3, r.snd_y, r.rcv_y).wait_recv()
    r.out_y[...] = (r.keep_y[...] + r.rcv_y[...].astype(F32)).astype(BF16)
    back_start(1, r.out_y, r.back_y)
    r.g_eup[...] = mm_tn(r.rows[0, :, :width], r.dpree[0]) + mm_tn(r.rows[1, :, :width], r.dpree[1])
    r.g_edown[...] = mm_tn(r.acte[0], r.grow[0]) + mm_tn(r.acte[1], r.grow[1])

    def finish_backward(section, slot, stream, above):
        grad = scatter_sum(slot)
        unit, inverse = normalize(stream[own, :].astype(F32))
        r.small[section : section + 1, :] = jnp.sum(grad * unit, axis=0, keepdims=True)
        r.small[4 + section : 5 + section, :] = jnp.sum(grad, axis=0, keepdims=True)
        grad = grad * r.prm[section : section + 1, :]
        shared = jnp.mean(grad, axis=-1, keepdims=True)
        along = jnp.mean(grad * unit, axis=-1, keepdims=True)
        grad = inverse * (grad - shared - unit * along) + above[own, :].astype(F32)
        r.gs[section, own, :] = grad.astype(BF16)
        gather_start(r.gs, section, 4 + section)

    back_wait(0, r.out_d, r.back_d)
    scatter_start(3, mm_tn(r.table[...], r.back_d[...]))
    finish_backward(3, 3, r.xs.at[2], r.cot)
    gather_wait(r.gs, 3, 7)

    def bias_row(index, section):
        r.small[index : index + 1, :] = jnp.sum(r.gs[section, own, :].astype(F32), axis=0, keepdims=True)

    def attention_backward(layer, section, slot):
        grad = r.gs[section + 1]
        dctx = mm_nt(r.w_out[layer], grad).astype(BF16)
        for micro in range(g.micro):
            for head in range(g.heads):
                at = token_slice(micro)
                weight = r.probs[layer, micro, head]
                low = weight.astype(BF16)
                dhead = dctx[head_slice(head), at]
                query = r.qkv[layer, block_of(0), head_slice(head), at]
                key = r.qkv[layer, block_of(1), head_slice(head), at]
                value = r.qkv[layer, block_of(2), head_slice(head), at]
                dprobs = mm_tn(value, dhead)
                delta = jnp.sum(weight * dprobs, axis=0, keepdims=True)
                dscores = (weight * (dprobs - delta)).astype(BF16)
                r.dqkv[block_of(0), head_slice(head), at] = (mm(key, dscores) * scale).astype(BF16)
                r.dqkv[block_of(1), head_slice(head), at] = (mm_nt(query, dscores) * scale).astype(BF16)
                r.dqkv[block_of(2), head_slice(head), at] = mm_nt(dhead, low).astype(BF16)
        flat = r.dqkv[...].reshape(3 * g.head_cols, g.tokens)
        scatter_start(slot, mm_tn(flat, r.w_qkv[layer]))
        bias_row(8 + layer, section + 1)

    def attention_weights(layer, section):
        flat = r.dqkv[...].reshape(3 * g.head_cols, g.tokens)
        grad_qkv = mm(flat, r.normed[2 * layer])
        if not g.direct:
            r.o_qkv[layer] = grad_qkv
            r.o_out[layer] = mm(r.ctx[layer], r.gs[section + 1])
            return
        r.tmp[0 : 3 * g.head_cols, :] = grad_qkv
        for at_core, at_chip, index, first in chunk_places():
            r.rq[layer, at_core, at_chip, index] = fold_wide(r.tmp, first)
        grad_pair(9 + layer, r.rq.at[layer], r.hq.at[layer])
        r.tmp[:, 0 : g.head_cols] = dot_as(r.gs[section + 1], r.ctx[layer], 0, 1)

    attention_backward(1, 2, 4)
    attention_weights(1, 2)
    if g.direct:
        r.tmp[:, g.head_cols : g.head_cols + GROUP] = jnp.zeros((width, GROUP), F32)
        fold_out(1)
        grad_pair(11, r.ro.at[:, :, :, 1], r.ho.at[1])
    finish_backward(2, 4, r.xs.at[1], r.gs.at[3])
    if g.direct:
        grad_qkv_send(1)
    gather_wait(r.gs, 2, 6)

    grad_two = r.gs[2]
    for block in range(hidden // g.block):
        at = slice(block * g.block, (block + 1) * g.block)
        r.dpre[:, at] = (r.dgelu[:, at] * mm(grad_two, r.w_down[:, at])).astype(BF16)
    scatter_start(5, mm(r.dpre[...], up_rows(slice(None))))
    bias_row(10, 2)
    sum_up = jnp.sum(r.dpre[...].astype(F32), axis=0, keepdims=True)
    if g.direct:
        grad_many_send(11, r.ro.at[:, :, :, 1], r.ho.at[1], r.ao.at[1], r.go_s.at[1], r.go_r.at[1])
        r.tmp[...] = mm_tn(r.gs[2], r.act[...])
        for at_core in range(2):
            for at_chip in range(g.chips):
                for at_sec in range(g.sections):
                    first = (at_sec * g.devices + 2 * at_chip + at_core) * g.cols
                    r.rd[at_core, at_chip, at_sec] = fold_wide(r.tmp, first)
        grad_pair(12, r.rd, r.hd)
        up_shape = (2, g.chips, hidden // g.devices, width)
        r.ru[:, :, :, 0:width] = mm_tn(r.dpre[...], r.normed[1]).astype(BF16).reshape(up_shape)
        column = jnp.broadcast_to(sum_up, (LANES, hidden)).T.astype(BF16)
        r.ru[:, :, :, width:] = column.reshape(2, g.chips, hidden // g.devices, LANES)
        grad_pair(13, r.ru, r.hu)
    else:
        r.o_down[...] = mm_tn(r.gs[2], r.act[...])
        r.o_up[...] = mm_tn(r.dpre[...], r.normed[1])
        r.o_bup[...] = jnp.broadcast_to(sum_up, r.o_bup.shape)
    finish_backward(1, 5, r.xs.at[0], r.gs.at[2])
    if g.direct:
        grad_many_send(12, r.rd, r.hd, r.ad, r.gd_s, r.gd_r)
        grad_up_send()
    gather_wait(r.gs, 1, 5)

    attention_backward(0, 0, 6)
    attention_weights(0, 0)
    finish_backward(0, 6, r.x0, r.gs.at[1])
    if g.direct:
        kinds = r.small[...]
        padded = jnp.concatenate([kinds, jnp.zeros((LANES - kinds.shape[0], width), F32)], axis=0)
        r.tmp[:, g.head_cols : g.head_cols + GROUP] = padded.T[:, 0:GROUP]
        fold_out(0)
        grad_pair(14, r.ro.at[:, :, :, 0], r.ho.at[0])
        grad_qkv_send(0)
        grad_many_send(14, r.ro.at[:, :, :, 0], r.ho.at[0], r.ao.at[0], r.go_s.at[0], r.go_r.at[0])

    back_wait(1, r.out_y, r.back_y)
    scatter_start(7, mm_tn(r.table[...], r.back_y[...]))
    r.xs[3, own, :] = (scatter_sum(7) + r.xs[2, own, :].astype(F32)).astype(BF16)
    gather_start(r.xs, 3, 3)
    if g.direct:
        grad_qkv_finish(1)
        grad_many_arrive(r.ad, r.gd_s, r.gd_r)
        for at_sec in range(g.sections):
            total = r.ad[0, at_sec].astype(F32)
            for at_chip in range(1, g.chips):
                total = total + r.ad[at_chip, at_sec].astype(F32)
            unfold_wide(r.o_down.at[at_sec], 0, total)
        for offset in range(1, g.chips):
            at_chip = lax.rem(chip + g.chips - offset, g.chips)
            grad_up_copy(offset, at_chip, at_chip).wait_recv()
        total = r.au[0].astype(F32)
        for at_chip in range(1, g.chips):
            total = total + r.au[at_chip].astype(F32)
        r.o_up[...] = total
        grad_qkv_finish(0)
        everyone = jnp.zeros((fold, tail_lane), F32)
        for layer in (1, 0):
            grad_many_arrive(r.ao.at[layer], r.go_s.at[layer], r.go_r.at[layer])
            for at_sec in range(g.sections):
                total = r.ao[layer, 0, at_sec].astype(F32)
                for at_chip in range(1, g.chips):
                    total = total + r.ao[layer, at_chip, at_sec].astype(F32)
                r.o_out[layer, at_sec, 0:fold, :] = total[:, 0:tail_lane]
                tails = slice(tail_lane, tail_lane + part_cols)
                r.o_out[layer, at_sec, fold : g.cols, 0:part_cols] = total[0:TAIL, tails]
                r.o_out[layer, at_sec, fold : g.cols, part_cols : 2 * part_cols] = total[TAIL:, tails]
                if layer == 0:
                    everyone = everyone + total[:, 0:tail_lane]
        r.o_small[0:fold, 0:GROUP] = everyone[:, g.head_cols : g.head_cols + GROUP]
        r.o_small[fold : g.cols, 0:GROUP] = everyone[0:TAIL, g.head_cols + GROUP : tail_lane]
    else:
        r.o_small[...] = r.small[...]
    gather_wait(r.xs, 3, 3)
    gather_wait(r.gs, 0, 4)
    r.sec_out[...] = r.xs[sec].astype(F32)
    r.sec_grad[...] = r.gs[sec].astype(F32)
    for copy in started:
        copy.wait_send()


def run_layers(g, operands):
    tokens, width, hidden, sections, chips = g.tokens, g.width, g.hidden, g.sections, g.chips
    slots = chips * g.span
    inner = operands["e_down"].shape[0]
    three = 3 * g.head_cols
    shape = jax.ShapeDtypeStruct
    vmem = pltpu.VMEM
    dma = pltpu.SemaphoreType.DMA
    top = g.cols - TAIL
    wide = width + width // 2
    up_rows = hidden // g.devices
    outs = {
        "sec_out": shape((tokens, width), F32),
        "sec_grad": shape((tokens, width), F32),
        "g_eup": shape((width, inner), F32),
        "g_edown": shape((inner, width), F32),
    }
    if g.direct:
        outs |= {
            "o_qkv": shape((2, 3, g.cols, width), F32),
            "o_out": shape((2, sections, g.cols, g.head_cols + 2 * GROUP), F32),
            "o_up": shape((up_rows, width + LANES), F32),
            "o_down": shape((sections, g.cols, width), F32),
            "o_small": shape((g.cols, LANES), F32),
        }
    else:
        outs |= {
            "o_qkv": shape((2, three, width), F32),
            "o_out": shape((2, g.head_cols, width), F32),
            "o_up": shape((hidden, width), F32),
            "o_down": shape((width, hidden), F32),
            "o_bup": shape((8, hidden), F32),
            "o_small": shape((g.small, width), F32),
        }
    scratch = {
        "xs": vmem((4, tokens, width), BF16),
        "gs": vmem((4, tokens, width), BF16),
        "normed": vmem((3, tokens, width), BF16),
        "wide": vmem((tokens, width + LANES), BF16),
        "qkv": vmem((2, 3, g.head_cols, tokens), BF16),
        "probs": vmem((2, g.micro, g.heads, g.seq, g.seq), F32),
        "ctx": vmem((2, g.head_cols, tokens), BF16),
        "act": vmem((tokens, hidden), BF16),
        "dgelu": vmem((tokens, hidden), F32),
        "dpre": vmem((tokens, hidden), BF16),
        "dqkv": vmem((3, g.head_cols, tokens), BF16),
        "part": vmem((8, tokens, width), BF16),
        "got": vmem((8, sections - 1, g.piece, width), BF16),
        "mine": vmem((tokens, width), F32),
        "table": vmem((slots, tokens), BF16),
        "disp": vmem((slots, width + LANES), BF16),
        "dispc": vmem((slots, width), BF16),
        "rows": vmem((2, slots, width + LANES), BF16),
        "crow": vmem((2, slots, width), BF16),
        "grow": vmem((2, slots, width), BF16),
        "acte": vmem((2, slots, inner), BF16),
        "dpree": vmem((2, slots, inner), BF16),
        "keep_d": vmem((slots, width), F32),
        "keep_y": vmem((slots, width), F32),
        "small": vmem((g.small, width), F32),
    }
    for name in ("snd_d", "snd_y", "rcv_d", "rcv_y", "out_d", "out_y", "back_d", "back_y"):
        scratch[name] = vmem((slots, width), BF16)
    for name in ("scat_s", "scat_r", "gath_s", "gath_r"):
        scratch[name] = dma((8, sections - 1))
    for name in ("disp_s", "disp_r", "back_s", "back_r"):
        scratch[name] = dma((2, chips - 1))
    scratch |= {"pair_s": dma((15,)), "pair_r": dma((15,))}
    if g.direct:
        scratch |= {
            "rq": vmem((2, 2, chips, 3, top, wide), BF16),
            "ro": vmem((2, chips, sections, 2, top, g.out_lanes), BF16),
            "ru": vmem((2, chips, up_rows, width + LANES), BF16),
            "rd": vmem((2, chips, sections, top, wide), BF16),
            "w_qkv": vmem((2, three, width), BF16),
            "w_out": vmem((2, g.head_cols, width), BF16),
            "w_down": vmem((width, hidden), BF16),
            "w_router": vmem((width, LANES), BF16),
            "b_up": vmem((8, hidden), F32),
            "prm": vmem((GROUP, width), F32),
            "tmp": vmem((width, width), F32),
            "hq": vmem((2, chips, 3, top, wide), BF16),
            "ho": vmem((2, chips, sections, top, g.out_lanes), BF16),
            "hu": vmem((chips, up_rows, width + LANES), BF16),
            "hd": vmem((chips, sections, top, wide), BF16),
            "aq": vmem((2, chips, 3, top, wide), BF16),
            "ao": vmem((2, chips, sections, top, g.out_lanes), BF16),
            "au": vmem((chips, up_rows, width + LANES), BF16),
            "ad": vmem((chips, sections, top, wide), BF16),
        }
        for name in ("wq", "gq"):
            scratch |= {name + "_s": dma((2, 3, chips)), name + "_r": dma((2, 3, chips))}
        for name in ("wo", "wd", "gd"):
            scratch |= {name + "_s": dma((sections, chips)), name + "_r": dma((sections, chips))}
        scratch |= {"go_s": dma((2, sections, chips)), "go_r": dma((2, sections, chips))}
        for name in ("wu", "gu"):
            scratch |= {name + "_s": dma((chips - 1,)), name + "_r": dma((chips - 1,))}
    whole = pl.BlockSpec(memory_space=pltpu.VMEM)
    names = (*operands, *outs, *scratch)
    results = pl.pallas_call(
        functools.partial(layers_kernel, g, names),
        out_shape=tuple(outs.values()),
        in_specs=[whole] * len(operands),
        out_specs=[whole] * len(outs),
        scratch_shapes=list(scratch.values()),
        compiler_params=pltpu.CompilerParams(
            collective_id=0, has_side_effects=True, vmem_limit_bytes=62 * 1024 * 1024
        ),
    )(*operands.values())
    return types.SimpleNamespace(**dict(zip(outs, results, strict=True)))


BOTH = ("section", "dp")


def fold_rows(array):
    *lead, rows, columns = array.shape
    tail = array[..., rows - TAIL :, :].reshape(*lead, TAIL, 2, columns // 2)
    tail = jnp.swapaxes(tail, -3, -2).reshape(*lead, 2 * TAIL, columns // 2)
    return array[..., : rows - TAIL, :], tail


def body(
    tokens, cotangent, lengths, routes, slots, norm_gain, norm_bias, attn_qkv, attn_out, attn_out_bias,
    ffn_up, ffn_up_bias, ffn_down, ffn_down_bias, router, expert_up, expert_down,
):
    sections, devices = lax.axis_size("section"), lax.axis_size("dp")
    sec, dev = lax.axis_index("section"), lax.axis_index("dp")
    micro, _, seq, width = tokens.shape
    experts = router.shape[1]
    chips = devices // 2
    head_cols = width // sections
    hidden = ffn_up.shape[1] * devices
    cap = 2 * seq // experts
    cols = ffn_down.shape[1]
    kinds = FIRST_ROUTER + experts
    direct = cols == 3 * TAIL and kinds <= GROUP and sections == 4 and ffn_up.shape[1] % 16 == 0
    g = types.SimpleNamespace(
        sections=sections, devices=devices, chips=chips, micro=micro, seq=seq, width=width, hidden=hidden,
        span=micro * cap, tokens=micro * seq, piece=micro * seq // sections, heads=head_cols // HEAD_DIM,
        head_cols=head_cols, cols=cols, block=256, small=-(-kinds // 8) * 8, direct=direct,
        out_lanes=head_cols + 2 * GROUP + LANES,
        router_lane=FIRST_ROUTER + (LANES - 2 * GROUP if direct else 0),
    )

    place = (routes[:, 0] * g.span + jnp.arange(micro)[:, None] * cap + slots[:, 0]).reshape(g.tokens)
    operands = {
        "x0": tokens.reshape(g.tokens, width),
        "cot": cotangent.reshape(g.tokens, width),
        "lens": jnp.broadcast_to(lengths, (micro, seq)),
        "place_row": place[None, :],
        "place_col": place[:, None],
        "e_up": expert_up[0],
        "e_down": expert_down[0],
    }
    if direct:
        mine = [norm_gain, norm_bias, attn_out_bias, ffn_down_bias[None], router.T]
        mine = jnp.concatenate(mine, axis=0).T
        mine = jnp.pad(mine, ((0, TAIL), (0, GROUP - kinds)))
        mine = jnp.concatenate([mine[: 2 * TAIL], mine[2 * TAIL :]], axis=1)
        mine = jnp.broadcast_to(mine, (sections, 2, 2 * TAIL, 2 * GROUP))
        shard = attn_out.transpose(0, 2, 1).reshape(2, cols, sections, head_cols).transpose(2, 0, 1, 3)
        top, tail = fold_rows(shard)
        spare = jnp.zeros((sections, 2, 2 * TAIL, LANES - head_cols // 2), BF16)
        operands["po"] = jnp.concatenate([top, mine, tail, spare], axis=-1)
        shard = attn_qkv.transpose(0, 2, 1).reshape(2, 3, cols, width)
        operands["pq"] = jnp.concatenate(fold_rows(shard), axis=-1)
        operands["pu"] = jnp.concatenate(
            [ffn_up.T, ffn_up_bias[:, None], jnp.zeros((ffn_up.shape[1], LANES - 1), BF16)], axis=1
        )
        shard = ffn_down.T.reshape(cols, sections, chips, 2, hidden // devices)
        shard = shard.transpose(1, 0, 3, 2, 4).reshape(sections, cols, hidden)
        operands["pd"] = jnp.concatenate(fold_rows(shard), axis=-1)
    else:

        def every(array, axis):
            return lax.all_gather(array, BOTH, axis=axis, tiled=True)

        def part_of(array, axis, size):
            return lax.dynamic_slice_in_dim(array, sec * size, size, axis)

        rows = [norm_gain, norm_bias, attn_out_bias, ffn_down_bias[None], router.T]
        params = every(jnp.concatenate(rows, axis=0), 1)
        params = jnp.pad(params, ((0, LANES - kinds), (0, 0)))
        b_up = lax.all_gather(ffn_up_bias, "dp", axis=0, tiled=True).astype(F32)
        full = part_of(every(attn_qkv, 2).reshape(2, width, 3, width), 3, head_cols)
        operands |= {
            "prm": params.astype(F32),
            "w_router": params.T,
            "b_up": jnp.broadcast_to(b_up, (8, hidden)),
            "w_qkv": full.transpose(0, 2, 3, 1).reshape(2, 3 * head_cols, width),
            "w_out": part_of(every(attn_out, 2), 1, head_cols),
            "w_up": lax.all_gather(ffn_up, "dp", axis=1, tiled=True).T,
            "w_down": part_of(every(ffn_down, 1), 0, hidden).T,
        }
    res = run_layers(g, operands)

    if direct:
        small = res.o_small[:, :kinds].T
        b_up_grad = res.o_up[:, width]
        grads = (
            small[0:4],
            small[4:8],
            res.o_qkv.reshape(2, 3 * cols, width).transpose(0, 2, 1),
            res.o_out[..., :head_cols].transpose(0, 1, 3, 2).reshape(2, width, cols),
            small[8:10],
            res.o_up[:, :width].T,
            b_up_grad,
            res.o_down.reshape(sections, cols, 2, chips, hidden // devices)
            .transpose(0, 3, 2, 4, 1)
            .reshape(sections * hidden, cols),
            small[10],
            small[FIRST_ROUTER:].T,
        )
    else:

        def embed(array, shape, axis, size):
            return lax.dynamic_update_slice_in_dim(jnp.zeros(shape, F32), array, sec * size, axis)

        def share(array, axis, over=BOTH):
            return lax.psum_scatter(array, over, scatter_dimension=axis, tiled=True)

        small = share(res.o_small[:kinds], 1)
        g_qkv = res.o_qkv.reshape(2, 3, head_cols, width).transpose(0, 3, 1, 2)
        g_qkv = embed(g_qkv, (2, width, 3, width), 3, head_cols).reshape(2, width, 3 * width)
        g_out = embed(res.o_out, (2, width, width), 1, head_cols)
        g_down = embed(res.o_down.T, (hidden * sections, width), 0, hidden)
        grads = (
            small[0:4], small[4:8], share(g_qkv, 2), share(g_out, 2), small[8:10], share(res.o_up.T, 1, "dp"),
            share(res.o_bup[0], 0, "dp"), share(g_down, 1), small[10], small[FIRST_ROUTER:].T,
        )
    out_shape = (1, micro, 1, seq, width)
    return (
        res.sec_out.reshape(out_shape),
        res.sec_grad.reshape(out_shape),
        *grads,
        res.g_eup[None],
        res.g_edown[None],
    )


def solution(mesh):
    batch = P(None, "dp", None, None)
    table = P(None, "dp", None)
    in_specs = (
        batch, batch, P(None, "dp"), table, table,
        P(None, BOTH), P(None, BOTH), P(None, None, BOTH), P(None, None, BOTH), P(None, BOTH),
        P(None, BOTH), P(BOTH), P(None, BOTH), P(BOTH), P(BOTH, None),
        P("dp", None, "section"), P("dp", "section", None),
    )
    streams = P("section", None, "dp", None, None)
    out_specs = (
        streams, streams,
        P(None, BOTH), P(None, BOTH), P(None, None, BOTH), P(None, None, BOTH), P(None, BOTH),
        P(None, BOTH), P(BOTH), P(None, BOTH), P(BOTH), P(BOTH, None),
        P("dp", None, "section"), P("dp", "section", None),
    )
    return jax.shard_map(body, mesh=mesh, in_specs=in_specs, out_specs=out_specs, check_vma=False)
```

```python
import functools
import types

import jax
import jax.numpy as jnp
from jax import lax
from jax.experimental import pallas as pl
from jax.experimental.pallas import tpu as pltpu
from jax.sharding import PartitionSpec as P

HEADS = 12
HEAD_DIM = 64
EPS = 1e-05
MASKED = -1000000000.0
MESH = pl.DeviceIdType.MESH
F32 = jnp.float32
BF16 = jnp.bfloat16
LANES = 128


def dot_as(left, right, left_dim, right_dim):
    return lax.dot_general(
        left, right, (((left_dim,), (right_dim,)), ((), ())), preferred_element_type=F32
    )


def mm(left, right):
    return dot_as(left, right, 1, 0)


def mm_nt(left, right):
    return dot_as(left, right, 1, 1)


def mm_tn(left, right):
    return dot_as(left, right, 0, 0)


def normalize(values):
    center = values - jnp.mean(values, axis=-1, keepdims=True)
    spread = jnp.mean(center * center, axis=-1, keepdims=True)
    inverse = lax.rsqrt(spread + EPS)
    return center * inverse, inverse


def gelu_parts(pre):
    half = 0.5 + 0.5 * lax.erf(pre * 0.7071067811865476)
    density = jnp.exp(-0.5 * pre * pre) * 0.3989422804014327
    return pre * half, half + pre * density


TAIL = 8
GROUP = 32
FIRST_ROUTER = 11


def layers_kernel(g, names, *refs):
    r = types.SimpleNamespace(**dict(zip(names, refs, strict=True)))
    width, span, hidden, cols, head_cols = g.width, g.span, g.hidden, g.cols, g.head_cols
    sec = lax.axis_index("section")
    dev = lax.axis_index("dp")
    core = lax.rem(dev, 2)
    chip = lax.div(dev, 2)
    sib = dev + 1 - 2 * core
    quarter = g.quarter
    shard_rows = hidden // g.devices
    block_rows = g.chips * quarter

    def peer_section(offset):
        return lax.rem(sec + offset, g.sections)

    def from_section(offset):
        return lax.rem(sec + g.sections - offset, g.sections)

    def peer_chip(offset):
        return lax.rem(chip + offset, g.chips)

    def from_chip(offset):
        return lax.rem(chip + g.chips - offset, g.chips)

    def rows_at(index, size):
        return pl.ds(pl.multiple_of(index * size, size), size)

    def piece_at(index):
        return rows_at(index, g.piece)

    own = piece_at(sec)

    def remote(source, target, send, arrive, where):
        return pltpu.make_async_remote_copy(
            src_ref=source, dst_ref=target, send_sem=send, recv_sem=arrive, device_id=where, device_id_type=MESH
        )

    def at_chip_core(index):
        return {"dp": 2 * index + core}

    started = []
    kept_back = {}

    def do_when(condition, action):
        if condition is None:
            action()
        else:
            pl.when(condition)(action)

    def launch(copy, buffer=None, when=None):
        do_when(when, copy.start)
        if buffer:
            kept_back.setdefault(buffer, []).append((copy, when))
        else:
            started.append((copy, when))

    def settle(buffer):
        for copy, when in kept_back.pop(buffer, []):
            do_when(when, copy.wait_send)

    barrier = pltpu.get_barrier_semaphore()
    partners = [(a, b) for a in range(g.sections) for b in range(g.chips) if a + b and (g.direct or a * b == 0)]
    for section_offset, chip_offset in partners:
        where = {"section": peer_section(section_offset), "dp": 2 * peer_chip(chip_offset) + core}
        pl.semaphore_signal(barrier, inc=1, device_id=where, device_id_type=MESH)
    pl.semaphore_signal(barrier, inc=1, device_id={"dp": sib}, device_id_type=MESH)

    def scatter_copy(slot, offset):
        return remote(
            r.part.at[slot, piece_at(peer_section(offset))], r.got.at[slot, offset - 1],
            r.scat_s.at[slot, offset - 1], r.scat_r.at[slot, offset - 1], {"section": peer_section(offset)},
        )

    def scatter_start(slot, value):
        r.part[slot] = value.astype(BF16)
        if slot != 7:
            r.mine[...] = value
        for offset in range(1, g.sections):
            launch(scatter_copy(slot, offset))

    def scatter_sum(slot):
        total = r.part[slot, own, :].astype(F32) if slot == 7 else r.mine[own, :]
        for offset in range(1, g.sections):
            scatter_copy(slot, offset).wait_recv()
            total = total + r.got[slot, offset - 1].astype(F32)
        return total

    def share_copy(place, send, arrive, offset, receiving):
        where = from_section(offset) if receiving else peer_section(offset)
        return remote(place, place, send.at[offset - 1], arrive.at[offset - 1], {"section": where})

    def gather_start(buffer, slot, sem):
        place = buffer.at[slot, own]
        for offset in range(1, g.sections):
            launch(share_copy(place, r.gath_s.at[sem], r.gath_r.at[sem], offset, False))

    def gather_wait(buffer, slot, sem):
        for offset in range(1, g.sections):
            place = buffer.at[slot, piece_at(from_section(offset))]
            share_copy(place, r.gath_s.at[sem], r.gath_r.at[sem], offset, True).wait_recv()

    def pair_copy(name, source, target):
        index = g.pairs.index(name)
        return remote(source, target, r.pair_s.at[index], r.pair_r.at[index], {"dp": sib})

    def pair_start(name, source, target, buffer=None):
        launch(pair_copy(name, source, target), buffer)

    def pair_wait(name, target):
        pair_copy(name, target, target).wait_recv()

    def line_copy(name, source, target, offset, receiving):
        index = g.lines.index(name)
        where = from_chip(offset) if receiving else peer_chip(offset)
        return remote(
            source, target, r.line_s.at[index, offset - 1], r.line_r.at[index, offset - 1], at_chip_core(where)
        )

    last_chip = g.chips - 1
    is_end = lax.rem(chip, max(last_chip, 1)) == 0
    is_mid = lax.rem(chip, max(last_chip, 1)) != 0
    line_order = (2, 1, 3) if g.relay else range(1, g.chips)
    outward = jnp.clip(chip - 1, 0, 1)

    def near_to(offset):
        return {1: chip != last_chip, last_chip: chip != 0}.get(offset) if g.relay else None

    def near_from(offset):
        return {1: chip != 0, last_chip: chip != last_chip}.get(offset) if g.relay else None

    def spread_start(name, source, target, buffer=None):
        for offset in line_order:
            launch(line_copy(name, source, target, offset, False), buffer, near_to(offset))

    def spread_relay(name, place, buffer):
        index = g.lines.index(name)
        copy = remote(
            place, place, r.line_s.at[index, last_chip], r.line_r.at[index, outward * 2],
            at_chip_core(outward * last_chip),
        )
        launch(copy, buffer, is_mid)

    def spread_wait(name, place_at, buffer):
        for offset in line_order:
            place = place_at(from_chip(offset))
            line_copy(name, place, place, offset, True).wait_recv()
            if g.relay and offset == 2:
                spread_relay(name, place, buffer)

    def far_wait(name, place_at):
        for offset in (1, last_chip):
            place = place_at(from_chip(offset))
            copy = line_copy(name, place, place, offset, True)
            pl.when(jnp.logical_not(near_from(offset)))(copy.wait_recv)

    def line_start(name, source_at, target, buffer=None):
        for offset in range(1, g.chips):
            launch(line_copy(name, source_at(peer_chip(offset)), target, offset, False), buffer)

    def line_wait(name, target_at):
        for offset in range(1, g.chips):
            target = target_at(from_chip(offset), offset)
            line_copy(name, target, target, offset, True).wait_recv()

    def rows_line_start(name, source, target):
        line_start(name, lambda at: source.at[rows_at(at, quarter)], target.at[core, g.my_part(sec), rows_at(chip, quarter)])
        target[core, g.my_part(sec), rows_at(chip, quarter), :] = source[rows_at(chip, quarter), :]

    def rows_plane_start(name, target):
        line_wait(name, lambda at, _: target.at[core, g.my_part(sec), rows_at(at, quarter)])
        place = target.at[core, g.my_part(sec)]
        if g.parts > 1:
            index = g.planes.index(name)
            for offset in range(1, g.sections):
                launch(share_copy(place, r.plane_s.at[index], r.plane_r.at[index], offset, False))
        pair_start(name + "0", place, place)

    def rows_plane_wait(name, target, offset):
        index = g.planes.index(name)
        place = target.at[core, from_section(offset)]
        share_copy(place, r.plane_s.at[index], r.plane_r.at[index], offset, True).wait_recv()
        pair_start(name + str(offset), place, place)

    def rows_pair_wait(name, target, offset):
        pair_wait(name + str(offset), target.at[1 - core, g.my_part(from_section(offset))])

    top = cols - TAIL
    half = width // 2
    part_cols = head_cols // 2
    tail_lane = head_cols + 2 * GROUP

    def qkv_section(at_dev, index, section):
        return lax.rem(lax.div(3 * at_dev + index, g.devices) - section + g.sections, g.sections)

    def qkv_send(layer, offsets):
        for index in range(3):
            to = qkv_section(dev, index, sec)
            for offset in offsets:
                copy = remote(
                    r.pq.at[layer, index], r.rq.at[layer, core, chip, index],
                    r.wq_s.at[layer, index, offset], r.wq_r.at[layer, index, offset],
                    {"section": to, "dp": 2 * peer_chip(offset) + core},
                )
                if offset:
                    launch(copy, None, near_to(offset))
                else:
                    pl.when(to != sec)(copy.start)

                    @pl.when(to == sec)
                    def _(index=index):
                        r.rq[layer, core, chip, index] = r.pq[layer, index]

    def qkv_arrive(layer, offsets):
        for offset in offsets:
            for index in range(3):
                at_chip = from_chip(offset)
                target = r.rq.at[layer, core, at_chip, index]
                origin = qkv_section(2 * at_chip + core, index, sec)
                copy = remote(
                    target, target, r.wq_s.at[layer, index, offset], r.wq_r.at[layer, index, offset],
                    {"section": origin, "dp": 2 * at_chip + core},
                )
                if offset:
                    do_when(near_from(offset), copy.wait_recv)
                else:

                    @pl.when(origin != sec)
                    def _(copy=copy):
                        copy.wait_recv()
                        copy.wait_send()

            if g.relay and offset == 2:
                spread_relay("qkv0", r.rq.at[0, core, from_chip(offset)], "qkv0")
        if g.relay and len(offsets) > 1:
            far_wait("qkv0", lambda at: r.rq.at[0, core, at])

    def out_copy(section_offset, offset, place, receiving):
        if receiving:
            to, at_chip = from_section(section_offset), from_chip(offset)
        else:
            to, at_chip = peer_section(section_offset), peer_chip(offset)
        source = place if receiving else r.po.at[to]
        return remote(
            source, place, r.wo_s.at[section_offset, offset], r.wo_r.at[section_offset, offset],
            {"section": to, "dp": 2 * at_chip + core},
        )

    def out_offsets():
        return [(a, b) for b in (*line_order, 0) for a in range(g.sections) if a + b]

    def plane_copy(name, source, target, offset, receiving):
        index = g.planes.index(name)
        where = from_section(offset) if receiving else peer_section(offset)
        return remote(
            source, target, r.plane_s.at[index, offset - 1], r.plane_r.at[index, offset - 1], {"section": where}
        )

    def pack_wide(block):
        tail = jnp.concatenate([block[top:, :half], block[top:, half:]], axis=0)
        return jnp.concatenate([block[:top], tail], axis=1).astype(BF16)

    def pack_out(block):
        small = jnp.concatenate([block[top:, head_cols:]] * 2, axis=0)
        tail = jnp.concatenate([block[top:, :part_cols], block[top:, part_cols:head_cols]], axis=0)
        empty = jnp.zeros((top, g.out_lanes - tail_lane - part_cols), F32)
        return jnp.concatenate([block[:top], small, tail, empty], axis=1).astype(BF16)

    def unpack_wide(target, first, piece):
        target[first : first + top, 0:width] = piece[:, 0:width]
        target[first + top : first + cols, 0:half] = piece[0:TAIL, width : width + half]
        target[first + top : first + cols, half:width] = piece[TAIL:, width : width + half]

    def unpack_out(target, first, piece, lane=0):
        last = slice(first + top, first + cols)
        tail = slice(tail_lane, tail_lane + part_cols)
        target[first : first + top, lane : lane + head_cols] = piece[:, 0:head_cols]
        target[last, lane : lane + part_cols] = piece[0:TAIL, tail]
        target[last, lane + part_cols : lane + head_cols] = piece[TAIL:, tail]

    def unpack_small(target, first, piece, lane):
        target[first : first + top, lane : lane + GROUP] = piece[:, head_cols : head_cols + GROUP]
        target[first + top : first + cols, lane : lane + GROUP] = piece[0:TAIL, head_cols + GROUP : tail_lane]

    def shard_places():
        for at_core in range(2):
            for at_chip in range(g.chips):
                for at_sec in range(g.sections):
                    yield at_core, at_chip, at_sec, (at_sec * g.devices + 2 * at_chip + at_core) * cols

    def chunk_places():
        for at_core in range(2):
            for at_chip in range(g.chips):
                for index in range(3):
                    yield at_core, at_chip, index, (3 * (2 * at_chip + at_core) + index) * cols

    def unfold_out(layer):
        for at_core, at_chip, at_sec, first in shard_places():
            if layer:
                piece = r.rd[at_core, at_chip, at_sec, :, width + half :].astype(F32)
            else:
                piece = r.ro[at_core, at_chip, at_sec].astype(F32)
                unpack_small(r.tmp, first, piece, head_cols)
            unpack_out(r.tmp, first, piece)
        flipped = r.tmp[:, 0:tail_lane].T
        r.w_out[layer] = flipped[:head_cols].astype(BF16)
        if layer == 0:
            r.prm[...] = flipped[head_cols : head_cols + GROUP]
            r.w_router[...] = r.tmp[:, tail_lane - LANES : tail_lane].astype(BF16)

    def unfold_qkv(layer):
        for at_core, at_chip, index, first in chunk_places():
            unpack_wide(r.tmp, first, r.rq[layer, at_core, at_chip, index].astype(F32))
        r.w_qkv[layer] = r.tmp[0 : 3 * head_cols, 0:width].astype(BF16)

    def unfold_down():
        for at_core, at_chip, at_sec, first in shard_places():
            unpack_wide(r.tmp, first, r.rd[at_core, at_chip, at_sec].astype(F32))
        r.w_down[...] = r.tmp[...].astype(BF16)

    def grad_line(name, buffer_at, landing, target, passed):
        pair_wait(name, landing)
        for at_chip in range(g.chips):
            block = buffer_at(at_chip)
            block[...] = (block[...].astype(F32) + landing[at_chip].astype(F32)).astype(BF16)
        if g.relay:
            index = g.lines.index(name)
            copy = remote(
                buffer_at(last_chip - chip), passed, r.line_s.at[index, last_chip], r.line_r.at[index, last_chip],
                at_chip_core(1 + lax.div(chip, last_chip)),
            )
            launch(copy, None, is_end)
            for offset in (1, last_chip):

                @pl.when(jnp.logical_not(near_from(offset)))
                def _(offset=offset):
                    target[offset - 1] = jnp.zeros_like(target[offset - 1])

        for offset in line_order:
            copy = line_copy(name, buffer_at(peer_chip(offset)), target.at[offset - 1], offset, False)
            if g.relay and offset == 2:
                pl.when(is_end)(copy.start)
                started.append((copy, None))
            else:
                launch(copy, None, near_to(offset))

    def grad_relay(name, buffer_at, target, passed):
        if g.relay:
            index = g.lines.index(name)
            block = buffer_at(peer_chip(2))
            copy = line_copy(name, block, target.at[1], 2, False)

            @pl.when(is_mid)
            def _():
                remote(
                    passed, passed, r.line_s.at[index, last_chip], r.line_r.at[index, last_chip],
                    at_chip_core(outward * last_chip),
                ).wait_recv()
                block[...] = (block[...].astype(F32) + passed[...].astype(F32)).astype(BF16)
                copy.start()

    def grad_line_sum(name, buffer_at, target):
        for offset in line_order:
            place = target.at[offset - 1]
            do_when(near_from(offset), line_copy(name, place, place, offset, True).wait_recv)
        total = buffer_at(chip)[...].astype(F32)
        for offset in range(1, g.chips):
            total = total + target[offset - 1].astype(F32)
        return total

    def qkv_at(layer):
        return lambda at: r.rq.at[layer, core, at]

    def down_at(at):
        return r.rd.at[core, at]

    def out_at(at):
        return r.ro.at[core, at]

    def up_at(at):
        return r.ru.at[at, core]

    def bias_at(at):
        return r.rb.at[at, core]

    def grad_plane(name, buffer_at, target, summed, final):
        summed[...] = grad_line_sum(name, buffer_at, target).astype(BF16)
        for offset in range(1, g.sections):
            source = summed.at[peer_section(offset)]
            launch(plane_copy(name, source, final.at[sec], offset, False))
        final[sec] = summed[sec]

    def grad_plane_wait(name, final):
        for offset in range(1, g.sections):
            place = final.at[from_section(offset)]
            plane_copy(name, place, place, offset, True).wait_recv()

    def grad_qkv_copy(layer, index, place, where):
        return remote(
            r.mq.at[layer, index], place, r.gq_s.at[layer, index], r.gq_r.at[layer, index], {"section": where}
        )

    def grad_qkv_plane(layer):
        r.mq[layer] = grad_line_sum("gqkv" + str(layer), qkv_at(layer), r.aq.at[layer]).astype(BF16)
        for index in range(3):
            to = qkv_section(dev, index, sec)
            copy = grad_qkv_copy(layer, index, r.fq.at[layer, index], to)
            pl.when(to != sec)(copy.start)

            @pl.when(to == sec)
            def _(index=index):
                r.fq[layer, index] = r.mq[layer, index]

    def grad_qkv_finish(layer):
        for index in range(3):
            origin = qkv_section(dev, index, sec)
            copy = grad_qkv_copy(layer, index, r.fq.at[layer, index], origin)

            @pl.when(origin != sec)
            def _(copy=copy):
                copy.wait_recv()
                copy.wait_send()

            unpack_wide(r.o_qkv.at[layer], index * cols, r.fq[layer, index].astype(F32))

    def norm_into(source, target, index):
        @pl.loop(0, g.sections)
        def _(step):
            at = piece_at(step)
            unit, _ = normalize(source[at, :].astype(F32))
            target[at, :] = (unit * r.prm[index : index + 1, :] + r.prm[4 + index : 5 + index, :]).astype(BF16)

    place_row = jnp.concatenate(
        [r.routes[m : m + 1] * span + m * g.cap + r.slots[m : m + 1] for m in range(g.micro)], axis=1
    )
    r.square[...] = jnp.zeros_like(r.square)
    if g.direct:
        r.square[0:4, 0:cols] = r.norm_gain[...].astype(F32)
        r.square[4:8, 0:cols] = r.norm_bias[...].astype(F32)
        r.square[8:10, 0:cols] = r.out_bias[...].astype(F32)
        r.square[10:11, 0:cols] = r.down_bias[...].astype(F32)
        r.pb[...] = jnp.zeros_like(r.pb)
        r.pb[:, 0:shard_rows] = jnp.broadcast_to(r.up_bias[...], (r.pb.shape[0], shard_rows))
        r.square[...] = r.square[...].T
        r.square[0:cols, FIRST_ROUTER : FIRST_ROUTER + g.experts] = r.router[...].astype(F32)
        shard = r.wo[0].astype(F32)
        mine = r.square[0:cols, 0:GROUP]
        for at_sec in range(g.sections):
            block = shard[:, at_sec * head_cols : (at_sec + 1) * head_cols]
            r.po[at_sec] = pack_out(jnp.concatenate([block, mine], axis=1))
        shard = r.wq[0].astype(F32)
        for index in range(3):
            r.pq[0, index] = pack_wide(shard[index * cols : (index + 1) * cols])
    pl.semaphore_wait(barrier, len(partners) + 1)
    if g.direct:
        for section_offset, offset in out_offsets():
            launch(out_copy(section_offset, offset, r.ro.at[core, chip, sec], False), None, near_to(offset))
        r.ro[core, chip, sec] = r.po[sec]
        qkv_send(0, (*line_order, 0))
        shard = r.wq[1].astype(F32)
        for index in range(3):
            r.pq[1, index] = pack_wide(shard[index * cols : (index + 1) * cols])
        shard, other = r.wd[...].astype(F32), r.wo[1].astype(F32)
        empty = jnp.zeros((cols, GROUP), F32)
        for at_sec in range(g.sections):
            r.pd[at_sec, :, 0 : width + half] = pack_wide(shard[:, at_sec * hidden : (at_sec + 1) * hidden])
            block = other[:, at_sec * head_cols : (at_sec + 1) * head_cols]
            r.pd[at_sec, :, width + half :] = pack_out(jnp.concatenate([block, empty], axis=1))

    slot_ids = lax.broadcasted_iota(jnp.int32, (quarter, g.tokens), 0)
    for expert in range(g.chips):
        first = expert * span + (sec * quarter if g.parts > 1 else 0)
        match = jnp.where(slot_ids + first == place_row, 1.0, 0.0)
        r.table[expert * quarter : (expert + 1) * quarter, :] = match.astype(BF16)
    r.dispc[...] = mm(r.table[...], r.cot[...]).astype(BF16)
    r.small[...] = jnp.zeros_like(r.small)
    if g.direct:
        for section_offset, offset in out_offsets():
            place = r.ro.at[core, from_chip(offset), from_section(section_offset)]
            do_when(near_from(offset), out_copy(section_offset, offset, place, True).wait_recv)
            if g.relay and (section_offset, offset) == (g.sections - 1, 2):
                spread_relay("out", r.ro.at[core, from_chip(offset)], "out")
        if g.relay:
            far_wait("out", lambda at: r.ro.at[core, at])
        pair_start("out", r.ro.at[core], r.ro.at[core], "out")
        qkv_arrive(0, (*line_order, 0))
        pair_start("qkv0", r.rq.at[0, core], r.rq.at[0, core], "qkv0")
        spread_start("bias", r.pb, r.rb.at[chip, core])
        r.rb[chip, core] = r.pb[...]
        spread_start("up", r.wu, r.ru.at[chip, core])
        r.ru[chip, core] = r.wu[...]
        for offset in range(1, g.sections):
            launch(plane_copy("down", r.pd.at[peer_section(offset)], r.rd.at[core, chip, sec], offset, False))
        r.rd[core, chip, sec] = r.pd[sec]
        qkv_send(1, [0])
        pair_wait("out", r.ro.at[1 - core])
        unfold_out(0)
        pair_wait("qkv0", r.rq.at[0, 1 - core])
        unfold_qkv(0)

    def weights_line_start():
        for offset in range(1, g.sections):
            place = r.rd.at[core, chip, from_section(offset)]
            plane_copy("down", place, place, offset, True).wait_recv()
        spread_start("down", r.rd.at[core, chip], r.rd.at[core, chip], "down")
        qkv_arrive(1, [0])
        spread_start("qkv1", r.rq.at[1, core, chip], r.rq.at[1, core, chip], "qkv1")

    key_ids = lax.broadcasted_iota(jnp.int32, (g.seq, g.seq), 0)
    query_ids = lax.broadcasted_iota(jnp.int32, (g.seq, g.seq), 1)
    scale = HEAD_DIM**-0.5

    def block_of(index):
        return lax.rem(index + sec, 3) if g.direct else index

    def head_slice(head):
        return slice(head * HEAD_DIM, (head + 1) * HEAD_DIM)

    def token_slice(micro):
        return slice(micro * g.seq, (micro + 1) * g.seq)

    def attention_forward(layer, stream, slot):
        norm_into(stream, r.normed.at[2 * layer], 2 * layer)
        packed = mm_nt(r.w_qkv[layer], r.normed[2 * layer]).astype(BF16)
        r.qkv[layer] = packed.reshape(3, head_cols, g.tokens)
        for micro in range(g.micro):
            allowed = (key_ids <= query_ids) & (key_ids < r.lens[micro : micro + 1, :])
            for head in range(g.heads):
                at = token_slice(micro)
                key = r.qkv[layer, block_of(1), head_slice(head), at]
                scores = mm_tn(key, r.qkv[layer, block_of(0), head_slice(head), at]) * scale
                scores = jnp.where(allowed, scores, MASKED)
                weight = jnp.exp(scores - jnp.max(scores, axis=0, keepdims=True))
                weight = weight / jnp.sum(weight, axis=0, keepdims=True)
                r.probs[layer, micro, head] = weight
                value = r.qkv[layer, block_of(2), head_slice(head), at]
                r.ctx[layer, head_slice(head), at] = mm(value, weight.astype(BF16)).astype(BF16)
        scatter_start(slot, mm_tn(r.ctx[layer], r.w_out[layer]))

    def finish_forward(section, bias, stream):
        total = scatter_sum(section) + bias + stream[own, :].astype(F32)
        r.xs[section, own, :] = total.astype(BF16)
        gather_start(r.xs, section, section)

    attention_forward(0, r.x0, 0)
    if g.direct:
        weights_line_start()
    finish_forward(0, r.prm[8:9, :], r.x0)
    if g.direct:
        spread_wait("bias", lambda at: r.rb.at[at, core], "bias")
        spread_wait("up", lambda at: r.ru.at[at, core], "up")
        pair_start("up", r.ru.at[:, core], r.ru.at[:, core], "up")
        pair_start("bias", r.rb.at[:, core], r.rb.at[:, core], "bias")
        pair_wait("up", r.ru.at[:, 1 - core])
        pair_wait("bias", r.rb.at[:, 1 - core])
        for at_dev in range(g.devices):
            row = r.rb[at_dev // 2, at_dev % 2, :, 0:shard_rows].astype(F32)
            r.b_up[:, at_dev * shard_rows : (at_dev + 1) * shard_rows] = row[0:TAIL]
    gather_wait(r.xs, 0, 0)

    def up_rows(at):
        if g.direct:
            return r.ru[...].reshape(hidden, width)[at]
        return r.w_up[at, :]

    norm_into(r.xs.at[0], r.normed.at[1], 1)
    for block in range(hidden // g.block):
        at = slice(block * g.block, (block + 1) * g.block)
        pre = mm_nt(r.normed[1], up_rows(at)) + r.b_up[0:1, at]
        value, slope = gelu_parts(pre)
        r.act[:, at] = value.astype(BF16)
        r.dgelu[:, at] = slope
    if g.direct:
        spread_wait("down", lambda at: r.rd.at[core, at], "down")
        pair_start("down", r.rd.at[core], r.rd.at[core], "down")
        pair_wait("down", r.rd.at[1 - core])
        unfold_down()
    scatter_start(1, mm_nt(r.act[...], r.w_down[...]))
    finish_forward(1, r.prm[10:11, :], r.xs.at[0])
    if g.direct:
        spread_wait("qkv1", lambda at: r.rq.at[1, core, at], "qkv1")
        pair_start("qkv1", r.rq.at[1, core], r.rq.at[1, core], "qkv1")
    rows_line_start("crow", r.dispc, r.crow)
    if g.direct:
        unfold_out(1)
        pair_wait("qkv1", r.rq.at[1, 1 - core])
        unfold_qkv(1)
    gather_wait(r.xs, 1, 1)

    attention_forward(1, r.xs.at[1], 2)
    finish_forward(2, r.prm[9:10, :], r.xs.at[1])
    gather_wait(r.xs, 2, 2)

    wide = r.wide
    norm_into(r.xs.at[2], wide.at[:, pl.ds(0, width)], 3)
    logits = mm(wide[:, :width], r.w_router[...])
    lane = lax.broadcasted_iota(jnp.int32, logits.shape, 1) - g.router_lane
    r.square[0 : g.micro, :] = jnp.concatenate(
        [place_row[:, token_slice(m)] for m in range(g.micro)], axis=0
    ).astype(F32)
    columns = r.square[...].T
    place_col = jnp.concatenate([columns[:, m : m + 1] for m in range(g.micro)], axis=0).astype(jnp.int32)
    chosen = (place_col >= lane * span) & (place_col < lane * span + span)
    score = jnp.sum(jnp.where(chosen, logits, 0.0), axis=-1, keepdims=True)
    gate = 1.0 / (1.0 + jnp.exp(-score))
    gate_high = gate.astype(BF16).astype(F32)
    lane = lax.broadcasted_iota(jnp.int32, (g.tokens, LANES), 1)
    pair = jnp.where(lane == 0, gate_high, jnp.where(lane == 1, gate - gate_high, 0.0))
    wide[:, width:] = pair.astype(BF16)
    r.disp[...] = mm(r.table[...], wide[...]).astype(BF16)
    rows_line_start("rows", r.disp, r.rows)
    rows_plane_start("crow", r.crow)
    rows_plane_start("rows", r.rows)
    if g.parts > 1:
        for offset in range(1, g.sections):
            rows_plane_wait("crow", r.crow, offset)

    own_router = FIRST_ROUTER + chip
    router_row = r.prm[pl.ds(own_router, 1), :]

    def expert_block(side, part, at, keep_first):
        row = r.rows[side, part, at, :width]
        tail = r.rows[side, part, at, width:].astype(F32)
        gate_row = tail[:, 0:1] + tail[:, 1:2]
        grad_row = (gate_row * r.crow[side, part, at, :].astype(F32)).astype(BF16)
        r.grow[side, part, at, :] = grad_row
        value, slope = gelu_parts(mm(row, r.e_up[...]))
        value = value.astype(BF16)
        r.acte[side, part, at, :] = value
        result = mm(value, r.e_down[...])
        total = jnp.sum(grad_row.astype(F32) * result, axis=-1, keepdims=True) * (1.0 - gate_row)
        inner = (slope * mm_nt(grad_row, r.e_down[...])).astype(BF16)
        r.dpree[side, part, at, :] = inner
        back = mm_nt(inner, r.e_up[...]) + total * router_row
        r.small[pl.ds(own_router, 1), :] += jnp.sum(row.astype(F32) * total, axis=0, keepdims=True)
        result = result * gate_row
        if keep_first:
            r.keep_d[part, at, :] = back
            r.keep_y[part, at, :] = result
        else:
            r.snd_d[part, at, :] = back.astype(BF16)
            r.snd_y[part, at, :] = result.astype(BF16)

    def expert_part(side, part, keep_first):
        if block_rows <= g.block:
            expert_block(side, part, slice(None), keep_first)
            return

        @pl.loop(0, block_rows // g.block)
        def _(step):
            expert_block(side, part, rows_at(step, g.block), keep_first)

    def merge(which, offset):
        part = g.my_part(from_section(offset))
        pair_wait(which + str(offset), rcv[which].at[part])
        return kept[which][part] + rcv[which][part].astype(F32)

    snd = {"d": r.snd_d, "y": r.snd_y}
    kept = {"d": r.keep_d, "y": r.keep_y}
    rcv = {"d": r.rcv_d, "y": r.rcv_y}

    def merge_send(offset):
        to = g.sections - offset
        r.out_d[offset - 1] = merge("d", offset).astype(BF16)
        launch(plane_copy("d", r.out_d.at[offset - 1], r.plane_d.at[to - 1], to, False))

    def expert_back_line():
        total = merge("d", 0)
        if g.parts > 1:
            for offset in range(1, g.sections):
                place = r.plane_d.at[offset - 1]
                plane_copy("d", place, place, offset, True).wait_recv()
                total = total + place[...].astype(F32)
        r.ret_d[...] = total.astype(BF16)
        line_start("d", lambda at: r.ret_d.at[rows_at(at, quarter)], r.back_d.at[rows_at(chip, quarter)])
        r.back_d[rows_at(chip, quarter), :] = r.ret_d[rows_at(chip, quarter), :]

    def expert_combine():
        line_wait("d", lambda at, _: r.back_d.at[rows_at(at, quarter)])
        scatter_start(3, mm_tn(r.table[...], r.back_d[...]))

    def results_combine():
        line_wait("y", lambda at, _: r.back_y.at[at])
        span_ids = lax.broadcasted_iota(jnp.int32, (g.chips * span, g.tokens), 0)
        whole = jnp.where(span_ids == place_row, 1.0, 0.0).astype(BF16)
        scatter_start(7, mm_tn(whole, r.back_y[...].reshape(g.chips * span, width)))

    offsets = range(1, g.sections) if g.parts > 1 else []
    rows_pair_wait("crow", r.crow, 0)
    expert_part(core, g.my_part(sec), True)
    rows_pair_wait("rows", r.rows, 0)
    expert_part(1 - core, g.my_part(sec), False)
    for which in ("d", "y"):
        place = g.my_part(sec)
        pair_start(which + "0", snd[which].at[place], rcv[which].at[place])
    for offset in offsets:
        rows_plane_wait("rows", r.rows, offset)
    for offset in offsets:
        part = from_section(offset)
        expert_part(core, part, True)
        rows_pair_wait("rows", r.rows, offset)
        rows_pair_wait("crow", r.crow, offset)
        expert_part(1 - core, part, False)
        for which in ("d", "y"):
            pair_start(which + str(offset), snd[which].at[part], rcv[which].at[part])
        if offset > 1:
            merge_send(offset - 1)
    if g.parts > 1:
        merge_send(g.sections - 1)
    expert_back_line()
    for offset in range(g.parts):
        r.ret_y[g.my_part(from_section(offset))] = merge("y", offset).astype(BF16)
    line_start("y", lambda at: r.ret_y.at[:, rows_at(at, quarter)], r.back_y.at[chip])
    r.back_y[chip] = r.ret_y[:, rows_at(chip, quarter), :]

    def flat(ref, side):
        value = ref[side]
        return value.reshape(g.parts * block_rows, value.shape[-1])

    def expert_weights(left, right, lanes):
        return mm_tn(flat(left, 0)[:, :lanes], flat(right, 0)) + mm_tn(flat(left, 1)[:, :lanes], flat(right, 1))

    r.g_eup[...] = expert_weights(r.rows, r.dpree, width)
    r.g_edown[...] = expert_weights(r.acte, r.grow, r.acte.shape[-1])

    def finish_backward(section, slot, stream, above):
        grad = scatter_sum(slot)
        unit, inverse = normalize(stream[own, :].astype(F32))
        r.small[section : section + 1, :] = jnp.sum(grad * unit, axis=0, keepdims=True)
        r.small[4 + section : 5 + section, :] = jnp.sum(grad, axis=0, keepdims=True)
        grad = grad * r.prm[section : section + 1, :]
        shared = jnp.mean(grad, axis=-1, keepdims=True)
        along = jnp.mean(grad * unit, axis=-1, keepdims=True)
        grad = inverse * (grad - shared - unit * along) + above[own, :].astype(F32)
        r.gs[section, own, :] = grad.astype(BF16)
        gather_start(r.gs, section, 4 + section)

    expert_combine()
    finish_backward(3, 3, r.xs.at[2], r.cot)
    gather_wait(r.gs, 3, 7)

    def bias_row(index, section):
        r.small[index : index + 1, :] = jnp.sum(r.gs[section, own, :].astype(F32), axis=0, keepdims=True)

    def attention_backward(layer, section, slot):
        grad = r.gs[section + 1]
        dctx = mm_nt(r.w_out[layer], grad).astype(BF16)
        for micro in range(g.micro):
            for head in range(g.heads):
                at = token_slice(micro)
                weight = r.probs[layer, micro, head]
                low = weight.astype(BF16)
                dhead = dctx[head_slice(head), at]
                query = r.qkv[layer, block_of(0), head_slice(head), at]
                key = r.qkv[layer, block_of(1), head_slice(head), at]
                value = r.qkv[layer, block_of(2), head_slice(head), at]
                dprobs = mm_tn(value, dhead)
                delta = jnp.sum(weight * dprobs, axis=0, keepdims=True)
                dscores = (weight * (dprobs - delta)).astype(BF16)
                r.dqkv[block_of(0), head_slice(head), at] = (mm(key, dscores) * scale).astype(BF16)
                r.dqkv[block_of(1), head_slice(head), at] = (mm_nt(query, dscores) * scale).astype(BF16)
                r.dqkv[block_of(2), head_slice(head), at] = mm_nt(dhead, low).astype(BF16)
        flat_grad = r.dqkv[...].reshape(3 * head_cols, g.tokens)
        scatter_start(slot, mm_tn(flat_grad, r.w_qkv[layer]))
        bias_row(8 + layer, section + 1)

    def attention_weights(layer, section):
        grad_qkv = mm(r.dqkv[...].reshape(3 * head_cols, g.tokens), r.normed[2 * layer])
        if not g.direct:
            r.o_qkv[layer] = grad_qkv
            r.o_out[layer] = mm(r.ctx[layer], r.gs[section + 1])
            return
        r.tmp[0 : 3 * head_cols, :] = grad_qkv
        settle("qkv" + str(layer))
        for at_core, at_chip, index, first in chunk_places():
            r.rq[layer, at_core, at_chip, index] = pack_wide(r.tmp[first : first + cols, :])
        name = "gqkv" + str(layer)
        pair_start(name, r.rq.at[layer, 1 - core], r.hq.at[layer])
        r.tmp[:, 0:head_cols] = dot_as(r.gs[section + 1], r.ctx[layer], 0, 1)
        if layer:
            settle("down")
            r.tmp[:, head_cols : head_cols + GROUP] = jnp.zeros((width, GROUP), F32)
            for at_core, at_chip, at_sec, first in shard_places():
                block = r.tmp[first : first + cols, 0 : head_cols + GROUP]
                r.rd[at_core, at_chip, at_sec, :, width + half :] = pack_out(block)

    attention_backward(1, 2, 4)
    attention_weights(1, 2)
    finish_backward(2, 4, r.xs.at[1], r.gs.at[3])
    if g.direct:
        grad_line("gqkv1", qkv_at(1), r.hq.at[1], r.aq.at[1], r.lq.at[1])
    gather_wait(r.gs, 2, 6)

    grad_two = r.gs[2]
    for block in range(hidden // g.block):
        at = slice(block * g.block, (block + 1) * g.block)
        r.dpre[:, at] = (r.dgelu[:, at] * mm(grad_two, r.w_down[:, at])).astype(BF16)
    scatter_start(5, mm(r.dpre[...], up_rows(slice(None))))
    bias_row(10, 2)
    if g.direct:
        grad_relay("gqkv1", qkv_at(1), r.aq.at[1], r.lq.at[1])
    sum_up = jnp.sum(r.dpre[...].astype(F32), axis=0, keepdims=True)
    if g.direct:
        r.tmp[...] = mm_tn(r.gs[2], r.act[...])
        for at_core, at_chip, at_sec, first in shard_places():
            r.rd[at_core, at_chip, at_sec, :, 0 : width + half] = pack_wide(r.tmp[first : first + cols, :])
        pair_start("gdown", r.rd.at[1 - core], r.hd)
        settle("up")
        settle("bias")
        r.ru[...] = mm_tn(r.dpre[...], r.normed[1]).astype(BF16).reshape(r.ru.shape)
        pair_start("gup", r.ru.at[:, 1 - core], r.hu)
        for at_dev in range(g.devices):
            row = sum_up[:, at_dev * shard_rows : (at_dev + 1) * shard_rows]
            row = jnp.broadcast_to(row, (r.pb.shape[0], shard_rows)).astype(BF16)
            r.rb[at_dev // 2, at_dev % 2, :, 0:shard_rows] = row
        pair_start("gbias", r.rb.at[:, 1 - core], r.hb)
    else:
        r.o_down[...] = mm_tn(r.gs[2], r.act[...])
        r.o_up[...] = mm_tn(r.dpre[...], r.normed[1])
        r.o_bup[...] = sum_up
    finish_backward(1, 5, r.xs.at[0], r.gs.at[2])
    if g.direct:
        grad_line("gbias", bias_at, r.hb, r.ab, r.lb)
        grad_line("gdown", down_at, r.hd, r.ad, r.ld)
        grad_line("gup", up_at, r.hu, r.au, r.lu)
    gather_wait(r.gs, 1, 5)

    attention_backward(0, 0, 6)
    attention_weights(0, 0)
    if g.direct:
        grad_relay("gbias", bias_at, r.ab, r.lb)
        grad_relay("gdown", down_at, r.ad, r.ld)
    finish_backward(0, 6, r.x0, r.gs.at[1])
    if g.direct:
        settle("out")
        kinds = r.small[...]
        padded = jnp.concatenate([kinds, jnp.zeros((LANES - kinds.shape[0], width), F32)], axis=0)
        r.tmp[:, head_cols : head_cols + GROUP] = padded.T[:, 0:GROUP]
        for at_core, at_chip, at_sec, first in shard_places():
            r.ro[at_core, at_chip, at_sec] = pack_out(r.tmp[first : first + cols, 0 : head_cols + GROUP])
        pair_start("gout", r.ro.at[1 - core], r.ho)
        grad_relay("gup", up_at, r.au, r.lu)
        grad_line("gqkv0", qkv_at(0), r.hq.at[0], r.aq.at[0], r.lq.at[0])
        grad_line("gout", out_at, r.ho, r.ao, r.lo)
    results_combine()
    if g.direct:
        grad_qkv_plane(1)
        grad_plane("gdown", down_at, r.ad, r.md, r.fd)
    if g.direct:
        grad_relay("gqkv0", qkv_at(0), r.aq.at[0], r.lq.at[0])
        grad_relay("gout", out_at, r.ao, r.lo)
    r.xs[3, own, :] = (scatter_sum(7) + r.xs[2, own, :].astype(F32)).astype(BF16)
    gather_start(r.xs, 3, 3)
    if g.direct:
        r.o_up[...] = grad_line_sum("gup", up_at, r.au)
        r.o_bup[...] = grad_line_sum("gbias", bias_at, r.ab)[0:1, 0:shard_rows]
        grad_qkv_finish(1)
        grad_plane_wait("gdown", r.fd)
        for at_sec in range(g.sections):
            piece = r.fd[at_sec].astype(F32)
            unpack_wide(r.o_down.at[:, pl.ds(at_sec * hidden, hidden)], 0, piece)
            unpack_out(r.o_out.at[1], 0, piece[:, width + half :], at_sec * head_cols)
        grad_qkv_plane(0)
        grad_plane("gout", out_at, r.ao, r.mo, r.fo)
        grad_qkv_finish(0)
        grad_plane_wait("gout", r.fo)
        everyone = jnp.zeros((top, g.out_lanes), F32)
        for at_sec in range(g.sections):
            piece = r.fo[at_sec].astype(F32)
            unpack_out(r.o_out.at[0], 0, piece, at_sec * head_cols)
            everyone = everyone + piece
        r.square[...] = jnp.zeros_like(r.square)
        unpack_small(r.square, 0, everyone, 0)
        r.o_router[...] = r.square[0:cols, FIRST_ROUTER : FIRST_ROUTER + g.experts]
        r.square[...] = r.square[...].T
        r.o_gain[...] = r.square[0:4, 0:cols]
        r.o_bias[...] = r.square[4:8, 0:cols]
        r.o_bout[...] = r.square[8:10, 0:cols]
        r.o_bdown[...] = r.square[10:11, 0:cols]
    else:
        r.o_small[...] = r.small[...]
    gather_wait(r.xs, 3, 3)
    gather_wait(r.gs, 0, 4)
    r.sec_out[...] = r.xs[sec]
    r.sec_grad[...] = r.gs[sec]
    for copy, when in started:
        do_when(when, copy.wait_send)


def run_layers(g, operands):
    tokens, width, hidden, sections, chips = g.tokens, g.width, g.hidden, g.sections, g.chips
    part_rows = chips * g.quarter
    inner = operands["e_down"].shape[0]
    three = 3 * g.head_cols
    shape = jax.ShapeDtypeStruct
    vmem = pltpu.VMEM
    dma = pltpu.SemaphoreType.DMA
    top = g.cols - TAIL
    wide = width + width // 2
    up_rows = hidden // g.devices
    outs = dict(
        sec_out=shape((tokens, width), BF16),
        sec_grad=shape((tokens, width), BF16),
        g_eup=shape((width, inner), F32),
        g_edown=shape((inner, width), F32),
    )
    if g.direct:
        outs |= dict(
            o_qkv=shape((2, 3 * g.cols, width), F32),
            o_out=shape((2, g.cols, width), F32),
            o_up=shape((up_rows, width), F32),
            o_down=shape((g.cols, sections * hidden), F32),
            o_gain=shape((4, g.cols), F32),
            o_bias=shape((4, g.cols), F32),
            o_bout=shape((2, g.cols), F32),
            o_bdown=shape((1, g.cols), F32),
            o_router=shape((g.cols, g.experts), F32),
            o_bup=shape((1, up_rows), F32),
        )
    else:
        outs |= dict(
            o_qkv=shape((2, three, width), F32),
            o_out=shape((2, g.head_cols, width), F32),
            o_up=shape((hidden, width), F32),
            o_down=shape((width, hidden), F32),
            o_bup=shape((1, hidden), F32),
            o_small=shape((g.small, width), F32),
        )
    scratch = dict(
        xs=vmem((4, tokens, width), BF16),
        gs=vmem((4, tokens, width), BF16),
        normed=vmem((3, tokens, width), BF16),
        wide=vmem((tokens, width + LANES), BF16),
        qkv=vmem((2, 3, g.head_cols, tokens), BF16),
        probs=vmem((2, g.micro, g.heads, g.seq, g.seq), F32),
        ctx=vmem((2, g.head_cols, tokens), BF16),
        act=vmem((tokens, hidden), BF16),
        dgelu=vmem((tokens, hidden), F32),
        dpre=vmem((tokens, hidden), BF16),
        dqkv=vmem((3, g.head_cols, tokens), BF16),
        part=vmem((8, tokens, width), BF16),
        got=vmem((8, sections - 1, g.piece, width), BF16),
        mine=vmem((tokens, width), F32),
        square=vmem((LANES, LANES), F32),
        table=vmem((part_rows, tokens), BF16),
        disp=vmem((part_rows, width + LANES), BF16),
        dispc=vmem((part_rows, width), BF16),
        rows=vmem((2, g.parts, part_rows, width + LANES), BF16),
        crow=vmem((2, g.parts, part_rows, width), BF16),
        grow=vmem((2, g.parts, part_rows, width), BF16),
        acte=vmem((2, g.parts, part_rows, inner), BF16),
        dpree=vmem((2, g.parts, part_rows, inner), BF16),
        small=vmem((g.small, width), F32),
    )
    for which in ("d", "y"):
        scratch["keep_" + which] = vmem((g.parts, part_rows, width), F32)
        for name in ("snd_", "rcv_"):
            scratch[name + which] = vmem((g.parts, part_rows, width), BF16)
    scratch |= dict(
        out_d=vmem((sections - 1, part_rows, width), BF16),
        plane_d=vmem((sections - 1, part_rows, width), BF16),
        ret_d=vmem((part_rows, width), BF16),
        back_d=vmem((part_rows, width), BF16),
        ret_y=vmem((g.parts, part_rows, width), BF16),
        back_y=vmem((chips, g.parts, g.quarter, width), BF16),
    )
    for name in ("scat_s", "scat_r", "gath_s", "gath_r"):
        scratch[name] = dma((8, sections - 1))
    for name, count, each in (("pair", len(g.pairs), 0), ("line", len(g.lines), chips), ("plane", len(g.planes), sections - 1)):
        sizes = (count, each) if each else (count,)
        scratch |= {name + "_s": dma(sizes), name + "_r": dma(sizes)}
    if g.direct:
        piece = (top, wide)
        both = (top, wide + g.out_lanes)
        out_piece = (top, g.out_lanes)
        up_piece = (up_rows, width)
        bias_piece = (2 * TAIL, LANES)
        scratch |= dict(
            pq=vmem((2, 3, *piece), BF16),
            po=vmem((sections, *out_piece), BF16),
            pb=vmem(bias_piece, BF16),
            rb=vmem((chips, 2, *bias_piece), BF16),
            hb=vmem((chips, *bias_piece), BF16),
            ab=vmem((chips - 1, *bias_piece), BF16),
            lb=vmem(bias_piece, BF16),
            lq=vmem((2, 3, *piece), BF16),
            lo=vmem((sections, *out_piece), BF16),
            lu=vmem(up_piece, BF16),
            ld=vmem((sections, *both), BF16),
            pd=vmem((sections, *both), BF16),
            rq=vmem((2, 2, chips, 3, *piece), BF16),
            ro=vmem((2, chips, sections, *out_piece), BF16),
            ru=vmem((chips, 2, *up_piece), BF16),
            rd=vmem((2, chips, sections, *both), BF16),
            w_qkv=vmem((2, three, width), BF16),
            w_out=vmem((2, g.head_cols, width), BF16),
            w_down=vmem((width, hidden), BF16),
            w_router=vmem((width, LANES), BF16),
            b_up=vmem((8, hidden), F32),
            prm=vmem((GROUP, width), F32),
            tmp=vmem((width, width), F32),
            hq=vmem((2, chips, 3, *piece), BF16),
            ho=vmem((chips, sections, *out_piece), BF16),
            hu=vmem((chips, *up_piece), BF16),
            hd=vmem((chips, sections, *both), BF16),
            aq=vmem((2, chips - 1, 3, *piece), BF16),
            ao=vmem((chips - 1, sections, *out_piece), BF16),
            au=vmem((chips - 1, *up_piece), BF16),
            ad=vmem((chips - 1, sections, *both), BF16),
            mq=vmem((2, 3, *piece), BF16),
            mo=vmem((sections, *out_piece), BF16),
            md=vmem((sections, *both), BF16),
            fq=vmem((2, 3, *piece), BF16),
            fo=vmem((sections, *out_piece), BF16),
            fd=vmem((sections, *both), BF16),
            wq_s=dma((2, 3, chips)),
            wq_r=dma((2, 3, chips)),
            wo_s=dma((sections, chips)),
            wo_r=dma((sections, chips)),
            gq_s=dma((2, 3)),
            gq_r=dma((2, 3)),
        )
    whole = pl.BlockSpec(memory_space=pltpu.VMEM)
    names = (*operands, *outs, *scratch)
    results = pl.pallas_call(
        functools.partial(layers_kernel, g, names),
        out_shape=tuple(outs.values()),
        in_specs=[whole] * len(operands),
        out_specs=[whole] * len(outs),
        scratch_shapes=list(scratch.values()),
        compiler_params=pltpu.CompilerParams(
            collective_id=0, has_side_effects=True, vmem_limit_bytes=62 * 1024 * 1024
        ),
    )(*operands.values())
    return types.SimpleNamespace(**dict(zip(outs, results, strict=True)))


BOTH = ("section", "dp")


def body(
    tokens, cotangent, lengths, routes, slots, norm_gain, norm_bias, attn_qkv, attn_out, attn_out_bias,
    ffn_up, ffn_up_bias, ffn_down, ffn_down_bias, router, expert_up, expert_down,
):
    sections, devices = lax.axis_size("section"), lax.axis_size("dp")
    sec = lax.axis_index("section")
    micro, _, seq, width = tokens.shape
    experts = router.shape[1]
    chips = devices // 2
    head_cols = width // sections
    hidden = ffn_up.shape[1] * devices
    cap = 2 * seq // experts
    span = micro * cap
    cols = ffn_down.shape[1]
    kinds = FIRST_ROUTER + experts
    direct = cols == 3 * TAIL and kinds <= GROUP and sections == 4 and ffn_up.shape[1] % 16 == 0
    parts = sections if span % (16 * sections) == 0 else 1
    numbers = [str(part) for part in range(parts)]
    g = types.SimpleNamespace(
        sections=sections, devices=devices, chips=chips, micro=micro, seq=seq, width=width, hidden=hidden, cap=cap,
        span=span, tokens=micro * seq, piece=micro * seq // sections, heads=head_cols // HEAD_DIM,
        head_cols=head_cols, cols=cols, block=256, small=-(-kinds // 8) * 8, direct=direct, experts=experts,
        out_lanes=head_cols + 2 * GROUP + LANES, parts=parts, quarter=span // parts,
        relay=direct and chips == 4,
        my_part=(lambda section: section) if parts > 1 else (lambda section: 0),
        router_lane=FIRST_ROUTER + (LANES - 2 * GROUP if direct else 0),
        pairs=[name + n for name in ("crow", "rows", "d", "y") for n in numbers]
        + (["out", "qkv0", "up", "bias", "down", "qkv1", "gqkv0", "gqkv1", "gdown", "gup", "gbias", "gout"] if direct else []),
        lines=["crow", "rows", "d", "y"]
        + (["out", "qkv0", "up", "bias", "down", "qkv1", "gqkv0", "gqkv1", "gdown", "gup", "gbias", "gout"] if direct else []),
        planes=["crow", "rows", "d"] + (["down", "gdown", "gout"] if direct else []),
    )

    operands = dict(
        x0=tokens.reshape(g.tokens, width),
        cot=cotangent.reshape(g.tokens, width),
        lens=lengths,
        routes=routes[:, 0],
        slots=slots[:, 0],
        e_up=expert_up[0],
        e_down=expert_down[0],
    )
    if direct:
        operands |= dict(
            norm_gain=norm_gain,
            norm_bias=norm_bias,
            out_bias=attn_out_bias,
            down_bias=ffn_down_bias[None],
            up_bias=ffn_up_bias[None],
            router=router,
            wq=attn_qkv.transpose(0, 2, 1),
            wo=attn_out.transpose(0, 2, 1),
            wu=ffn_up.T,
            wd=ffn_down.T,
        )
    else:

        def every(array, axis):
            return lax.all_gather(array, BOTH, axis=axis, tiled=True)

        def part_of(array, axis, size):
            return lax.dynamic_slice_in_dim(array, sec * size, size, axis)

        rows = [norm_gain, norm_bias, attn_out_bias, ffn_down_bias[None], router.T]
        params = every(jnp.concatenate(rows, axis=0), 1)
        params = jnp.pad(params, ((0, LANES - kinds), (0, 0)))
        b_up = lax.all_gather(ffn_up_bias, "dp", axis=0, tiled=True).astype(F32)
        full = part_of(every(attn_qkv, 2).reshape(2, width, 3, width), 3, head_cols)
        operands |= dict(
            prm=params.astype(F32),
            w_router=params.T,
            b_up=b_up[None],
            w_qkv=full.transpose(0, 2, 3, 1).reshape(2, 3 * head_cols, width),
            w_out=part_of(every(attn_out, 2), 1, head_cols),
            w_up=lax.all_gather(ffn_up, "dp", axis=1, tiled=True).T,
            w_down=part_of(every(ffn_down, 1), 0, hidden).T,
        )
    res = run_layers(g, operands)

    if direct:
        grads = (
            res.o_gain, res.o_bias, res.o_qkv.transpose(0, 2, 1), res.o_out.transpose(0, 2, 1), res.o_bout,
            res.o_up.T, res.o_bup[0], res.o_down.T, res.o_bdown[0], res.o_router,
        )
    else:

        def embed(array, shape, axis, size):
            return lax.dynamic_update_slice_in_dim(jnp.zeros(shape, F32), array, sec * size, axis)

        def share(array, axis, over=BOTH):
            return lax.psum_scatter(array, over, scatter_dimension=axis, tiled=True)

        small = share(res.o_small[:kinds], 1)
        g_qkv = res.o_qkv.reshape(2, 3, head_cols, width).transpose(0, 3, 1, 2)
        g_qkv = embed(g_qkv, (2, width, 3, width), 3, head_cols).reshape(2, width, 3 * width)
        g_out = embed(res.o_out, (2, width, width), 1, head_cols)
        g_down = embed(res.o_down.T, (hidden * sections, width), 0, hidden)
        grads = (
            small[0:4], small[4:8], share(g_qkv, 2), share(g_out, 2), small[8:10], share(res.o_up.T, 1, "dp"),
            share(res.o_bup[0], 0, "dp"), share(g_down, 1), small[10], small[FIRST_ROUTER:].T,
        )
    out_shape = (1, micro, 1, seq, width)
    return (
        res.sec_out.reshape(out_shape).astype(F32),
        res.sec_grad.reshape(out_shape).astype(F32),
        *grads,
        res.g_eup[None],
        res.g_edown[None],
    )


def solution(mesh):
    batch = P(None, "dp", None, None)
    table = P(None, "dp", None)
    in_specs = (
        batch, batch, P(None, "dp"), table, table,
        P(None, BOTH), P(None, BOTH), P(None, None, BOTH), P(None, None, BOTH), P(None, BOTH),
        P(None, BOTH), P(BOTH), P(None, BOTH), P(BOTH), P(BOTH, None),
        P("dp", None, "section"), P("dp", "section", None),
    )
    streams = P("section", None, "dp", None, None)
    out_specs = (
        streams, streams,
        P(None, BOTH), P(None, BOTH), P(None, None, BOTH), P(None, None, BOTH), P(None, BOTH),
        P(None, BOTH), P(BOTH), P(None, BOTH), P(BOTH), P(BOTH, None),
        P("dp", None, "section"), P("dp", "section", None),
    )
    return jax.shard_map(body, mesh=mesh, in_specs=in_specs, out_specs=out_specs, check_vma=False)
```

```python
import functools
import types

import jax
import jax.numpy as jnp
from jax import lax
from jax.experimental import pallas as pl
from jax.experimental.pallas import tpu as pltpu
from jax.sharding import PartitionSpec as P

HEADS = 12
HEAD_DIM = 64
EPS = 1e-05
MASKED = -1000000000.0
MESH = pl.DeviceIdType.MESH
F32 = jnp.float32
BF16 = jnp.bfloat16
LANES = 128


def dot_as(left, right, left_dim, right_dim):
    return lax.dot_general(
        left, right, (((left_dim,), (right_dim,)), ((), ())), preferred_element_type=F32
    )


def mm(left, right):
    return dot_as(left, right, 1, 0)


def mm_nt(left, right):
    return dot_as(left, right, 1, 1)


def mm_tn(left, right):
    return dot_as(left, right, 0, 0)


def normalize(values):
    center = values - jnp.mean(values, axis=-1, keepdims=True)
    spread = jnp.mean(center * center, axis=-1, keepdims=True)
    inverse = lax.rsqrt(spread + EPS)
    return center * inverse, inverse


def gelu_parts(pre):
    half = 0.5 + 0.5 * lax.erf(pre * 0.7071067811865476)
    density = jnp.exp(-0.5 * pre * pre) * 0.3989422804014327
    return pre * half, half + pre * density


TAIL = 8
GROUP = 32
FIRST_ROUTER = 11


def layers_kernel(g, names, *refs):
    r = types.SimpleNamespace(**dict(zip(names, refs, strict=True)))
    width, span, hidden, cols, head_cols = g.width, g.span, g.hidden, g.cols, g.head_cols
    sec = lax.axis_index("section")
    dev = lax.axis_index("dp")
    core = lax.rem(dev, 2)
    chip = lax.div(dev, 2)
    sib = dev + 1 - 2 * core
    quarter = g.quarter
    shard_rows = hidden // g.devices
    block_rows = g.chips * quarter

    def peer_section(offset):
        return lax.rem(sec + offset, g.sections)

    def from_section(offset):
        return lax.rem(sec + g.sections - offset, g.sections)

    def peer_chip(offset):
        return lax.rem(chip + offset, g.chips)

    def from_chip(offset):
        return lax.rem(chip + g.chips - offset, g.chips)

    def rows_at(index, size):
        return pl.ds(pl.multiple_of(index * size, size), size)

    def piece_at(index):
        return rows_at(index, g.piece)

    own = piece_at(sec)

    def remote(source, target, send, arrive, where):
        return pltpu.make_async_remote_copy(
            src_ref=source, dst_ref=target, send_sem=send, recv_sem=arrive, device_id=where, device_id_type=MESH
        )

    def at_chip_core(index):
        return {"dp": 2 * index + core}

    started = []
    kept_back = {}

    def do_when(condition, action):
        if condition is None:
            action()
        else:
            pl.when(condition)(action)

    def launch(copy, buffer=None, when=None):
        do_when(when, copy.start)
        if buffer:
            kept_back.setdefault(buffer, []).append((copy, when))
        else:
            started.append((copy, when))

    def settle(buffer):
        for copy, when in kept_back.pop(buffer, []):
            do_when(when, copy.wait_send)

    barrier = pltpu.get_barrier_semaphore()
    partners = [(a, b) for a in range(g.sections) for b in range(g.chips) if a + b and (g.direct or a * b == 0)]
    for section_offset, chip_offset in partners:
        where = {"section": peer_section(section_offset), "dp": 2 * peer_chip(chip_offset) + core}
        pl.semaphore_signal(barrier, inc=1, device_id=where, device_id_type=MESH)
    pl.semaphore_signal(barrier, inc=1, device_id={"dp": sib}, device_id_type=MESH)

    def local(index, source, target):
        return pltpu.make_async_copy(source, target, r.local_s.at[index])

    loads = [local(0, r.e_up, r.v_up), local(1, r.e_down, r.v_down)]
    stores = [local(2, r.v_gup, r.g_eup), local(3, r.v_gdown, r.g_edown)]
    for copy in loads:
        copy.start()

    def scatter_copy(slot, offset):
        return remote(
            r.part.at[slot, piece_at(peer_section(offset))], r.got.at[slot, offset - 1],
            r.scat_s.at[slot, offset - 1], r.scat_r.at[slot, offset - 1], {"section": peer_section(offset)},
        )

    def scatter_start(slot, value):
        r.part[slot] = value.astype(BF16)
        if slot != 7:
            r.mine[...] = value
        for offset in range(1, g.sections):
            launch(scatter_copy(slot, offset))

    def scatter_sum(slot):
        total = r.part[slot, own, :].astype(F32) if slot == 7 else r.mine[own, :]
        for offset in range(1, g.sections):
            scatter_copy(slot, offset).wait_recv()
            total = total + r.got[slot, offset - 1].astype(F32)
        return total

    def share_copy(place, send, arrive, offset, receiving):
        where = from_section(offset) if receiving else peer_section(offset)
        return remote(place, place, send.at[offset - 1], arrive.at[offset - 1], {"section": where})

    def gather_start(buffer, slot, sem):
        place = buffer.at[slot, own]
        for offset in range(1, g.sections):
            launch(share_copy(place, r.gath_s.at[sem], r.gath_r.at[sem], offset, False))

    def gather_wait(buffer, slot, sem):
        for offset in range(1, g.sections):
            place = buffer.at[slot, piece_at(from_section(offset))]
            share_copy(place, r.gath_s.at[sem], r.gath_r.at[sem], offset, True).wait_recv()

    def pair_copy(name, source, target):
        index = g.pairs.index(name)
        return remote(source, target, r.pair_s.at[index], r.pair_r.at[index], {"dp": sib})

    def pair_start(name, source, target, buffer=None):
        launch(pair_copy(name, source, target), buffer)

    def pair_wait(name, target):
        pair_copy(name, target, target).wait_recv()

    def line_copy(name, source, target, offset, receiving):
        index = g.lines.index(name)
        where = from_chip(offset) if receiving else peer_chip(offset)
        return remote(
            source, target, r.line_s.at[index, offset - 1], r.line_r.at[index, offset - 1], at_chip_core(where)
        )

    last_chip = g.chips - 1
    is_end = lax.rem(chip, max(last_chip, 1)) == 0
    is_mid = lax.rem(chip, max(last_chip, 1)) != 0
    line_order = (2, 1, 3) if g.relay else range(1, g.chips)
    outward = jnp.clip(chip - 1, 0, 1)

    def near_to(offset):
        return {1: chip != last_chip, last_chip: chip != 0}.get(offset) if g.relay else None

    def near_from(offset):
        return {1: chip != 0, last_chip: chip != last_chip}.get(offset) if g.relay else None

    def spread_start(name, source, target, buffer=None):
        for offset in line_order:
            launch(line_copy(name, source, target, offset, False), buffer, near_to(offset))

    def spread_relay(name, place, buffer):
        index = g.lines.index(name)
        copy = remote(
            place, place, r.line_s.at[index, last_chip], r.line_r.at[index, outward * 2],
            at_chip_core(outward * last_chip),
        )
        launch(copy, buffer, is_mid)

    def spread_wait(name, place_at, buffer):
        for offset in line_order:
            place = place_at(from_chip(offset))
            line_copy(name, place, place, offset, True).wait_recv()
            if g.relay and offset == 2:
                spread_relay(name, place, buffer)

    def far_wait(name, place_at):
        for offset in (1, last_chip):
            place = place_at(from_chip(offset))
            copy = line_copy(name, place, place, offset, True)
            pl.when(jnp.logical_not(near_from(offset)))(copy.wait_recv)

    def line_start(name, source_at, target, buffer=None):
        for offset in range(1, g.chips):
            launch(line_copy(name, source_at(peer_chip(offset)), target, offset, False), buffer)

    def line_wait(name, target_at):
        for offset in range(1, g.chips):
            target = target_at(from_chip(offset), offset)
            line_copy(name, target, target, offset, True).wait_recv()

    def rows_line_start(name, source, target):
        line_start(name, lambda at: source.at[rows_at(at, quarter)], target.at[core, g.my_part(sec), rows_at(chip, quarter)])
        target[core, g.my_part(sec), rows_at(chip, quarter), :] = source[rows_at(chip, quarter), :]

    def rows_plane_start(name, target):
        line_wait(name, lambda at, _: target.at[core, g.my_part(sec), rows_at(at, quarter)])
        place = target.at[core, g.my_part(sec)]
        if g.parts > 1:
            index = g.planes.index(name)
            for offset in range(1, g.sections):
                launch(share_copy(place, r.plane_s.at[index], r.plane_r.at[index], offset, False))
        pair_start(name + "0", place, place)

    def rows_plane_wait(name, target, offset):
        index = g.planes.index(name)
        place = target.at[core, from_section(offset)]
        share_copy(place, r.plane_s.at[index], r.plane_r.at[index], offset, True).wait_recv()
        pair_start(name + str(offset), place, place)

    def rows_pair_wait(name, target, offset):
        pair_wait(name + str(offset), target.at[1 - core, g.my_part(from_section(offset))])

    top = cols - TAIL
    half = width // 2
    part_cols = head_cols // 2
    tail_lane = head_cols + 2 * GROUP

    def qkv_section(at_dev, index, section):
        return lax.rem(lax.div(3 * at_dev + index, g.devices) - section + g.sections, g.sections)

    def qkv_send(layer, offsets):
        for index in range(3):
            to = qkv_section(dev, index, sec)
            for offset in offsets:
                copy = remote(
                    r.pq.at[layer, index], r.rq.at[layer, core, chip, index],
                    r.wq_s.at[layer, index, offset], r.wq_r.at[layer, index, offset],
                    {"section": to, "dp": 2 * peer_chip(offset) + core},
                )
                if offset:
                    launch(copy, None, near_to(offset))
                else:
                    pl.when(to != sec)(copy.start)

                    @pl.when(to == sec)
                    def _(index=index):
                        r.rq[layer, core, chip, index] = r.pq[layer, index]

    def qkv_arrive(layer, offsets):
        for offset in offsets:
            for index in range(3):
                at_chip = from_chip(offset)
                target = r.rq.at[layer, core, at_chip, index]
                origin = qkv_section(2 * at_chip + core, index, sec)
                copy = remote(
                    target, target, r.wq_s.at[layer, index, offset], r.wq_r.at[layer, index, offset],
                    {"section": origin, "dp": 2 * at_chip + core},
                )
                if offset:
                    do_when(near_from(offset), copy.wait_recv)
                else:

                    @pl.when(origin != sec)
                    def _(copy=copy):
                        copy.wait_recv()
                        copy.wait_send()

            if g.relay and offset == 2:
                spread_relay("qkv0", r.rq.at[0, core, from_chip(offset)], "qkv0")
        if g.relay and len(offsets) > 1:
            far_wait("qkv0", lambda at: r.rq.at[0, core, at])

    def out_copy(section_offset, offset, place, receiving):
        if receiving:
            to, at_chip = from_section(section_offset), from_chip(offset)
        else:
            to, at_chip = peer_section(section_offset), peer_chip(offset)
        source = place if receiving else r.po.at[to]
        return remote(
            source, place, r.wo_s.at[section_offset, offset], r.wo_r.at[section_offset, offset],
            {"section": to, "dp": 2 * at_chip + core},
        )

    def out_offsets():
        return [(a, b) for b in (*line_order, 0) for a in range(g.sections) if a + b]

    def plane_copy(name, source, target, offset, receiving):
        index = g.planes.index(name)
        where = from_section(offset) if receiving else peer_section(offset)
        return remote(
            source, target, r.plane_s.at[index, offset - 1], r.plane_r.at[index, offset - 1], {"section": where}
        )

    def pack_wide(block):
        tail = jnp.concatenate([block[top:, :half], block[top:, half:]], axis=0)
        return jnp.concatenate([block[:top], tail], axis=1).astype(BF16)

    def pack_out(block):
        small = jnp.concatenate([block[top:, head_cols:]] * 2, axis=0)
        tail = jnp.concatenate([block[top:, :part_cols], block[top:, part_cols:head_cols]], axis=0)
        empty = jnp.zeros((top, g.out_lanes - tail_lane - part_cols), F32)
        return jnp.concatenate([block[:top], small, tail, empty], axis=1).astype(BF16)

    def unpack_wide(target, first, piece):
        target[first : first + top, 0:width] = piece[:, 0:width]
        target[first + top : first + cols, 0:half] = piece[0:TAIL, width : width + half]
        target[first + top : first + cols, half:width] = piece[TAIL:, width : width + half]

    def unpack_out(target, first, piece, lane=0):
        last = slice(first + top, first + cols)
        tail = slice(tail_lane, tail_lane + part_cols)
        target[first : first + top, lane : lane + head_cols] = piece[:, 0:head_cols]
        target[last, lane : lane + part_cols] = piece[0:TAIL, tail]
        target[last, lane + part_cols : lane + head_cols] = piece[TAIL:, tail]

    def unpack_small(target, first, piece, lane):
        target[first : first + top, lane : lane + GROUP] = piece[:, head_cols : head_cols + GROUP]
        target[first + top : first + cols, lane : lane + GROUP] = piece[0:TAIL, head_cols + GROUP : tail_lane]

    def shard_places():
        for at_core in range(2):
            for at_chip in range(g.chips):
                for at_sec in range(g.sections):
                    yield at_core, at_chip, at_sec, (at_sec * g.devices + 2 * at_chip + at_core) * cols

    def chunk_places():
        for at_core in range(2):
            for at_chip in range(g.chips):
                for index in range(3):
                    yield at_core, at_chip, index, (3 * (2 * at_chip + at_core) + index) * cols

    def unfold_out(layer):
        for at_core, at_chip, at_sec, first in shard_places():
            if layer:
                piece = r.rd[at_core, at_chip, at_sec, :, width + half :].astype(F32)
            else:
                piece = r.ro[at_core, at_chip, at_sec].astype(F32)
                unpack_small(r.tmp, first, piece, head_cols)
            unpack_out(r.tmp, first, piece)
        flipped = r.tmp[:, 0:tail_lane].T
        r.w_out[layer] = flipped[:head_cols].astype(BF16)
        if layer == 0:
            r.prm[...] = flipped[head_cols : head_cols + GROUP]
            r.w_router[...] = r.tmp[:, tail_lane - LANES : tail_lane].astype(BF16)

    def unfold_qkv(layer):
        for at_core, at_chip, index, first in chunk_places():
            unpack_wide(r.tmp, first, r.rq[layer, at_core, at_chip, index].astype(F32))
        r.w_qkv[layer] = r.tmp[0 : 3 * head_cols, 0:width].astype(BF16)

    def unfold_down():
        for at_core, at_chip, at_sec, first in shard_places():
            unpack_wide(r.tmp, first, r.rd[at_core, at_chip, at_sec].astype(F32))
        r.w_down[...] = r.tmp[...].astype(BF16)

    def grad_line(name, buffer_at, landing, target, passed):
        pair_wait(name, landing)
        for at_chip in range(g.chips):
            block = buffer_at(at_chip)
            block[...] = (block[...].astype(F32) + landing[at_chip].astype(F32)).astype(BF16)
        if g.relay:
            index = g.lines.index(name)
            copy = remote(
                buffer_at(last_chip - chip), passed, r.line_s.at[index, last_chip], r.line_r.at[index, last_chip],
                at_chip_core(1 + lax.div(chip, last_chip)),
            )
            launch(copy, None, is_end)
            for offset in (1, last_chip):

                @pl.when(jnp.logical_not(near_from(offset)))
                def _(offset=offset):
                    target[offset - 1] = jnp.zeros_like(target[offset - 1])

        for offset in line_order:
            copy = line_copy(name, buffer_at(peer_chip(offset)), target.at[offset - 1], offset, False)
            if g.relay and offset == 2:
                pl.when(is_end)(copy.start)
                started.append((copy, None))
            else:
                launch(copy, None, near_to(offset))

    def grad_relay(name, buffer_at, target, passed):
        if g.relay:
            index = g.lines.index(name)
            block = buffer_at(peer_chip(2))
            copy = line_copy(name, block, target.at[1], 2, False)

            @pl.when(is_mid)
            def _():
                remote(
                    passed, passed, r.line_s.at[index, last_chip], r.line_r.at[index, last_chip],
                    at_chip_core(outward * last_chip),
                ).wait_recv()
                block[...] = (block[...].astype(F32) + passed[...].astype(F32)).astype(BF16)
                copy.start()

    def grad_line_sum(name, buffer_at, target):
        for offset in line_order:
            place = target.at[offset - 1]
            do_when(near_from(offset), line_copy(name, place, place, offset, True).wait_recv)
        total = buffer_at(chip)[...].astype(F32)
        for offset in range(1, g.chips):
            total = total + target[offset - 1].astype(F32)
        return total

    def qkv_at(layer):
        return lambda at: r.rq.at[layer, core, at]

    def down_at(at):
        return r.rd.at[core, at]

    def out_at(at):
        return r.ro.at[core, at]

    def up_at(at):
        return r.ru.at[at, core]

    def bias_at(at):
        return r.rb.at[at, core]

    def grad_plane(name, buffer_at, target, summed, final):
        summed[...] = grad_line_sum(name, buffer_at, target).astype(BF16)
        for offset in range(1, g.sections):
            source = summed.at[peer_section(offset)]
            launch(plane_copy(name, source, final.at[sec], offset, False))
        final[sec] = summed[sec]

    def grad_plane_wait(name, final):
        for offset in range(1, g.sections):
            place = final.at[from_section(offset)]
            plane_copy(name, place, place, offset, True).wait_recv()

    def grad_qkv_copy(layer, index, place, where):
        return remote(
            r.mq.at[layer, index], place, r.gq_s.at[layer, index], r.gq_r.at[layer, index], {"section": where}
        )

    def grad_qkv_plane(layer):
        r.mq[layer] = grad_line_sum("gqkv" + str(layer), qkv_at(layer), r.aq.at[layer]).astype(BF16)
        for index in range(3):
            to = qkv_section(dev, index, sec)
            copy = grad_qkv_copy(layer, index, r.fq.at[layer, index], to)
            pl.when(to != sec)(copy.start)

            @pl.when(to == sec)
            def _(index=index):
                r.fq[layer, index] = r.mq[layer, index]

    def grad_qkv_finish(layer):
        for index in range(3):
            origin = qkv_section(dev, index, sec)
            copy = grad_qkv_copy(layer, index, r.fq.at[layer, index], origin)

            @pl.when(origin != sec)
            def _(copy=copy):
                copy.wait_recv()
                copy.wait_send()

            unpack_wide(r.o_qkv.at[layer], index * cols, r.fq[layer, index].astype(F32))

    def norm_into(source, target, index):
        @pl.loop(0, g.sections)
        def _(step):
            at = piece_at(step)
            unit, _ = normalize(source[at, :].astype(F32))
            target[at, :] = (unit * r.prm[index : index + 1, :] + r.prm[4 + index : 5 + index, :]).astype(BF16)

    place_row = jnp.concatenate(
        [r.routes[m : m + 1] * span + m * g.cap + r.slots[m : m + 1] for m in range(g.micro)], axis=1
    )
    r.square[...] = jnp.zeros_like(r.square)
    if g.direct:
        r.square[0:4, 0:cols] = r.norm_gain[...].astype(F32)
        r.square[4:8, 0:cols] = r.norm_bias[...].astype(F32)
        r.square[8:10, 0:cols] = r.out_bias[...].astype(F32)
        r.square[10:11, 0:cols] = r.down_bias[...].astype(F32)
        r.pb[...] = jnp.zeros_like(r.pb)
        r.pb[:, 0:shard_rows] = jnp.broadcast_to(r.up_bias[...], (r.pb.shape[0], shard_rows))
        r.square[FIRST_ROUTER : FIRST_ROUTER + g.experts, 0:cols] = r.router[...].astype(F32)
        r.square[...] = r.square[...].T
        shard = r.wo[0].astype(F32)
        mine = r.square[0:cols, 0:GROUP]
        for at_sec in range(g.sections):
            block = shard[:, at_sec * head_cols : (at_sec + 1) * head_cols]
            r.po[at_sec] = pack_out(jnp.concatenate([block, mine], axis=1))
        shard = r.wq[0].astype(F32)
        for index in range(3):
            r.pq[0, index] = pack_wide(shard[index * cols : (index + 1) * cols])
    pl.semaphore_wait(barrier, len(partners) + 1)
    if g.direct:
        for section_offset, offset in out_offsets():
            launch(out_copy(section_offset, offset, r.ro.at[core, chip, sec], False), None, near_to(offset))
        r.ro[core, chip, sec] = r.po[sec]
        qkv_send(0, (*line_order, 0))
        shard = r.wq[1].astype(F32)
        for index in range(3):
            r.pq[1, index] = pack_wide(shard[index * cols : (index + 1) * cols])
        shard, other = r.wd[...].astype(F32), r.wo[1].astype(F32)
        empty = jnp.zeros((cols, GROUP), F32)
        for at_sec in range(g.sections):
            r.pd[at_sec, :, 0 : width + half] = pack_wide(shard[:, at_sec * hidden : (at_sec + 1) * hidden])
            block = other[:, at_sec * head_cols : (at_sec + 1) * head_cols]
            r.pd[at_sec, :, width + half :] = pack_out(jnp.concatenate([block, empty], axis=1))

    slot_ids = lax.broadcasted_iota(jnp.int32, (quarter, g.tokens), 0)
    for expert in range(g.chips):
        first = expert * span + (sec * quarter if g.parts > 1 else 0)
        match = jnp.where(slot_ids + first == place_row, 1.0, 0.0)
        r.table[expert * quarter : (expert + 1) * quarter, :] = match.astype(BF16)
    r.dispc[...] = mm(r.table[...], r.cot[...]).astype(BF16)
    r.small[...] = jnp.zeros_like(r.small)
    if g.direct:
        for section_offset, offset in out_offsets():
            place = r.ro.at[core, from_chip(offset), from_section(section_offset)]
            do_when(near_from(offset), out_copy(section_offset, offset, place, True).wait_recv)
            if g.relay and (section_offset, offset) == (g.sections - 1, 2):
                spread_relay("out", r.ro.at[core, from_chip(offset)], "out")
        if g.relay:
            far_wait("out", lambda at: r.ro.at[core, at])
        pair_start("out", r.ro.at[core], r.ro.at[core], "out")
        qkv_arrive(0, (*line_order, 0))
        pair_start("qkv0", r.rq.at[0, core], r.rq.at[0, core], "qkv0")
        spread_start("bias", r.pb, r.rb.at[chip, core])
        r.rb[chip, core] = r.pb[...]
        spread_start("up", r.wu, r.ru.at[chip, core])
        r.ru[chip, core] = r.wu[...]
        for offset in range(1, g.sections):
            launch(plane_copy("down", r.pd.at[peer_section(offset)], r.rd.at[core, chip, sec], offset, False))
        r.rd[core, chip, sec] = r.pd[sec]
        qkv_send(1, [0])
        pair_wait("out", r.ro.at[1 - core])
        unfold_out(0)
        pair_wait("qkv0", r.rq.at[0, 1 - core])
        unfold_qkv(0)

    def weights_line_start():
        for offset in range(1, g.sections):
            place = r.rd.at[core, chip, from_section(offset)]
            plane_copy("down", place, place, offset, True).wait_recv()
        spread_start("down", r.rd.at[core, chip], r.rd.at[core, chip], "down")
        qkv_arrive(1, [0])
        spread_start("qkv1", r.rq.at[1, core, chip], r.rq.at[1, core, chip], "qkv1")

    key_ids = lax.broadcasted_iota(jnp.int32, (g.seq, g.seq), 0)
    query_ids = lax.broadcasted_iota(jnp.int32, (g.seq, g.seq), 1)
    scale = HEAD_DIM**-0.5

    def block_of(index):
        return lax.rem(index + sec, 3) if g.direct else index

    def head_slice(head):
        return slice(head * HEAD_DIM, (head + 1) * HEAD_DIM)

    def token_slice(micro):
        return slice(micro * g.seq, (micro + 1) * g.seq)

    def attention_forward(layer, stream, slot):
        norm_into(stream, r.normed.at[2 * layer], 2 * layer)
        packed = mm_nt(r.w_qkv[layer], r.normed[2 * layer]).astype(BF16)
        r.qkv[layer] = packed.reshape(3, head_cols, g.tokens)
        for micro in range(g.micro):
            allowed = (key_ids <= query_ids) & (key_ids < r.lens[:, micro : micro + 1])
            for head in range(g.heads):
                at = token_slice(micro)
                key = r.qkv[layer, block_of(1), head_slice(head), at]
                scores = mm_tn(key, r.qkv[layer, block_of(0), head_slice(head), at]) * scale
                scores = jnp.where(allowed, scores, MASKED)
                weight = jnp.exp(scores - jnp.max(scores, axis=0, keepdims=True))
                weight = weight / jnp.sum(weight, axis=0, keepdims=True)
                r.probs[layer, micro, head] = weight
                value = r.qkv[layer, block_of(2), head_slice(head), at]
                r.ctx[layer, head_slice(head), at] = mm(value, weight.astype(BF16)).astype(BF16)
        scatter_start(slot, mm_tn(r.ctx[layer], r.w_out[layer]))

    def finish_forward(section, bias, stream):
        total = scatter_sum(section) + bias + stream[own, :].astype(F32)
        r.xs[section, own, :] = total.astype(BF16)
        gather_start(r.xs, section, section)

    attention_forward(0, r.x0, 0)
    if g.direct:
        weights_line_start()
    finish_forward(0, r.prm[8:9, :], r.x0)
    if g.direct:
        spread_wait("bias", lambda at: r.rb.at[at, core], "bias")
        spread_wait("up", lambda at: r.ru.at[at, core], "up")
        pair_start("up", r.ru.at[:, core], r.ru.at[:, core], "up")
        pair_start("bias", r.rb.at[:, core], r.rb.at[:, core], "bias")
        pair_wait("up", r.ru.at[:, 1 - core])
        pair_wait("bias", r.rb.at[:, 1 - core])
        for at_dev in range(g.devices):
            row = r.rb[at_dev // 2, at_dev % 2, :, 0:shard_rows].astype(F32)
            r.b_up[:, at_dev * shard_rows : (at_dev + 1) * shard_rows] = row[0:TAIL]
    gather_wait(r.xs, 0, 0)

    def up_rows(at):
        if g.direct:
            return r.ru[...].reshape(hidden, width)[at]
        return r.w_up[at, :]

    norm_into(r.xs.at[0], r.normed.at[1], 1)
    for block in range(hidden // g.block):
        at = slice(block * g.block, (block + 1) * g.block)
        pre = mm_nt(r.normed[1], up_rows(at)) + r.b_up[0:1, at]
        value, slope = gelu_parts(pre)
        r.act[:, at] = value.astype(BF16)
        r.dgelu[:, at] = slope
    if g.direct:
        spread_wait("down", lambda at: r.rd.at[core, at], "down")
        pair_start("down", r.rd.at[core], r.rd.at[core], "down")
        pair_wait("down", r.rd.at[1 - core])
        unfold_down()
    scatter_start(1, mm_nt(r.act[...], r.w_down[...]))
    finish_forward(1, r.prm[10:11, :], r.xs.at[0])
    if g.direct:
        spread_wait("qkv1", lambda at: r.rq.at[1, core, at], "qkv1")
        pair_start("qkv1", r.rq.at[1, core], r.rq.at[1, core], "qkv1")
    rows_line_start("crow", r.dispc, r.crow)
    if g.direct:
        unfold_out(1)
        pair_wait("qkv1", r.rq.at[1, 1 - core])
        unfold_qkv(1)
    gather_wait(r.xs, 1, 1)

    attention_forward(1, r.xs.at[1], 2)
    finish_forward(2, r.prm[9:10, :], r.xs.at[1])
    gather_wait(r.xs, 2, 2)

    wide = r.wide
    norm_into(r.xs.at[2], wide.at[:, pl.ds(0, width)], 3)
    logits = mm(wide[:, :width], r.w_router[...])
    lane = lax.broadcasted_iota(jnp.int32, logits.shape, 1) - g.router_lane
    r.square[0 : g.micro, :] = jnp.concatenate(
        [place_row[:, token_slice(m)] for m in range(g.micro)], axis=0
    ).astype(F32)
    columns = r.square[...].T
    place_col = jnp.concatenate([columns[:, m : m + 1] for m in range(g.micro)], axis=0).astype(jnp.int32)
    chosen = (place_col >= lane * span) & (place_col < lane * span + span)
    score = jnp.sum(jnp.where(chosen, logits, 0.0), axis=-1, keepdims=True)
    gate = 1.0 / (1.0 + jnp.exp(-score))
    gate_high = gate.astype(BF16).astype(F32)
    lane = lax.broadcasted_iota(jnp.int32, (g.tokens, LANES), 1)
    pair = jnp.where(lane == 0, gate_high, jnp.where(lane == 1, gate - gate_high, 0.0))
    wide[:, width:] = pair.astype(BF16)
    r.disp[...] = mm(r.table[...], wide[...]).astype(BF16)
    rows_line_start("rows", r.disp, r.rows)
    rows_plane_start("crow", r.crow)
    rows_plane_start("rows", r.rows)

    own_router = FIRST_ROUTER + chip
    router_row = r.prm[pl.ds(own_router, 1), :]

    def expert_block(side, part, at, keep_first):
        row = r.rows[side, part, at, :width]
        tail = r.rows[side, part, at, width:].astype(F32)
        gate_row = tail[:, 0:1] + tail[:, 1:2]
        grad_row = (gate_row * r.crow[side, part, at, :].astype(F32)).astype(BF16)
        r.grow[side, part, at, :] = grad_row
        value, slope = gelu_parts(mm(row, r.v_up[...]))
        value = value.astype(BF16)
        r.acte[side, part, at, :] = value
        result = mm(value, r.v_down[...])
        total = jnp.sum(grad_row.astype(F32) * result, axis=-1, keepdims=True) * (1.0 - gate_row)
        inner = (slope * mm_nt(grad_row, r.v_down[...])).astype(BF16)
        r.dpree[side, part, at, :] = inner
        back = mm_nt(inner, r.v_up[...]) + total * router_row
        r.small[pl.ds(own_router, 1), :] += jnp.sum(row.astype(F32) * total, axis=0, keepdims=True)
        result = result * gate_row
        if keep_first:
            r.keep_d[part, at, :] = back
            r.keep_y[part, at, :] = result
        else:
            r.snd_d[part, at, :] = back.astype(BF16)
            r.snd_y[part, at, :] = result.astype(BF16)

    def expert_part(side, part, keep_first):
        if block_rows <= g.block:
            expert_block(side, part, slice(None), keep_first)
            return

        @pl.loop(0, block_rows // g.block)
        def _(step):
            expert_block(side, part, rows_at(step, g.block), keep_first)

    def merge(which, offset):
        part = g.my_part(from_section(offset))
        pair_wait(which + str(offset), rcv[which].at[part])
        return kept[which][part] + rcv[which][part].astype(F32)

    snd = {"d": r.snd_d, "y": r.snd_y}
    kept = {"d": r.keep_d, "y": r.keep_y}
    rcv = {"d": r.rcv_d, "y": r.rcv_y}

    def merge_send(offset):
        to = g.sections - offset
        r.out_d[offset - 1] = merge("d", offset).astype(BF16)
        launch(plane_copy("d", r.out_d.at[offset - 1], r.plane_d.at[to - 1], to, False))

    def expert_back_line():
        total = merge("d", 0)
        if g.parts > 1:
            for offset in range(1, g.sections):
                place = r.plane_d.at[offset - 1]
                plane_copy("d", place, place, offset, True).wait_recv()
                total = total + place[...].astype(F32)
        r.ret_d[...] = total.astype(BF16)
        line_start("d", lambda at: r.ret_d.at[rows_at(at, quarter)], r.back_d.at[rows_at(chip, quarter)])
        r.back_d[rows_at(chip, quarter), :] = r.ret_d[rows_at(chip, quarter), :]

    def expert_combine():
        line_wait("d", lambda at, _: r.back_d.at[rows_at(at, quarter)])
        line_start("y", lambda at: r.ret_y.at[:, rows_at(at, quarter)], r.back_y.at[chip])
        r.back_y[chip] = r.ret_y[:, rows_at(chip, quarter), :]
        scatter_start(3, mm_tn(r.table[...], r.back_d[...]))

    def results_combine():
        line_wait("y", lambda at, _: r.back_y.at[at])
        span_ids = lax.broadcasted_iota(jnp.int32, (g.chips * span, g.tokens), 0)
        whole = jnp.where(span_ids == place_row, 1.0, 0.0).astype(BF16)
        scatter_start(7, mm_tn(whole, r.back_y[...].reshape(g.chips * span, width)))

    offsets = range(1, g.sections) if g.parts > 1 else []
    for copy in loads:
        copy.wait()
    expert_part(core, g.my_part(sec), True)
    rows_pair_wait("crow", r.crow, 0)
    rows_pair_wait("rows", r.rows, 0)
    expert_part(1 - core, g.my_part(sec), False)
    for which in ("d", "y"):
        place = g.my_part(sec)
        pair_start(which + "0", snd[which].at[place], rcv[which].at[place])
    for offset in offsets:
        rows_plane_wait("crow", r.crow, offset)
    for offset in offsets:
        rows_plane_wait("rows", r.rows, offset)
    for offset in offsets:
        part = from_section(offset)
        expert_part(core, part, True)
        rows_pair_wait("rows", r.rows, offset)
        rows_pair_wait("crow", r.crow, offset)
        expert_part(1 - core, part, False)
        for which in ("d", "y"):
            pair_start(which + str(offset), snd[which].at[part], rcv[which].at[part])
        if offset > 1:
            merge_send(offset - 1)
    if g.parts > 1:
        merge_send(g.sections - 1)
    expert_back_line()
    for offset in range(g.parts):
        r.ret_y[g.my_part(from_section(offset))] = merge("y", offset).astype(BF16)

    def flat(ref, side):
        value = ref[side]
        return value.reshape(g.parts * block_rows, value.shape[-1])

    def expert_weights(left, right, lanes):
        return mm_tn(flat(left, 0)[:, :lanes], flat(right, 0)) + mm_tn(flat(left, 1)[:, :lanes], flat(right, 1))

    r.v_gup[...] = expert_weights(r.rows, r.dpree, width)
    r.v_gdown[...] = expert_weights(r.acte, r.grow, r.acte.shape[-1])
    for copy in stores:
        copy.start()

    def finish_backward(section, slot, stream, above):
        grad = scatter_sum(slot)
        unit, inverse = normalize(stream[own, :].astype(F32))
        r.small[section : section + 1, :] = jnp.sum(grad * unit, axis=0, keepdims=True)
        r.small[4 + section : 5 + section, :] = jnp.sum(grad, axis=0, keepdims=True)
        grad = grad * r.prm[section : section + 1, :]
        shared = jnp.mean(grad, axis=-1, keepdims=True)
        along = jnp.mean(grad * unit, axis=-1, keepdims=True)
        grad = inverse * (grad - shared - unit * along) + above[own, :].astype(F32)
        r.gs[section, own, :] = grad.astype(BF16)
        gather_start(r.gs, section, 4 + section)

    expert_combine()
    finish_backward(3, 3, r.xs.at[2], r.cot)
    gather_wait(r.gs, 3, 7)

    def bias_row(index, section):
        r.small[index : index + 1, :] = jnp.sum(r.gs[section, own, :].astype(F32), axis=0, keepdims=True)

    def attention_backward(layer, section, slot):
        grad = r.gs[section + 1]
        dctx = mm_nt(r.w_out[layer], grad).astype(BF16)
        for micro in range(g.micro):
            for head in range(g.heads):
                at = token_slice(micro)
                weight = r.probs[layer, micro, head]
                low = weight.astype(BF16)
                dhead = dctx[head_slice(head), at]
                query = r.qkv[layer, block_of(0), head_slice(head), at]
                key = r.qkv[layer, block_of(1), head_slice(head), at]
                value = r.qkv[layer, block_of(2), head_slice(head), at]
                dprobs = mm_tn(value, dhead)
                delta = jnp.sum(weight * dprobs, axis=0, keepdims=True)
                dscores = (weight * (dprobs - delta)).astype(BF16)
                r.dqkv[block_of(0), head_slice(head), at] = (mm(key, dscores) * scale).astype(BF16)
                r.dqkv[block_of(1), head_slice(head), at] = (mm_nt(query, dscores) * scale).astype(BF16)
                r.dqkv[block_of(2), head_slice(head), at] = mm_nt(dhead, low).astype(BF16)
        flat_grad = r.dqkv[...].reshape(3 * head_cols, g.tokens)
        scatter_start(slot, mm_tn(flat_grad, r.w_qkv[layer]))
        bias_row(8 + layer, section + 1)

    def attention_weights(layer, section):
        grad_qkv = mm(r.dqkv[...].reshape(3 * head_cols, g.tokens), r.normed[2 * layer])
        if not g.direct:
            r.o_qkv[layer] = grad_qkv
            r.o_out[layer] = mm(r.ctx[layer], r.gs[section + 1])
            return
        r.tmp[0 : 3 * head_cols, :] = grad_qkv
        settle("qkv" + str(layer))
        for at_core, at_chip, index, first in chunk_places():
            r.rq[layer, at_core, at_chip, index] = pack_wide(r.tmp[first : first + cols, :])
        name = "gqkv" + str(layer)
        pair_start(name, r.rq.at[layer, 1 - core], r.hq.at[layer])
        r.tmp[:, 0:head_cols] = dot_as(r.gs[section + 1], r.ctx[layer], 0, 1)
        if layer:
            settle("down")
            r.tmp[:, head_cols : head_cols + GROUP] = jnp.zeros((width, GROUP), F32)
            for at_core, at_chip, at_sec, first in shard_places():
                block = r.tmp[first : first + cols, 0 : head_cols + GROUP]
                r.rd[at_core, at_chip, at_sec, :, width + half :] = pack_out(block)

    attention_backward(1, 2, 4)
    attention_weights(1, 2)
    finish_backward(2, 4, r.xs.at[1], r.gs.at[3])
    if g.direct:
        grad_line("gqkv1", qkv_at(1), r.hq.at[1], r.aq.at[1], r.lq.at[1])
    gather_wait(r.gs, 2, 6)

    grad_two = r.gs[2]
    for block in range(hidden // g.block):
        at = slice(block * g.block, (block + 1) * g.block)
        r.dpre[:, at] = (r.dgelu[:, at] * mm(grad_two, r.w_down[:, at])).astype(BF16)
    scatter_start(5, mm(r.dpre[...], up_rows(slice(None))))
    bias_row(10, 2)
    if g.direct:
        grad_relay("gqkv1", qkv_at(1), r.aq.at[1], r.lq.at[1])
    sum_up = jnp.sum(r.dpre[...].astype(F32), axis=0, keepdims=True)
    if g.direct:
        r.tmp[...] = mm_tn(r.gs[2], r.act[...])
        for at_core, at_chip, at_sec, first in shard_places():
            r.rd[at_core, at_chip, at_sec, :, 0 : width + half] = pack_wide(r.tmp[first : first + cols, :])
        pair_start("gdown", r.rd.at[1 - core], r.hd)
        settle("up")
        settle("bias")
        r.ru[...] = mm_tn(r.dpre[...], r.normed[1]).astype(BF16).reshape(r.ru.shape)
        pair_start("gup", r.ru.at[:, 1 - core], r.hu)
        for at_dev in range(g.devices):
            row = sum_up[:, at_dev * shard_rows : (at_dev + 1) * shard_rows]
            row = jnp.broadcast_to(row, (r.pb.shape[0], shard_rows)).astype(BF16)
            r.rb[at_dev // 2, at_dev % 2, :, 0:shard_rows] = row
        pair_start("gbias", r.rb.at[:, 1 - core], r.hb)
    else:
        r.o_down[...] = mm_tn(r.gs[2], r.act[...])
        r.o_up[...] = mm_tn(r.dpre[...], r.normed[1])
        r.o_bup[...] = sum_up
    finish_backward(1, 5, r.xs.at[0], r.gs.at[2])
    if g.direct:
        grad_line("gbias", bias_at, r.hb, r.ab, r.lb)
        grad_line("gdown", down_at, r.hd, r.ad, r.ld)
        grad_line("gup", up_at, r.hu, r.au, r.lu)
    gather_wait(r.gs, 1, 5)

    attention_backward(0, 0, 6)
    results_combine()
    attention_weights(0, 0)
    if g.direct:
        grad_relay("gbias", bias_at, r.ab, r.lb)
        grad_relay("gdown", down_at, r.ad, r.ld)
    finish_backward(0, 6, r.x0, r.gs.at[1])
    r.xs[3, own, :] = (scatter_sum(7) + r.xs[2, own, :].astype(F32)).astype(BF16)
    gather_start(r.xs, 3, 3)
    if g.direct:
        settle("out")
        kinds = r.small[...]
        padded = jnp.concatenate([kinds, jnp.zeros((LANES - kinds.shape[0], width), F32)], axis=0)
        r.tmp[:, head_cols : head_cols + GROUP] = padded.T[:, 0:GROUP]
        for at_core, at_chip, at_sec, first in shard_places():
            r.ro[at_core, at_chip, at_sec] = pack_out(r.tmp[first : first + cols, 0 : head_cols + GROUP])
        pair_start("gout", r.ro.at[1 - core], r.ho)
        grad_relay("gup", up_at, r.au, r.lu)
        grad_line("gqkv0", qkv_at(0), r.hq.at[0], r.aq.at[0], r.lq.at[0])
        grad_line("gout", out_at, r.ho, r.ao, r.lo)
    if g.direct:
        grad_qkv_plane(1)
        grad_plane("gdown", down_at, r.ad, r.md, r.fd)
    if g.direct:
        grad_relay("gqkv0", qkv_at(0), r.aq.at[0], r.lq.at[0])
        grad_relay("gout", out_at, r.ao, r.lo)
    if g.direct:
        r.o_up[...] = grad_line_sum("gup", up_at, r.au)
        r.o_bup[...] = grad_line_sum("gbias", bias_at, r.ab)[0:1, 0:shard_rows]
        grad_qkv_finish(1)
        grad_plane_wait("gdown", r.fd)
        for at_sec in range(g.sections):
            piece = r.fd[at_sec].astype(F32)
            unpack_wide(r.o_down.at[:, pl.ds(at_sec * hidden, hidden)], 0, piece)
            unpack_out(r.o_out.at[1], 0, piece[:, width + half :], at_sec * head_cols)
        grad_qkv_plane(0)
        grad_plane("gout", out_at, r.ao, r.mo, r.fo)
        grad_qkv_finish(0)
        grad_plane_wait("gout", r.fo)
        everyone = jnp.zeros((top, g.out_lanes), F32)
        for at_sec in range(g.sections):
            piece = r.fo[at_sec].astype(F32)
            unpack_out(r.o_out.at[0], 0, piece, at_sec * head_cols)
            everyone = everyone + piece
        r.square[...] = jnp.zeros_like(r.square)
        unpack_small(r.square, 0, everyone, 0)
        r.square[...] = r.square[...].T
        r.o_router[...] = r.square[FIRST_ROUTER : FIRST_ROUTER + g.experts, 0:cols]
        r.o_gain[...] = r.square[0:4, 0:cols]
        r.o_bias[...] = r.square[4:8, 0:cols]
        r.o_bout[...] = r.square[8:10, 0:cols]
        r.o_bdown[...] = r.square[10:11, 0:cols]
    else:
        r.o_small[...] = r.small[...]
    gather_wait(r.xs, 3, 3)
    gather_wait(r.gs, 0, 4)
    r.sec_out[...] = r.xs[sec]
    r.sec_grad[...] = r.gs[sec]
    for copy in stores:
        copy.wait()
    for copy, when in started:
        do_when(when, copy.wait_send)


def run_layers(g, operands):
    tokens, width, hidden, sections, chips = g.tokens, g.width, g.hidden, g.sections, g.chips
    part_rows = chips * g.quarter
    inner = operands["e_down"].shape[0]
    three = 3 * g.head_cols
    shape = jax.ShapeDtypeStruct
    vmem = pltpu.VMEM
    dma = pltpu.SemaphoreType.DMA
    top = g.cols - TAIL
    wide = width + width // 2
    up_rows = hidden // g.devices
    outs = dict(
        sec_out=shape((tokens, width), BF16),
        sec_grad=shape((tokens, width), BF16),
        g_eup=shape((width, inner), F32),
        g_edown=shape((inner, width), F32),
    )
    if g.direct:
        outs |= dict(
            o_qkv=shape((2, 3 * g.cols, width), F32),
            o_out=shape((2, g.cols, width), F32),
            o_up=shape((up_rows, width), F32),
            o_down=shape((g.cols, sections * hidden), F32),
            o_gain=shape((4, g.cols), F32),
            o_bias=shape((4, g.cols), F32),
            o_bout=shape((2, g.cols), F32),
            o_bdown=shape((1, g.cols), F32),
            o_router=shape((g.experts, g.cols), F32),
            o_bup=shape((1, up_rows), F32),
        )
    else:
        outs |= dict(
            o_qkv=shape((2, three, width), F32),
            o_out=shape((2, g.head_cols, width), F32),
            o_up=shape((hidden, width), F32),
            o_down=shape((width, hidden), F32),
            o_bup=shape((1, hidden), F32),
            o_small=shape((g.small, width), F32),
        )
    scratch = dict(
        xs=vmem((4, tokens, width), BF16),
        gs=vmem((4, tokens, width), BF16),
        normed=vmem((3, tokens, width), BF16),
        wide=vmem((tokens, width + LANES), BF16),
        qkv=vmem((2, 3, g.head_cols, tokens), BF16),
        probs=vmem((2, g.micro, g.heads, g.seq, g.seq), F32),
        ctx=vmem((2, g.head_cols, tokens), BF16),
        act=vmem((tokens, hidden), BF16),
        dgelu=vmem((tokens, hidden), F32),
        dpre=vmem((tokens, hidden), BF16),
        dqkv=vmem((3, g.head_cols, tokens), BF16),
        part=vmem((8, tokens, width), BF16),
        got=vmem((8, sections - 1, g.piece, width), BF16),
        mine=vmem((tokens, width), F32),
        square=vmem((LANES, LANES), F32),
        table=vmem((part_rows, tokens), BF16),
        disp=vmem((part_rows, width + LANES), BF16),
        dispc=vmem((part_rows, width), BF16),
        rows=vmem((2, g.parts, part_rows, width + LANES), BF16),
        crow=vmem((2, g.parts, part_rows, width), BF16),
        grow=vmem((2, g.parts, part_rows, width), BF16),
        acte=vmem((2, g.parts, part_rows, inner), BF16),
        dpree=vmem((2, g.parts, part_rows, inner), BF16),
        small=vmem((g.small, width), F32),
        v_up=vmem((width, inner), BF16),
        v_down=vmem((inner, width), BF16),
        v_gup=vmem((width, inner), F32),
        v_gdown=vmem((inner, width), F32),
        local_s=dma((4,)),
    )
    for which in ("d", "y"):
        scratch["keep_" + which] = vmem((g.parts, part_rows, width), F32)
        for name in ("snd_", "rcv_"):
            scratch[name + which] = vmem((g.parts, part_rows, width), BF16)
    scratch |= dict(
        out_d=vmem((sections - 1, part_rows, width), BF16),
        plane_d=vmem((sections - 1, part_rows, width), BF16),
        ret_d=vmem((part_rows, width), BF16),
        back_d=vmem((part_rows, width), BF16),
        ret_y=vmem((g.parts, part_rows, width), BF16),
        back_y=vmem((chips, g.parts, g.quarter, width), BF16),
    )
    for name in ("scat_s", "scat_r", "gath_s", "gath_r"):
        scratch[name] = dma((8, sections - 1))
    for name, count, each in (("pair", len(g.pairs), 0), ("line", len(g.lines), chips), ("plane", len(g.planes), sections - 1)):
        sizes = (count, each) if each else (count,)
        scratch |= {name + "_s": dma(sizes), name + "_r": dma(sizes)}
    if g.direct:
        piece = (top, wide)
        both = (top, wide + g.out_lanes)
        out_piece = (top, g.out_lanes)
        up_piece = (up_rows, width)
        bias_piece = (2 * TAIL, LANES)
        scratch |= dict(
            pq=vmem((2, 3, *piece), BF16),
            po=vmem((sections, *out_piece), BF16),
            pb=vmem(bias_piece, BF16),
            rb=vmem((chips, 2, *bias_piece), BF16),
            hb=vmem((chips, *bias_piece), BF16),
            ab=vmem((chips - 1, *bias_piece), BF16),
            lb=vmem(bias_piece, BF16),
            lq=vmem((2, 3, *piece), BF16),
            lo=vmem((sections, *out_piece), BF16),
            lu=vmem(up_piece, BF16),
            ld=vmem((sections, *both), BF16),
            pd=vmem((sections, *both), BF16),
            rq=vmem((2, 2, chips, 3, *piece), BF16),
            ro=vmem((2, chips, sections, *out_piece), BF16),
            ru=vmem((chips, 2, *up_piece), BF16),
            rd=vmem((2, chips, sections, *both), BF16),
            w_qkv=vmem((2, three, width), BF16),
            w_out=vmem((2, g.head_cols, width), BF16),
            w_down=vmem((width, hidden), BF16),
            w_router=vmem((width, LANES), BF16),
            b_up=vmem((8, hidden), F32),
            prm=vmem((GROUP, width), F32),
            tmp=vmem((width, width), F32),
            hq=vmem((2, chips, 3, *piece), BF16),
            ho=vmem((chips, sections, *out_piece), BF16),
            hu=vmem((chips, *up_piece), BF16),
            hd=vmem((chips, sections, *both), BF16),
            aq=vmem((2, chips - 1, 3, *piece), BF16),
            ao=vmem((chips - 1, sections, *out_piece), BF16),
            au=vmem((chips - 1, *up_piece), BF16),
            ad=vmem((chips - 1, sections, *both), BF16),
            mq=vmem((2, 3, *piece), BF16),
            mo=vmem((sections, *out_piece), BF16),
            md=vmem((sections, *both), BF16),
            fq=vmem((2, 3, *piece), BF16),
            fo=vmem((sections, *out_piece), BF16),
            fd=vmem((sections, *both), BF16),
            wq_s=dma((2, 3, chips)),
            wq_r=dma((2, 3, chips)),
            wo_s=dma((sections, chips)),
            wo_r=dma((sections, chips)),
            gq_s=dma((2, 3)),
            gq_r=dma((2, 3)),
        )
    whole = pl.BlockSpec(memory_space=pltpu.VMEM)
    placed = pl.BlockSpec(memory_space=pl.ANY)
    apart = ("e_up", "e_down", "g_eup", "g_edown")
    names = (*operands, *outs, *scratch)
    results = pl.pallas_call(
        functools.partial(layers_kernel, g, names),
        out_shape=tuple(outs.values()),
        in_specs=[placed if name in apart else whole for name in operands],
        out_specs=[placed if name in apart else whole for name in outs],
        scratch_shapes=list(scratch.values()),
        compiler_params=pltpu.CompilerParams(
            collective_id=0, has_side_effects=True, vmem_limit_bytes=62 * 1024 * 1024
        ),
    )(*operands.values())
    return types.SimpleNamespace(**dict(zip(outs, results, strict=True)))


def finish_kernel(count, *refs):
    ins, outs, held = refs[:count], refs[count : 2 * count], refs[2 * count : 3 * count]
    wide, sems = refs[3 * count : 3 * count + 2], refs[-1]
    loads = [pltpu.make_async_copy(ins[i], held[i], sems.at[0, i]) for i in range(count)]
    stores = [pltpu.make_async_copy((wide[i] if i < 2 else held[i]), outs[i], sems.at[1, i]) for i in range(count)]
    for copy in loads:
        copy.start()
    for i in range(count):
        loads[i].wait()
        if i < 2:
            wide[i][...] = held[i][...].astype(F32)
        stores[i].start()
    for copy in stores:
        copy.wait()


def finish(arrays):
    count = len(arrays)
    placed = [pl.BlockSpec(memory_space=pl.ANY)] * count
    held = [pltpu.VMEM(array.shape, array.dtype) for array in arrays]
    wide = [pltpu.VMEM(array.shape, F32) for array in arrays[:2]]
    return pl.pallas_call(
        functools.partial(finish_kernel, count),
        out_shape=tuple(jax.ShapeDtypeStruct(array.shape, F32) for array in arrays),
        in_specs=placed,
        out_specs=placed,
        scratch_shapes=[*held, *wide, pltpu.SemaphoreType.DMA((2, count))],
        compiler_params=pltpu.CompilerParams(vmem_limit_bytes=62 * 1024 * 1024),
    )(*arrays)


BOTH = ("section", "dp")


def body(
    tokens, cotangent, lengths, routes, slots, norm_gain, norm_bias, attn_qkv, attn_out, attn_out_bias,
    ffn_up, ffn_up_bias, ffn_down, ffn_down_bias, router, expert_up, expert_down,
):
    sections, devices = lax.axis_size("section"), lax.axis_size("dp")
    sec = lax.axis_index("section")
    micro, _, seq, width = tokens.shape
    experts = router.shape[1]
    chips = devices // 2
    head_cols = width // sections
    hidden = ffn_up.shape[1] * devices
    cap = 2 * seq // experts
    span = micro * cap
    cols = ffn_down.shape[1]
    kinds = FIRST_ROUTER + experts
    direct = cols == 3 * TAIL and kinds <= GROUP and sections == 4 and ffn_up.shape[1] % 16 == 0
    parts = sections if span % (16 * sections) == 0 else 1
    numbers = [str(part) for part in range(parts)]
    g = types.SimpleNamespace(
        sections=sections, devices=devices, chips=chips, micro=micro, seq=seq, width=width, hidden=hidden, cap=cap,
        span=span, tokens=micro * seq, piece=micro * seq // sections, heads=head_cols // HEAD_DIM,
        head_cols=head_cols, cols=cols, block=256, small=-(-kinds // 8) * 8, direct=direct, experts=experts,
        out_lanes=head_cols + 2 * GROUP + LANES, parts=parts, quarter=span // parts,
        relay=direct and chips == 4,
        my_part=(lambda section: section) if parts > 1 else (lambda section: 0),
        router_lane=FIRST_ROUTER + (LANES - 2 * GROUP if direct else 0),
        pairs=[name + n for name in ("crow", "rows", "d", "y") for n in numbers]
        + (["out", "qkv0", "up", "bias", "down", "qkv1", "gqkv0", "gqkv1", "gdown", "gup", "gbias", "gout"] if direct else []),
        lines=["crow", "rows", "d", "y"]
        + (["out", "qkv0", "up", "bias", "down", "qkv1", "gqkv0", "gqkv1", "gdown", "gup", "gbias", "gout"] if direct else []),
        planes=["crow", "rows", "d"] + (["down", "gdown", "gout"] if direct else []),
    )

    operands = dict(
        x0=tokens.reshape(g.tokens, width),
        cot=cotangent.reshape(g.tokens, width),
        lens=lengths.T,
        routes=routes[:, 0],
        slots=slots[:, 0],
        e_up=expert_up[0],
        e_down=expert_down[0],
    )
    if direct:
        operands |= dict(
            norm_gain=norm_gain,
            norm_bias=norm_bias,
            out_bias=attn_out_bias,
            down_bias=ffn_down_bias[None],
            up_bias=ffn_up_bias[None],
            router=router.T,
            wq=attn_qkv.transpose(0, 2, 1),
            wo=attn_out.transpose(0, 2, 1),
            wu=ffn_up.T,
            wd=ffn_down.T,
        )
    else:

        def every(array, axis):
            return lax.all_gather(array, BOTH, axis=axis, tiled=True)

        def part_of(array, axis, size):
            return lax.dynamic_slice_in_dim(array, sec * size, size, axis)

        rows = [norm_gain, norm_bias, attn_out_bias, ffn_down_bias[None], router.T]
        params = every(jnp.concatenate(rows, axis=0), 1)
        params = jnp.pad(params, ((0, LANES - kinds), (0, 0)))
        b_up = lax.all_gather(ffn_up_bias, "dp", axis=0, tiled=True).astype(F32)
        full = part_of(every(attn_qkv, 2).reshape(2, width, 3, width), 3, head_cols)
        operands |= dict(
            prm=params.astype(F32),
            w_router=params.T,
            b_up=b_up[None],
            w_qkv=full.transpose(0, 2, 3, 1).reshape(2, 3 * head_cols, width),
            w_out=part_of(every(attn_out, 2), 1, head_cols),
            w_up=lax.all_gather(ffn_up, "dp", axis=1, tiled=True).T,
            w_down=part_of(every(ffn_down, 1), 0, hidden).T,
        )
    res = run_layers(g, operands)

    if direct:
        names = list(vars(res))
        done = finish([getattr(res, name) for name in names])
        res = types.SimpleNamespace(**dict(zip(names, done, strict=True)))
        grads = (
            res.o_gain, res.o_bias, res.o_qkv.transpose(0, 2, 1), res.o_out.transpose(0, 2, 1), res.o_bout,
            res.o_up.T, res.o_bup[0], res.o_down.T, res.o_bdown[0], res.o_router.T,
        )
    else:

        def embed(array, shape, axis, size):
            return lax.dynamic_update_slice_in_dim(jnp.zeros(shape, F32), array, sec * size, axis)

        def share(array, axis, over=BOTH):
            return lax.psum_scatter(array, over, scatter_dimension=axis, tiled=True)

        small = share(res.o_small[:kinds], 1)
        g_qkv = res.o_qkv.reshape(2, 3, head_cols, width).transpose(0, 3, 1, 2)
        g_qkv = embed(g_qkv, (2, width, 3, width), 3, head_cols).reshape(2, width, 3 * width)
        g_out = embed(res.o_out, (2, width, width), 1, head_cols)
        g_down = embed(res.o_down.T, (hidden * sections, width), 0, hidden)
        grads = (
            small[0:4], small[4:8], share(g_qkv, 2), share(g_out, 2), small[8:10], share(res.o_up.T, 1, "dp"),
            share(res.o_bup[0], 0, "dp"), share(g_down, 1), small[10], small[FIRST_ROUTER:].T,
        )
    out_shape = (1, micro, 1, seq, width)
    return (
        res.sec_out.reshape(out_shape).astype(F32),
        res.sec_grad.reshape(out_shape).astype(F32),
        *grads,
        res.g_eup[None],
        res.g_edown[None],
    )


def solution(mesh):
    batch = P(None, "dp", None, None)
    table = P(None, "dp", None)
    in_specs = (
        batch, batch, P(None, "dp"), table, table,
        P(None, BOTH), P(None, BOTH), P(None, None, BOTH), P(None, None, BOTH), P(None, BOTH),
        P(None, BOTH), P(BOTH), P(None, BOTH), P(BOTH), P(BOTH, None),
        P("dp", None, "section"), P("dp", "section", None),
    )
    streams = P("section", None, "dp", None, None)
    out_specs = (
        streams, streams,
        P(None, BOTH), P(None, BOTH), P(None, None, BOTH), P(None, None, BOTH), P(None, BOTH),
        P(None, BOTH), P(BOTH), P(None, BOTH), P(BOTH), P(BOTH, None),
        P("dp", None, "section"), P("dp", "section", None),
    )
    return jax.shard_map(body, mesh=mesh, in_specs=in_specs, out_specs=out_specs, check_vma=False)
```

```python
import functools
import types

import jax
import jax.numpy as jnp
from jax import lax
from jax.experimental import pallas as pl
from jax.experimental.pallas import tpu as pltpu
from jax.sharding import PartitionSpec as P

HEADS = 12
HEAD_DIM = 64
EPS = 1e-05
MASKED = -1000000000.0
MESH = pl.DeviceIdType.MESH
F32 = jnp.float32
BF16 = jnp.bfloat16
LANES = 128


def dot_as(left, right, left_dim, right_dim):
    return lax.dot_general(
        left, right, (((left_dim,), (right_dim,)), ((), ())), preferred_element_type=F32
    )


def mm(left, right):
    return dot_as(left, right, 1, 0)


def mm_nt(left, right):
    return dot_as(left, right, 1, 1)


def mm_tn(left, right):
    return dot_as(left, right, 0, 0)


def normalize(values):
    center = values - jnp.mean(values, axis=-1, keepdims=True)
    spread = jnp.mean(center * center, axis=-1, keepdims=True)
    inverse = lax.rsqrt(spread + EPS)
    return center * inverse, inverse


def gelu_parts(pre):
    half = 0.5 + 0.5 * lax.erf(pre * 0.7071067811865476)
    density = jnp.exp(-0.5 * pre * pre) * 0.3989422804014327
    return pre * half, half + pre * density


TAIL = 8
GROUP = 32
FIRST_ROUTER = 11


def layers_kernel(g, names, *refs):
    r = types.SimpleNamespace(**dict(zip(names, refs, strict=True)))
    width, span, hidden, cols, head_cols = g.width, g.span, g.hidden, g.cols, g.head_cols
    sec = lax.axis_index("section")
    dev = lax.axis_index("dp")
    core = lax.rem(dev, 2)
    chip = lax.div(dev, 2)
    sib = dev + 1 - 2 * core
    quarter = g.quarter
    shard_rows = hidden // g.devices
    block_rows = g.chips * quarter

    def peer_section(offset):
        return lax.rem(sec + offset, g.sections)

    def from_section(offset):
        return lax.rem(sec + g.sections - offset, g.sections)

    def peer_chip(offset):
        return lax.rem(chip + offset, g.chips)

    def from_chip(offset):
        return lax.rem(chip + g.chips - offset, g.chips)

    def rows_at(index, size):
        return pl.ds(pl.multiple_of(index * size, size), size)

    def piece_at(index):
        return rows_at(index, g.piece)

    own = piece_at(sec)

    def remote(source, target, send, arrive, where):
        return pltpu.make_async_remote_copy(
            src_ref=source, dst_ref=target, send_sem=send, recv_sem=arrive, device_id=where, device_id_type=MESH
        )

    def at_chip_core(index):
        return {"dp": 2 * index + core}

    started = []
    kept_back = {}

    def do_when(condition, action):
        if condition is None:
            action()
        else:
            pl.when(condition)(action)

    def launch(copy, buffer=None, when=None):
        do_when(when, copy.start)
        if buffer:
            kept_back.setdefault(buffer, []).append((copy, when))
        else:
            started.append((copy, when))

    def settle(buffer):
        for copy, when in kept_back.pop(buffer, []):
            do_when(when, copy.wait_send)

    barrier = pltpu.get_barrier_semaphore()
    partners = [(a, b) for a in range(g.sections) for b in range(g.chips) if a + b and (g.direct or a * b == 0)]
    for section_offset, chip_offset in partners:
        where = {"section": peer_section(section_offset), "dp": 2 * peer_chip(chip_offset) + core}
        pl.semaphore_signal(barrier, inc=1, device_id=where, device_id_type=MESH)
    pl.semaphore_signal(barrier, inc=1, device_id={"dp": sib}, device_id_type=MESH)

    def local(index, source, target):
        return pltpu.make_async_copy(source, target, r.local_s.at[index])

    loads = [local(0, r.e_up, r.v_up), local(1, r.e_down, r.v_down)]
    stores = [local(2, r.v_gup, r.g_eup), local(3, r.v_gdown, r.g_edown)]
    for copy in loads:
        copy.start()

    def scatter_copy(slot, offset):
        return remote(
            r.part.at[slot, piece_at(peer_section(offset))], r.got.at[slot, offset - 1],
            r.scat_s.at[slot, offset - 1], r.scat_r.at[slot, offset - 1], {"section": peer_section(offset)},
        )

    def scatter_start(slot, value):
        r.part[slot] = value.astype(BF16)
        if slot != 7:
            r.mine[...] = value
        for offset in range(1, g.sections):
            launch(scatter_copy(slot, offset))

    def scatter_sum(slot):
        total = r.part[slot, own, :].astype(F32) if slot == 7 else r.mine[own, :]
        for offset in range(1, g.sections):
            scatter_copy(slot, offset).wait_recv()
            total = total + r.got[slot, offset - 1].astype(F32)
        return total

    def share_copy(place, send, arrive, offset, receiving):
        where = from_section(offset) if receiving else peer_section(offset)
        return remote(place, place, send.at[offset - 1], arrive.at[offset - 1], {"section": where})

    def gather_start(buffer, slot, sem):
        place = buffer.at[slot, own]
        for offset in range(1, g.sections):
            launch(share_copy(place, r.gath_s.at[sem], r.gath_r.at[sem], offset, False))

    def gather_wait(buffer, slot, sem):
        for offset in range(1, g.sections):
            place = buffer.at[slot, piece_at(from_section(offset))]
            share_copy(place, r.gath_s.at[sem], r.gath_r.at[sem], offset, True).wait_recv()

    def pair_copy(name, source, target):
        index = g.pairs.index(name)
        return remote(source, target, r.pair_s.at[index], r.pair_r.at[index], {"dp": sib})

    def pair_start(name, source, target, buffer=None):
        launch(pair_copy(name, source, target), buffer)

    def pair_wait(name, target):
        pair_copy(name, target, target).wait_recv()

    def line_copy(name, source, target, offset, receiving):
        index = g.lines.index(name)
        where = from_chip(offset) if receiving else peer_chip(offset)
        return remote(
            source, target, r.line_s.at[index, offset - 1], r.line_r.at[index, offset - 1], at_chip_core(where)
        )

    last_chip = g.chips - 1
    is_end = lax.rem(chip, max(last_chip, 1)) == 0
    is_mid = lax.rem(chip, max(last_chip, 1)) != 0
    line_order = (2, 1, 3) if g.relay else range(1, g.chips)
    outward = jnp.clip(chip - 1, 0, 1)

    def near_to(offset):
        return {1: chip != last_chip, last_chip: chip != 0}.get(offset) if g.relay else None

    def near_from(offset):
        return {1: chip != 0, last_chip: chip != last_chip}.get(offset) if g.relay else None

    def spread_start(name, source, target, buffer=None):
        for offset in line_order:
            launch(line_copy(name, source, target, offset, False), buffer, near_to(offset))

    def spread_relay(name, place, buffer):
        index = g.lines.index(name)
        copy = remote(
            place, place, r.line_s.at[index, last_chip], r.line_r.at[index, outward * 2],
            at_chip_core(outward * last_chip),
        )
        launch(copy, buffer, is_mid)

    def spread_wait(name, place_at, buffer):
        for offset in line_order:
            place = place_at(from_chip(offset))
            line_copy(name, place, place, offset, True).wait_recv()
            if g.relay and offset == 2:
                spread_relay(name, place, buffer)

    def far_wait(name, place_at):
        for offset in (1, last_chip):
            place = place_at(from_chip(offset))
            copy = line_copy(name, place, place, offset, True)
            pl.when(jnp.logical_not(near_from(offset)))(copy.wait_recv)

    def line_start(name, source_at, target, buffer=None):
        for offset in range(1, g.chips):
            launch(line_copy(name, source_at(peer_chip(offset)), target, offset, False), buffer)

    def line_wait(name, target_at):
        for offset in range(1, g.chips):
            target = target_at(from_chip(offset), offset)
            line_copy(name, target, target, offset, True).wait_recv()

    def rows_line_start(name, source, target):
        line_start(name, lambda at: source.at[rows_at(at, quarter)], target.at[core, g.my_part(sec), rows_at(chip, quarter)])
        target[core, g.my_part(sec), rows_at(chip, quarter), :] = source[rows_at(chip, quarter), :]

    def rows_plane_start(name, target):
        line_wait(name, lambda at, _: target.at[core, g.my_part(sec), rows_at(at, quarter)])
        place = target.at[core, g.my_part(sec)]
        if g.parts > 1:
            index = g.planes.index(name)
            for offset in range(1, g.sections):
                launch(share_copy(place, r.plane_s.at[index], r.plane_r.at[index], offset, False))
        pair_start(name + "0", place, place)

    def rows_plane_wait(name, target, offset):
        index = g.planes.index(name)
        place = target.at[core, from_section(offset)]
        share_copy(place, r.plane_s.at[index], r.plane_r.at[index], offset, True).wait_recv()
        pair_start(name + str(offset), place, place)

    def rows_pair_wait(name, target, offset):
        pair_wait(name + str(offset), target.at[1 - core, g.my_part(from_section(offset))])

    top = cols - TAIL
    half = width // 2
    part_cols = head_cols // 2
    tail_lane = head_cols + 2 * GROUP

    def qkv_section(at_dev, index, section):
        return lax.rem(lax.div(3 * at_dev + index, g.devices) - section + g.sections, g.sections)

    def qkv_send(layer, offsets):
        for index in range(3):
            to = qkv_section(dev, index, sec)
            for offset in offsets:
                copy = remote(
                    r.pq.at[layer, index], r.rq.at[layer, core, chip, index],
                    r.wq_s.at[layer, index, offset], r.wq_r.at[layer, index, offset],
                    {"section": to, "dp": 2 * peer_chip(offset) + core},
                )
                if offset:
                    launch(copy, None, near_to(offset))
                else:
                    pl.when(to != sec)(copy.start)

                    @pl.when(to == sec)
                    def _(index=index):
                        r.rq[layer, core, chip, index] = r.pq[layer, index]

    def qkv_arrive(layer, offsets):
        for offset in offsets:
            for index in range(3):
                at_chip = from_chip(offset)
                target = r.rq.at[layer, core, at_chip, index]
                origin = qkv_section(2 * at_chip + core, index, sec)
                copy = remote(
                    target, target, r.wq_s.at[layer, index, offset], r.wq_r.at[layer, index, offset],
                    {"section": origin, "dp": 2 * at_chip + core},
                )
                if offset:
                    do_when(near_from(offset), copy.wait_recv)
                else:

                    @pl.when(origin != sec)
                    def _(copy=copy):
                        copy.wait_recv()
                        copy.wait_send()

            if g.relay and offset == 2:
                spread_relay("qkv0", r.rq.at[0, core, from_chip(offset)], "qkv0")
        if g.relay and len(offsets) > 1:
            far_wait("qkv0", lambda at: r.rq.at[0, core, at])

    def out_copy(section_offset, offset, place, receiving):
        if receiving:
            to, at_chip = from_section(section_offset), from_chip(offset)
        else:
            to, at_chip = peer_section(section_offset), peer_chip(offset)
        source = place if receiving else r.po.at[0, to]
        return remote(
            source, place, r.wo_s.at[section_offset, offset], r.wo_r.at[section_offset, offset],
            {"section": to, "dp": 2 * at_chip + core},
        )

    def out_offsets():
        return [(a, b) for b in (*line_order, 0) for a in range(g.sections) if a + b]

    def plane_copy(name, source, target, offset, receiving):
        index = g.planes.index(name)
        where = from_section(offset) if receiving else peer_section(offset)
        return remote(
            source, target, r.plane_s.at[index, offset - 1], r.plane_r.at[index, offset - 1], {"section": where}
        )

    def pack_wide(block):
        tail = jnp.concatenate([block[top:, :half], block[top:, half:]], axis=0)
        return jnp.concatenate([block[:top], tail], axis=1).astype(BF16)

    def pack_out(block):
        small = jnp.concatenate([block[top:, head_cols:]] * 2, axis=0)
        tail = jnp.concatenate([block[top:, :part_cols], block[top:, part_cols:head_cols]], axis=0)
        empty = jnp.zeros((top, g.out_lanes - tail_lane - part_cols), F32)
        return jnp.concatenate([block[:top], small, tail, empty], axis=1).astype(BF16)

    def unpack_wide(target, first, piece):
        target[first : first + top, 0:width] = piece[:, 0:width]
        target[first + top : first + cols, 0:half] = piece[0:TAIL, width : width + half]
        target[first + top : first + cols, half:width] = piece[TAIL:, width : width + half]

    def unpack_out(target, first, piece, lane=0):
        last = slice(first + top, first + cols)
        tail = slice(tail_lane, tail_lane + part_cols)
        target[first : first + top, lane : lane + head_cols] = piece[:, 0:head_cols]
        target[last, lane : lane + part_cols] = piece[0:TAIL, tail]
        target[last, lane + part_cols : lane + head_cols] = piece[TAIL:, tail]

    def unpack_small(target, first, piece, lane):
        target[first : first + top, lane : lane + GROUP] = piece[:, head_cols : head_cols + GROUP]
        target[first + top : first + cols, lane : lane + GROUP] = piece[0:TAIL, head_cols + GROUP : tail_lane]

    def shard_places():
        for at_core in range(2):
            for at_chip in range(g.chips):
                for at_sec in range(g.sections):
                    yield at_core, at_chip, at_sec, (at_sec * g.devices + 2 * at_chip + at_core) * cols

    def chunk_places():
        for at_core in range(2):
            for at_chip in range(g.chips):
                for index in range(3):
                    yield at_core, at_chip, index, (3 * (2 * at_chip + at_core) + index) * cols

    def unfold_out(layer):
        for at_core, at_chip, at_sec, first in shard_places():
            piece = r.ro[layer, at_core, at_chip, at_sec].astype(F32)
            if layer == 0:
                unpack_small(r.tmp, first, piece, head_cols)
            unpack_out(r.tmp, first, piece)
        flipped = r.tmp[:, 0:tail_lane].T
        r.w_out[layer] = flipped[:head_cols].astype(BF16)
        if layer == 0:
            r.prm[...] = flipped[head_cols : head_cols + GROUP]
            r.w_router[...] = r.tmp[:, tail_lane - LANES : tail_lane].astype(BF16)

    def unfold_qkv(layer):
        for at_core, at_chip, index, first in chunk_places():
            unpack_wide(r.tmp, first, r.rq[layer, at_core, at_chip, index].astype(F32))
        r.w_qkv[layer] = r.tmp[0 : 3 * head_cols, 0:width].astype(BF16)

    def unfold_down():
        for at_core, at_chip, at_sec, first in shard_places():
            unpack_wide(r.tmp, first, r.rd[at_core, at_chip, at_sec].astype(F32))
        r.w_down[...] = r.tmp[...].astype(BF16)

    def grad_line(name, buffer_at, landing, target, passed):
        pair_wait(name, landing)
        for at_chip in range(g.chips):
            block = buffer_at(at_chip)
            block[...] = (block[...].astype(F32) + landing[at_chip].astype(F32)).astype(BF16)
        if g.relay:
            index = g.lines.index(name)
            copy = remote(
                buffer_at(last_chip - chip), passed, r.line_s.at[index, last_chip], r.line_r.at[index, last_chip],
                at_chip_core(1 + lax.div(chip, last_chip)),
            )
            launch(copy, None, is_end)
            for offset in (1, last_chip):

                @pl.when(jnp.logical_not(near_from(offset)))
                def _(offset=offset):
                    target[offset - 1] = jnp.zeros_like(target[offset - 1])

        for offset in line_order:
            copy = line_copy(name, buffer_at(peer_chip(offset)), target.at[offset - 1], offset, False)
            if g.relay and offset == 2:
                pl.when(is_end)(copy.start)
                started.append((copy, None))
            else:
                launch(copy, None, near_to(offset))

    def grad_relay(name, buffer_at, target, passed):
        if g.relay:
            index = g.lines.index(name)
            block = buffer_at(peer_chip(2))
            copy = line_copy(name, block, target.at[1], 2, False)

            @pl.when(is_mid)
            def _():
                remote(
                    passed, passed, r.line_s.at[index, last_chip], r.line_r.at[index, last_chip],
                    at_chip_core(outward * last_chip),
                ).wait_recv()
                block[...] = (block[...].astype(F32) + passed[...].astype(F32)).astype(BF16)
                copy.start()

    def grad_line_sum(name, buffer_at, target):
        for offset in line_order:
            place = target.at[offset - 1]
            do_when(near_from(offset), line_copy(name, place, place, offset, True).wait_recv)
        total = buffer_at(chip)[...].astype(F32)
        for offset in range(1, g.chips):
            total = total + target[offset - 1].astype(F32)
        return total

    def qkv_at(layer):
        return lambda at: r.rq.at[layer, core, at]

    def down_at(at):
        return r.rd.at[core, at]

    def out_at(layer):
        return lambda at: r.ro.at[layer, core, at]

    def up_at(at):
        return r.ru.at[at, core]

    def bias_at(at):
        return r.rb.at[at, core]

    def grad_plane(name, buffer_at, target, summed, final):
        summed[...] = grad_line_sum(name, buffer_at, target).astype(BF16)
        for offset in range(1, g.sections):
            source = summed.at[peer_section(offset)]
            launch(plane_copy(name, source, final.at[sec], offset, False))
        final[sec] = summed[sec]

    def grad_plane_wait(name, final):
        for offset in range(1, g.sections):
            place = final.at[from_section(offset)]
            plane_copy(name, place, place, offset, True).wait_recv()

    def grad_qkv_copy(layer, index, place, where):
        return remote(
            r.mq.at[layer, index], place, r.gq_s.at[layer, index], r.gq_r.at[layer, index], {"section": where}
        )

    def grad_qkv_plane(layer):
        r.mq[layer] = grad_line_sum("gqkv" + str(layer), qkv_at(layer), r.aq.at[layer]).astype(BF16)
        for index in range(3):
            to = qkv_section(dev, index, sec)
            copy = grad_qkv_copy(layer, index, r.fq.at[layer, index], to)
            pl.when(to != sec)(copy.start)

            @pl.when(to == sec)
            def _(index=index):
                r.fq[layer, index] = r.mq[layer, index]

    def grad_qkv_finish(layer):
        for index in range(3):
            origin = qkv_section(dev, index, sec)
            copy = grad_qkv_copy(layer, index, r.fq.at[layer, index], origin)

            @pl.when(origin != sec)
            def _(copy=copy):
                copy.wait_recv()
                copy.wait_send()

            unpack_wide(r.o_qkv.at[layer], index * cols, r.fq[layer, index].astype(F32))

    def norm_into(source, target, index):
        @pl.loop(0, g.sections)
        def _(step):
            at = piece_at(step)
            unit, _ = normalize(source[at, :].astype(F32))
            target[at, :] = (unit * r.prm[index : index + 1, :] + r.prm[4 + index : 5 + index, :]).astype(BF16)

    place_row = jnp.concatenate(
        [r.routes[m : m + 1] * span + m * g.cap + r.slots[m : m + 1] for m in range(g.micro)], axis=1
    )
    r.square[...] = jnp.zeros_like(r.square)
    if g.direct:
        r.square[0:4, 0:cols] = r.norm_gain[...].astype(F32)
        r.square[4:8, 0:cols] = r.norm_bias[...].astype(F32)
        r.square[8:10, 0:cols] = r.out_bias[...].astype(F32)
        r.square[10:11, 0:cols] = r.down_bias[...].astype(F32)
        r.pb[...] = jnp.zeros_like(r.pb)
        r.pb[:, 0:shard_rows] = jnp.broadcast_to(r.up_bias[...], (r.pb.shape[0], shard_rows))
        r.square[FIRST_ROUTER : FIRST_ROUTER + g.experts, 0:cols] = r.router[...].astype(F32)
        r.square[...] = r.square[...].T
        shard = r.wo[0].astype(F32)
        mine = r.square[0:cols, 0:GROUP]
        for at_sec in range(g.sections):
            block = shard[:, at_sec * head_cols : (at_sec + 1) * head_cols]
            r.po[0, at_sec] = pack_out(jnp.concatenate([block, mine], axis=1))
        shard = r.wq[0].astype(F32)
        for index in range(3):
            r.pq[0, index] = pack_wide(shard[index * cols : (index + 1) * cols])
    pl.semaphore_wait(barrier, len(partners) + 1)
    if g.direct:
        for section_offset, offset in out_offsets():
            launch(out_copy(section_offset, offset, r.ro.at[0, core, chip, sec], False), None, near_to(offset))
        r.ro[0, core, chip, sec] = r.po[0, sec]
        qkv_send(0, (*line_order, 0))
        shard = r.wq[1].astype(F32)
        for index in range(3):
            r.pq[1, index] = pack_wide(shard[index * cols : (index + 1) * cols])
        shard, other = r.wd[...].astype(F32), r.wo[1].astype(F32)
        empty = jnp.zeros((cols, GROUP), F32)
        for at_sec in range(g.sections):
            r.pd[at_sec] = pack_wide(shard[:, at_sec * hidden : (at_sec + 1) * hidden])
            block = other[:, at_sec * head_cols : (at_sec + 1) * head_cols]
            r.po[1, at_sec] = pack_out(jnp.concatenate([block, empty], axis=1))

    slot_ids = lax.broadcasted_iota(jnp.int32, (quarter, g.tokens), 0)
    for expert in range(g.chips):
        first = expert * span + (sec * quarter if g.parts > 1 else 0)
        match = jnp.where(slot_ids + first == place_row, 1.0, 0.0)
        r.table[expert * quarter : (expert + 1) * quarter, :] = match.astype(BF16)
    r.dispc[...] = mm(r.table[...], r.cot[...]).astype(BF16)
    r.small[...] = jnp.zeros_like(r.small)
    if g.direct:
        for section_offset, offset in out_offsets():
            place = r.ro.at[0, core, from_chip(offset), from_section(section_offset)]
            do_when(near_from(offset), out_copy(section_offset, offset, place, True).wait_recv)
            if g.relay and (section_offset, offset) == (g.sections - 1, 2):
                spread_relay("out0", r.ro.at[0, core, from_chip(offset)], "out0")
        if g.relay:
            far_wait("out0", lambda at: r.ro.at[0, core, at])
        pair_start("out0", r.ro.at[0, core], r.ro.at[0, core], "out0")
        qkv_arrive(0, (*line_order, 0))
        pair_start("qkv0", r.rq.at[0, core], r.rq.at[0, core], "qkv0")
        spread_start("bias", r.pb, r.rb.at[chip, core])
        r.rb[chip, core] = r.pb[...]
        spread_start("up", r.wu, r.ru.at[chip, core])
        r.ru[chip, core] = r.wu[...]
        for offset in range(1, g.sections):
            launch(plane_copy("down", r.pd.at[peer_section(offset)], r.rd.at[core, chip, sec], offset, False))
        r.rd[core, chip, sec] = r.pd[sec]
        qkv_send(1, [0])
        for offset in range(1, g.sections):
            place = r.ro.at[1, core, chip, sec]
            launch(plane_copy("out1", r.po.at[1, peer_section(offset)], place, offset, False))
        r.ro[1, core, chip, sec] = r.po[1, sec]
        pair_wait("out0", r.ro.at[0, 1 - core])
        unfold_out(0)
        pair_wait("qkv0", r.rq.at[0, 1 - core])
        unfold_qkv(0)

    def weights_line_start():
        for offset in range(1, g.sections):
            place = r.rd.at[core, chip, from_section(offset)]
            plane_copy("down", place, place, offset, True).wait_recv()
        spread_start("down", r.rd.at[core, chip], r.rd.at[core, chip], "down")
        qkv_arrive(1, [0])
        spread_start("qkv1", r.rq.at[1, core, chip], r.rq.at[1, core, chip], "qkv1")
        for offset in range(1, g.sections):
            place = r.ro.at[1, core, chip, from_section(offset)]
            plane_copy("out1", place, place, offset, True).wait_recv()
        spread_start("out1", r.ro.at[1, core, chip], r.ro.at[1, core, chip], "out1")

    key_ids = lax.broadcasted_iota(jnp.int32, (g.seq, g.seq), 0)
    query_ids = lax.broadcasted_iota(jnp.int32, (g.seq, g.seq), 1)
    scale = HEAD_DIM**-0.5

    def block_of(index):
        return lax.rem(index + sec, 3) if g.direct else index

    def head_slice(head):
        return slice(head * HEAD_DIM, (head + 1) * HEAD_DIM)

    def token_slice(micro):
        return slice(micro * g.seq, (micro + 1) * g.seq)

    def attention_forward(layer, stream, slot):
        norm_into(stream, r.normed.at[2 * layer], 2 * layer)
        packed = mm_nt(r.w_qkv[layer], r.normed[2 * layer]).astype(BF16)
        r.qkv[layer] = packed.reshape(3, head_cols, g.tokens)
        for micro in range(g.micro):
            allowed = (key_ids <= query_ids) & (key_ids < r.lens[:, micro : micro + 1])
            for head in range(g.heads):
                at = token_slice(micro)
                key = r.qkv[layer, block_of(1), head_slice(head), at]
                scores = mm_tn(key, r.qkv[layer, block_of(0), head_slice(head), at]) * scale
                scores = jnp.where(allowed, scores, MASKED)
                weight = jnp.exp(scores - jnp.max(scores, axis=0, keepdims=True))
                weight = weight / jnp.sum(weight, axis=0, keepdims=True)
                r.probs[layer, micro, head] = weight
                value = r.qkv[layer, block_of(2), head_slice(head), at]
                r.ctx[layer, head_slice(head), at] = mm(value, weight.astype(BF16)).astype(BF16)
        scatter_start(slot, mm_tn(r.ctx[layer], r.w_out[layer]))

    def finish_forward(section, bias, stream):
        total = scatter_sum(section) + bias + stream[own, :].astype(F32)
        r.xs[section, own, :] = total.astype(BF16)
        gather_start(r.xs, section, section)

    attention_forward(0, r.x0, 0)
    if g.direct:
        weights_line_start()
    finish_forward(0, r.prm[8:9, :], r.x0)
    if g.direct:
        spread_wait("bias", lambda at: r.rb.at[at, core], "bias")
        spread_wait("up", lambda at: r.ru.at[at, core], "up")
        pair_start("up", r.ru.at[:, core], r.ru.at[:, core], "up")
        pair_start("bias", r.rb.at[:, core], r.rb.at[:, core], "bias")
        pair_wait("up", r.ru.at[:, 1 - core])
        pair_wait("bias", r.rb.at[:, 1 - core])
        for at_dev in range(g.devices):
            row = r.rb[at_dev // 2, at_dev % 2, :, 0:shard_rows].astype(F32)
            r.b_up[:, at_dev * shard_rows : (at_dev + 1) * shard_rows] = row[0:TAIL]
    gather_wait(r.xs, 0, 0)

    def up_rows(at):
        if g.direct:
            return r.ru[...].reshape(hidden, width)[at]
        return r.w_up[at, :]

    norm_into(r.xs.at[0], r.normed.at[1], 1)
    for block in range(hidden // g.block):
        at = slice(block * g.block, (block + 1) * g.block)
        pre = mm_nt(r.normed[1], up_rows(at)) + r.b_up[0:1, at]
        value, slope = gelu_parts(pre)
        r.act[:, at] = value.astype(BF16)
        r.dgelu[:, at] = slope
    if g.direct:
        spread_wait("down", lambda at: r.rd.at[core, at], "down")
        pair_start("down", r.rd.at[core], r.rd.at[core], "down")
        pair_wait("down", r.rd.at[1 - core])
        unfold_down()
    scatter_start(1, mm_nt(r.act[...], r.w_down[...]))
    finish_forward(1, r.prm[10:11, :], r.xs.at[0])
    if g.direct:
        spread_wait("qkv1", lambda at: r.rq.at[1, core, at], "qkv1")
        pair_start("qkv1", r.rq.at[1, core], r.rq.at[1, core], "qkv1")
        spread_wait("out1", lambda at: r.ro.at[1, core, at], "out1")
        pair_start("out1", r.ro.at[1, core], r.ro.at[1, core], "out1")
    rows_line_start("crow", r.dispc, r.crow)
    if g.direct:
        pair_wait("qkv1", r.rq.at[1, 1 - core])
        unfold_qkv(1)
        pair_wait("out1", r.ro.at[1, 1 - core])
        unfold_out(1)
    gather_wait(r.xs, 1, 1)

    attention_forward(1, r.xs.at[1], 2)
    finish_forward(2, r.prm[9:10, :], r.xs.at[1])
    r.square[0 : g.micro, :] = jnp.concatenate(
        [place_row[:, token_slice(m)] for m in range(g.micro)], axis=0
    ).astype(F32)
    columns = r.square[...].T
    place_col = jnp.concatenate([columns[:, m : m + 1] for m in range(g.micro)], axis=0).astype(jnp.int32)
    gather_wait(r.xs, 2, 2)
    rows_plane_start("crow", r.crow)

    wide = r.wide
    norm_into(r.xs.at[2], wide.at[:, pl.ds(0, width)], 3)
    logits = mm(wide[:, :width], r.w_router[...])
    lane = lax.broadcasted_iota(jnp.int32, logits.shape, 1) - g.router_lane
    chosen = (place_col >= lane * span) & (place_col < lane * span + span)
    score = jnp.sum(jnp.where(chosen, logits, 0.0), axis=-1, keepdims=True)
    gate = 1.0 / (1.0 + jnp.exp(-score))
    gate_high = gate.astype(BF16).astype(F32)
    lane = lax.broadcasted_iota(jnp.int32, (g.tokens, LANES), 1)
    pair = jnp.where(lane == 0, gate_high, jnp.where(lane == 1, gate - gate_high, 0.0))
    wide[:, width:] = pair.astype(BF16)
    r.disp[...] = mm(r.table[...], wide[...]).astype(BF16)
    rows_line_start("rows", r.disp, r.rows)
    rows_plane_start("rows", r.rows)

    own_router = FIRST_ROUTER + chip
    router_row = r.prm[pl.ds(own_router, 1), :]

    def expert_block(side, part, at, keep_first):
        row = r.rows[side, part, at, :width]
        tail = r.rows[side, part, at, width:].astype(F32)
        gate_row = tail[:, 0:1] + tail[:, 1:2]
        grad_row = (gate_row * r.crow[side, part, at, :].astype(F32)).astype(BF16)
        r.grow[side, part, at, :] = grad_row
        value, slope = gelu_parts(mm(row, r.v_up[...]))
        value = value.astype(BF16)
        r.acte[side, part, at, :] = value
        result = mm(value, r.v_down[...])
        total = jnp.sum(grad_row.astype(F32) * result, axis=-1, keepdims=True) * (1.0 - gate_row)
        inner = (slope * mm_nt(grad_row, r.v_down[...])).astype(BF16)
        r.dpree[side, part, at, :] = inner
        back = mm_nt(inner, r.v_up[...]) + total * router_row
        r.small[pl.ds(own_router, 1), :] += jnp.sum(row.astype(F32) * total, axis=0, keepdims=True)
        result = result * gate_row
        if keep_first:
            r.keep_d[part, at, :] = back
            r.keep_y[part, at, :] = result
        else:
            r.snd_d[part, at, :] = back.astype(BF16)
            r.snd_y[part, at, :] = result.astype(BF16)

    def expert_part(side, part, keep_first):
        if block_rows <= g.block:
            expert_block(side, part, slice(None), keep_first)
            return

        @pl.loop(0, block_rows // g.block)
        def _(step):
            expert_block(side, part, rows_at(step, g.block), keep_first)

    def merge(which, offset):
        part = g.my_part(from_section(offset))
        pair_wait(which + str(offset), rcv[which].at[part])
        return kept[which][part] + rcv[which][part].astype(F32)

    snd = {"d": r.snd_d, "y": r.snd_y}
    kept = {"d": r.keep_d, "y": r.keep_y}
    rcv = {"d": r.rcv_d, "y": r.rcv_y}

    def merge_send(offset):
        to = g.sections - offset
        r.out_d[offset - 1] = merge("d", offset).astype(BF16)
        launch(plane_copy("d", r.out_d.at[offset - 1], r.plane_d.at[to - 1], to, False))

    def expert_back_line():
        total = merge("d", 0)
        if g.parts > 1:
            for offset in range(1, g.sections):
                place = r.plane_d.at[offset - 1]
                plane_copy("d", place, place, offset, True).wait_recv()
                total = total + place[...].astype(F32)
        r.ret_d[...] = total.astype(BF16)
        line_start("d", lambda at: r.ret_d.at[rows_at(at, quarter)], r.back_d.at[rows_at(chip, quarter)])
        r.back_d[rows_at(chip, quarter), :] = r.ret_d[rows_at(chip, quarter), :]

    def expert_combine():
        line_wait("d", lambda at, _: r.back_d.at[rows_at(at, quarter)])
        line_start("y", lambda at: r.ret_y.at[:, rows_at(at, quarter)], r.back_y.at[chip])
        r.back_y[chip] = r.ret_y[:, rows_at(chip, quarter), :]
        scatter_start(3, mm_tn(r.table[...], r.back_d[...]))

    def results_combine():
        line_wait("y", lambda at, _: r.back_y.at[at])
        span_ids = lax.broadcasted_iota(jnp.int32, (g.chips * span, g.tokens), 0)
        whole = jnp.where(span_ids == place_row, 1.0, 0.0).astype(BF16)
        scatter_start(7, mm_tn(whole, r.back_y[...].reshape(g.chips * span, width)))

    offsets = range(1, g.sections) if g.parts > 1 else []
    for copy in loads:
        copy.wait()
    expert_part(core, g.my_part(sec), True)
    rows_pair_wait("crow", r.crow, 0)
    rows_pair_wait("rows", r.rows, 0)
    expert_part(1 - core, g.my_part(sec), False)
    for which in ("d", "y"):
        place = g.my_part(sec)
        pair_start(which + "0", snd[which].at[place], rcv[which].at[place])
    def part_arrive(offset):
        rows_plane_wait("crow", r.crow, offset)
        rows_plane_wait("rows", r.rows, offset)
        expert_part(core, from_section(offset), True)

    def part_finish(offset):
        part = from_section(offset)
        rows_pair_wait("crow", r.crow, offset)
        rows_pair_wait("rows", r.rows, offset)
        expert_part(1 - core, part, False)
        for which in ("d", "y"):
            pair_start(which + str(offset), snd[which].at[part], rcv[which].at[part])
        if offset > 1:
            merge_send(offset - 1)

    for offset in offsets:
        part_arrive(offset)
        if offset > 1:
            part_finish(offset - 1)
    if g.parts > 1:
        part_finish(g.sections - 1)
    if g.parts > 1:
        merge_send(g.sections - 1)
    expert_back_line()
    for offset in range(g.parts):
        r.ret_y[g.my_part(from_section(offset))] = merge("y", offset).astype(BF16)

    def flat(ref, side):
        value = ref[side]
        return value.reshape(g.parts * block_rows, value.shape[-1])

    def expert_weights(left, right, lanes):
        return mm_tn(flat(left, 0)[:, :lanes], flat(right, 0)) + mm_tn(flat(left, 1)[:, :lanes], flat(right, 1))

    r.v_gup[...] = expert_weights(r.rows, r.dpree, width)
    r.v_gdown[...] = expert_weights(r.acte, r.grow, r.acte.shape[-1])
    for copy in stores:
        copy.start()

    def finish_backward(section, slot, stream, above):
        grad = scatter_sum(slot)
        unit, inverse = normalize(stream[own, :].astype(F32))
        r.small[section : section + 1, :] = jnp.sum(grad * unit, axis=0, keepdims=True)
        r.small[4 + section : 5 + section, :] = jnp.sum(grad, axis=0, keepdims=True)
        grad = grad * r.prm[section : section + 1, :]
        shared = jnp.mean(grad, axis=-1, keepdims=True)
        along = jnp.mean(grad * unit, axis=-1, keepdims=True)
        grad = inverse * (grad - shared - unit * along) + above[own, :].astype(F32)
        r.gs[section, own, :] = grad.astype(BF16)
        gather_start(r.gs, section, 4 + section)

    expert_combine()
    finish_backward(3, 3, r.xs.at[2], r.cot)
    gather_wait(r.gs, 3, 7)

    def bias_row(index, section):
        r.small[index : index + 1, :] = jnp.sum(r.gs[section, own, :].astype(F32), axis=0, keepdims=True)

    def attention_backward(layer, section, slot):
        grad = r.gs[section + 1]
        dctx = mm_nt(r.w_out[layer], grad).astype(BF16)
        for micro in range(g.micro):
            for head in range(g.heads):
                at = token_slice(micro)
                weight = r.probs[layer, micro, head]
                low = weight.astype(BF16)
                dhead = dctx[head_slice(head), at]
                query = r.qkv[layer, block_of(0), head_slice(head), at]
                key = r.qkv[layer, block_of(1), head_slice(head), at]
                value = r.qkv[layer, block_of(2), head_slice(head), at]
                dprobs = mm_tn(value, dhead)
                delta = jnp.sum(weight * dprobs, axis=0, keepdims=True)
                dscores = (weight * (dprobs - delta)).astype(BF16)
                r.dqkv[block_of(0), head_slice(head), at] = (mm(key, dscores) * scale).astype(BF16)
                r.dqkv[block_of(1), head_slice(head), at] = (mm_nt(query, dscores) * scale).astype(BF16)
                r.dqkv[block_of(2), head_slice(head), at] = mm_nt(dhead, low).astype(BF16)
        flat_grad = r.dqkv[...].reshape(3 * head_cols, g.tokens)
        scatter_start(slot, mm_tn(flat_grad, r.w_qkv[layer]))
        bias_row(8 + layer, section + 1)

    def attention_weights(layer, section):
        grad_qkv = mm(r.dqkv[...].reshape(3 * head_cols, g.tokens), r.normed[2 * layer])
        if not g.direct:
            r.o_qkv[layer] = grad_qkv
            r.o_out[layer] = mm(r.ctx[layer], r.gs[section + 1])
            return
        r.tmp[0 : 3 * head_cols, :] = grad_qkv
        settle("qkv" + str(layer))
        for at_core, at_chip, index, first in chunk_places():
            r.rq[layer, at_core, at_chip, index] = pack_wide(r.tmp[first : first + cols, :])
        name = "gqkv" + str(layer)
        pair_start(name, r.rq.at[layer, 1 - core], r.hq.at[layer])
        r.tmp[:, 0:head_cols] = dot_as(r.gs[section + 1], r.ctx[layer], 0, 1)
        if layer:
            r.tmp[:, head_cols : head_cols + GROUP] = jnp.zeros((width, GROUP), F32)
            out_weights(1)

    def out_weights(layer):
        settle("out" + str(layer))
        for at_core, at_chip, at_sec, first in shard_places():
            block = r.tmp[first : first + cols, 0 : head_cols + GROUP]
            r.ro[layer, at_core, at_chip, at_sec] = pack_out(block)
        pair_start("gout" + str(layer), r.ro.at[layer, 1 - core], r.ho.at[layer])

    attention_backward(1, 2, 4)
    attention_weights(1, 2)
    if g.direct:
        grad_line("gqkv1", qkv_at(1), r.hq.at[1], r.aq.at[1], r.lq.at[1])
        grad_line("gout1", out_at(1), r.ho.at[1], r.ao.at[1], r.lo.at[1])
    finish_backward(2, 4, r.xs.at[1], r.gs.at[3])
    gather_wait(r.gs, 2, 6)

    grad_two = r.gs[2]
    for block in range(hidden // g.block):
        at = slice(block * g.block, (block + 1) * g.block)
        r.dpre[:, at] = (r.dgelu[:, at] * mm(grad_two, r.w_down[:, at])).astype(BF16)
    scatter_start(5, mm(r.dpre[...], up_rows(slice(None))))
    bias_row(10, 2)
    if g.direct:
        grad_relay("gqkv1", qkv_at(1), r.aq.at[1], r.lq.at[1])
        grad_relay("gout1", out_at(1), r.ao.at[1], r.lo.at[1])
    sum_up = jnp.sum(r.dpre[...].astype(F32), axis=0, keepdims=True)
    if g.direct:
        r.tmp[...] = mm_tn(r.gs[2], r.act[...])
        settle("down")
        for at_core, at_chip, at_sec, first in shard_places():
            r.rd[at_core, at_chip, at_sec] = pack_wide(r.tmp[first : first + cols, :])
        pair_start("gdown", r.rd.at[1 - core], r.hd)
        settle("up")
        settle("bias")
        r.ru[...] = mm_tn(r.dpre[...], r.normed[1]).astype(BF16).reshape(r.ru.shape)
        pair_start("gup", r.ru.at[:, 1 - core], r.hu)
        for at_dev in range(g.devices):
            row = sum_up[:, at_dev * shard_rows : (at_dev + 1) * shard_rows]
            row = jnp.broadcast_to(row, (r.pb.shape[0], shard_rows)).astype(BF16)
            r.rb[at_dev // 2, at_dev % 2, :, 0:shard_rows] = row
        pair_start("gbias", r.rb.at[:, 1 - core], r.hb)
        grad_line("gdown", down_at, r.hd, r.ad, r.ld)
    else:
        r.o_down[...] = mm_tn(r.gs[2], r.act[...])
        r.o_up[...] = mm_tn(r.dpre[...], r.normed[1])
        r.o_bup[...] = sum_up
    finish_backward(1, 5, r.xs.at[0], r.gs.at[2])
    if g.direct:
        grad_line("gup", up_at, r.hu, r.au, r.lu)
        grad_line("gbias", bias_at, r.hb, r.ab, r.lb)
        grad_relay("gdown", down_at, r.ad, r.ld)
    gather_wait(r.gs, 1, 5)

    attention_backward(0, 0, 6)
    results_combine()
    attention_weights(0, 0)
    if g.direct:
        grad_line("gqkv0", qkv_at(0), r.hq.at[0], r.aq.at[0], r.lq.at[0])
        grad_relay("gup", up_at, r.au, r.lu)
        grad_relay("gbias", bias_at, r.ab, r.lb)
    finish_backward(0, 6, r.x0, r.gs.at[1])
    r.xs[3, own, :] = (scatter_sum(7) + r.xs[2, own, :].astype(F32)).astype(BF16)
    gather_start(r.xs, 3, 3)
    if g.direct:
        kinds = r.small[...]
        padded = jnp.concatenate([kinds, jnp.zeros((LANES - kinds.shape[0], width), F32)], axis=0)
        r.tmp[:, head_cols : head_cols + GROUP] = padded.T[:, 0:GROUP]
        out_weights(0)
        grad_line("gout0", out_at(0), r.ho.at[0], r.ao.at[0], r.lo.at[0])
    if g.direct:
        grad_qkv_plane(1)
        grad_plane("gdown", down_at, r.ad, r.md, r.fd)
    if g.direct:
        grad_relay("gqkv0", qkv_at(0), r.aq.at[0], r.lq.at[0])
        grad_relay("gout0", out_at(0), r.ao.at[0], r.lo.at[0])
        grad_plane("gout1", out_at(1), r.ao.at[1], r.mo.at[1], r.fo.at[1])
    if g.direct:
        r.o_up[...] = grad_line_sum("gup", up_at, r.au)
        r.o_bup[...] = grad_line_sum("gbias", bias_at, r.ab)[0:1, 0:shard_rows]
        grad_qkv_finish(1)
        grad_plane_wait("gdown", r.fd)
        for at_sec in range(g.sections):
            piece = r.fd[at_sec].astype(F32)
            unpack_wide(r.o_down.at[:, pl.ds(at_sec * hidden, hidden)], 0, piece)
        grad_qkv_plane(0)
        grad_plane("gout0", out_at(0), r.ao.at[0], r.mo.at[0], r.fo.at[0])
        grad_plane_wait("gout1", r.fo.at[1])
        for at_sec in range(g.sections):
            unpack_out(r.o_out.at[1], 0, r.fo[1, at_sec].astype(F32), at_sec * head_cols)
        grad_qkv_finish(0)
        grad_plane_wait("gout0", r.fo.at[0])
        everyone = jnp.zeros((top, g.out_lanes), F32)
        for at_sec in range(g.sections):
            piece = r.fo[0, at_sec].astype(F32)
            unpack_out(r.o_out.at[0], 0, piece, at_sec * head_cols)
            everyone = everyone + piece
        r.square[...] = jnp.zeros_like(r.square)
        unpack_small(r.square, 0, everyone, 0)
        r.square[...] = r.square[...].T
        r.o_router[...] = r.square[FIRST_ROUTER : FIRST_ROUTER + g.experts, 0:cols]
        r.o_gain[...] = r.square[0:4, 0:cols]
        r.o_bias[...] = r.square[4:8, 0:cols]
        r.o_bout[...] = r.square[8:10, 0:cols]
        r.o_bdown[...] = r.square[10:11, 0:cols]
    else:
        r.o_small[...] = r.small[...]
    gather_wait(r.xs, 3, 3)
    gather_wait(r.gs, 0, 4)
    r.sec_out[...] = r.xs[sec]
    r.sec_grad[...] = r.gs[sec]
    for copy in stores:
        copy.wait()
    for copy, when in started:
        do_when(when, copy.wait_send)


def run_layers(g, operands):
    tokens, width, hidden, sections, chips = g.tokens, g.width, g.hidden, g.sections, g.chips
    part_rows = chips * g.quarter
    inner = operands["e_down"].shape[0]
    three = 3 * g.head_cols
    shape = jax.ShapeDtypeStruct
    vmem = pltpu.VMEM
    dma = pltpu.SemaphoreType.DMA
    top = g.cols - TAIL
    wide = width + width // 2
    up_rows = hidden // g.devices
    outs = dict(
        sec_out=shape((tokens, width), BF16),
        sec_grad=shape((tokens, width), BF16),
        g_eup=shape((width, inner), F32),
        g_edown=shape((inner, width), F32),
    )
    if g.direct:
        outs |= dict(
            o_qkv=shape((2, 3 * g.cols, width), F32),
            o_out=shape((2, g.cols, width), F32),
            o_up=shape((up_rows, width), F32),
            o_down=shape((g.cols, sections * hidden), F32),
            o_gain=shape((4, g.cols), F32),
            o_bias=shape((4, g.cols), F32),
            o_bout=shape((2, g.cols), F32),
            o_bdown=shape((1, g.cols), F32),
            o_router=shape((g.experts, g.cols), F32),
            o_bup=shape((1, up_rows), F32),
        )
    else:
        outs |= dict(
            o_qkv=shape((2, three, width), F32),
            o_out=shape((2, g.head_cols, width), F32),
            o_up=shape((hidden, width), F32),
            o_down=shape((width, hidden), F32),
            o_bup=shape((1, hidden), F32),
            o_small=shape((g.small, width), F32),
        )
    scratch = dict(
        xs=vmem((4, tokens, width), BF16),
        gs=vmem((4, tokens, width), BF16),
        normed=vmem((3, tokens, width), BF16),
        wide=vmem((tokens, width + LANES), BF16),
        qkv=vmem((2, 3, g.head_cols, tokens), BF16),
        probs=vmem((2, g.micro, g.heads, g.seq, g.seq), F32),
        ctx=vmem((2, g.head_cols, tokens), BF16),
        act=vmem((tokens, hidden), BF16),
        dgelu=vmem((tokens, hidden), F32),
        dpre=vmem((tokens, hidden), BF16),
        dqkv=vmem((3, g.head_cols, tokens), BF16),
        part=vmem((8, tokens, width), BF16),
        got=vmem((8, sections - 1, g.piece, width), BF16),
        mine=vmem((tokens, width), F32),
        square=vmem((LANES, LANES), F32),
        table=vmem((part_rows, tokens), BF16),
        disp=vmem((part_rows, width + LANES), BF16),
        dispc=vmem((part_rows, width), BF16),
        rows=vmem((2, g.parts, part_rows, width + LANES), BF16),
        crow=vmem((2, g.parts, part_rows, width), BF16),
        grow=vmem((2, g.parts, part_rows, width), BF16),
        acte=vmem((2, g.parts, part_rows, inner), BF16),
        dpree=vmem((2, g.parts, part_rows, inner), BF16),
        small=vmem((g.small, width), F32),
        v_up=vmem((width, inner), BF16),
        v_down=vmem((inner, width), BF16),
        v_gup=vmem((width, inner), F32),
        v_gdown=vmem((inner, width), F32),
        local_s=dma((4,)),
    )
    for which in ("d", "y"):
        scratch["keep_" + which] = vmem((g.parts, part_rows, width), F32)
        for name in ("snd_", "rcv_"):
            scratch[name + which] = vmem((g.parts, part_rows, width), BF16)
    scratch |= dict(
        out_d=vmem((sections - 1, part_rows, width), BF16),
        plane_d=vmem((sections - 1, part_rows, width), BF16),
        ret_d=vmem((part_rows, width), BF16),
        back_d=vmem((part_rows, width), BF16),
        ret_y=vmem((g.parts, part_rows, width), BF16),
        back_y=vmem((chips, g.parts, g.quarter, width), BF16),
    )
    for name in ("scat_s", "scat_r", "gath_s", "gath_r"):
        scratch[name] = dma((8, sections - 1))
    for name, count, each in (("pair", len(g.pairs), 0), ("line", len(g.lines), chips), ("plane", len(g.planes), sections - 1)):
        sizes = (count, each) if each else (count,)
        scratch |= {name + "_s": dma(sizes), name + "_r": dma(sizes)}
    if g.direct:
        piece = (top, wide)
        out_piece = (top, g.out_lanes)
        up_piece = (up_rows, width)
        bias_piece = (2 * TAIL, LANES)
        scratch |= dict(
            pq=vmem((2, 3, *piece), BF16),
            po=vmem((2, sections, *out_piece), BF16),
            pb=vmem(bias_piece, BF16),
            rb=vmem((chips, 2, *bias_piece), BF16),
            hb=vmem((chips, *bias_piece), BF16),
            ab=vmem((chips - 1, *bias_piece), BF16),
            lb=vmem(bias_piece, BF16),
            lq=vmem((2, 3, *piece), BF16),
            lo=vmem((2, sections, *out_piece), BF16),
            lu=vmem(up_piece, BF16),
            ld=vmem((sections, *piece), BF16),
            pd=vmem((sections, *piece), BF16),
            rq=vmem((2, 2, chips, 3, *piece), BF16),
            ro=vmem((2, 2, chips, sections, *out_piece), BF16),
            ru=vmem((chips, 2, *up_piece), BF16),
            rd=vmem((2, chips, sections, *piece), BF16),
            w_qkv=vmem((2, three, width), BF16),
            w_out=vmem((2, g.head_cols, width), BF16),
            w_down=vmem((width, hidden), BF16),
            w_router=vmem((width, LANES), BF16),
            b_up=vmem((8, hidden), F32),
            prm=vmem((GROUP, width), F32),
            tmp=vmem((width, width), F32),
            hq=vmem((2, chips, 3, *piece), BF16),
            ho=vmem((2, chips, sections, *out_piece), BF16),
            hu=vmem((chips, *up_piece), BF16),
            hd=vmem((chips, sections, *piece), BF16),
            aq=vmem((2, chips - 1, 3, *piece), BF16),
            ao=vmem((2, chips - 1, sections, *out_piece), BF16),
            au=vmem((chips - 1, *up_piece), BF16),
            ad=vmem((chips - 1, sections, *piece), BF16),
            mq=vmem((2, 3, *piece), BF16),
            mo=vmem((2, sections, *out_piece), BF16),
            md=vmem((sections, *piece), BF16),
            fq=vmem((2, 3, *piece), BF16),
            fo=vmem((2, sections, *out_piece), BF16),
            fd=vmem((sections, *piece), BF16),
            wq_s=dma((2, 3, chips)),
            wq_r=dma((2, 3, chips)),
            wo_s=dma((sections, chips)),
            wo_r=dma((sections, chips)),
            gq_s=dma((2, 3)),
            gq_r=dma((2, 3)),
        )
    whole = pl.BlockSpec(memory_space=pltpu.VMEM)
    placed = pl.BlockSpec(memory_space=pl.ANY)
    apart = ("e_up", "e_down", "g_eup", "g_edown")
    names = (*operands, *outs, *scratch)
    results = pl.pallas_call(
        functools.partial(layers_kernel, g, names),
        out_shape=tuple(outs.values()),
        in_specs=[placed if name in apart else whole for name in operands],
        out_specs=[placed if name in apart else whole for name in outs],
        scratch_shapes=list(scratch.values()),
        compiler_params=pltpu.CompilerParams(
            collective_id=0, has_side_effects=True, vmem_limit_bytes=62 * 1024 * 1024
        ),
    )(*operands.values())
    return types.SimpleNamespace(**dict(zip(outs, results, strict=True)))


def finish_kernel(count, *refs):
    ins, outs, held = refs[:count], refs[count : 2 * count], refs[2 * count : 3 * count]
    wide, sems = refs[3 * count : 3 * count + 2], refs[-1]
    loads = [pltpu.make_async_copy(ins[i], held[i], sems.at[0, i]) for i in range(count)]
    stores = [pltpu.make_async_copy((wide[i] if i < 2 else held[i]), outs[i], sems.at[1, i]) for i in range(count)]
    for copy in loads:
        copy.start()
    for i in range(count):
        loads[i].wait()
        if i < 2:
            wide[i][...] = held[i][...].astype(F32)
        stores[i].start()
    for copy in stores:
        copy.wait()


def finish(arrays):
    count = len(arrays)
    placed = [pl.BlockSpec(memory_space=pl.ANY)] * count
    held = [pltpu.VMEM(array.shape, array.dtype) for array in arrays]
    wide = [pltpu.VMEM(array.shape, F32) for array in arrays[:2]]
    return pl.pallas_call(
        functools.partial(finish_kernel, count),
        out_shape=tuple(jax.ShapeDtypeStruct(array.shape, F32) for array in arrays),
        in_specs=placed,
        out_specs=placed,
        scratch_shapes=[*held, *wide, pltpu.SemaphoreType.DMA((2, count))],
        compiler_params=pltpu.CompilerParams(vmem_limit_bytes=62 * 1024 * 1024),
    )(*arrays)


BOTH = ("section", "dp")


def body(
    tokens, cotangent, lengths, routes, slots, norm_gain, norm_bias, attn_qkv, attn_out, attn_out_bias,
    ffn_up, ffn_up_bias, ffn_down, ffn_down_bias, router, expert_up, expert_down,
):
    sections, devices = lax.axis_size("section"), lax.axis_size("dp")
    sec = lax.axis_index("section")
    micro, _, seq, width = tokens.shape
    experts = router.shape[1]
    chips = devices // 2
    head_cols = width // sections
    hidden = ffn_up.shape[1] * devices
    cap = 2 * seq // experts
    span = micro * cap
    cols = ffn_down.shape[1]
    kinds = FIRST_ROUTER + experts
    direct = cols == 3 * TAIL and kinds <= GROUP and sections == 4 and ffn_up.shape[1] % 16 == 0
    parts = sections if span % (16 * sections) == 0 else 1
    numbers = [str(part) for part in range(parts)]
    g = types.SimpleNamespace(
        sections=sections, devices=devices, chips=chips, micro=micro, seq=seq, width=width, hidden=hidden, cap=cap,
        span=span, tokens=micro * seq, piece=micro * seq // sections, heads=head_cols // HEAD_DIM,
        head_cols=head_cols, cols=cols, block=256, small=-(-kinds // 8) * 8, direct=direct, experts=experts,
        out_lanes=head_cols + 2 * GROUP + LANES, parts=parts, quarter=span // parts,
        relay=direct and chips == 4,
        my_part=(lambda section: section) if parts > 1 else (lambda section: 0),
        router_lane=FIRST_ROUTER + (LANES - 2 * GROUP if direct else 0),
        pairs=[name + n for name in ("crow", "rows", "d", "y") for n in numbers]
        + ([
            "out0", "qkv0", "up", "bias", "down", "qkv1", "out1",
            "gqkv0", "gqkv1", "gdown", "gup", "gbias", "gout0", "gout1",
        ] if direct else []),
        lines=["crow", "rows", "d", "y"]
        + ([
            "out0", "qkv0", "up", "bias", "down", "qkv1", "out1",
            "gqkv0", "gqkv1", "gdown", "gup", "gbias", "gout0", "gout1",
        ] if direct else []),
        planes=["crow", "rows", "d"] + (["down", "out1", "gdown", "gout0", "gout1"] if direct else []),
    )

    operands = dict(
        x0=tokens.reshape(g.tokens, width),
        cot=cotangent.reshape(g.tokens, width),
        lens=lengths.T,
        routes=routes[:, 0],
        slots=slots[:, 0],
        e_up=expert_up[0],
        e_down=expert_down[0],
    )
    if direct:
        operands |= dict(
            norm_gain=norm_gain,
            norm_bias=norm_bias,
            out_bias=attn_out_bias,
            down_bias=ffn_down_bias[None],
            up_bias=ffn_up_bias[None],
            router=router.T,
            wq=attn_qkv.transpose(0, 2, 1),
            wo=attn_out.transpose(0, 2, 1),
            wu=ffn_up.T,
            wd=ffn_down.T,
        )
    else:

        def every(array, axis):
            return lax.all_gather(array, BOTH, axis=axis, tiled=True)

        def part_of(array, axis, size):
            return lax.dynamic_slice_in_dim(array, sec * size, size, axis)

        rows = [norm_gain, norm_bias, attn_out_bias, ffn_down_bias[None], router.T]
        params = every(jnp.concatenate(rows, axis=0), 1)
        params = jnp.pad(params, ((0, LANES - kinds), (0, 0)))
        b_up = lax.all_gather(ffn_up_bias, "dp", axis=0, tiled=True).astype(F32)
        full = part_of(every(attn_qkv, 2).reshape(2, width, 3, width), 3, head_cols)
        operands |= dict(
            prm=params.astype(F32),
            w_router=params.T,
            b_up=b_up[None],
            w_qkv=full.transpose(0, 2, 3, 1).reshape(2, 3 * head_cols, width),
            w_out=part_of(every(attn_out, 2), 1, head_cols),
            w_up=lax.all_gather(ffn_up, "dp", axis=1, tiled=True).T,
            w_down=part_of(every(ffn_down, 1), 0, hidden).T,
        )
    res = run_layers(g, operands)

    if direct:
        names = list(vars(res))
        done = finish([getattr(res, name) for name in names])
        res = types.SimpleNamespace(**dict(zip(names, done, strict=True)))
        grads = (
            res.o_gain, res.o_bias, res.o_qkv.transpose(0, 2, 1), res.o_out.transpose(0, 2, 1), res.o_bout,
            res.o_up.T, res.o_bup[0], res.o_down.T, res.o_bdown[0], res.o_router.T,
        )
    else:

        def embed(array, shape, axis, size):
            return lax.dynamic_update_slice_in_dim(jnp.zeros(shape, F32), array, sec * size, axis)

        def share(array, axis, over=BOTH):
            return lax.psum_scatter(array, over, scatter_dimension=axis, tiled=True)

        small = share(res.o_small[:kinds], 1)
        g_qkv = res.o_qkv.reshape(2, 3, head_cols, width).transpose(0, 3, 1, 2)
        g_qkv = embed(g_qkv, (2, width, 3, width), 3, head_cols).reshape(2, width, 3 * width)
        g_out = embed(res.o_out, (2, width, width), 1, head_cols)
        g_down = embed(res.o_down.T, (hidden * sections, width), 0, hidden)
        grads = (
            small[0:4], small[4:8], share(g_qkv, 2), share(g_out, 2), small[8:10], share(res.o_up.T, 1, "dp"),
            share(res.o_bup[0], 0, "dp"), share(g_down, 1), small[10], small[FIRST_ROUTER:].T,
        )
    out_shape = (1, micro, 1, seq, width)
    return (
        res.sec_out.reshape(out_shape).astype(F32),
        res.sec_grad.reshape(out_shape).astype(F32),
        *grads,
        res.g_eup[None],
        res.g_edown[None],
    )


def solution(mesh):
    batch = P(None, "dp", None, None)
    table = P(None, "dp", None)
    in_specs = (
        batch, batch, P(None, "dp"), table, table,
        P(None, BOTH), P(None, BOTH), P(None, None, BOTH), P(None, None, BOTH), P(None, BOTH),
        P(None, BOTH), P(BOTH), P(None, BOTH), P(BOTH), P(BOTH, None),
        P("dp", None, "section"), P("dp", "section", None),
    )
    streams = P("section", None, "dp", None, None)
    out_specs = (
        streams, streams,
        P(None, BOTH), P(None, BOTH), P(None, None, BOTH), P(None, None, BOTH), P(None, BOTH),
        P(None, BOTH), P(BOTH), P(None, BOTH), P(BOTH), P(BOTH, None),
        P("dp", None, "section"), P("dp", "section", None),
    )
    return jax.shard_map(body, mesh=mesh, in_specs=in_specs, out_specs=out_specs, check_vma=False)
```

```python
import functools
import types

import jax
import jax.numpy as jnp
from jax import lax
from jax.experimental import pallas as pl
from jax.experimental.pallas import tpu as pltpu
from jax.sharding import PartitionSpec as P

HEADS = 12
HEAD_DIM = 64
EPS = 1e-05
MASKED = -1000000000.0
MESH = pl.DeviceIdType.MESH
F32 = jnp.float32
BF16 = jnp.bfloat16
LANES = 128


def dot_as(left, right, left_dim, right_dim):
    return lax.dot_general(
        left, right, (((left_dim,), (right_dim,)), ((), ())), preferred_element_type=F32
    )


def mm(left, right):
    return dot_as(left, right, 1, 0)


def mm_nt(left, right):
    return dot_as(left, right, 1, 1)


def mm_tn(left, right):
    return dot_as(left, right, 0, 0)


def normalize(values):
    center = values - jnp.mean(values, axis=-1, keepdims=True)
    spread = jnp.mean(center * center, axis=-1, keepdims=True)
    inverse = lax.rsqrt(spread + EPS)
    return center * inverse, inverse


def gelu_parts(pre):
    half = 0.5 + 0.5 * lax.erf(pre * 0.7071067811865476)
    density = jnp.exp(-0.5 * pre * pre) * 0.3989422804014327
    return pre * half, half + pre * density


TAIL = 8
GROUP = 32
FIRST_ROUTER = 11


def layers_kernel(g, names, *refs):
    r = types.SimpleNamespace(**dict(zip(names, refs, strict=True)))
    width, span, hidden, cols, head_cols = g.width, g.span, g.hidden, g.cols, g.head_cols
    sec = lax.axis_index("section")
    dev = lax.axis_index("dp")
    core = lax.rem(dev, 2)
    chip = lax.div(dev, 2)
    sib = dev + 1 - 2 * core
    quarter = g.quarter
    shard_rows = hidden // g.devices
    block_rows = g.chips * quarter

    def peer_section(offset):
        return lax.rem(sec + offset, g.sections)

    def from_section(offset):
        return lax.rem(sec + g.sections - offset, g.sections)

    def peer_chip(offset):
        return lax.rem(chip + offset, g.chips)

    def from_chip(offset):
        return lax.rem(chip + g.chips - offset, g.chips)

    def rows_at(index, size):
        return pl.ds(pl.multiple_of(index * size, size), size)

    def remote(source, target, send, arrive, where):
        return pltpu.make_async_remote_copy(
            src_ref=source, dst_ref=target, send_sem=send, recv_sem=arrive, device_id=where, device_id_type=MESH
        )

    def at_chip_core(index):
        return {"dp": 2 * index + core}

    started = []
    kept_back = {}

    def do_when(condition, action):
        if condition is None:
            action()
        else:
            pl.when(condition)(action)

    def launch(copy, buffer=None, when=None):
        do_when(when, copy.start)
        if buffer:
            kept_back.setdefault(buffer, []).append((copy, when))
        else:
            started.append((copy, when))

    def settle(buffer):
        for copy, when in kept_back.pop(buffer, []):
            do_when(when, copy.wait_send)

    barrier = pltpu.get_barrier_semaphore()
    partners = [(a, b) for a in range(g.sections) for b in range(g.chips) if a + b and (g.direct or a * b == 0)]
    for section_offset, chip_offset in partners:
        where = {"section": peer_section(section_offset), "dp": 2 * peer_chip(chip_offset) + core}
        pl.semaphore_signal(barrier, inc=1, device_id=where, device_id_type=MESH)
    pl.semaphore_signal(barrier, inc=1, device_id={"dp": sib}, device_id_type=MESH)

    def local(index, source, target):
        return pltpu.make_async_copy(source, target, r.local_s.at[index])

    loads = [local(0, r.e_up, r.v_up), local(1, r.e_down, r.v_down)]
    stores = [local(2, r.v_gup, r.g_eup), local(3, r.v_gdown, r.g_edown)]
    for copy in loads:
        copy.start()

    def token_slice(micro):
        return slice(micro * g.seq, (micro + 1) * g.seq)

    def piece_at(micro, section):
        return pl.ds(pl.multiple_of(micro * g.seq + section * g.piece, g.piece), g.piece)

    def own(micro):
        return piece_at(micro, sec)

    def scatter_copy(slot, micro, offset):
        return remote(
            r.part.at[slot, piece_at(micro, peer_section(offset))], r.got.at[slot, micro, offset - 1],
            r.scat_s.at[slot, micro, offset - 1], r.scat_r.at[slot, micro, offset - 1],
            {"section": peer_section(offset)},
        )

    def scatter_start(slot, micro, value):
        r.part[slot, token_slice(micro), :] = value.astype(BF16)
        if slot != 7:
            r.mine[token_slice(micro), :] = value
        for offset in range(1, g.sections):
            launch(scatter_copy(slot, micro, offset))

    def scatter_sum(slot, micro):
        at = own(micro)
        total = r.part[slot, at, :].astype(F32) if slot == 7 else r.mine[at, :]
        for offset in range(1, g.sections):
            scatter_copy(slot, micro, offset).wait_recv()
            total = total + r.got[slot, micro, offset - 1].astype(F32)
        return total

    def share_copy(place, send, arrive, offset, receiving):
        where = from_section(offset) if receiving else peer_section(offset)
        return remote(place, place, send.at[offset - 1], arrive.at[offset - 1], {"section": where})

    def gather_start(buffer, slot, sem, micro):
        place = buffer.at[slot, own(micro)]
        for offset in range(1, g.sections):
            launch(share_copy(place, r.gath_s.at[sem, micro], r.gath_r.at[sem, micro], offset, False))

    def gather_wait(buffer, slot, sem, micro):
        for offset in range(1, g.sections):
            place = buffer.at[slot, piece_at(micro, from_section(offset))]
            share_copy(place, r.gath_s.at[sem, micro], r.gath_r.at[sem, micro], offset, True).wait_recv()

    def pair_copy(name, source, target):
        index = g.pairs.index(name)
        return remote(source, target, r.pair_s.at[index], r.pair_r.at[index], {"dp": sib})

    def pair_start(name, source, target, buffer=None):
        launch(pair_copy(name, source, target), buffer)

    def pair_wait(name, target):
        pair_copy(name, target, target).wait_recv()

    def line_copy(name, source, target, offset, receiving):
        index = g.lines.index(name)
        where = from_chip(offset) if receiving else peer_chip(offset)
        return remote(
            source, target, r.line_s.at[index, offset - 1], r.line_r.at[index, offset - 1], at_chip_core(where)
        )

    last_chip = g.chips - 1
    is_end = lax.rem(chip, max(last_chip, 1)) == 0
    is_mid = lax.rem(chip, max(last_chip, 1)) != 0
    line_order = (2, 1, 3) if g.relay else range(1, g.chips)
    outward = jnp.clip(chip - 1, 0, 1)

    def near_to(offset):
        return {1: chip != last_chip, last_chip: chip != 0}.get(offset) if g.relay else None

    def near_from(offset):
        return {1: chip != 0, last_chip: chip != last_chip}.get(offset) if g.relay else None

    def spread_start(name, source, target, buffer=None):
        for offset in line_order:
            launch(line_copy(name, source, target, offset, False), buffer, near_to(offset))

    def spread_relay(name, place, buffer):
        index = g.lines.index(name)
        copy = remote(
            place, place, r.line_s.at[index, last_chip], r.line_r.at[index, outward * 2],
            at_chip_core(outward * last_chip),
        )
        launch(copy, buffer, is_mid)

    def spread_wait(name, place_at, buffer):
        for offset in line_order:
            place = place_at(from_chip(offset))
            line_copy(name, place, place, offset, True).wait_recv()
            if g.relay and offset == 2:
                spread_relay(name, place, buffer)

    def far_wait(name, place_at):
        for offset in (1, last_chip):
            place = place_at(from_chip(offset))
            copy = line_copy(name, place, place, offset, True)
            pl.when(jnp.logical_not(near_from(offset)))(copy.wait_recv)

    def line_start(name, source_at, target, buffer=None):
        for offset in range(1, g.chips):
            launch(line_copy(name, source_at(peer_chip(offset)), target, offset, False), buffer)

    def line_wait(name, target_at):
        for offset in range(1, g.chips):
            target = target_at(from_chip(offset), offset)
            line_copy(name, target, target, offset, True).wait_recv()

    def rows_plane_start(name, place, offset0):
        if g.parts > 1:
            index = g.planes.index(name)
            for offset in range(1, g.sections):
                launch(share_copy(place, r.plane_s.at[index], r.plane_r.at[index], offset, False))
        pair_start(offset0, place, place)

    def rows_plane_wait(name, place, offset, pair):
        index = g.planes.index(name)
        share_copy(place, r.plane_s.at[index], r.plane_r.at[index], offset, True).wait_recv()
        pair_start(pair, place, place)

    top = cols - TAIL
    half = width // 2
    part_cols = head_cols // 2
    tail_lane = head_cols + 2 * GROUP

    def qkv_section(at_dev, index, section):
        return lax.rem(lax.div(3 * at_dev + index, g.devices) - section + g.sections, g.sections)

    def qkv_send(layer, offsets):
        for index in range(3):
            to = qkv_section(dev, index, sec)
            for offset in offsets:
                copy = remote(
                    r.pq.at[layer, index], r.rq.at[layer, core, chip, index],
                    r.wq_s.at[layer, index, offset], r.wq_r.at[layer, index, offset],
                    {"section": to, "dp": 2 * peer_chip(offset) + core},
                )
                if offset:
                    launch(copy, None, near_to(offset))
                else:
                    pl.when(to != sec)(copy.start)

                    @pl.when(to == sec)
                    def _(index=index):
                        r.rq[layer, core, chip, index] = r.pq[layer, index]

    def qkv_arrive(layer, offsets):
        for offset in offsets:
            for index in range(3):
                at_chip = from_chip(offset)
                target = r.rq.at[layer, core, at_chip, index]
                origin = qkv_section(2 * at_chip + core, index, sec)
                copy = remote(
                    target, target, r.wq_s.at[layer, index, offset], r.wq_r.at[layer, index, offset],
                    {"section": origin, "dp": 2 * at_chip + core},
                )
                if offset:
                    do_when(near_from(offset), copy.wait_recv)
                else:

                    @pl.when(origin != sec)
                    def _(copy=copy):
                        copy.wait_recv()
                        copy.wait_send()

            if g.relay and offset == 2:
                spread_relay("qkv0", r.rq.at[0, core, from_chip(offset)], "qkv0")
        if g.relay and len(offsets) > 1:
            far_wait("qkv0", lambda at: r.rq.at[0, core, at])

    def out_copy(section_offset, offset, place, receiving):
        if receiving:
            to, at_chip = from_section(section_offset), from_chip(offset)
        else:
            to, at_chip = peer_section(section_offset), peer_chip(offset)
        source = place if receiving else r.po.at[0, to]
        return remote(
            source, place, r.wo_s.at[section_offset, offset], r.wo_r.at[section_offset, offset],
            {"section": to, "dp": 2 * at_chip + core},
        )

    def out_offsets():
        return [(a, b) for b in (*line_order, 0) for a in range(g.sections) if a + b]

    def plane_copy(name, source, target, offset, receiving):
        index = g.planes.index(name)
        where = from_section(offset) if receiving else peer_section(offset)
        return remote(
            source, target, r.plane_s.at[index, offset - 1], r.plane_r.at[index, offset - 1], {"section": where}
        )

    def pack_wide(block):
        tail = jnp.concatenate([block[top:, :half], block[top:, half:]], axis=0)
        return jnp.concatenate([block[:top], tail], axis=1).astype(BF16)

    def pack_out(block):
        small = jnp.concatenate([block[top:, head_cols:]] * 2, axis=0)
        tail = jnp.concatenate([block[top:, :part_cols], block[top:, part_cols:head_cols]], axis=0)
        empty = jnp.zeros((top, g.out_lanes - tail_lane - part_cols), F32)
        return jnp.concatenate([block[:top], small, tail, empty], axis=1).astype(BF16)

    def unpack_wide(target, first, piece):
        target[first : first + top, 0:width] = piece[:, 0:width]
        target[first + top : first + cols, 0:half] = piece[0:TAIL, width : width + half]
        target[first + top : first + cols, half:width] = piece[TAIL:, width : width + half]

    def unpack_out(target, first, piece, lane=0):
        last = slice(first + top, first + cols)
        tail = slice(tail_lane, tail_lane + part_cols)
        target[first : first + top, lane : lane + head_cols] = piece[:, 0:head_cols]
        target[last, lane : lane + part_cols] = piece[0:TAIL, tail]
        target[last, lane + part_cols : lane + head_cols] = piece[TAIL:, tail]

    def unpack_small(target, first, piece, lane):
        target[first : first + top, lane : lane + GROUP] = piece[:, head_cols : head_cols + GROUP]
        target[first + top : first + cols, lane : lane + GROUP] = piece[0:TAIL, head_cols + GROUP : tail_lane]

    def shard_places():
        for at_core in range(2):
            for at_chip in range(g.chips):
                for at_sec in range(g.sections):
                    yield at_core, at_chip, at_sec, (at_sec * g.devices + 2 * at_chip + at_core) * cols

    def chunk_places():
        for at_core in range(2):
            for at_chip in range(g.chips):
                for index in range(3):
                    yield at_core, at_chip, index, (3 * (2 * at_chip + at_core) + index) * cols

    def unfold_out(layer):
        for at_core, at_chip, at_sec, first in shard_places():
            piece = r.ro[layer, at_core, at_chip, at_sec].astype(F32)
            if layer == 0:
                unpack_small(r.tmp, first, piece, head_cols)
            unpack_out(r.tmp, first, piece)
        flipped = r.tmp[:, 0:tail_lane].T
        r.w_out[layer] = flipped[:head_cols].astype(BF16)
        if layer == 0:
            r.prm[...] = flipped[head_cols : head_cols + GROUP]
            r.w_router[...] = r.tmp[:, tail_lane - LANES : tail_lane].astype(BF16)

    def unfold_qkv(layer):
        for at_core, at_chip, index, first in chunk_places():
            unpack_wide(r.tmp, first, r.rq[layer, at_core, at_chip, index].astype(F32))
        r.w_qkv[layer] = r.tmp[0 : 3 * head_cols, 0:width].astype(BF16)

    def unfold_down():
        for at_core, at_chip, at_sec, first in shard_places():
            unpack_wide(r.tmp, first, r.rd[at_core, at_chip, at_sec].astype(F32))
        r.w_down[...] = r.tmp[...].astype(BF16)

    def grad_line(name, buffer_at, landing, target, passed):
        pair_wait(name, landing)
        for at_chip in range(g.chips):
            block = buffer_at(at_chip)
            block[...] = (block[...].astype(F32) + landing[at_chip].astype(F32)).astype(BF16)
        if g.relay:
            index = g.lines.index(name)
            copy = remote(
                buffer_at(last_chip - chip), passed, r.line_s.at[index, last_chip], r.line_r.at[index, last_chip],
                at_chip_core(1 + lax.div(chip, last_chip)),
            )
            launch(copy, None, is_end)
            for offset in (1, last_chip):

                @pl.when(jnp.logical_not(near_from(offset)))
                def _(offset=offset):
                    target[offset - 1] = jnp.zeros_like(target[offset - 1])

        for offset in line_order:
            copy = line_copy(name, buffer_at(peer_chip(offset)), target.at[offset - 1], offset, False)
            if g.relay and offset == 2:
                pl.when(is_end)(copy.start)
                started.append((copy, None))
            else:
                launch(copy, None, near_to(offset))

    def grad_relay(name, buffer_at, target, passed):
        if g.relay:
            index = g.lines.index(name)
            block = buffer_at(peer_chip(2))
            copy = line_copy(name, block, target.at[1], 2, False)

            @pl.when(is_mid)
            def _():
                remote(
                    passed, passed, r.line_s.at[index, last_chip], r.line_r.at[index, last_chip],
                    at_chip_core(outward * last_chip),
                ).wait_recv()
                block[...] = (block[...].astype(F32) + passed[...].astype(F32)).astype(BF16)
                copy.start()

    def grad_line_sum(name, buffer_at, target):
        for offset in line_order:
            place = target.at[offset - 1]
            do_when(near_from(offset), line_copy(name, place, place, offset, True).wait_recv)
        total = buffer_at(chip)[...].astype(F32)
        for offset in range(1, g.chips):
            total = total + target[offset - 1].astype(F32)
        return total

    def qkv_at(layer):
        return lambda at: r.rq.at[layer, core, at]

    def down_at(at):
        return r.rd.at[core, at]

    def out_at(layer):
        return lambda at: r.ro.at[layer, core, at]

    def up_at(at):
        return r.ru.at[at, core]

    def bias_at(at):
        return r.rb.at[at, core]

    def grad_plane(name, buffer_at, target, summed, final):
        summed[...] = grad_line_sum(name, buffer_at, target).astype(BF16)
        for offset in range(1, g.sections):
            source = summed.at[peer_section(offset)]
            launch(plane_copy(name, source, final.at[sec], offset, False))
        final[sec] = summed[sec]

    def grad_plane_wait(name, final):
        for offset in range(1, g.sections):
            place = final.at[from_section(offset)]
            plane_copy(name, place, place, offset, True).wait_recv()

    def grad_qkv_copy(layer, index, place, where):
        return remote(
            r.mq.at[layer, index], place, r.gq_s.at[layer, index], r.gq_r.at[layer, index], {"section": where}
        )

    def grad_qkv_plane(layer):
        r.mq[layer] = grad_line_sum("gqkv" + str(layer), qkv_at(layer), r.aq.at[layer]).astype(BF16)
        for index in range(3):
            to = qkv_section(dev, index, sec)
            copy = grad_qkv_copy(layer, index, r.fq.at[layer, index], to)
            pl.when(to != sec)(copy.start)

            @pl.when(to == sec)
            def _(index=index):
                r.fq[layer, index] = r.mq[layer, index]

    def grad_qkv_finish(layer):
        for index in range(3):
            origin = qkv_section(dev, index, sec)
            copy = grad_qkv_copy(layer, index, r.fq.at[layer, index], origin)

            @pl.when(origin != sec)
            def _(copy=copy):
                copy.wait_recv()
                copy.wait_send()

            unpack_wide(r.o_qkv.at[layer], index * cols, r.fq[layer, index].astype(F32))

    def norm_into(source, target, index, micro):
        rows = g.seq // 2

        @pl.loop(0, 2)
        def _(step):
            at = rows_at(micro * 2 + step, rows)
            unit, _ = normalize(source[at, :].astype(F32))
            target[at, :] = (unit * r.prm[index : index + 1, :] + r.prm[4 + index : 5 + index, :]).astype(BF16)

    place_row = jnp.concatenate(
        [r.routes[m : m + 1] * span + m * g.cap + r.slots[m : m + 1] for m in range(g.micro)], axis=1
    )
    r.square[...] = jnp.zeros_like(r.square)
    if g.direct:
        r.square[0:4, 0:cols] = r.norm_gain[...].astype(F32)
        r.square[4:8, 0:cols] = r.norm_bias[...].astype(F32)
        r.square[8:10, 0:cols] = r.out_bias[...].astype(F32)
        r.square[10:11, 0:cols] = r.down_bias[...].astype(F32)
        r.pb[...] = jnp.zeros_like(r.pb)
        r.pb[:, 0:shard_rows] = jnp.broadcast_to(r.up_bias[...], (r.pb.shape[0], shard_rows))
        r.square[FIRST_ROUTER : FIRST_ROUTER + g.experts, 0:cols] = r.router[...].astype(F32)
        r.square[...] = r.square[...].T
        shard = r.wo[0].astype(F32)
        mine = r.square[0:cols, 0:GROUP]
        for at_sec in range(g.sections):
            block = shard[:, at_sec * head_cols : (at_sec + 1) * head_cols]
            r.po[0, at_sec] = pack_out(jnp.concatenate([block, mine], axis=1))
        shard = r.wq[0].astype(F32)
        for index in range(3):
            r.pq[0, index] = pack_wide(shard[index * cols : (index + 1) * cols])
    pl.semaphore_wait(barrier, len(partners) + 1)
    if g.direct:
        for section_offset, offset in out_offsets():
            launch(out_copy(section_offset, offset, r.ro.at[0, core, chip, sec], False), None, near_to(offset))
        r.ro[0, core, chip, sec] = r.po[0, sec]
        qkv_send(0, (*line_order, 0))
        shard = r.wq[1].astype(F32)
        for index in range(3):
            r.pq[1, index] = pack_wide(shard[index * cols : (index + 1) * cols])
        shard, other = r.wd[...].astype(F32), r.wo[1].astype(F32)
        empty = jnp.zeros((cols, GROUP), F32)
        for at_sec in range(g.sections):
            r.pd[at_sec] = pack_wide(shard[:, at_sec * hidden : (at_sec + 1) * hidden])
            block = other[:, at_sec * head_cols : (at_sec + 1) * head_cols]
            r.po[1, at_sec] = pack_out(jnp.concatenate([block, empty], axis=1))

    slot_ids = lax.broadcasted_iota(jnp.int32, (quarter, g.tokens), 0)

    def slot_match(expert, part, group):
        first = expert * span + group * (span // g.groups) + part * quarter
        return jnp.where(slot_ids + first == place_row, 1.0, 0.0).astype(BF16)

    def group_tokens(group):
        count = g.tokens // g.groups
        return slice(group * count, (group + 1) * count)

    for group in range(g.groups):
        for expert in range(g.chips):
            match = slot_match(expert, g.my_part(sec), group)
            r.table[group, expert * quarter : (expert + 1) * quarter, :] = match[:, group_tokens(group)]
        sent = mm(r.table[group], r.cot[group_tokens(group), :]).astype(BF16)
        r.dispc[:, group] = sent.reshape(g.chips, quarter, width)
    r.small[...] = jnp.zeros_like(r.small)
    if g.direct:
        for section_offset, offset in out_offsets():
            place = r.ro.at[0, core, from_chip(offset), from_section(section_offset)]
            do_when(near_from(offset), out_copy(section_offset, offset, place, True).wait_recv)
            if g.relay and (section_offset, offset) == (g.sections - 1, 2):
                spread_relay("out0", r.ro.at[0, core, from_chip(offset)], "out0")
        if g.relay:
            far_wait("out0", lambda at: r.ro.at[0, core, at])
        pair_start("out0", r.ro.at[0, core], r.ro.at[0, core], "out0")
        qkv_arrive(0, (*line_order, 0))
        pair_start("qkv0", r.rq.at[0, core], r.rq.at[0, core], "qkv0")
        spread_start("bias", r.pb, r.rb.at[chip, core])
        r.rb[chip, core] = r.pb[...]
        spread_start("up", r.wu, r.ru.at[chip, core])
        r.ru[chip, core] = r.wu[...]
        for offset in range(1, g.sections):
            launch(plane_copy("down", r.pd.at[peer_section(offset)], r.rd.at[core, chip, sec], offset, False))
        r.rd[core, chip, sec] = r.pd[sec]
        qkv_send(1, [0])
        for offset in range(1, g.sections):
            place = r.ro.at[1, core, chip, sec]
            launch(plane_copy("out1", r.po.at[1, peer_section(offset)], place, offset, False))
        r.ro[1, core, chip, sec] = r.po[1, sec]
        pair_wait("out0", r.ro.at[0, 1 - core])
        unfold_out(0)
        pair_wait("qkv0", r.rq.at[0, 1 - core])
        unfold_qkv(0)

    def weights_line_start():
        for offset in range(1, g.sections):
            place = r.rd.at[core, chip, from_section(offset)]
            plane_copy("down", place, place, offset, True).wait_recv()
        spread_start("down", r.rd.at[core, chip], r.rd.at[core, chip], "down")
        qkv_arrive(1, [0])
        spread_start("qkv1", r.rq.at[1, core, chip], r.rq.at[1, core, chip], "qkv1")
        for offset in range(1, g.sections):
            place = r.ro.at[1, core, chip, from_section(offset)]
            plane_copy("out1", place, place, offset, True).wait_recv()
        spread_start("out1", r.ro.at[1, core, chip], r.ro.at[1, core, chip], "out1")

    key_ids = lax.broadcasted_iota(jnp.int32, (g.seq, g.seq), 0)
    query_ids = lax.broadcasted_iota(jnp.int32, (g.seq, g.seq), 1)
    scale = HEAD_DIM**-0.5
    micros = range(g.micro)

    def block_of(index):
        return lax.rem(index + sec, 3) if g.direct else index

    def head_slice(head):
        return slice(head * HEAD_DIM, (head + 1) * HEAD_DIM)

    def attention_forward(layer, stream, slot, micro):
        at = token_slice(micro)
        norm_into(stream, r.normed.at[2 * layer], 2 * layer, micro)
        packed = mm_nt(r.w_qkv[layer], r.normed[2 * layer, at, :]).astype(BF16)
        r.qkv[layer, :, :, at] = packed.reshape(3, head_cols, g.seq)
        allowed = (key_ids <= query_ids) & (key_ids < r.lens[:, micro : micro + 1])
        for head in range(g.heads):
            key = r.qkv[layer, block_of(1), head_slice(head), at]
            scores = mm_tn(key, r.qkv[layer, block_of(0), head_slice(head), at]) * scale
            scores = jnp.where(allowed, scores, MASKED)
            weight = jnp.exp(scores - jnp.max(scores, axis=0, keepdims=True))
            weight = weight / jnp.sum(weight, axis=0, keepdims=True)
            r.probs[layer, micro, head] = weight
            value = r.qkv[layer, block_of(2), head_slice(head), at]
            r.ctx[layer, head_slice(head), at] = mm(value, weight.astype(BF16)).astype(BF16)
        scatter_start(slot, micro, mm_tn(r.ctx[layer, :, at], r.w_out[layer]))

    def finish_forward(section, bias, stream, micro):
        total = scatter_sum(section, micro) + bias + stream[own(micro), :].astype(F32)
        r.xs[section, own(micro), :] = total.astype(BF16)
        gather_start(r.xs, section, section, micro)

    for micro in micros:
        attention_forward(0, r.x0, 0, micro)
    if g.direct:
        weights_line_start()
    for micro in micros:
        finish_forward(0, r.prm[8:9, :], r.x0, micro)
    if g.direct:
        spread_wait("bias", lambda at: r.rb.at[at, core], "bias")
        spread_wait("up", lambda at: r.ru.at[at, core], "up")
        pair_start("up", r.ru.at[:, core], r.ru.at[:, core], "up")
        pair_start("bias", r.rb.at[:, core], r.rb.at[:, core], "bias")
        pair_wait("up", r.ru.at[:, 1 - core])
        pair_wait("bias", r.rb.at[:, 1 - core])
        for at_dev in range(g.devices):
            row = r.rb[at_dev // 2, at_dev % 2, :, 0:shard_rows].astype(F32)
            r.b_up[:, at_dev * shard_rows : (at_dev + 1) * shard_rows] = row[0:TAIL]

    def up_rows(at):
        if g.direct:
            return r.ru[...].reshape(hidden, width)[at]
        return r.w_up[at, :]

    def hidden_blocks():
        return [slice(first, first + g.block) for first in range(0, hidden, g.block)]

    for micro in micros:
        rows = token_slice(micro)
        gather_wait(r.xs, 0, 0, micro)
        norm_into(r.xs.at[0], r.normed.at[1], 1, micro)
        for at in hidden_blocks():
            value, slope = gelu_parts(mm_nt(r.normed[1, rows, :], up_rows(at)) + r.b_up[0:1, at])
            r.act[rows, at] = value.astype(BF16)
            r.dgelu[rows, at] = slope
    if g.direct:
        spread_wait("down", lambda at: r.rd.at[core, at], "down")
        pair_start("down", r.rd.at[core], r.rd.at[core], "down")
        pair_wait("down", r.rd.at[1 - core])
        unfold_down()
    for micro in micros:
        scatter_start(1, micro, mm_nt(r.act[token_slice(micro), :], r.w_down[...]))
    for micro in micros:
        finish_forward(1, r.prm[10:11, :], r.xs.at[0], micro)
    if g.direct:
        spread_wait("qkv1", lambda at: r.rq.at[1, core, at], "qkv1")
        pair_start("qkv1", r.rq.at[1, core], r.rq.at[1, core], "qkv1")
        spread_wait("out1", lambda at: r.ro.at[1, core, at], "out1")
        pair_start("out1", r.ro.at[1, core], r.ro.at[1, core], "out1")

    def crow_at(part, side):
        return r.crow.at[part, :, side]

    def crow_line(offset, receiving):
        at_chip = from_chip(offset) if receiving else peer_chip(offset)
        place = r.crow.at[g.my_part(sec), :, core, rows_at(at_chip if receiving else chip, quarter)]
        return line_copy("crow", place if receiving else r.dispc.at[at_chip], place, offset, receiving)

    for offset in range(1, g.chips):
        launch(crow_line(offset, False))
    r.crow[g.my_part(sec), :, core, rows_at(chip, quarter), :] = r.dispc[chip]

    if g.direct:
        pair_wait("qkv1", r.rq.at[1, 1 - core])
        unfold_qkv(1)
        pair_wait("out1", r.ro.at[1, 1 - core])
        unfold_out(1)
    for micro in micros:
        gather_wait(r.xs, 1, 1, micro)
        attention_forward(1, r.xs.at[1], 2, micro)
    for micro in micros:
        finish_forward(2, r.prm[9:10, :], r.xs.at[1], micro)
    r.square[0 : g.micro, :] = jnp.concatenate(
        [place_row[:, token_slice(micro)] for micro in micros], axis=0
    ).astype(F32)
    columns = r.square[...].T

    wide = r.wide

    def gates(micro):
        at = token_slice(micro)
        norm_into(r.xs.at[2], wide.at[:, pl.ds(0, width)], 3, micro)
        logits = mm(wide[at, :width], r.w_router[...])
        lane = lax.broadcasted_iota(jnp.int32, logits.shape, 1) - g.router_lane
        place_col = columns[:, micro : micro + 1].astype(jnp.int32)
        chosen = (place_col >= lane * span) & (place_col < lane * span + span)
        score = jnp.sum(jnp.where(chosen, logits, 0.0), axis=-1, keepdims=True)
        gate = 1.0 / (1.0 + jnp.exp(-score))
        gate_high = gate.astype(BF16).astype(F32)
        lane = lax.broadcasted_iota(jnp.int32, (g.seq, LANES), 1)
        pair = jnp.where(lane == 0, gate_high, jnp.where(lane == 1, gate - gate_high, 0.0))
        wide[at, width:] = pair.astype(BF16)

    groups = range(g.groups)

    def rows_at_part(part, group, side):
        return r.rows.at[part, group, side]

    def rows_line_start(group):
        name = "rows" + str(group)
        r.disp[group] = mm(r.table[group], wide[group_tokens(group), :]).astype(BF16)
        place = r.rows.at[g.my_part(sec), group, core, rows_at(chip, quarter)]
        line_start(name, lambda at: r.disp.at[group, rows_at(at, quarter)], place)
        r.rows[g.my_part(sec), group, core, rows_at(chip, quarter), :] = r.disp[group, rows_at(chip, quarter), :]

    def rows_line_wait(group):
        name = "rows" + str(group)
        mine = r.rows.at[g.my_part(sec), group, core]
        line_wait(name, lambda at, _: mine.at[rows_at(at, quarter)])
        rows_plane_start(name, mine, "rows0" + str(group))

    for micro in micros:
        gather_wait(r.xs, 2, 2, micro)
        if micro == 0:
            for offset in range(1, g.chips):
                crow_line(offset, True).wait_recv()
            rows_plane_start("crow", crow_at(g.my_part(sec), core), "crow0")
        gates(micro)
        if g.groups > 1:
            rows_line_start(micro)
    if g.groups == 1:
        rows_line_start(0)
    for group in groups:
        rows_line_wait(group)
    for copy in loads:
        copy.wait()

    own_router = FIRST_ROUTER + chip
    router_row = r.prm[pl.ds(own_router, 1), :]
    snd = dict(d=r.snd_d, y=r.snd_y)
    kept = dict(d=r.keep_d, y=r.keep_y)
    rcv = dict(d=r.rcv_d, y=r.rcv_y)

    def expert_block(wide_rows, cot_rows):
        row = wide_rows[:, :width]
        tail = wide_rows[:, width:].astype(F32)
        gate_row = tail[:, 0:1] + tail[:, 1:2]
        grad_row = (gate_row * cot_rows.astype(F32)).astype(BF16)
        value, slope = gelu_parts(mm(row, r.v_up[...]))
        value = value.astype(BF16)
        result = mm(value, r.v_down[...])
        total = jnp.sum(grad_row.astype(F32) * result, axis=-1, keepdims=True) * (1.0 - gate_row)
        inner = (slope * mm_nt(grad_row, r.v_down[...])).astype(BF16)
        back = mm_nt(inner, r.v_up[...]) + total * router_row
        r.small[pl.ds(own_router, 1), :] += jnp.sum(row.astype(F32) * total, axis=0, keepdims=True)
        return grad_row, value, inner, back, result * gate_row

    def expert_part(part, group):
        both = 2 * block_rows
        if both <= g.block:
            found = expert_block(
                r.rows[part, group].reshape(both, width + LANES), r.crow[part, group].reshape(both, width)
            )
            for target, value in zip((r.grow, r.acte, r.dpree), found[:3], strict=True):
                target[part, group] = value.reshape(2, block_rows, value.shape[-1])
            r.both[0] = found[3].reshape(2, block_rows, width)
            r.both[1] = found[4].reshape(2, block_rows, width)
        else:
            for side in range(2):

                @pl.loop(0, block_rows // g.block)
                def _(step, side=side):
                    at = rows_at(step, g.block)
                    found = expert_block(r.rows[part, group, side, at, :], r.crow[part, group, side, at, :])
                    for target, value in zip((r.grow, r.acte, r.dpree), found[:3], strict=True):
                        target[part, group, side, at, :] = value
                    r.both[0, side, at, :] = found[3]
                    r.both[1, side, at, :] = found[4]

        for which, value in (("d", r.both.at[0]), ("y", r.both.at[1])):
            kept[which][part, group] = value[core]
            snd[which][part, group] = value[1 - core].astype(BF16)

    def merge(which, offset, group):
        part = g.my_part(from_section(offset))
        pair_wait(which + str(offset) + str(group), rcv[which].at[part, group])
        return kept[which][part, group] + rcv[which][part, group].astype(F32)

    def merge_send(offset, group):
        to = g.sections - offset
        r.out_d[offset - 1, group] = merge("d", offset, group).astype(BF16)
        name = "d" + str(group)
        launch(plane_copy(name, r.out_d.at[offset - 1, group], r.plane_d.at[to - 1, group], to, False))

    def part_work(offset, group):
        part = g.my_part(from_section(offset))
        tag = str(offset) + str(group)
        if group == 0:
            pair_wait("crow" + str(offset), crow_at(part, 1 - core))
        pair_wait("rows" + tag, rows_at_part(part, group, 1 - core))
        expert_part(part, group)
        for which in ("d", "y"):
            pair_start(which + tag, snd[which].at[part, group], rcv[which].at[part, group])

    def expert_back_line(group):
        name = "d" + str(group)
        total = merge("d", 0, group)
        if g.parts > 1:
            for offset in range(1, g.sections):
                place = r.plane_d.at[offset - 1, group]
                plane_copy(name, place, place, offset, True).wait_recv()
                total = total + place[...].astype(F32)
        r.ret_d[group] = total.astype(BF16)
        place = r.back_d.at[group, rows_at(chip, quarter)]
        line_start(name, lambda at: r.ret_d.at[group, rows_at(at, quarter)], place)
        r.back_d[group, rows_at(chip, quarter), :] = r.ret_d[group, rows_at(chip, quarter), :]

    def expert_combine(group):
        line_wait("d" + str(group), lambda at, _: r.back_d.at[group, rows_at(at, quarter)])
        value = mm_tn(r.table[group], r.back_d[group])
        if g.groups > 1:
            scatter_start(3, group, value)
        else:
            for micro in micros:
                scatter_start(3, micro, value[token_slice(micro)])

    def results_combine():
        line_wait("y", lambda at, _: r.back_y.at[at])
        places = [(e, p, q) for e in range(g.chips) for p in range(g.parts) for q in groups]
        match = jnp.concatenate([slot_match(*place) for place in places], axis=0)
        value = mm_tn(match, r.back_y[...].reshape(g.chips * span, width))
        for micro in micros:
            scatter_start(7, micro, value[token_slice(micro)])

    offsets = range(1, g.sections) if g.parts > 1 else []
    for group in groups:
        part_work(0, group)
    for offset in offsets:
        part = from_section(offset)
        rows_plane_wait("crow", crow_at(part, core), offset, "crow" + str(offset))
    for group in groups:
        tag = str(group)
        for offset in offsets:
            place = rows_at_part(from_section(offset), group, core)
            rows_plane_wait("rows" + tag, place, offset, "rows" + str(offset) + tag)
        for offset in offsets:
            part_work(offset, group)
            if offset > 1:
                merge_send(offset - 1, group)
        if g.parts > 1:
            merge_send(g.sections - 1, group)
    for group in groups:
        expert_back_line(group)
    for offset in range(g.parts):
        for group in groups:
            r.ret_y[g.my_part(from_section(offset)), group] = merge("y", offset, group).astype(BF16)

    def expert_weights(left, right):
        rows = g.parts * g.groups * 2 * block_rows
        return mm_tn(left.reshape(rows, left.shape[-1]), right.reshape(rows, right.shape[-1]))

    r.v_gup[...] = expert_weights(r.rows[:, :, :, :, :width], r.dpree[...])
    r.v_gdown[...] = expert_weights(r.acte[...], r.grow[...])
    for copy in stores:
        copy.start()

    def add_small(index, micro, value):
        if micro == 0:
            r.small[index : index + 1, :] = value
        else:
            r.small[index : index + 1, :] += value

    def finish_backward(section, slot, stream, above, micro):
        grad = scatter_sum(slot, micro)
        unit, inverse = normalize(stream[own(micro), :].astype(F32))
        add_small(section, micro, jnp.sum(grad * unit, axis=0, keepdims=True))
        add_small(4 + section, micro, jnp.sum(grad, axis=0, keepdims=True))
        grad = grad * r.prm[section : section + 1, :]
        shared = jnp.mean(grad, axis=-1, keepdims=True)
        along = jnp.mean(grad * unit, axis=-1, keepdims=True)
        grad = inverse * (grad - shared - unit * along) + above[own(micro), :].astype(F32)
        r.gs[section, own(micro), :] = grad.astype(BF16)
        gather_start(r.gs, section, 4 + section, micro)

    for group in groups:
        expert_combine(group)
    line_start("y", lambda at: r.ret_y.at[:, :, rows_at(at, quarter)], r.back_y.at[chip])
    r.back_y[chip] = r.ret_y[:, :, rows_at(chip, quarter), :]
    for micro in micros:
        finish_backward(3, 3, r.xs.at[2], r.cot, micro)

    def bias_row(index, section):
        for micro in micros:
            value = r.gs[section, own(micro), :].astype(F32)
            add_small(index, micro, jnp.sum(value, axis=0, keepdims=True))

    def attention_backward(layer, section, slot, micro):
        at = token_slice(micro)
        dctx = mm_nt(r.w_out[layer], r.gs[section + 1, at, :]).astype(BF16)
        for head in range(g.heads):
            weight = r.probs[layer, micro, head]
            low = weight.astype(BF16)
            dhead = dctx[head_slice(head)]
            query = r.qkv[layer, block_of(0), head_slice(head), at]
            key = r.qkv[layer, block_of(1), head_slice(head), at]
            value = r.qkv[layer, block_of(2), head_slice(head), at]
            dprobs = mm_tn(value, dhead)
            delta = jnp.sum(weight * dprobs, axis=0, keepdims=True)
            dscores = (weight * (dprobs - delta)).astype(BF16)
            r.dqkv[block_of(0), head_slice(head), at] = (mm(key, dscores) * scale).astype(BF16)
            r.dqkv[block_of(1), head_slice(head), at] = (mm_nt(query, dscores) * scale).astype(BF16)
            r.dqkv[block_of(2), head_slice(head), at] = mm_nt(dhead, low).astype(BF16)
        flat_grad = r.dqkv[:, :, at].reshape(3 * head_cols, g.seq)
        scatter_start(slot, micro, mm_tn(flat_grad, r.w_qkv[layer]))

    def attention_weights(layer, section):
        grad_qkv = mm(r.dqkv[...].reshape(3 * head_cols, g.tokens), r.normed[2 * layer])
        if not g.direct:
            r.o_qkv[layer] = grad_qkv
            r.o_out[layer] = mm(r.ctx[layer], r.gs[section + 1])
            return
        r.tmp[0 : 3 * head_cols, :] = grad_qkv
        settle("qkv" + str(layer))
        for at_core, at_chip, index, first in chunk_places():
            r.rq[layer, at_core, at_chip, index] = pack_wide(r.tmp[first : first + cols, :])
        name = "gqkv" + str(layer)
        pair_start(name, r.rq.at[layer, 1 - core], r.hq.at[layer])
        r.tmp[:, 0:head_cols] = dot_as(r.gs[section + 1], r.ctx[layer], 0, 1)
        if layer:
            r.tmp[:, head_cols : head_cols + GROUP] = jnp.zeros((width, GROUP), F32)
            out_weights(1)

    def out_weights(layer):
        settle("out" + str(layer))
        for at_core, at_chip, at_sec, first in shard_places():
            block = r.tmp[first : first + cols, 0 : head_cols + GROUP]
            r.ro[layer, at_core, at_chip, at_sec] = pack_out(block)
        pair_start("gout" + str(layer), r.ro.at[layer, 1 - core], r.ho.at[layer])

    for micro in micros:
        gather_wait(r.gs, 3, 7, micro)
        attention_backward(1, 2, 4, micro)
    bias_row(9, 3)
    attention_weights(1, 2)
    finish_backward(2, 4, r.xs.at[1], r.gs.at[3], 0)
    if g.direct:
        grad_line("gqkv1", qkv_at(1), r.hq.at[1], r.aq.at[1], r.lq.at[1])
        grad_line("gout1", out_at(1), r.ho.at[1], r.ao.at[1], r.lo.at[1])
    for micro in micros[1:]:
        finish_backward(2, 4, r.xs.at[1], r.gs.at[3], micro)

    for micro in micros:
        rows = token_slice(micro)
        gather_wait(r.gs, 2, 6, micro)
        grad_two = r.gs[2, rows, :]
        for at in hidden_blocks():
            r.dpre[rows, at] = (r.dgelu[rows, at] * mm(grad_two, r.w_down[:, at])).astype(BF16)
        scatter_start(5, micro, mm(r.dpre[rows, :], up_rows(slice(None))))
    bias_row(10, 2)
    sum_up = jnp.sum(r.dpre[...].astype(F32), axis=0, keepdims=True)
    if g.direct:
        grad_relay("gqkv1", qkv_at(1), r.aq.at[1], r.lq.at[1])
        grad_relay("gout1", out_at(1), r.ao.at[1], r.lo.at[1])
        r.tmp[...] = mm_tn(r.gs[2], r.act[...])
        settle("down")
        for at_core, at_chip, at_sec, first in shard_places():
            r.rd[at_core, at_chip, at_sec] = pack_wide(r.tmp[first : first + cols, :])
        pair_start("gdown", r.rd.at[1 - core], r.hd)
        settle("up")
        settle("bias")
        r.ru[...] = mm_tn(r.dpre[...], r.normed[1]).astype(BF16).reshape(r.ru.shape)
        pair_start("gup", r.ru.at[:, 1 - core], r.hu)
        for at_dev in range(g.devices):
            row = sum_up[:, at_dev * shard_rows : (at_dev + 1) * shard_rows]
            row = jnp.broadcast_to(row, (r.pb.shape[0], shard_rows)).astype(BF16)
            r.rb[at_dev // 2, at_dev % 2, :, 0:shard_rows] = row
        pair_start("gbias", r.rb.at[:, 1 - core], r.hb)
        grad_line("gdown", down_at, r.hd, r.ad, r.ld)
    else:
        r.o_down[...] = mm_tn(r.gs[2], r.act[...])
        r.o_up[...] = mm_tn(r.dpre[...], r.normed[1])
        r.o_bup[...] = sum_up
    for micro in micros:
        finish_backward(1, 5, r.xs.at[0], r.gs.at[2], micro)
    if g.direct:
        grad_line("gup", up_at, r.hu, r.au, r.lu)
        grad_line("gbias", bias_at, r.hb, r.ab, r.lb)
        grad_relay("gdown", down_at, r.ad, r.ld)

    for micro in micros:
        gather_wait(r.gs, 1, 5, micro)
        attention_backward(0, 0, 6, micro)
    bias_row(8, 1)
    attention_weights(0, 0)
    finish_backward(0, 6, r.x0, r.gs.at[1], 0)
    if g.direct:
        grad_line("gqkv0", qkv_at(0), r.hq.at[0], r.aq.at[0], r.lq.at[0])
    for micro in micros[1:]:
        finish_backward(0, 6, r.x0, r.gs.at[1], micro)
    if g.direct:
        kinds = r.small[...]
        padded = jnp.concatenate([kinds, jnp.zeros((LANES - kinds.shape[0], width), F32)], axis=0)
        r.tmp[:, head_cols : head_cols + GROUP] = padded.T[:, 0:GROUP]
        out_weights(0)
        grad_line("gout0", out_at(0), r.ho.at[0], r.ao.at[0], r.lo.at[0])
        grad_relay("gup", up_at, r.au, r.lu)
        grad_relay("gbias", bias_at, r.ab, r.lb)
    results_combine()
    if g.direct:
        grad_qkv_plane(1)
        grad_plane("gout1", out_at(1), r.ao.at[1], r.mo.at[1], r.fo.at[1])
        grad_plane("gdown", down_at, r.ad, r.md, r.fd)
        grad_relay("gqkv0", qkv_at(0), r.aq.at[0], r.lq.at[0])
        grad_relay("gout0", out_at(0), r.ao.at[0], r.lo.at[0])
    for micro in micros:
        r.xs[3, own(micro), :] = (scatter_sum(7, micro) + r.xs[2, own(micro), :].astype(F32)).astype(BF16)
        gather_start(r.xs, 3, 3, micro)
    if g.direct:
        r.o_up[...] = grad_line_sum("gup", up_at, r.au)
        r.o_bup[...] = grad_line_sum("gbias", bias_at, r.ab)[0:1, 0:shard_rows]
        grad_qkv_finish(1)
        grad_plane_wait("gdown", r.fd)
        for at_sec in range(g.sections):
            piece = r.fd[at_sec].astype(F32)
            unpack_wide(r.o_down.at[:, pl.ds(at_sec * hidden, hidden)], 0, piece)
        grad_qkv_plane(0)
        grad_plane("gout0", out_at(0), r.ao.at[0], r.mo.at[0], r.fo.at[0])
        grad_plane_wait("gout1", r.fo.at[1])
        for at_sec in range(g.sections):
            unpack_out(r.o_out.at[1], 0, r.fo[1, at_sec].astype(F32), at_sec * head_cols)
        grad_qkv_finish(0)
        grad_plane_wait("gout0", r.fo.at[0])
        everyone = jnp.zeros((top, g.out_lanes), F32)
        for at_sec in range(g.sections):
            piece = r.fo[0, at_sec].astype(F32)
            unpack_out(r.o_out.at[0], 0, piece, at_sec * head_cols)
            everyone = everyone + piece
        r.square[...] = jnp.zeros_like(r.square)
        unpack_small(r.square, 0, everyone, 0)
        r.square[...] = r.square[...].T
        r.o_router[...] = r.square[FIRST_ROUTER : FIRST_ROUTER + g.experts, 0:cols]
        r.o_gain[...] = r.square[0:4, 0:cols]
        r.o_bias[...] = r.square[4:8, 0:cols]
        r.o_bout[...] = r.square[8:10, 0:cols]
        r.o_bdown[...] = r.square[10:11, 0:cols]
    else:
        r.o_small[...] = r.small[...]
    for micro in micros:
        gather_wait(r.xs, 3, 3, micro)
        gather_wait(r.gs, 0, 4, micro)
    r.sec_out[...] = r.xs[sec]
    r.sec_grad[...] = r.gs[sec]
    for copy in stores:
        copy.wait()
    for copy, when in started:
        do_when(when, copy.wait_send)


def run_layers(g, operands):
    tokens, width, hidden, sections, chips = g.tokens, g.width, g.hidden, g.sections, g.chips
    part_rows = chips * g.quarter
    inner = operands["e_down"].shape[0]
    three = 3 * g.head_cols
    shape = jax.ShapeDtypeStruct
    vmem = pltpu.VMEM
    dma = pltpu.SemaphoreType.DMA
    top = g.cols - TAIL
    wide = width + width // 2
    up_rows = hidden // g.devices
    outs = dict(
        sec_out=shape((tokens, width), BF16),
        sec_grad=shape((tokens, width), BF16),
        g_eup=shape((width, inner), F32),
        g_edown=shape((inner, width), F32),
    )
    if g.direct:
        outs |= dict(
            o_qkv=shape((2, 3 * g.cols, width), F32),
            o_out=shape((2, g.cols, width), F32),
            o_up=shape((up_rows, width), F32),
            o_down=shape((g.cols, sections * hidden), F32),
            o_gain=shape((4, g.cols), F32),
            o_bias=shape((4, g.cols), F32),
            o_bout=shape((2, g.cols), F32),
            o_bdown=shape((1, g.cols), F32),
            o_router=shape((g.experts, g.cols), F32),
            o_bup=shape((1, up_rows), F32),
        )
    else:
        outs |= dict(
            o_qkv=shape((2, three, width), F32),
            o_out=shape((2, g.head_cols, width), F32),
            o_up=shape((hidden, width), F32),
            o_down=shape((width, hidden), F32),
            o_bup=shape((1, hidden), F32),
            o_small=shape((g.small, width), F32),
        )
    scratch = dict(
        xs=vmem((4, tokens, width), BF16),
        gs=vmem((4, tokens, width), BF16),
        normed=vmem((3, tokens, width), BF16),
        wide=vmem((tokens, width + LANES), BF16),
        qkv=vmem((2, 3, g.head_cols, tokens), BF16),
        probs=vmem((2, g.micro, g.heads, g.seq, g.seq), F32),
        ctx=vmem((2, g.head_cols, tokens), BF16),
        act=vmem((tokens, hidden), BF16),
        dgelu=vmem((tokens, hidden), F32),
        dpre=vmem((tokens, hidden), BF16),
        dqkv=vmem((3, g.head_cols, tokens), BF16),
        part=vmem((8, tokens, width), BF16),
        got=vmem((8, g.micro, sections - 1, g.piece, width), BF16),
        mine=vmem((tokens, width), F32),
        square=vmem((LANES, LANES), F32),
        table=vmem((g.groups, part_rows, tokens // g.groups), BF16),
        disp=vmem((g.groups, part_rows, width + LANES), BF16),
        dispc=vmem((chips, g.groups, g.quarter, width), BF16),
        rows=vmem((g.parts, g.groups, 2, part_rows, width + LANES), BF16),
        crow=vmem((g.parts, g.groups, 2, part_rows, width), BF16),
        grow=vmem((g.parts, g.groups, 2, part_rows, width), BF16),
        acte=vmem((g.parts, g.groups, 2, part_rows, inner), BF16),
        dpree=vmem((g.parts, g.groups, 2, part_rows, inner), BF16),
        both=vmem((2, 2, part_rows, width), F32),
        small=vmem((g.small, width), F32),
        v_up=vmem((width, inner), BF16),
        v_down=vmem((inner, width), BF16),
        v_gup=vmem((width, inner), F32),
        v_gdown=vmem((inner, width), F32),
        local_s=dma((4,)),
    )
    for which in ("d", "y"):
        scratch["keep_" + which] = vmem((g.parts, g.groups, part_rows, width), F32)
        for name in ("snd_", "rcv_"):
            scratch[name + which] = vmem((g.parts, g.groups, part_rows, width), BF16)
    scratch |= dict(
        out_d=vmem((sections - 1, g.groups, part_rows, width), BF16),
        plane_d=vmem((sections - 1, g.groups, part_rows, width), BF16),
        ret_d=vmem((g.groups, part_rows, width), BF16),
        back_d=vmem((g.groups, part_rows, width), BF16),
        ret_y=vmem((g.parts, g.groups, part_rows, width), BF16),
        back_y=vmem((chips, g.parts, g.groups, g.quarter, width), BF16),
    )
    for name in ("scat_s", "scat_r", "gath_s", "gath_r"):
        scratch[name] = dma((8, g.micro, sections - 1))
    for name, count, each in (("pair", len(g.pairs), 0), ("line", len(g.lines), chips), ("plane", len(g.planes), sections - 1)):
        sizes = (count, each) if each else (count,)
        scratch |= {name + "_s": dma(sizes), name + "_r": dma(sizes)}
    if g.direct:
        piece = (top, wide)
        out_piece = (top, g.out_lanes)
        up_piece = (up_rows, width)
        bias_piece = (2 * TAIL, LANES)
        scratch |= dict(
            pq=vmem((2, 3, *piece), BF16),
            po=vmem((2, sections, *out_piece), BF16),
            pb=vmem(bias_piece, BF16),
            rb=vmem((chips, 2, *bias_piece), BF16),
            hb=vmem((chips, *bias_piece), BF16),
            ab=vmem((chips - 1, *bias_piece), BF16),
            lb=vmem(bias_piece, BF16),
            lq=vmem((2, 3, *piece), BF16),
            lo=vmem((2, sections, *out_piece), BF16),
            lu=vmem(up_piece, BF16),
            ld=vmem((sections, *piece), BF16),
            pd=vmem((sections, *piece), BF16),
            rq=vmem((2, 2, chips, 3, *piece), BF16),
            ro=vmem((2, 2, chips, sections, *out_piece), BF16),
            ru=vmem((chips, 2, *up_piece), BF16),
            rd=vmem((2, chips, sections, *piece), BF16),
            w_qkv=vmem((2, three, width), BF16),
            w_out=vmem((2, g.head_cols, width), BF16),
            w_down=vmem((width, hidden), BF16),
            w_router=vmem((width, LANES), BF16),
            b_up=vmem((8, hidden), F32),
            prm=vmem((GROUP, width), F32),
            tmp=vmem((width, width), F32),
            hq=vmem((2, chips, 3, *piece), BF16),
            ho=vmem((2, chips, sections, *out_piece), BF16),
            hu=vmem((chips, *up_piece), BF16),
            hd=vmem((chips, sections, *piece), BF16),
            aq=vmem((2, chips - 1, 3, *piece), BF16),
            ao=vmem((2, chips - 1, sections, *out_piece), BF16),
            au=vmem((chips - 1, *up_piece), BF16),
            ad=vmem((chips - 1, sections, *piece), BF16),
            mq=vmem((2, 3, *piece), BF16),
            mo=vmem((2, sections, *out_piece), BF16),
            md=vmem((sections, *piece), BF16),
            fq=vmem((2, 3, *piece), BF16),
            fo=vmem((2, sections, *out_piece), BF16),
            fd=vmem((sections, *piece), BF16),
            wq_s=dma((2, 3, chips)),
            wq_r=dma((2, 3, chips)),
            wo_s=dma((sections, chips)),
            wo_r=dma((sections, chips)),
            gq_s=dma((2, 3)),
            gq_r=dma((2, 3)),
        )
    whole = pl.BlockSpec(memory_space=pltpu.VMEM)
    placed = pl.BlockSpec(memory_space=pl.ANY)
    apart = ("e_up", "e_down", "g_eup", "g_edown")
    names = (*operands, *outs, *scratch)
    results = pl.pallas_call(
        functools.partial(layers_kernel, g, names),
        out_shape=tuple(outs.values()),
        in_specs=[placed if name in apart else whole for name in operands],
        out_specs=[placed if name in apart else whole for name in outs],
        scratch_shapes=list(scratch.values()),
        compiler_params=pltpu.CompilerParams(
            collective_id=0, has_side_effects=True, vmem_limit_bytes=62 * 1024 * 1024
        ),
    )(*operands.values())
    return types.SimpleNamespace(**dict(zip(outs, results, strict=True)))


def finish_kernel(count, *refs):
    ins, outs, held = refs[:count], refs[count : 2 * count], refs[2 * count : 3 * count]
    wide, sems = refs[3 * count : 3 * count + 2], refs[-1]
    loads = [pltpu.make_async_copy(ins[i], held[i], sems.at[0, i]) for i in range(count)]
    stores = [pltpu.make_async_copy((wide[i] if i < 2 else held[i]), outs[i], sems.at[1, i]) for i in range(count)]
    for copy in loads:
        copy.start()
    for i in range(count):
        loads[i].wait()
        if i < 2:
            wide[i][...] = held[i][...].astype(F32)
        stores[i].start()
    for copy in stores:
        copy.wait()


def finish(arrays):
    count = len(arrays)
    placed = [pl.BlockSpec(memory_space=pl.ANY)] * count
    held = [pltpu.VMEM(array.shape, array.dtype) for array in arrays]
    wide = [pltpu.VMEM(array.shape, F32) for array in arrays[:2]]
    return pl.pallas_call(
        functools.partial(finish_kernel, count),
        out_shape=tuple(jax.ShapeDtypeStruct(array.shape, F32) for array in arrays),
        in_specs=placed,
        out_specs=placed,
        scratch_shapes=[*held, *wide, pltpu.SemaphoreType.DMA((2, count))],
        compiler_params=pltpu.CompilerParams(vmem_limit_bytes=62 * 1024 * 1024),
    )(*arrays)


BOTH = ("section", "dp")


def body(
    tokens, cotangent, lengths, routes, slots, norm_gain, norm_bias, attn_qkv, attn_out, attn_out_bias,
    ffn_up, ffn_up_bias, ffn_down, ffn_down_bias, router, expert_up, expert_down,
):
    sections, devices = lax.axis_size("section"), lax.axis_size("dp")
    sec = lax.axis_index("section")
    micro, _, seq, width = tokens.shape
    experts = router.shape[1]
    chips = devices // 2
    head_cols = width // sections
    hidden = ffn_up.shape[1] * devices
    cap = 2 * seq // experts
    span = micro * cap
    cols = ffn_down.shape[1]
    kinds = FIRST_ROUTER + experts
    direct = cols == 3 * TAIL and kinds <= GROUP and sections == 4 and ffn_up.shape[1] % 16 == 0
    parts = sections if span % (16 * sections) == 0 else 1
    groups = micro if cap % (16 * parts) == 0 else 1
    group_names = [str(group) for group in range(groups)]
    part_names = [str(part) for part in range(parts)]
    both_names = [a + b for a in part_names for b in group_names]
    g = types.SimpleNamespace(
        sections=sections, devices=devices, chips=chips, micro=micro, seq=seq, width=width, hidden=hidden, cap=cap,
        span=span, tokens=micro * seq, piece=seq // sections, heads=head_cols // HEAD_DIM,
        head_cols=head_cols, cols=cols, block=256, small=-(-kinds // 8) * 8, direct=direct, experts=experts,
        out_lanes=head_cols + 2 * GROUP + LANES, parts=parts, groups=groups, quarter=span // (parts * groups),
        relay=direct and chips == 4,
        my_part=(lambda section: section) if parts > 1 else (lambda section: 0),
        router_lane=FIRST_ROUTER + (LANES - 2 * GROUP if direct else 0),
        pairs=["crow" + a for a in part_names]
        + [name + a for name in ("rows", "d", "y") for a in both_names]
        + ([
            "out0", "qkv0", "up", "bias", "down", "qkv1", "out1",
            "gqkv0", "gqkv1", "gdown", "gup", "gbias", "gout0", "gout1",
        ] if direct else []),
        lines=["crow", "y"]
        + [name + b for name in ("rows", "d") for b in group_names]
        + ([
            "out0", "qkv0", "up", "bias", "down", "qkv1", "out1",
            "gqkv0", "gqkv1", "gdown", "gup", "gbias", "gout0", "gout1",
        ] if direct else []),
        planes=["crow"]
        + [name + b for name in ("rows", "d") for b in group_names] + (["down", "out1", "gdown", "gout0", "gout1"] if direct else []),
    )

    operands = dict(
        x0=tokens.reshape(g.tokens, width),
        cot=cotangent.reshape(g.tokens, width),
        lens=lengths.T,
        routes=routes[:, 0],
        slots=slots[:, 0],
        e_up=expert_up[0],
        e_down=expert_down[0],
    )
    if direct:
        operands |= dict(
            norm_gain=norm_gain,
            norm_bias=norm_bias,
            out_bias=attn_out_bias,
            down_bias=ffn_down_bias[None],
            up_bias=ffn_up_bias[None],
            router=router.T,
            wq=attn_qkv.transpose(0, 2, 1),
            wo=attn_out.transpose(0, 2, 1),
            wu=ffn_up.T,
            wd=ffn_down.T,
        )
    else:

        def every(array, axis):
            return lax.all_gather(array, BOTH, axis=axis, tiled=True)

        def part_of(array, axis, size):
            return lax.dynamic_slice_in_dim(array, sec * size, size, axis)

        rows = [norm_gain, norm_bias, attn_out_bias, ffn_down_bias[None], router.T]
        params = every(jnp.concatenate(rows, axis=0), 1)
        params = jnp.pad(params, ((0, LANES - kinds), (0, 0)))
        b_up = lax.all_gather(ffn_up_bias, "dp", axis=0, tiled=True).astype(F32)
        full = part_of(every(attn_qkv, 2).reshape(2, width, 3, width), 3, head_cols)
        operands |= dict(
            prm=params.astype(F32),
            w_router=params.T,
            b_up=b_up[None],
            w_qkv=full.transpose(0, 2, 3, 1).reshape(2, 3 * head_cols, width),
            w_out=part_of(every(attn_out, 2), 1, head_cols),
            w_up=lax.all_gather(ffn_up, "dp", axis=1, tiled=True).T,
            w_down=part_of(every(ffn_down, 1), 0, hidden).T,
        )
    res = run_layers(g, operands)

    if direct:
        names = list(vars(res))
        done = finish([getattr(res, name) for name in names])
        res = types.SimpleNamespace(**dict(zip(names, done, strict=True)))
        grads = (
            res.o_gain, res.o_bias, res.o_qkv.transpose(0, 2, 1), res.o_out.transpose(0, 2, 1), res.o_bout,
            res.o_up.T, res.o_bup[0], res.o_down.T, res.o_bdown[0], res.o_router.T,
        )
    else:

        def embed(array, shape, axis, size):
            return lax.dynamic_update_slice_in_dim(jnp.zeros(shape, F32), array, sec * size, axis)

        def share(array, axis, over=BOTH):
            return lax.psum_scatter(array, over, scatter_dimension=axis, tiled=True)

        small = share(res.o_small[:kinds], 1)
        g_qkv = res.o_qkv.reshape(2, 3, head_cols, width).transpose(0, 3, 1, 2)
        g_qkv = embed(g_qkv, (2, width, 3, width), 3, head_cols).reshape(2, width, 3 * width)
        g_out = embed(res.o_out, (2, width, width), 1, head_cols)
        g_down = embed(res.o_down.T, (hidden * sections, width), 0, hidden)
        grads = (
            small[0:4], small[4:8], share(g_qkv, 2), share(g_out, 2), small[8:10], share(res.o_up.T, 1, "dp"),
            share(res.o_bup[0], 0, "dp"), share(g_down, 1), small[10], small[FIRST_ROUTER:].T,
        )
    out_shape = (1, micro, 1, seq, width)
    return (
        res.sec_out.reshape(out_shape).astype(F32),
        res.sec_grad.reshape(out_shape).astype(F32),
        *grads,
        res.g_eup[None],
        res.g_edown[None],
    )


def solution(mesh):
    batch = P(None, "dp", None, None)
    table = P(None, "dp", None)
    in_specs = (
        batch, batch, P(None, "dp"), table, table,
        P(None, BOTH), P(None, BOTH), P(None, None, BOTH), P(None, None, BOTH), P(None, BOTH),
        P(None, BOTH), P(BOTH), P(None, BOTH), P(BOTH), P(BOTH, None),
        P("dp", None, "section"), P("dp", "section", None),
    )
    streams = P("section", None, "dp", None, None)
    out_specs = (
        streams, streams,
        P(None, BOTH), P(None, BOTH), P(None, None, BOTH), P(None, None, BOTH), P(None, BOTH),
        P(None, BOTH), P(BOTH), P(None, BOTH), P(BOTH), P(BOTH, None),
        P("dp", None, "section"), P("dp", "section", None),
    )
    return jax.shard_map(body, mesh=mesh, in_specs=in_specs, out_specs=out_specs, check_vma=False)
```

```python
import functools
import types

import jax
import jax.numpy as jnp
from jax import lax
from jax.experimental import pallas as pl
from jax.experimental.pallas import tpu as pltpu
from jax.sharding import PartitionSpec as P

HEADS = 12
HEAD_DIM = 64
EPS = 1e-05
MASKED = -1000000000.0
MESH = pl.DeviceIdType.MESH
F32 = jnp.float32
BF16 = jnp.bfloat16
LANES = 128


def dot_as(left, right, left_dim, right_dim):
    return lax.dot_general(
        left, right, (((left_dim,), (right_dim,)), ((), ())), preferred_element_type=F32
    )


def mm(left, right):
    return dot_as(left, right, 1, 0)


def mm_nt(left, right):
    return dot_as(left, right, 1, 1)


def mm_tn(left, right):
    return dot_as(left, right, 0, 0)


def normalize(values):
    center = values - jnp.mean(values, axis=-1, keepdims=True)
    spread = jnp.mean(center * center, axis=-1, keepdims=True)
    inverse = lax.rsqrt(spread + EPS)
    return center * inverse, inverse


def gelu_parts(pre):
    half = 0.5 + 0.5 * lax.erf(pre * 0.7071067811865476)
    density = jnp.exp(-0.5 * pre * pre) * 0.3989422804014327
    return pre * half, half + pre * density


TAIL = 8
GROUP = 32
FIRST_ROUTER = 11


def layers_kernel(g, names, *refs):
    r = types.SimpleNamespace(**dict(zip(names, refs, strict=True)))
    width, span, hidden, cols, head_cols = g.width, g.span, g.hidden, g.cols, g.head_cols
    sec = lax.axis_index("section")
    dev = lax.axis_index("dp")
    core = lax.rem(dev, 2)
    chip = lax.div(dev, 2)
    sib = dev + 1 - 2 * core
    quarter = g.quarter
    shard_rows = hidden // g.devices
    block_rows = g.chips * quarter

    def peer_section(offset):
        return lax.rem(sec + offset, g.sections)

    def from_section(offset):
        return lax.rem(sec + g.sections - offset, g.sections)

    def peer_chip(offset):
        return lax.rem(chip + offset, g.chips)

    def from_chip(offset):
        return lax.rem(chip + g.chips - offset, g.chips)

    def rows_at(index, size):
        return pl.ds(pl.multiple_of(index * size, size), size)

    def remote(source, target, send, arrive, where):
        return pltpu.make_async_remote_copy(
            src_ref=source, dst_ref=target, send_sem=send, recv_sem=arrive, device_id=where, device_id_type=MESH
        )

    def at_chip_core(index):
        return {"dp": 2 * index + core}

    started = []
    kept_back = {}

    def do_when(condition, action):
        if condition is None:
            action()
        else:
            pl.when(condition)(action)

    def launch(copy, buffer=None, when=None):
        do_when(when, copy.start)
        if buffer:
            kept_back.setdefault(buffer, []).append((copy, when))
        else:
            started.append((copy, when))

    def settle(buffer):
        for copy, when in kept_back.pop(buffer, []):
            do_when(when, copy.wait_send)

    barrier = pltpu.get_barrier_semaphore()
    partners = [(a, b) for a in range(g.sections) for b in range(g.chips) if a + b and (g.direct or a * b == 0)]
    for section_offset, chip_offset in partners:
        where = {"section": peer_section(section_offset), "dp": 2 * peer_chip(chip_offset) + core}
        pl.semaphore_signal(barrier, inc=1, device_id=where, device_id_type=MESH)
    pl.semaphore_signal(barrier, inc=1, device_id={"dp": sib}, device_id_type=MESH)

    def local(index, source, target):
        return pltpu.make_async_copy(source, target, r.local_s.at[index])

    held = vars(r)
    loads = {name: local(i, held["h_" + name], held[name]) for i, name in enumerate(g.loads)}
    stores = [local(len(loads), r.v_gup, r.g_eup), local(len(loads) + 1, r.v_gdown, r.g_edown)]
    for copy in loads.values():
        copy.start()

    def token_slice(micro):
        return slice(micro * g.seq, (micro + 1) * g.seq)

    def piece_at(micro, section):
        return pl.ds(pl.multiple_of(micro * g.seq + section * g.piece, g.piece), g.piece)

    def own(micro):
        return piece_at(micro, sec)

    def scatter_copy(slot, micro, offset):
        return remote(
            r.part.at[slot, piece_at(micro, peer_section(offset))], r.got.at[slot, micro, offset - 1],
            r.scat_s.at[slot, micro, offset - 1], r.scat_r.at[slot, micro, offset - 1],
            {"section": peer_section(offset)},
        )

    def scatter_start(slot, micro, value):
        r.part[slot, token_slice(micro), :] = value.astype(BF16)
        if slot != 7:
            r.mine[token_slice(micro), :] = value
        for offset in range(1, g.sections):
            launch(scatter_copy(slot, micro, offset))

    def scatter_sum(slot, micro):
        at = own(micro)
        total = r.part[slot, at, :].astype(F32) if slot == 7 else r.mine[at, :]
        for offset in range(1, g.sections):
            scatter_copy(slot, micro, offset).wait_recv()
            total = total + r.got[slot, micro, offset - 1].astype(F32)
        return total

    def share_copy(place, send, arrive, offset, receiving):
        where = from_section(offset) if receiving else peer_section(offset)
        return remote(place, place, send.at[offset - 1], arrive.at[offset - 1], {"section": where})

    def gather_start(buffer, slot, sem, micro):
        place = buffer.at[slot, own(micro)]
        for offset in range(1, g.sections):
            launch(share_copy(place, r.gath_s.at[sem, micro], r.gath_r.at[sem, micro], offset, False))

    def gather_wait(buffer, slot, sem, micro):
        for offset in range(1, g.sections):
            place = buffer.at[slot, piece_at(micro, from_section(offset))]
            share_copy(place, r.gath_s.at[sem, micro], r.gath_r.at[sem, micro], offset, True).wait_recv()

    def pair_copy(name, source, target):
        index = g.pairs.index(name)
        return remote(source, target, r.pair_s.at[index], r.pair_r.at[index], {"dp": sib})

    def pair_start(name, source, target, buffer=None):
        launch(pair_copy(name, source, target), buffer)

    def pair_wait(name, target):
        pair_copy(name, target, target).wait_recv()

    def line_copy(name, source, target, offset, receiving):
        index = g.lines.index(name)
        where = from_chip(offset) if receiving else peer_chip(offset)
        return remote(
            source, target, r.line_s.at[index, offset - 1], r.line_r.at[index, offset - 1], at_chip_core(where)
        )

    last_chip = g.chips - 1
    is_end = lax.rem(chip, max(last_chip, 1)) == 0
    is_mid = lax.rem(chip, max(last_chip, 1)) != 0
    line_order = (2, 1, 3) if g.relay else range(1, g.chips)
    outward = jnp.clip(chip - 1, 0, 1)

    def near_to(offset):
        return {1: chip != last_chip, last_chip: chip != 0}.get(offset) if g.relay else None

    def near_from(offset):
        return {1: chip != 0, last_chip: chip != last_chip}.get(offset) if g.relay else None

    def spread_first(name, source, target, buffer=None):
        if g.relay:
            for offset, when in ((2, is_end), (1, chip == 2), (3, chip == 1)):
                launch(line_copy(name, source, target, offset, False), buffer, when)

    def spread_more(name, source, target, buffer=None):
        if g.relay:
            for offset, when in ((2, is_mid), (1, chip < 2), (3, chip > 1)):
                launch(line_copy(name, source, target, offset, False), buffer, when)
        else:
            for offset in line_order:
                launch(line_copy(name, source, target, offset, False), buffer)

    def spread_relay(name, place, buffer):
        index = g.lines.index(name)
        copy = remote(
            place, place, r.line_s.at[index, last_chip], r.line_r.at[index, outward * 2],
            at_chip_core(outward * last_chip),
        )
        launch(copy, buffer, is_mid)

    def spread_pass(name, place_at, buffer):
        if g.relay:
            place = place_at(from_chip(2))
            line_copy(name, place, place, 2, True).wait_recv()
            spread_relay(name, place, buffer)

    def spread_wait(name, place_at):
        for offset in (1, 3) if g.relay else line_order:
            place = place_at(from_chip(offset))
            line_copy(name, place, place, offset, True).wait_recv()

    def far_wait(name, place_at):
        for offset in (1, last_chip):
            place = place_at(from_chip(offset))
            copy = line_copy(name, place, place, offset, True)
            pl.when(jnp.logical_not(near_from(offset)))(copy.wait_recv)

    def line_start(name, source_at, target, buffer=None):
        for offset in range(1, g.chips):
            launch(line_copy(name, source_at(peer_chip(offset)), target, offset, False), buffer)

    def line_wait(name, target_at):
        for offset in range(1, g.chips):
            target = target_at(from_chip(offset), offset)
            line_copy(name, target, target, offset, True).wait_recv()

    def rows_plane_start(name, place_at, pair):
        for offset in range(1, g.parts):
            launch(plane_copy(name, place_at(0), place_at(offset), offset, False))
        pair_start(pair + "0", place_at(0), place_at(0))

    def rows_plane_wait(name, place, offset, pair):
        plane_copy(name, place, place, offset, True).wait_recv()
        pair_start(pair + str(offset), place, place)

    top = cols - TAIL
    half = width // 2
    part_cols = head_cols // 2
    tail_lane = head_cols + 2 * GROUP

    def qkv_section(at_dev, index, section):
        return lax.rem(lax.div(3 * at_dev + index, g.devices) - section + g.sections, g.sections)

    def qkv_send(layer, offsets):
        for index in range(3):
            to = qkv_section(dev, index, sec)
            for offset in offsets:
                copy = remote(
                    r.pq.at[layer, index], r.rq.at[layer, core, chip, index],
                    r.wq_s.at[layer, index, offset], r.wq_r.at[layer, index, offset],
                    {"section": to, "dp": 2 * peer_chip(offset) + core},
                )
                if offset:
                    launch(copy, None, near_to(offset))
                else:
                    pl.when(to != sec)(copy.start)

                    @pl.when(to == sec)
                    def _(index=index):
                        r.rq[layer, core, chip, index] = r.pq[layer, index]

    def qkv_arrive(layer, offsets):
        for offset in offsets:
            for index in range(3):
                at_chip = from_chip(offset)
                target = r.rq.at[layer, core, at_chip, index]
                origin = qkv_section(2 * at_chip + core, index, sec)
                copy = remote(
                    target, target, r.wq_s.at[layer, index, offset], r.wq_r.at[layer, index, offset],
                    {"section": origin, "dp": 2 * at_chip + core},
                )
                if offset:
                    do_when(near_from(offset), copy.wait_recv)
                else:

                    @pl.when(origin != sec)
                    def _(copy=copy):
                        copy.wait_recv()
                        copy.wait_send()

            if g.relay and offset == 2:
                spread_relay("qkv0", r.rq.at[0, core, from_chip(offset)], "qkv0")
        if g.relay and len(offsets) > 1:
            far_wait("qkv0", lambda at: r.rq.at[0, core, at])

    def out_copy(section_offset, offset, place, receiving):
        if receiving:
            to, at_chip = from_section(section_offset), from_chip(offset)
        else:
            to, at_chip = peer_section(section_offset), peer_chip(offset)
        source = place if receiving else r.po.at[0, to]
        return remote(
            source, place, r.wo_s.at[section_offset, offset], r.wo_r.at[section_offset, offset],
            {"section": to, "dp": 2 * at_chip + core},
        )

    def out_offsets():
        return [(a, b) for b in (*line_order, 0) for a in range(g.sections) if a + b]

    def plane_copy(name, source, target, offset, receiving):
        index = g.planes.index(name)
        where = from_section(offset) if receiving else peer_section(offset)
        return remote(
            source, target, r.plane_s.at[index, offset - 1], r.plane_r.at[index, offset - 1], {"section": where}
        )

    def pack_wide(block):
        tail = jnp.concatenate([block[top:, :half], block[top:, half:]], axis=0)
        return jnp.concatenate([block[:top], tail], axis=1).astype(BF16)

    def pack_out(block):
        small = jnp.concatenate([block[top:, head_cols:]] * 2, axis=0)
        tail = jnp.concatenate([block[top:, :part_cols], block[top:, part_cols:head_cols]], axis=0)
        empty = jnp.zeros((top, g.out_lanes - tail_lane - part_cols), F32)
        return jnp.concatenate([block[:top], small, tail, empty], axis=1).astype(BF16)

    def unpack_wide(target, first, piece):
        target[first : first + top, 0:width] = piece[:, 0:width]
        target[first + top : first + cols, 0:half] = piece[0:TAIL, width : width + half]
        target[first + top : first + cols, half:width] = piece[TAIL:, width : width + half]

    def unpack_out(target, first, piece, lane=0):
        last = slice(first + top, first + cols)
        tail = slice(tail_lane, tail_lane + part_cols)
        target[first : first + top, lane : lane + head_cols] = piece[:, 0:head_cols]
        target[last, lane : lane + part_cols] = piece[0:TAIL, tail]
        target[last, lane + part_cols : lane + head_cols] = piece[TAIL:, tail]

    def unpack_small(target, first, piece, lane):
        target[first : first + top, lane : lane + GROUP] = piece[:, head_cols : head_cols + GROUP]
        target[first + top : first + cols, lane : lane + GROUP] = piece[0:TAIL, head_cols + GROUP : tail_lane]

    def shard_places():
        for at_core in range(2):
            for at_chip in range(g.chips):
                for at_sec in range(g.sections):
                    yield at_core, at_chip, at_sec, (at_sec * g.devices + 2 * at_chip + at_core) * cols

    def chunk_places():
        for at_core in range(2):
            for at_chip in range(g.chips):
                for index in range(3):
                    yield at_core, at_chip, index, (3 * (2 * at_chip + at_core) + index) * cols

    def unfold_out(layer):
        for at_core, at_chip, at_sec, first in shard_places():
            piece = r.ro[layer, at_core, at_chip, at_sec].astype(F32)
            if layer == 0:
                unpack_small(r.tmp, first, piece, head_cols)
            unpack_out(r.tmp, first, piece)
        flipped = r.tmp[:, 0:tail_lane].T
        r.w_out[layer] = flipped[:head_cols].astype(BF16)
        if layer == 0:
            r.prm[...] = flipped[head_cols : head_cols + GROUP]
            r.w_router[...] = r.tmp[:, tail_lane - LANES : tail_lane].astype(BF16)

    def unfold_qkv(layer):
        for at_core, at_chip, index, first in chunk_places():
            unpack_wide(r.tmp, first, r.rq[layer, at_core, at_chip, index].astype(F32))
        r.w_qkv[layer] = r.tmp[0 : 3 * head_cols, 0:width].astype(BF16)

    def unfold_down():
        for at_core, at_chip, at_sec, first in shard_places():
            unpack_wide(r.tmp, first, r.rd[at_core, at_chip, at_sec].astype(F32))
        r.w_down[...] = r.tmp[...].astype(BF16)

    def grad_line(name, buffer_at, landing, target, passed):
        pair_wait(name, landing)
        for at_chip in range(g.chips):
            block = buffer_at(at_chip)
            block[...] = (block[...].astype(F32) + landing[at_chip].astype(F32)).astype(BF16)
        if g.relay:
            index = g.lines.index(name)
            copy = remote(
                buffer_at(last_chip - chip), passed, r.line_s.at[index, last_chip], r.line_r.at[index, last_chip],
                at_chip_core(1 + lax.div(chip, last_chip)),
            )
            launch(copy, None, is_end)
            for offset in (1, last_chip):

                @pl.when(jnp.logical_not(near_from(offset)))
                def _(offset=offset):
                    target[offset - 1] = jnp.zeros_like(target[offset - 1])

        for offset in line_order:
            copy = line_copy(name, buffer_at(peer_chip(offset)), target.at[offset - 1], offset, False)
            if g.relay and offset == 2:
                pl.when(is_end)(copy.start)
                started.append((copy, None))
            else:
                launch(copy, None, near_to(offset))

    def grad_relay(name, buffer_at, target, passed):
        if g.relay:
            index = g.lines.index(name)
            block = buffer_at(peer_chip(2))
            copy = line_copy(name, block, target.at[1], 2, False)

            @pl.when(is_mid)
            def _():
                remote(
                    passed, passed, r.line_s.at[index, last_chip], r.line_r.at[index, last_chip],
                    at_chip_core(outward * last_chip),
                ).wait_recv()
                block[...] = (block[...].astype(F32) + passed[...].astype(F32)).astype(BF16)
                copy.start()

    def grad_line_sum(name, buffer_at, target):
        for offset in line_order:
            place = target.at[offset - 1]
            do_when(near_from(offset), line_copy(name, place, place, offset, True).wait_recv)
        total = buffer_at(chip)[...].astype(F32)
        for offset in range(1, g.chips):
            total = total + target[offset - 1].astype(F32)
        return total

    def qkv_at(layer):
        return lambda at: r.rq.at[layer, core, at]

    def down_at(at):
        return r.rd.at[core, at]

    def out_at(layer):
        return lambda at: r.ro.at[layer, core, at]

    def up_at(at):
        return r.ru.at[at, core]

    def bias_at(at):
        return r.rb.at[at, core]

    def grad_plane(name, buffer_at, target, summed, final):
        summed[...] = grad_line_sum(name, buffer_at, target).astype(BF16)
        for offset in range(1, g.sections):
            source = summed.at[peer_section(offset)]
            launch(plane_copy(name, source, final.at[sec], offset, False))
        final[sec] = summed[sec]

    def grad_plane_wait(name, final):
        for offset in range(1, g.sections):
            place = final.at[from_section(offset)]
            plane_copy(name, place, place, offset, True).wait_recv()

    def grad_qkv_copy(layer, index, place, where):
        return remote(
            r.mq.at[layer, index], place, r.gq_s.at[layer, index], r.gq_r.at[layer, index], {"section": where}
        )

    def grad_qkv_plane(layer):
        r.mq[layer] = grad_line_sum("gqkv" + str(layer), qkv_at(layer), r.aq.at[layer]).astype(BF16)
        for index in range(3):
            to = qkv_section(dev, index, sec)
            copy = grad_qkv_copy(layer, index, r.fq.at[layer, index], to)
            pl.when(to != sec)(copy.start)

            @pl.when(to == sec)
            def _(index=index):
                r.fq[layer, index] = r.mq[layer, index]

    def grad_qkv_finish(layer):
        for index in range(3):
            origin = qkv_section(dev, index, sec)
            copy = grad_qkv_copy(layer, index, r.fq.at[layer, index], origin)

            @pl.when(origin != sec)
            def _(copy=copy):
                copy.wait_recv()
                copy.wait_send()

            unpack_wide(r.o_qkv.at[layer], index * cols, r.fq[layer, index].astype(F32))

    def norm_into(source, target, index, micro):
        rows = g.seq // 2

        @pl.loop(0, 2)
        def _(step):
            at = rows_at(micro * 2 + step, rows)
            unit, _ = normalize(source[at, :].astype(F32))
            target[at, :] = (unit * r.prm[index : index + 1, :] + r.prm[4 + index : 5 + index, :]).astype(BF16)

    place_row = jnp.concatenate(
        [r.routes[m : m + 1] * span + m * g.cap + r.slots[m : m + 1] for m in range(g.micro)], axis=1
    )
    r.square[...] = jnp.zeros_like(r.square)
    if g.direct:
        r.square[0:4, 0:cols] = r.norm_gain[...].astype(F32)
        r.square[4:8, 0:cols] = r.norm_bias[...].astype(F32)
        r.square[8:10, 0:cols] = r.out_bias[...].astype(F32)
        r.square[10:11, 0:cols] = r.down_bias[...].astype(F32)
        r.pb[...] = jnp.zeros_like(r.pb)
        r.pb[:, 0:shard_rows] = jnp.broadcast_to(r.up_bias[...], (r.pb.shape[0], shard_rows))
        r.square[FIRST_ROUTER : FIRST_ROUTER + g.experts, 0:cols] = r.router[...].astype(F32)
        r.square[...] = r.square[...].T
        loads["wo"].wait()
        loads["wq"].wait()
        shard = r.wo[0].astype(F32)
        mine = r.square[0:cols, 0:GROUP]
        for at_sec in range(g.sections):
            block = shard[:, at_sec * head_cols : (at_sec + 1) * head_cols]
            r.po[0, at_sec] = pack_out(jnp.concatenate([block, mine], axis=1))
        shard = r.wq[0].astype(F32)
        for index in range(3):
            r.pq[0, index] = pack_wide(shard[index * cols : (index + 1) * cols])
    pl.semaphore_wait(barrier, len(partners) + 1)
    if g.direct:
        for section_offset, offset in out_offsets():
            launch(out_copy(section_offset, offset, r.ro.at[0, core, chip, sec], False), None, near_to(offset))
        r.ro[0, core, chip, sec] = r.po[0, sec]
        qkv_send(0, (*line_order, 0))
        loads["wu"].wait()
        loads["wd"].wait()
        shard = r.wq[1].astype(F32)
        for index in range(3):
            r.pq[1, index] = pack_wide(shard[index * cols : (index + 1) * cols])
        shard, other = r.wd[...].astype(F32), r.wo[1].astype(F32)
        empty = jnp.zeros((cols, GROUP), F32)
        for at_sec in range(g.sections):
            r.pd[at_sec] = pack_wide(shard[:, at_sec * hidden : (at_sec + 1) * hidden])
            block = other[:, at_sec * head_cols : (at_sec + 1) * head_cols]
            r.po[1, at_sec] = pack_out(jnp.concatenate([block, empty], axis=1))

    loads["x0"].wait()
    loads["cot"].wait()
    slot_ids = lax.broadcasted_iota(jnp.int32, (quarter, g.tokens), 0)

    def slot_match(expert, part, group):
        first = expert * span + group * (span // g.groups) + part * quarter
        return jnp.where(slot_ids + first == place_row, 1.0, 0.0).astype(BF16)

    def group_tokens(group):
        count = g.tokens // g.groups
        return slice(group * count, (group + 1) * count)

    for group in range(g.groups):
        for expert in range(g.chips):
            match = slot_match(expert, g.my_part(sec), group)
            r.table[group, expert * quarter : (expert + 1) * quarter, :] = match[:, group_tokens(group)]
        sent = mm(r.table[group], r.cot[group_tokens(group), :]).astype(BF16)
        r.dispc[:, group] = sent.reshape(g.chips, quarter, width)
    r.small[...] = jnp.zeros_like(r.small)
    if g.direct:
        for section_offset, offset in out_offsets():
            place = r.ro.at[0, core, from_chip(offset), from_section(section_offset)]
            do_when(near_from(offset), out_copy(section_offset, offset, place, True).wait_recv)
            if g.relay and (section_offset, offset) == (g.sections - 1, 2):
                spread_relay("out0", r.ro.at[0, core, from_chip(offset)], "out0")
        if g.relay:
            far_wait("out0", lambda at: r.ro.at[0, core, at])
        pair_start("out0", r.ro.at[0, core], r.ro.at[0, core], "out0")
        qkv_arrive(0, (*line_order, 0))
        pair_start("qkv0", r.rq.at[0, core], r.rq.at[0, core], "qkv0")
        spread_first("bias", r.pb, r.rb.at[chip, core])
        spread_more("bias", r.pb, r.rb.at[chip, core])
        r.rb[chip, core] = r.pb[...]
        spread_first("up", r.wu, r.ru.at[chip, core])
        r.ru[chip, core] = r.wu[...]
        for offset in range(1, g.sections):
            launch(plane_copy("down", r.pd.at[peer_section(offset)], r.rd.at[core, chip, sec], offset, False))
        r.rd[core, chip, sec] = r.pd[sec]
        qkv_send(1, [0])
        for offset in range(1, g.sections):
            place = r.ro.at[1, core, chip, sec]
            launch(plane_copy("out1", r.po.at[1, peer_section(offset)], place, offset, False))
        r.ro[1, core, chip, sec] = r.po[1, sec]
        pair_wait("out0", r.ro.at[0, 1 - core])
        unfold_out(0)
        pair_wait("qkv0", r.rq.at[0, 1 - core])
        unfold_qkv(0)

    def plane_arrive(name, place_at):
        for offset in range(1, g.sections):
            place = place_at(from_section(offset))
            plane_copy(name, place, place, offset, True).wait_recv()

    def up_place(at):
        return r.ru.at[at, core]

    def bias_place(at):
        return r.rb.at[at, core]

    def down_place(at):
        return r.rd.at[core, at]

    def qkv_place(at):
        return r.rq.at[1, core, at]

    def out_place(at):
        return r.ro.at[1, core, at]

    def own_first(name, place_at):
        spread_first(name, place_at(chip), place_at(chip), name)

    def own_more(name, place_at):
        spread_more(name, place_at(chip), place_at(chip), name)

    key_ids = lax.broadcasted_iota(jnp.int32, (g.seq, g.seq), 0)
    query_ids = lax.broadcasted_iota(jnp.int32, (g.seq, g.seq), 1)
    scale = HEAD_DIM**-0.5
    micros = range(g.micro)

    def block_of(index):
        return lax.rem(index + sec, 3) if g.direct else index

    def head_slice(head):
        return slice(head * HEAD_DIM, (head + 1) * HEAD_DIM)

    def attention_forward(layer, stream, slot, micro):
        at = token_slice(micro)
        norm_into(stream, r.normed.at[2 * layer], 2 * layer, micro)
        packed = mm_nt(r.w_qkv[layer], r.normed[2 * layer, at, :]).astype(BF16)
        r.qkv[layer, :, :, at] = packed.reshape(3, head_cols, g.seq)
        allowed = (key_ids <= query_ids) & (key_ids < r.lens[:, micro : micro + 1])
        for head in range(g.heads):
            key = r.qkv[layer, block_of(1), head_slice(head), at]
            scores = mm_tn(key, r.qkv[layer, block_of(0), head_slice(head), at]) * scale
            scores = jnp.where(allowed, scores, MASKED)
            weight = jnp.exp(scores - jnp.max(scores, axis=0, keepdims=True))
            weight = weight / jnp.sum(weight, axis=0, keepdims=True)
            r.probs[layer, micro, head] = weight
            value = r.qkv[layer, block_of(2), head_slice(head), at]
            r.ctx[layer, head_slice(head), at] = mm(value, weight.astype(BF16)).astype(BF16)
        scatter_start(slot, micro, mm_tn(r.ctx[layer, :, at], r.w_out[layer]))

    def finish_forward(section, bias, stream, micro):
        total = scatter_sum(section, micro) + bias + stream[own(micro), :].astype(F32)
        r.xs[section, own(micro), :] = total.astype(BF16)
        gather_start(r.xs, section, section, micro)

    for micro in micros:
        attention_forward(0, r.x0, 0, micro)
        if g.direct and micro == 0:
            spread_more("up", r.wu, r.ru.at[chip, core])
    if g.direct:
        spread_pass("bias", bias_place, "bias")
        spread_pass("up", up_place, "up")
        plane_arrive("down", lambda at: r.rd.at[core, chip, at])
        own_first("down", down_place)
    for micro in micros:
        finish_forward(0, r.prm[8:9, :], r.x0, micro)
    if g.direct:
        own_more("down", down_place)
        spread_wait("bias", bias_place)
        spread_wait("up", up_place)
        pair_start("up", r.ru.at[:, core], r.ru.at[:, core], "up")
        pair_start("bias", r.rb.at[:, core], r.rb.at[:, core], "bias")
        pair_wait("up", r.ru.at[:, 1 - core])
        pair_wait("bias", r.rb.at[:, 1 - core])
        for at_dev in range(g.devices):
            row = r.rb[at_dev // 2, at_dev % 2, :, 0:shard_rows].astype(F32)
            r.b_up[:, at_dev * shard_rows : (at_dev + 1) * shard_rows] = row[0:TAIL]

    def up_rows(at):
        if g.direct:
            return r.ru[...].reshape(hidden, width)[at]
        return r.w_up[at, :]

    def hidden_blocks():
        return [slice(first, first + g.block) for first in range(0, hidden, g.block)]

    for micro in micros:
        rows = token_slice(micro)
        gather_wait(r.xs, 0, 0, micro)
        norm_into(r.xs.at[0], r.normed.at[1], 1, micro)
        for at in hidden_blocks():
            value, slope = gelu_parts(mm_nt(r.normed[1, rows, :], up_rows(at)) + r.b_up[0:1, at])
            r.act[rows, at] = value.astype(BF16)
            r.dgelu[rows, at] = slope
        if g.direct and micro == 0:
            spread_pass("down", down_place, "down")
            qkv_arrive(1, [0])
            own_first("qkv1", qkv_place)
            own_more("qkv1", qkv_place)
    if g.direct:
        spread_wait("down", down_place)
        pair_start("down", r.rd.at[core], r.rd.at[core], "down")
        plane_arrive("out1", lambda at: r.ro.at[1, core, chip, at])
        own_first("out1", out_place)
        own_more("out1", out_place)
        pair_wait("down", r.rd.at[1 - core])
        unfold_down()
    for micro in micros:
        scatter_start(1, micro, mm_nt(r.act[token_slice(micro), :], r.w_down[...]))
    if g.direct:
        spread_pass("qkv1", qkv_place, "qkv1")
    for micro in micros:
        finish_forward(1, r.prm[10:11, :], r.xs.at[0], micro)
        if g.direct and micro == 0:
            spread_pass("out1", out_place, "out1")
    if g.direct:
        spread_wait("qkv1", qkv_place)
        pair_start("qkv1", r.rq.at[1, core], r.rq.at[1, core], "qkv1")
        spread_wait("out1", out_place)
        pair_start("out1", r.ro.at[1, core], r.ro.at[1, core], "out1")

    def crow_at(part, side):
        return r.crow.at[:, part, side]

    def crow_line(offset, receiving):
        at_chip = from_chip(offset) if receiving else peer_chip(offset)
        place = r.crow.at[:, 0, core, rows_at(at_chip if receiving else chip, quarter)]
        return line_copy("crow", place if receiving else r.dispc.at[at_chip], place, offset, receiving)

    for offset in range(1, g.chips):
        launch(crow_line(offset, False))
    r.crow[:, 0, core, rows_at(chip, quarter), :] = r.dispc[chip]

    if g.direct:
        pair_wait("qkv1", r.rq.at[1, 1 - core])
        unfold_qkv(1)
        pair_wait("out1", r.ro.at[1, 1 - core])
        unfold_out(1)
    for micro in micros:
        gather_wait(r.xs, 1, 1, micro)
        attention_forward(1, r.xs.at[1], 2, micro)
    for micro in micros:
        finish_forward(2, r.prm[9:10, :], r.xs.at[1], micro)
    r.square[0 : g.micro, :] = jnp.concatenate(
        [place_row[:, token_slice(micro)] for micro in micros], axis=0
    ).astype(F32)
    columns = r.square[...].T

    wide = r.wide

    def gates(micro):
        at = token_slice(micro)
        norm_into(r.xs.at[2], wide.at[:, pl.ds(0, width)], 3, micro)
        logits = mm(wide[at, :width], r.w_router[...])
        lane = lax.broadcasted_iota(jnp.int32, logits.shape, 1) - g.router_lane
        place_col = columns[:, micro : micro + 1].astype(jnp.int32)
        chosen = (place_col >= lane * span) & (place_col < lane * span + span)
        score = jnp.sum(jnp.where(chosen, logits, 0.0), axis=-1, keepdims=True)
        gate = 1.0 / (1.0 + jnp.exp(-score))
        gate_high = gate.astype(BF16).astype(F32)
        lane = lax.broadcasted_iota(jnp.int32, (g.seq, LANES), 1)
        pair = jnp.where(lane == 0, gate_high, jnp.where(lane == 1, gate - gate_high, 0.0))
        wide[at, width:] = pair.astype(BF16)

    groups = range(g.groups)

    def rows_place(group, side):
        return lambda part: r.rows.at[group, part, side]

    def rows_line_start(group):
        name = "rows" + str(group)
        r.disp[group] = mm(r.table[group], wide[group_tokens(group), :]).astype(BF16)
        place = r.rows.at[group, 0, core, rows_at(chip, quarter)]
        line_start(name, lambda at: r.disp.at[group, rows_at(at, quarter)], place)
        r.rows[group, 0, core, rows_at(chip, quarter), :] = r.disp[group, rows_at(chip, quarter), :]

    def rows_line_wait(group):
        name = "rows" + str(group)
        mine = r.rows.at[group, 0, core]
        line_wait(name, lambda at, _: mine.at[rows_at(at, quarter)])
        rows_plane_start(name, rows_place(group, core), name)

    for micro in micros:
        gather_wait(r.xs, 2, 2, micro)
        if micro == 0:
            for offset in range(1, g.chips):
                crow_line(offset, True).wait_recv()
            rows_plane_start("crow", lambda part: crow_at(part, core), "crow")
        gates(micro)
        if g.groups > 1:
            rows_line_start(micro)
    if g.groups == 1:
        rows_line_start(0)
    for group in groups:
        rows_line_wait(group)
    loads["e_up"].wait()
    loads["e_down"].wait()

    own_router = FIRST_ROUTER + chip
    router_row = r.prm[pl.ds(own_router, 1), :]
    snd = dict(d=r.snd_d, y=r.snd_y)
    kept = dict(d=r.keep_d, y=r.keep_y)
    rcv = dict(d=r.rcv_d, y=r.rcv_y)

    def expert_block(wide_rows, cot_rows):
        row = wide_rows[:, :width]
        tail = wide_rows[:, width:].astype(F32)
        gate_row = tail[:, 0:1] + tail[:, 1:2]
        grad_row = (gate_row * cot_rows.astype(F32)).astype(BF16)
        value, slope = gelu_parts(mm(row, r.e_up[...]))
        value = value.astype(BF16)
        result = mm(value, r.e_down[...])
        total = jnp.sum(grad_row.astype(F32) * result, axis=-1, keepdims=True) * (1.0 - gate_row)
        inner = (slope * mm_nt(grad_row, r.e_down[...])).astype(BF16)
        back = mm_nt(inner, r.e_up[...]) + total * router_row
        r.small[pl.ds(own_router, 1), :] += jnp.sum(row.astype(F32) * total, axis=0, keepdims=True)
        return grad_row, value, inner, back, result * gate_row

    def expert_parts(group, first, count):
        parts = slice(first, first + count)
        each = 2 * block_rows
        if each <= g.block:
            lead = (count, 2, block_rows)
            found = expert_block(
                r.rows[group, parts].reshape(count * each, width + LANES),
                r.crow[group, parts].reshape(count * each, width),
            )
            for target, value in zip((r.grow, r.acte, r.dpree), found[:3], strict=True):
                target[group, parts] = value.reshape(*lead, value.shape[-1])
            r.both[0, parts] = found[3].reshape(*lead, width)
            r.both[1, parts] = found[4].reshape(*lead, width)
        else:
            for part in range(first, first + count):
                for side in range(2):

                    @pl.loop(0, block_rows // g.block)
                    def _(step, part=part, side=side):
                        at = rows_at(step, g.block)
                        found = expert_block(r.rows[group, part, side, at, :], r.crow[group, part, side, at, :])
                        for target, value in zip((r.grow, r.acte, r.dpree), found[:3], strict=True):
                            target[group, part, side, at, :] = value
                        r.both[0, part, side, at, :] = found[3]
                        r.both[1, part, side, at, :] = found[4]

        for which, value in (("d", r.both.at[0]), ("y", r.both.at[1])):
            for part in range(first, first + count):
                snd[which][group, part] = value[part, 1 - core].astype(BF16)
                place = rcv[which].at[group, part]
                pair_start(which + str(group) + str(part), snd[which].at[group, part], place)
                kept[which][group, part] = value[part, core]

    def merge(which, offset, group):
        pair_wait(which + str(group) + str(offset), rcv[which].at[group, offset])
        return kept[which][group, offset] + rcv[which][group, offset].astype(F32)

    def merge_send(offset, group):
        to = g.sections - offset
        r.out_d[offset - 1, group] = merge("d", offset, group).astype(BF16)
        name = "d" + str(group)
        launch(plane_copy(name, r.out_d.at[offset - 1, group], r.plane_d.at[to - 1, group], to, False))

    def parts_work(group, first, count):
        for part in range(first, first + count):
            if group == 0:
                pair_wait("crow" + str(part), crow_at(part, 1 - core))
            pair_wait("rows" + str(group) + str(part), rows_place(group, 1 - core)(part))
        expert_parts(group, first, count)

    def results_line(group):
        for offset in range(g.parts):
            r.ret_y[group, offset] = merge("y", offset, group).astype(BF16)
        name = "y" + str(group)
        line_start(name, lambda at: r.ret_y.at[group, :, rows_at(at, quarter)], r.back_y.at[chip, group])
        r.back_y[chip, group] = r.ret_y[group, :, rows_at(chip, quarter), :]

    def expert_back_line(group):
        name = "d" + str(group)
        total = merge("d", 0, group)
        if g.parts > 1:
            for offset in range(1, g.sections):
                place = r.plane_d.at[offset - 1, group]
                plane_copy(name, place, place, offset, True).wait_recv()
                total = total + place[...].astype(F32)
        r.ret_d[group] = total.astype(BF16)
        place = r.back_d.at[group, rows_at(chip, quarter)]
        line_start(name, lambda at: r.ret_d.at[group, rows_at(at, quarter)], place)
        r.back_d[group, rows_at(chip, quarter), :] = r.ret_d[group, rows_at(chip, quarter), :]

    def expert_combine(group):
        line_wait("d" + str(group), lambda at, _: r.back_d.at[group, rows_at(at, quarter)])
        value = mm_tn(r.table[group], r.back_d[group])
        if g.groups > 1:
            scatter_start(3, group, value)
        else:
            for micro in micros:
                scatter_start(3, micro, value[token_slice(micro)])

    def results_combine():
        for group in groups:
            line_wait("y" + str(group), lambda at, _: r.back_y.at[at, group])
        places = [(e, q, p) for e in range(g.chips) for q in groups for p in range(g.parts)]
        match = [slot_match(e, g.my_part(from_section(p)), q) for e, q, p in places]
        match = jnp.concatenate(match, axis=0)
        value = mm_tn(match, r.back_y[...].reshape(g.chips * span, width))
        for micro in micros:
            scatter_start(7, micro, value[token_slice(micro)])

    offsets = range(1, g.parts)
    for group in groups:
        parts_work(group, 0, 1)
    for offset in offsets:
        rows_plane_wait("crow", crow_at(offset, core), offset, "crow")
    for group in groups:
        name = "rows" + str(group)
        for offset in offsets:
            rows_plane_wait(name, rows_place(group, core)(offset), offset, name)
        if g.parts > 1:
            parts_work(group, 1, g.parts - 1)
        for offset in offsets:
            merge_send(offset, group)
        if group < g.groups - 1:
            results_line(group)
    for group in groups:
        expert_back_line(group)

    def expert_weights(left, right):
        rows = g.groups * g.parts * 2 * block_rows
        return mm_tn(left.reshape(rows, left.shape[-1]), right.reshape(rows, right.shape[-1]))

    r.v_gup[...] = expert_weights(r.rows[:, :, :, :, :width], r.dpree[...])
    r.v_gdown[...] = expert_weights(r.acte[...], r.grow[...])
    for copy in stores:
        copy.start()

    def add_small(index, micro, value):
        if micro == 0:
            r.small[index : index + 1, :] = value
        else:
            r.small[index : index + 1, :] += value

    def finish_backward(section, slot, stream, above, micro):
        grad = scatter_sum(slot, micro)
        unit, inverse = normalize(stream[own(micro), :].astype(F32))
        add_small(section, micro, jnp.sum(grad * unit, axis=0, keepdims=True))
        add_small(4 + section, micro, jnp.sum(grad, axis=0, keepdims=True))
        grad = grad * r.prm[section : section + 1, :]
        shared = jnp.mean(grad, axis=-1, keepdims=True)
        along = jnp.mean(grad * unit, axis=-1, keepdims=True)
        grad = inverse * (grad - shared - unit * along) + above[own(micro), :].astype(F32)
        r.gs[section, own(micro), :] = grad.astype(BF16)
        gather_start(r.gs, section, 4 + section, micro)

    for group in groups:
        expert_combine(group)
    results_line(g.groups - 1)
    for micro in micros:
        finish_backward(3, 3, r.xs.at[2], r.cot, micro)

    def bias_row(index, section):
        for micro in micros:
            value = r.gs[section, own(micro), :].astype(F32)
            add_small(index, micro, jnp.sum(value, axis=0, keepdims=True))

    def attention_backward(layer, section, slot, micro):
        at = token_slice(micro)
        dctx = mm_nt(r.w_out[layer], r.gs[section + 1, at, :]).astype(BF16)
        for head in range(g.heads):
            weight = r.probs[layer, micro, head]
            low = weight.astype(BF16)
            dhead = dctx[head_slice(head)]
            query = r.qkv[layer, block_of(0), head_slice(head), at]
            key = r.qkv[layer, block_of(1), head_slice(head), at]
            value = r.qkv[layer, block_of(2), head_slice(head), at]
            dprobs = mm_tn(value, dhead)
            delta = jnp.sum(weight * dprobs, axis=0, keepdims=True)
            dscores = (weight * (dprobs - delta)).astype(BF16)
            r.dqkv[block_of(0), head_slice(head), at] = (mm(key, dscores) * scale).astype(BF16)
            r.dqkv[block_of(1), head_slice(head), at] = (mm_nt(query, dscores) * scale).astype(BF16)
            r.dqkv[block_of(2), head_slice(head), at] = mm_nt(dhead, low).astype(BF16)
        flat_grad = r.dqkv[:, :, at].reshape(3 * head_cols, g.seq)
        scatter_start(slot, micro, mm_tn(flat_grad, r.w_qkv[layer]))

    def attention_weights(layer, section):
        grad_qkv = mm(r.dqkv[...].reshape(3 * head_cols, g.tokens), r.normed[2 * layer])
        if not g.direct:
            r.o_qkv[layer] = grad_qkv
            r.o_out[layer] = mm(r.ctx[layer], r.gs[section + 1])
            return
        r.tmp[0 : 3 * head_cols, :] = grad_qkv
        settle("qkv" + str(layer))
        for at_core, at_chip, index, first in chunk_places():
            r.rq[layer, at_core, at_chip, index] = pack_wide(r.tmp[first : first + cols, :])
        name = "gqkv" + str(layer)
        pair_start(name, r.rq.at[layer, 1 - core], r.hq.at[layer])
        r.tmp[:, 0:head_cols] = dot_as(r.gs[section + 1], r.ctx[layer], 0, 1)
        if layer:
            r.tmp[:, head_cols : head_cols + GROUP] = jnp.zeros((width, GROUP), F32)
            out_weights(1)

    def out_weights(layer):
        settle("out" + str(layer))
        for at_core, at_chip, at_sec, first in shard_places():
            block = r.tmp[first : first + cols, 0 : head_cols + GROUP]
            r.ro[layer, at_core, at_chip, at_sec] = pack_out(block)
        pair_start("gout" + str(layer), r.ro.at[layer, 1 - core], r.ho.at[layer])

    for micro in micros:
        gather_wait(r.gs, 3, 7, micro)
        attention_backward(1, 2, 4, micro)
    bias_row(9, 3)
    attention_weights(1, 2)
    if g.direct:
        grad_line("gqkv1", qkv_at(1), r.hq.at[1], r.aq.at[1], r.lq.at[1])
    finish_backward(2, 4, r.xs.at[1], r.gs.at[3], 0)
    if g.direct:
        grad_line("gout1", out_at(1), r.ho.at[1], r.ao.at[1], r.lo.at[1])
    for micro in micros[1:]:
        finish_backward(2, 4, r.xs.at[1], r.gs.at[3], micro)

    for micro in micros:
        rows = token_slice(micro)
        gather_wait(r.gs, 2, 6, micro)
        grad_two = r.gs[2, rows, :]
        for at in hidden_blocks():
            r.dpre[rows, at] = (r.dgelu[rows, at] * mm(grad_two, r.w_down[:, at])).astype(BF16)
        scatter_start(5, micro, mm(r.dpre[rows, :], up_rows(slice(None))))
    bias_row(10, 2)
    sum_up = jnp.sum(r.dpre[...].astype(F32), axis=0, keepdims=True)
    if g.direct:
        grad_relay("gqkv1", qkv_at(1), r.aq.at[1], r.lq.at[1])
        grad_relay("gout1", out_at(1), r.ao.at[1], r.lo.at[1])
        r.tmp[...] = mm_tn(r.gs[2], r.act[...])
        settle("down")
        for at_core, at_chip, at_sec, first in shard_places():
            r.rd[at_core, at_chip, at_sec] = pack_wide(r.tmp[first : first + cols, :])
        pair_start("gdown", r.rd.at[1 - core], r.hd)
        settle("up")
        settle("bias")
        r.ru[...] = mm_tn(r.dpre[...], r.normed[1]).astype(BF16).reshape(r.ru.shape)
        pair_start("gup", r.ru.at[:, 1 - core], r.hu)
        for at_dev in range(g.devices):
            row = sum_up[:, at_dev * shard_rows : (at_dev + 1) * shard_rows]
            row = jnp.broadcast_to(row, (r.pb.shape[0], shard_rows)).astype(BF16)
            r.rb[at_dev // 2, at_dev % 2, :, 0:shard_rows] = row
        pair_start("gbias", r.rb.at[:, 1 - core], r.hb)
        grad_line("gdown", down_at, r.hd, r.ad, r.ld)
    else:
        r.o_down[...] = mm_tn(r.gs[2], r.act[...])
        r.o_up[...] = mm_tn(r.dpre[...], r.normed[1])
        r.o_bup[...] = sum_up
    for micro in micros:
        finish_backward(1, 5, r.xs.at[0], r.gs.at[2], micro)
    if g.direct:
        grad_line("gbias", bias_at, r.hb, r.ab, r.lb)
        grad_relay("gdown", down_at, r.ad, r.ld)

    for micro in micros:
        gather_wait(r.gs, 1, 5, micro)
        attention_backward(0, 0, 6, micro)
    bias_row(8, 1)
    attention_weights(0, 0)
    finish_backward(0, 6, r.x0, r.gs.at[1], 0)
    if g.direct:
        grad_line("gqkv0", qkv_at(0), r.hq.at[0], r.aq.at[0], r.lq.at[0])
    for micro in micros[1:]:
        finish_backward(0, 6, r.x0, r.gs.at[1], micro)
    if g.direct:
        kinds = r.small[...]
        padded = jnp.concatenate([kinds, jnp.zeros((LANES - kinds.shape[0], width), F32)], axis=0)
        r.tmp[:, head_cols : head_cols + GROUP] = padded.T[:, 0:GROUP]
        out_weights(0)
        grad_line("gout0", out_at(0), r.ho.at[0], r.ao.at[0], r.lo.at[0])
        grad_line("gup", up_at, r.hu, r.au, r.lu)
        grad_relay("gbias", bias_at, r.ab, r.lb)
    results_combine()
    if g.direct:
        grad_qkv_plane(1)
        grad_plane("gout1", out_at(1), r.ao.at[1], r.mo.at[1], r.fo.at[1])
        grad_plane("gdown", down_at, r.ad, r.md, r.fd)
        grad_relay("gqkv0", qkv_at(0), r.aq.at[0], r.lq.at[0])
        grad_relay("gout0", out_at(0), r.ao.at[0], r.lo.at[0])
    for micro in micros:
        r.xs[3, own(micro), :] = (scatter_sum(7, micro) + r.xs[2, own(micro), :].astype(F32)).astype(BF16)
        gather_start(r.xs, 3, 3, micro)
    if g.direct:
        grad_relay("gup", up_at, r.au, r.lu)
        grad_qkv_plane(0)
        grad_plane("gout0", out_at(0), r.ao.at[0], r.mo.at[0], r.fo.at[0])
        grad_qkv_finish(1)
        grad_plane_wait("gdown", r.fd)
        for at_sec in range(g.sections):
            piece = r.fd[at_sec].astype(F32)
            unpack_wide(r.o_down.at[:, pl.ds(at_sec * hidden, hidden)], 0, piece)
        r.o_up[...] = grad_line_sum("gup", up_at, r.au)
        r.o_bup[...] = grad_line_sum("gbias", bias_at, r.ab)[0:1, 0:shard_rows]
        grad_plane_wait("gout1", r.fo.at[1])
        for at_sec in range(g.sections):
            unpack_out(r.o_out.at[1], 0, r.fo[1, at_sec].astype(F32), at_sec * head_cols)
        grad_qkv_finish(0)
        grad_plane_wait("gout0", r.fo.at[0])
        everyone = jnp.zeros((top, g.out_lanes), F32)
        for at_sec in range(g.sections):
            piece = r.fo[0, at_sec].astype(F32)
            unpack_out(r.o_out.at[0], 0, piece, at_sec * head_cols)
            everyone = everyone + piece
        r.square[...] = jnp.zeros_like(r.square)
        unpack_small(r.square, 0, everyone, 0)
        r.square[...] = r.square[...].T
        r.o_router[...] = r.square[FIRST_ROUTER : FIRST_ROUTER + g.experts, 0:cols]
        r.o_gain[...] = r.square[0:4, 0:cols]
        r.o_bias[...] = r.square[4:8, 0:cols]
        r.o_bout[...] = r.square[8:10, 0:cols]
        r.o_bdown[...] = r.square[10:11, 0:cols]
    else:
        r.o_small[...] = r.small[...]
    for micro in micros:
        gather_wait(r.xs, 3, 3, micro)
        gather_wait(r.gs, 0, 4, micro)
    r.sec_out[...] = r.xs[sec]
    r.sec_grad[...] = r.gs[sec]
    for copy in stores:
        copy.wait()
    for copy, when in started:
        do_when(when, copy.wait_send)


def run_layers(g, operands):
    tokens, width, hidden, sections, chips = g.tokens, g.width, g.hidden, g.sections, g.chips
    part_rows = chips * g.quarter
    inner = operands["h_e_down"].shape[0]
    three = 3 * g.head_cols
    shape = jax.ShapeDtypeStruct
    vmem = pltpu.VMEM
    dma = pltpu.SemaphoreType.DMA
    top = g.cols - TAIL
    wide = width + width // 2
    up_rows = hidden // g.devices
    outs = dict(
        sec_out=shape((tokens, width), BF16),
        sec_grad=shape((tokens, width), BF16),
        g_eup=shape((width, inner), F32),
        g_edown=shape((inner, width), F32),
    )
    if g.direct:
        outs |= dict(
            o_qkv=shape((2, 3 * g.cols, width), F32),
            o_out=shape((2, g.cols, width), F32),
            o_up=shape((up_rows, width), F32),
            o_down=shape((g.cols, sections * hidden), F32),
            o_gain=shape((4, g.cols), F32),
            o_bias=shape((4, g.cols), F32),
            o_bout=shape((2, g.cols), F32),
            o_bdown=shape((1, g.cols), F32),
            o_router=shape((g.experts, g.cols), F32),
            o_bup=shape((1, up_rows), F32),
        )
    else:
        outs |= dict(
            o_qkv=shape((2, three, width), F32),
            o_out=shape((2, g.head_cols, width), F32),
            o_up=shape((hidden, width), F32),
            o_down=shape((width, hidden), F32),
            o_bup=shape((1, hidden), F32),
            o_small=shape((g.small, width), F32),
        )
    scratch = dict(
        xs=vmem((4, tokens, width), BF16),
        gs=vmem((4, tokens, width), BF16),
        normed=vmem((3, tokens, width), BF16),
        wide=vmem((tokens, width + LANES), BF16),
        qkv=vmem((2, 3, g.head_cols, tokens), BF16),
        probs=vmem((2, g.micro, g.heads, g.seq, g.seq), F32),
        ctx=vmem((2, g.head_cols, tokens), BF16),
        act=vmem((tokens, hidden), BF16),
        dgelu=vmem((tokens, hidden), F32),
        dpre=vmem((tokens, hidden), BF16),
        dqkv=vmem((3, g.head_cols, tokens), BF16),
        part=vmem((8, tokens, width), BF16),
        got=vmem((8, g.micro, sections - 1, g.piece, width), BF16),
        mine=vmem((tokens, width), F32),
        square=vmem((LANES, LANES), F32),
        table=vmem((g.groups, part_rows, tokens // g.groups), BF16),
        disp=vmem((g.groups, part_rows, width + LANES), BF16),
        dispc=vmem((chips, g.groups, g.quarter, width), BF16),
        rows=vmem((g.groups, g.parts, 2, part_rows, width + LANES), BF16),
        crow=vmem((g.groups, g.parts, 2, part_rows, width), BF16),
        grow=vmem((g.groups, g.parts, 2, part_rows, width), BF16),
        acte=vmem((g.groups, g.parts, 2, part_rows, inner), BF16),
        dpree=vmem((g.groups, g.parts, 2, part_rows, inner), BF16),
        both=vmem((2, g.parts, 2, part_rows, width), F32),
        small=vmem((g.small, width), F32),
        v_gup=vmem((width, inner), F32),
        v_gdown=vmem((inner, width), F32),
        local_s=dma((len(g.loads) + 2,)),
    )
    for name in g.loads:
        scratch[name] = vmem(operands["h_" + name].shape, BF16)
    for which in ("d", "y"):
        scratch["keep_" + which] = vmem((g.groups, g.parts, part_rows, width), F32)
        for name in ("snd_", "rcv_"):
            scratch[name + which] = vmem((g.groups, g.parts, part_rows, width), BF16)
    scratch |= dict(
        out_d=vmem((sections - 1, g.groups, part_rows, width), BF16),
        plane_d=vmem((sections - 1, g.groups, part_rows, width), BF16),
        ret_d=vmem((g.groups, part_rows, width), BF16),
        back_d=vmem((g.groups, part_rows, width), BF16),
        ret_y=vmem((g.groups, g.parts, part_rows, width), BF16),
        back_y=vmem((chips, g.groups, g.parts, g.quarter, width), BF16),
    )
    for name in ("scat_s", "scat_r", "gath_s", "gath_r"):
        scratch[name] = dma((8, g.micro, sections - 1))
    for name, count, each in (("pair", len(g.pairs), 0), ("line", len(g.lines), chips), ("plane", len(g.planes), sections - 1)):
        sizes = (count, each) if each else (count,)
        scratch |= {name + "_s": dma(sizes), name + "_r": dma(sizes)}
    if g.direct:
        piece = (top, wide)
        out_piece = (top, g.out_lanes)
        up_piece = (up_rows, width)
        bias_piece = (2 * TAIL, LANES)
        scratch |= dict(
            pq=vmem((2, 3, *piece), BF16),
            po=vmem((2, sections, *out_piece), BF16),
            pb=vmem(bias_piece, BF16),
            rb=vmem((chips, 2, *bias_piece), BF16),
            hb=vmem((chips, *bias_piece), BF16),
            ab=vmem((chips - 1, *bias_piece), BF16),
            lb=vmem(bias_piece, BF16),
            lq=vmem((2, 3, *piece), BF16),
            lo=vmem((2, sections, *out_piece), BF16),
            lu=vmem(up_piece, BF16),
            ld=vmem((sections, *piece), BF16),
            pd=vmem((sections, *piece), BF16),
            rq=vmem((2, 2, chips, 3, *piece), BF16),
            ro=vmem((2, 2, chips, sections, *out_piece), BF16),
            ru=vmem((chips, 2, *up_piece), BF16),
            rd=vmem((2, chips, sections, *piece), BF16),
            w_qkv=vmem((2, three, width), BF16),
            w_out=vmem((2, g.head_cols, width), BF16),
            w_down=vmem((width, hidden), BF16),
            w_router=vmem((width, LANES), BF16),
            b_up=vmem((8, hidden), F32),
            prm=vmem((GROUP, width), F32),
            tmp=vmem((width, width), F32),
            hq=vmem((2, chips, 3, *piece), BF16),
            ho=vmem((2, chips, sections, *out_piece), BF16),
            hu=vmem((chips, *up_piece), BF16),
            hd=vmem((chips, sections, *piece), BF16),
            aq=vmem((2, chips - 1, 3, *piece), BF16),
            ao=vmem((2, chips - 1, sections, *out_piece), BF16),
            au=vmem((chips - 1, *up_piece), BF16),
            ad=vmem((chips - 1, sections, *piece), BF16),
            mq=vmem((2, 3, *piece), BF16),
            mo=vmem((2, sections, *out_piece), BF16),
            md=vmem((sections, *piece), BF16),
            fq=vmem((2, 3, *piece), BF16),
            fo=vmem((2, sections, *out_piece), BF16),
            fd=vmem((sections, *piece), BF16),
            wq_s=dma((2, 3, chips)),
            wq_r=dma((2, 3, chips)),
            wo_s=dma((sections, chips)),
            wo_r=dma((sections, chips)),
            gq_s=dma((2, 3)),
            gq_r=dma((2, 3)),
        )
    whole = pl.BlockSpec(memory_space=pltpu.VMEM)
    placed = pl.BlockSpec(memory_space=pl.ANY)
    apart = ["h_" + name for name in g.loads] + ["g_eup", "g_edown"]
    names = (*operands, *outs, *scratch)
    results = pl.pallas_call(
        functools.partial(layers_kernel, g, names),
        out_shape=tuple(outs.values()),
        in_specs=[placed if name in apart else whole for name in operands],
        out_specs=[placed if name in apart else whole for name in outs],
        scratch_shapes=list(scratch.values()),
        compiler_params=pltpu.CompilerParams(
            collective_id=0, has_side_effects=True, vmem_limit_bytes=62 * 1024 * 1024
        ),
    )(*operands.values())
    return types.SimpleNamespace(**dict(zip(outs, results, strict=True)))


def finish_kernel(count, *refs):
    ins, outs, held = refs[:count], refs[count : 2 * count], refs[2 * count : 3 * count]
    wide, sems = refs[3 * count : 3 * count + 2], refs[-1]
    loads = [pltpu.make_async_copy(ins[i], held[i], sems.at[0, i]) for i in range(count)]
    stores = [pltpu.make_async_copy((wide[i] if i < 2 else held[i]), outs[i], sems.at[1, i]) for i in range(count)]
    for copy in loads:
        copy.start()
    for i in range(count):
        loads[i].wait()
        if i < 2:
            wide[i][...] = held[i][...].astype(F32)
        stores[i].start()
    for copy in stores:
        copy.wait()


def finish(arrays):
    count = len(arrays)
    placed = [pl.BlockSpec(memory_space=pl.ANY)] * count
    held = [pltpu.VMEM(array.shape, array.dtype) for array in arrays]
    wide = [pltpu.VMEM(array.shape, F32) for array in arrays[:2]]
    return pl.pallas_call(
        functools.partial(finish_kernel, count),
        out_shape=tuple(jax.ShapeDtypeStruct(array.shape, F32) for array in arrays),
        in_specs=placed,
        out_specs=placed,
        scratch_shapes=[*held, *wide, pltpu.SemaphoreType.DMA((2, count))],
        compiler_params=pltpu.CompilerParams(vmem_limit_bytes=62 * 1024 * 1024),
    )(*arrays)


BOTH = ("section", "dp")


def body(
    tokens, cotangent, lengths, routes, slots, norm_gain, norm_bias, attn_qkv, attn_out, attn_out_bias,
    ffn_up, ffn_up_bias, ffn_down, ffn_down_bias, router, expert_up, expert_down,
):
    sections, devices = lax.axis_size("section"), lax.axis_size("dp")
    sec = lax.axis_index("section")
    micro, _, seq, width = tokens.shape
    experts = router.shape[1]
    chips = devices // 2
    head_cols = width // sections
    hidden = ffn_up.shape[1] * devices
    cap = 2 * seq // experts
    span = micro * cap
    cols = ffn_down.shape[1]
    kinds = FIRST_ROUTER + experts
    direct = cols == 3 * TAIL and kinds <= GROUP and sections == 4 and ffn_up.shape[1] % 16 == 0
    parts = sections if span % (16 * sections) == 0 else 1
    groups = micro if cap % (16 * parts) == 0 else 1
    group_names = [str(group) for group in range(groups)]
    part_names = [str(part) for part in range(parts)]
    both_names = [a + b for a in group_names for b in part_names]
    g = types.SimpleNamespace(
        sections=sections, devices=devices, chips=chips, micro=micro, seq=seq, width=width, hidden=hidden, cap=cap,
        span=span, tokens=micro * seq, piece=seq // sections, heads=head_cols // HEAD_DIM,
        head_cols=head_cols, cols=cols, block=256, small=-(-kinds // 8) * 8, direct=direct, experts=experts,
        out_lanes=head_cols + 2 * GROUP + LANES, parts=parts, groups=groups, quarter=span // (parts * groups),
        loads=(["wo", "wq"] if direct else []) + ["x0", "cot"] + (["wu", "wd"] if direct else []) + ["e_up", "e_down"],
        relay=direct and chips == 4,
        my_part=(lambda section: section) if parts > 1 else (lambda section: 0),
        router_lane=FIRST_ROUTER + (LANES - 2 * GROUP if direct else 0),
        pairs=["crow" + a for a in part_names]
        + [name + a for name in ("rows", "d", "y") for a in both_names]
        + ([
            "out0", "qkv0", "up", "bias", "down", "qkv1", "out1",
            "gqkv0", "gqkv1", "gdown", "gup", "gbias", "gout0", "gout1",
        ] if direct else []),
        lines=["crow"]
        + [name + b for name in ("rows", "d", "y") for b in group_names]
        + ([
            "out0", "qkv0", "up", "bias", "down", "qkv1", "out1",
            "gqkv0", "gqkv1", "gdown", "gup", "gbias", "gout0", "gout1",
        ] if direct else []),
        planes=["crow"]
        + [name + b for name in ("rows", "d") for b in group_names] + (["down", "out1", "gdown", "gout0", "gout1"] if direct else []),
    )

    operands = dict(
        h_x0=tokens.reshape(g.tokens, width),
        h_cot=cotangent.reshape(g.tokens, width),
        lens=lengths.T,
        routes=routes[:, 0],
        slots=slots[:, 0],
        h_e_up=expert_up[0],
        h_e_down=expert_down[0],
    )
    if direct:
        operands |= dict(
            norm_gain=norm_gain,
            norm_bias=norm_bias,
            out_bias=attn_out_bias,
            down_bias=ffn_down_bias[None],
            up_bias=ffn_up_bias[None],
            router=router.T,
            h_wq=attn_qkv.transpose(0, 2, 1),
            h_wo=attn_out.transpose(0, 2, 1),
            h_wu=ffn_up.T,
            h_wd=ffn_down.T,
        )
    else:

        def every(array, axis):
            return lax.all_gather(array, BOTH, axis=axis, tiled=True)

        def part_of(array, axis, size):
            return lax.dynamic_slice_in_dim(array, sec * size, size, axis)

        rows = [norm_gain, norm_bias, attn_out_bias, ffn_down_bias[None], router.T]
        params = every(jnp.concatenate(rows, axis=0), 1)
        params = jnp.pad(params, ((0, LANES - kinds), (0, 0)))
        b_up = lax.all_gather(ffn_up_bias, "dp", axis=0, tiled=True).astype(F32)
        full = part_of(every(attn_qkv, 2).reshape(2, width, 3, width), 3, head_cols)
        operands |= dict(
            prm=params.astype(F32),
            w_router=params.T,
            b_up=b_up[None],
            w_qkv=full.transpose(0, 2, 3, 1).reshape(2, 3 * head_cols, width),
            w_out=part_of(every(attn_out, 2), 1, head_cols),
            w_up=lax.all_gather(ffn_up, "dp", axis=1, tiled=True).T,
            w_down=part_of(every(ffn_down, 1), 0, hidden).T,
        )
    res = run_layers(g, operands)

    if direct:
        names = list(vars(res))
        done = finish([getattr(res, name) for name in names])
        res = types.SimpleNamespace(**dict(zip(names, done, strict=True)))
        grads = (
            res.o_gain, res.o_bias, res.o_qkv.transpose(0, 2, 1), res.o_out.transpose(0, 2, 1), res.o_bout,
            res.o_up.T, res.o_bup[0], res.o_down.T, res.o_bdown[0], res.o_router.T,
        )
    else:

        def embed(array, shape, axis, size):
            return lax.dynamic_update_slice_in_dim(jnp.zeros(shape, F32), array, sec * size, axis)

        def share(array, axis, over=BOTH):
            return lax.psum_scatter(array, over, scatter_dimension=axis, tiled=True)

        small = share(res.o_small[:kinds], 1)
        g_qkv = res.o_qkv.reshape(2, 3, head_cols, width).transpose(0, 3, 1, 2)
        g_qkv = embed(g_qkv, (2, width, 3, width), 3, head_cols).reshape(2, width, 3 * width)
        g_out = embed(res.o_out, (2, width, width), 1, head_cols)
        g_down = embed(res.o_down.T, (hidden * sections, width), 0, hidden)
        grads = (
            small[0:4], small[4:8], share(g_qkv, 2), share(g_out, 2), small[8:10], share(res.o_up.T, 1, "dp"),
            share(res.o_bup[0], 0, "dp"), share(g_down, 1), small[10], small[FIRST_ROUTER:].T,
        )
    out_shape = (1, micro, 1, seq, width)
    return (
        res.sec_out.reshape(out_shape).astype(F32),
        res.sec_grad.reshape(out_shape).astype(F32),
        *grads,
        res.g_eup[None],
        res.g_edown[None],
    )


def solution(mesh):
    batch = P(None, "dp", None, None)
    table = P(None, "dp", None)
    in_specs = (
        batch, batch, P(None, "dp"), table, table,
        P(None, BOTH), P(None, BOTH), P(None, None, BOTH), P(None, None, BOTH), P(None, BOTH),
        P(None, BOTH), P(BOTH), P(None, BOTH), P(BOTH), P(BOTH, None),
        P("dp", None, "section"), P("dp", "section", None),
    )
    streams = P("section", None, "dp", None, None)
    out_specs = (
        streams, streams,
        P(None, BOTH), P(None, BOTH), P(None, None, BOTH), P(None, None, BOTH), P(None, BOTH),
        P(None, BOTH), P(BOTH), P(None, BOTH), P(BOTH), P(BOTH, None),
        P("dp", None, "section"), P("dp", "section", None),
    )
    return jax.shard_map(body, mesh=mesh, in_specs=in_specs, out_specs=out_specs, check_vma=False)
```

```python
import functools
import types

import jax
import jax.numpy as jnp
from jax import lax
from jax.experimental import pallas as pl
from jax.experimental.pallas import tpu as pltpu
from jax.sharding import PartitionSpec as P

HEADS = 12
HEAD_DIM = 64
EPS = 1e-05
MASKED = -1000000000.0
MESH = pl.DeviceIdType.MESH
F32 = jnp.float32
BF16 = jnp.bfloat16
LANES = 128


def dot_as(left, right, left_dim, right_dim):
    return lax.dot_general(
        left, right, (((left_dim,), (right_dim,)), ((), ())), preferred_element_type=F32
    )


def mm(left, right):
    return dot_as(left, right, 1, 0)


def mm_nt(left, right):
    return dot_as(left, right, 1, 1)


def mm_tn(left, right):
    return dot_as(left, right, 0, 0)


def normalize(values):
    center = values - jnp.mean(values, axis=-1, keepdims=True)
    spread = jnp.mean(center * center, axis=-1, keepdims=True)
    inverse = lax.rsqrt(spread + EPS)
    return center * inverse, inverse


def gelu_parts(pre):
    half = 0.5 + 0.5 * lax.erf(pre * 0.7071067811865476)
    density = jnp.exp(-0.5 * pre * pre) * 0.3989422804014327
    return pre * half, half + pre * density


TAIL = 8
GROUP = 32
FIRST_ROUTER = 11


def layers_kernel(g, names, *refs):
    r = types.SimpleNamespace(**dict(zip(names, refs, strict=True)))
    width, span, hidden, cols, head_cols = g.width, g.span, g.hidden, g.cols, g.head_cols
    sec = lax.axis_index("section")
    dev = lax.axis_index("dp")
    core = lax.rem(dev, 2)
    chip = lax.div(dev, 2)
    sib = dev + 1 - 2 * core
    quarter = g.quarter
    shard_rows = hidden // g.devices
    block_rows = g.chips * quarter

    def peer_section(offset):
        return lax.rem(sec + offset, g.sections)

    def from_section(offset):
        return lax.rem(sec + g.sections - offset, g.sections)

    def peer_chip(offset):
        return lax.rem(chip + offset, g.chips)

    def from_chip(offset):
        return lax.rem(chip + g.chips - offset, g.chips)

    def rows_at(index, size):
        return pl.ds(pl.multiple_of(index * size, size), size)

    def remote(source, target, send, arrive, where):
        return pltpu.make_async_remote_copy(
            src_ref=source, dst_ref=target, send_sem=send, recv_sem=arrive, device_id=where, device_id_type=MESH
        )

    def at_chip_core(index):
        return {"dp": 2 * index + core}

    started = []
    kept_back = {}

    def do_when(condition, action):
        if condition is None:
            action()
        else:
            pl.when(condition)(action)

    def launch(copy, buffer=None, when=None):
        do_when(when, copy.start)
        if buffer:
            kept_back.setdefault(buffer, []).append((copy, when))
        else:
            started.append((copy, when))

    def settle(buffer):
        for copy, when in kept_back.pop(buffer, []):
            do_when(when, copy.wait_send)

    barrier = pltpu.get_barrier_semaphore()
    partners = [(a, b) for a in range(g.sections) for b in range(g.chips) if a + b and (g.direct or a * b == 0)]
    for section_offset, chip_offset in partners:
        where = {"section": peer_section(section_offset), "dp": 2 * peer_chip(chip_offset) + core}
        pl.semaphore_signal(barrier, inc=1, device_id=where, device_id_type=MESH)
    pl.semaphore_signal(barrier, inc=1, device_id={"dp": sib}, device_id_type=MESH)

    def local(index, source, target):
        return pltpu.make_async_copy(source, target, r.local_s.at[index])

    held = vars(r)
    loads = {name: local(i, held["h_" + name], held[name]) for i, name in enumerate(g.loads)}
    stores = []

    def store(*some):
        for name in some:
            index = len(loads) + g.stores.index(name)
            stores.append(local(index, held[name], held["h_" + name]))
            stores[-1].start()

    for copy in loads.values():
        copy.start()

    def token_slice(micro):
        return slice(micro * g.seq, (micro + 1) * g.seq)

    def piece_at(micro, section):
        return pl.ds(pl.multiple_of(micro * g.seq + section * g.piece, g.piece), g.piece)

    def own(micro):
        return piece_at(micro, sec)

    def scatter_copy(slot, micro, offset):
        return remote(
            r.part.at[slot, piece_at(micro, peer_section(offset))], r.got.at[slot, micro, offset - 1],
            r.scat_s.at[0], r.scat_r.at[slot, micro], {"section": peer_section(offset)},
        )

    def all_pieces(slot, micro, arrive):
        place = r.got.at[slot, micro]
        remote(place, place, r.scat_s.at[0], arrive, {"section": peer_section(1)}).wait_recv()

    def scatter_start(slot, micro, value):
        r.part[slot, token_slice(micro), :] = value.astype(BF16)
        if slot != 7:
            r.mine[token_slice(micro), :] = value
        for offset in range(1, g.sections):
            scatter_copy(slot, micro, offset).start()

    def scatter_sum(slot, micro):
        at = own(micro)
        total = r.part[slot, at, :].astype(F32) if slot == 7 else r.mine[at, :]
        all_pieces(slot, micro, r.scat_r.at[slot, micro])
        for offset in range(1, g.sections):
            total = total + r.got[slot, micro, offset - 1].astype(F32)
        return total

    def gather_start(buffer, slot, sem, micro):
        place = buffer.at[slot, own(micro)]
        for offset in range(1, g.sections):
            remote(place, place, r.gath_s.at[0], r.gath_r.at[sem, micro], {"section": peer_section(offset)}).start()

    def gather_wait(buffer, slot, sem, micro):
        all_pieces(sem, micro, r.gath_r.at[sem, micro])

    def exchanges_left():
        for sem in (r.scat_s, r.gath_s):
            remote(r.got, r.got, sem.at[0], r.scat_r.at[0, 0], {"section": peer_section(1)}).wait_send()

    def pair_copy(name, source, target):
        index = g.pairs.index(name)
        return remote(source, target, r.pair_s.at[index], r.pair_r.at[index], {"dp": sib})

    def pair_start(name, source, target, buffer=None):
        launch(pair_copy(name, source, target), buffer)

    def pair_wait(name, target):
        pair_copy(name, target, target).wait_recv()

    def line_copy(name, source, target, offset, receiving):
        index = g.lines.index(name)
        where = from_chip(offset) if receiving else peer_chip(offset)
        return remote(
            source, target, r.line_s.at[index, offset - 1], r.line_r.at[index, offset - 1], at_chip_core(where)
        )

    last_chip = g.chips - 1
    is_end = lax.rem(chip, max(last_chip, 1)) == 0
    is_mid = lax.rem(chip, max(last_chip, 1)) != 0
    line_order = (2, 1, 3) if g.relay else range(1, g.chips)
    outward = jnp.clip(chip - 1, 0, 1)

    def near_to(offset):
        return {1: chip != last_chip, last_chip: chip != 0}.get(offset) if g.relay else None

    def near_from(offset):
        return {1: chip != 0, last_chip: chip != last_chip}.get(offset) if g.relay else None

    def spread_first(name, source, target, buffer=None):
        if g.relay:
            for offset, when in ((2, is_end), (1, chip == 2), (3, chip == 1)):
                launch(line_copy(name, source, target, offset, False), buffer, when)

    def spread_more(name, source, target, buffer=None):
        if g.relay:
            for offset, when in ((2, is_mid), (1, chip < 2), (3, chip > 1)):
                launch(line_copy(name, source, target, offset, False), buffer, when)
        else:
            for offset in line_order:
                launch(line_copy(name, source, target, offset, False), buffer)

    def spread_relay(name, place, buffer):
        index = g.lines.index(name)
        copy = remote(
            place, place, r.line_s.at[index, last_chip], r.line_r.at[index, outward * 2],
            at_chip_core(outward * last_chip),
        )
        launch(copy, buffer, is_mid)

    def spread_pass(name, place_at, buffer):
        if g.relay:
            place = place_at(from_chip(2))
            line_copy(name, place, place, 2, True).wait_recv()
            spread_relay(name, place, buffer)

    def spread_wait(name, place_at):
        for offset in (1, 3) if g.relay else line_order:
            place = place_at(from_chip(offset))
            line_copy(name, place, place, offset, True).wait_recv()

    def far_wait(name, place_at):
        for offset in (1, last_chip):
            place = place_at(from_chip(offset))
            copy = line_copy(name, place, place, offset, True)
            pl.when(jnp.logical_not(near_from(offset)))(copy.wait_recv)

    def line_start(name, source_at, target, buffer=None):
        for offset in range(1, g.chips):
            launch(line_copy(name, source_at(peer_chip(offset)), target, offset, False), buffer)

    def line_wait(name, target_at):
        for offset in range(1, g.chips):
            target = target_at(from_chip(offset), offset)
            line_copy(name, target, target, offset, True).wait_recv()

    def rows_plane_start(name, place_at, pair):
        for offset in range(1, g.parts):
            launch(plane_copy(name, place_at(0), place_at(offset), offset, False))
        pair_start(pair + "0", place_at(0), place_at(0))

    def rows_plane_wait(name, place, offset, pair):
        plane_copy(name, place, place, offset, True).wait_recv()
        pair_start(pair + str(offset), place, place)

    top = cols - TAIL
    half = width // 2
    part_cols = head_cols // 2
    tail_lane = head_cols + 2 * GROUP

    def qkv_section(at_dev, index, section):
        return lax.rem(lax.div(3 * at_dev + index, g.devices) - section + g.sections, g.sections)

    def qkv_send(layer, offsets):
        for index in range(3):
            to = qkv_section(dev, index, sec)
            for offset in offsets:
                copy = remote(
                    r.pq.at[layer, index], r.rq.at[layer, core, chip, index],
                    r.wq_s.at[index, offset + layer * g.chips], r.wq_r.at[index, offset + layer * g.chips],
                    {"section": to, "dp": 2 * peer_chip(offset) + core},
                )
                if offset:
                    launch(copy, None, near_to(offset))
                else:
                    pl.when(to != sec)(copy.start)

                    @pl.when(to == sec)
                    def _(index=index):
                        r.rq[layer, core, chip, index] = r.pq[layer, index]

    def qkv_arrive(layer, offsets):
        for offset in offsets:
            for index in range(3):
                at_chip = from_chip(offset)
                target = r.rq.at[layer, core, at_chip, index]
                origin = qkv_section(2 * at_chip + core, index, sec)
                copy = remote(
                    target, target, r.wq_s.at[index, offset + layer * g.chips],
                    r.wq_r.at[index, offset + layer * g.chips],
                    {"section": origin, "dp": 2 * at_chip + core},
                )
                if offset:
                    do_when(near_from(offset), copy.wait_recv)
                else:

                    @pl.when(origin != sec)
                    def _(copy=copy):
                        copy.wait_recv()
                        copy.wait_send()

            if g.relay and offset == 2:
                spread_relay("qkv0", r.rq.at[0, core, from_chip(offset)], "qkv0")
        if g.relay and len(offsets) > 1:
            far_wait("qkv0", lambda at: r.rq.at[0, core, at])

    def out_copy(section_offset, offset, place, receiving):
        if receiving:
            to, at_chip = from_section(section_offset), from_chip(offset)
        else:
            to, at_chip = peer_section(section_offset), peer_chip(offset)
        source = place if receiving else r.po.at[0, to]
        return remote(
            source, place, r.wo_s.at[section_offset, offset], r.wo_r.at[section_offset, offset],
            {"section": to, "dp": 2 * at_chip + core},
        )

    def out_offsets():
        return [(a, b) for b in (*line_order, 0) for a in range(g.sections) if a + b]

    def plane_copy(name, source, target, offset, receiving):
        index = g.planes.index(name)
        where = from_section(offset) if receiving else peer_section(offset)
        return remote(
            source, target, r.plane_s.at[index, offset - 1], r.plane_r.at[index, offset - 1], {"section": where}
        )

    def pack_wide(block):
        tail = jnp.concatenate([block[top:, :half], block[top:, half:]], axis=0)
        return jnp.concatenate([block[:top], tail], axis=1).astype(BF16)

    def pack_out(block):
        small = jnp.concatenate([block[top:, head_cols:]] * 2, axis=0)
        tail = jnp.concatenate([block[top:, :part_cols], block[top:, part_cols:head_cols]], axis=0)
        empty = jnp.zeros((top, g.out_lanes - tail_lane - part_cols), F32)
        return jnp.concatenate([block[:top], small, tail, empty], axis=1).astype(BF16)

    def unpack_wide(target, first, piece):
        target[first : first + top, 0:width] = piece[:, 0:width]
        target[first + top : first + cols, 0:half] = piece[0:TAIL, width : width + half]
        target[first + top : first + cols, half:width] = piece[TAIL:, width : width + half]

    def unpack_out(target, first, piece, lane=0):
        last = slice(first + top, first + cols)
        tail = slice(tail_lane, tail_lane + part_cols)
        target[first : first + top, lane : lane + head_cols] = piece[:, 0:head_cols]
        target[last, lane : lane + part_cols] = piece[0:TAIL, tail]
        target[last, lane + part_cols : lane + head_cols] = piece[TAIL:, tail]

    def unpack_small(target, first, piece, lane):
        target[first : first + top, lane : lane + GROUP] = piece[:, head_cols : head_cols + GROUP]
        target[first + top : first + cols, lane : lane + GROUP] = piece[0:TAIL, head_cols + GROUP : tail_lane]

    def shard_places():
        for at_core in range(2):
            for at_chip in range(g.chips):
                for at_sec in range(g.sections):
                    yield at_core, at_chip, at_sec, (at_sec * g.devices + 2 * at_chip + at_core) * cols

    def chunk_places():
        for at_core in range(2):
            for at_chip in range(g.chips):
                for index in range(3):
                    yield at_core, at_chip, index, (3 * (2 * at_chip + at_core) + index) * cols

    def unfold_out(layer):
        for at_core, at_chip, at_sec, first in shard_places():
            piece = r.ro[layer, at_core, at_chip, at_sec].astype(F32)
            if layer == 0:
                unpack_small(r.tmp, first, piece, head_cols)
            unpack_out(r.tmp, first, piece)
        flipped = r.tmp[:, 0:tail_lane].T
        r.w_out[layer] = flipped[:head_cols].astype(BF16)
        if layer == 0:
            r.prm[...] = flipped[head_cols : head_cols + GROUP]
            r.w_router[...] = r.tmp[:, tail_lane - LANES : tail_lane].astype(BF16)

    def unfold_qkv(layer):
        for at_core, at_chip, index, first in chunk_places():
            unpack_wide(r.tmp, first, r.rq[layer, at_core, at_chip, index].astype(F32))
        r.w_qkv[layer] = r.tmp[0 : 3 * head_cols, 0:width].astype(BF16)

    def unfold_down():
        for at_core, at_chip, at_sec, first in shard_places():
            unpack_wide(r.tmp, first, r.rd[at_core, at_chip, at_sec].astype(F32))
        r.w_down[...] = r.tmp[...].astype(BF16)

    def grad_line(name, buffer_at, landing, target, passed):
        pair_wait(name, landing)
        for at_chip in range(g.chips):
            block = buffer_at(at_chip)
            block[...] = (block[...].astype(F32) + landing[at_chip].astype(F32)).astype(BF16)
        if g.relay:
            index = g.lines.index(name)
            copy = remote(
                buffer_at(last_chip - chip), passed, r.line_s.at[index, last_chip], r.line_r.at[index, last_chip],
                at_chip_core(1 + lax.div(chip, last_chip)),
            )
            launch(copy, None, is_end)
            for offset in (1, last_chip):

                @pl.when(jnp.logical_not(near_from(offset)))
                def _(offset=offset):
                    target[offset - 1] = jnp.zeros_like(target[offset - 1])

        for offset in line_order:
            copy = line_copy(name, buffer_at(peer_chip(offset)), target.at[offset - 1], offset, False)
            if g.relay and offset == 2:
                pl.when(is_end)(copy.start)
                started.append((copy, None))
            else:
                launch(copy, None, near_to(offset))

    def grad_relay(name, buffer_at, target, passed):
        if g.relay:
            index = g.lines.index(name)
            block = buffer_at(peer_chip(2))
            copy = line_copy(name, block, target.at[1], 2, False)

            @pl.when(is_mid)
            def _():
                remote(
                    passed, passed, r.line_s.at[index, last_chip], r.line_r.at[index, last_chip],
                    at_chip_core(outward * last_chip),
                ).wait_recv()
                block[...] = (block[...].astype(F32) + passed[...].astype(F32)).astype(BF16)
                copy.start()

    def grad_line_sum(name, buffer_at, target):
        for offset in line_order:
            place = target.at[offset - 1]
            do_when(near_from(offset), line_copy(name, place, place, offset, True).wait_recv)
        total = buffer_at(chip)[...].astype(F32)
        for offset in range(1, g.chips):
            total = total + target[offset - 1].astype(F32)
        return total

    def qkv_at(layer):
        return lambda at: r.rq.at[layer, core, at]

    def down_at(at):
        return r.rd.at[core, at]

    def out_at(layer):
        return lambda at: r.ro.at[layer, core, at]

    def up_at(at):
        return r.ru.at[at, core]

    def bias_at(at):
        return r.rb.at[at, core]

    def grad_plane(name, buffer_at, target, summed, final):
        summed[...] = grad_line_sum(name, buffer_at, target).astype(BF16)
        for offset in range(1, g.sections):
            source = summed.at[peer_section(offset)]
            launch(plane_copy(name, source, final.at[sec], offset, False))
        final[sec] = summed[sec]

    def grad_plane_wait(name, final):
        for offset in range(1, g.sections):
            place = final.at[from_section(offset)]
            plane_copy(name, place, place, offset, True).wait_recv()

    def grad_qkv_copy(layer, index, place, where):
        return remote(
            r.mq.at[layer, index], place, r.gq_s.at[layer, index], r.gq_r.at[layer, index], {"section": where}
        )

    def grad_qkv_plane(layer):
        r.mq[layer] = grad_line_sum("gqkv" + str(layer), qkv_at(layer), r.aq.at[layer]).astype(BF16)
        for index in range(3):
            to = qkv_section(dev, index, sec)
            copy = grad_qkv_copy(layer, index, r.fq.at[layer, index], to)
            pl.when(to != sec)(copy.start)

            @pl.when(to == sec)
            def _(index=index):
                r.fq[layer, index] = r.mq[layer, index]

    def grad_qkv_finish(layer):
        for index in range(3):
            origin = qkv_section(dev, index, sec)
            copy = grad_qkv_copy(layer, index, r.fq.at[layer, index], origin)

            @pl.when(origin != sec)
            def _(copy=copy):
                copy.wait_recv()
                copy.wait_send()

            unpack_wide(r.o_qkv.at[layer], index * cols, r.fq[layer, index].astype(F32))

    def norm_into(source, target, index, micro):
        rows = g.seq // 2

        @pl.loop(0, 2)
        def _(step):
            at = rows_at(micro * 2 + step, rows)
            unit, _ = normalize(source[at, :].astype(F32))
            target[at, :] = (unit * r.prm[index : index + 1, :] + r.prm[4 + index : 5 + index, :]).astype(BF16)

    place_row = jnp.concatenate(
        [r.routes[m : m + 1] * span + m * g.cap + r.slots[m : m + 1] for m in range(g.micro)], axis=1
    )
    r.square[...] = jnp.zeros_like(r.square)
    if g.direct:
        r.square[0:4, 0:cols] = r.norm_gain[...].astype(F32)
        r.square[4:8, 0:cols] = r.norm_bias[...].astype(F32)
        r.square[8:10, 0:cols] = r.out_bias[...].astype(F32)
        r.square[10:11, 0:cols] = r.down_bias[...].astype(F32)
        r.pb[...] = jnp.zeros_like(r.pb)
        r.pb[:, 0:shard_rows] = jnp.broadcast_to(r.up_bias[...], (r.pb.shape[0], shard_rows))
        r.square[FIRST_ROUTER : FIRST_ROUTER + g.experts, 0:cols] = r.router[...].astype(F32)
        r.square[...] = r.square[...].T
        loads["wo"].wait()
        loads["wq"].wait()
        shard = r.wo[0].astype(F32)
        mine = r.square[0:cols, 0:GROUP]
        for at_sec in range(g.sections):
            block = shard[:, at_sec * head_cols : (at_sec + 1) * head_cols]
            r.po[0, at_sec] = pack_out(jnp.concatenate([block, mine], axis=1))
        shard = r.wq[0].astype(F32)
        for index in range(3):
            r.pq[0, index] = pack_wide(shard[index * cols : (index + 1) * cols])
    pl.semaphore_wait(barrier, len(partners) + 1)
    if g.direct:
        for section_offset, offset in out_offsets():
            launch(out_copy(section_offset, offset, r.ro.at[0, core, chip, sec], False), None, near_to(offset))
        r.ro[0, core, chip, sec] = r.po[0, sec]
        qkv_send(0, (*line_order, 0))
        loads["wu"].wait()
        loads["wd"].wait()
        shard = r.wq[1].astype(F32)
        for index in range(3):
            r.pq[1, index] = pack_wide(shard[index * cols : (index + 1) * cols])
        shard, other = r.wd[...].astype(F32), r.wo[1].astype(F32)
        empty = jnp.zeros((cols, GROUP), F32)
        for at_sec in range(g.sections):
            r.pd[at_sec] = pack_wide(shard[:, at_sec * hidden : (at_sec + 1) * hidden])
            block = other[:, at_sec * head_cols : (at_sec + 1) * head_cols]
            r.po[1, at_sec] = pack_out(jnp.concatenate([block, empty], axis=1))

    loads["x0"].wait()
    loads["cot"].wait()
    slot_ids = lax.broadcasted_iota(jnp.int32, (quarter, g.tokens), 0)

    def slot_match(expert, part, group):
        first = expert * span + group * (span // g.groups) + part * quarter
        return jnp.where(slot_ids + first == place_row, 1.0, 0.0).astype(BF16)

    def group_tokens(group):
        count = g.tokens // g.groups
        return slice(group * count, (group + 1) * count)

    for group in range(g.groups):
        for expert in range(g.chips):
            match = slot_match(expert, g.my_part(sec), group)
            r.table[group, expert * quarter : (expert + 1) * quarter, :] = match[:, group_tokens(group)]
        sent = mm(r.table[group], r.cot[group_tokens(group), :]).astype(BF16)
        r.dispc[:, group] = sent.reshape(g.chips, quarter, width)
    r.small[...] = jnp.zeros_like(r.small)
    if g.direct:
        for section_offset, offset in out_offsets():
            place = r.ro.at[0, core, from_chip(offset), from_section(section_offset)]
            do_when(near_from(offset), out_copy(section_offset, offset, place, True).wait_recv)
            if g.relay and (section_offset, offset) == (g.sections - 1, 2):
                spread_relay("out0", r.ro.at[0, core, from_chip(offset)], "out0")
        if g.relay:
            far_wait("out0", lambda at: r.ro.at[0, core, at])
        pair_start("out0", r.ro.at[0, core], r.ro.at[0, core], "out0")
        qkv_arrive(0, (*line_order, 0))
        pair_start("qkv0", r.rq.at[0, core], r.rq.at[0, core], "qkv0")
        spread_first("bias", r.pb, r.rb.at[chip, core])
        spread_more("bias", r.pb, r.rb.at[chip, core])
        r.rb[chip, core] = r.pb[...]
        spread_first("up", r.wu, r.ru.at[chip, core])
        r.ru[chip, core] = r.wu[...]
        for offset in range(1, g.sections):
            launch(plane_copy("down", r.pd.at[peer_section(offset)], r.rd.at[core, chip, sec], offset, False))
        r.rd[core, chip, sec] = r.pd[sec]
        qkv_send(1, [0])
        for offset in range(1, g.sections):
            place = r.ro.at[1, core, chip, sec]
            launch(plane_copy("out1", r.po.at[1, peer_section(offset)], place, offset, False))
        r.ro[1, core, chip, sec] = r.po[1, sec]
        pair_wait("out0", r.ro.at[0, 1 - core])
        unfold_out(0)
        pair_wait("qkv0", r.rq.at[0, 1 - core])
        unfold_qkv(0)

    def plane_arrive(name, place_at):
        for offset in range(1, g.sections):
            place = place_at(from_section(offset))
            plane_copy(name, place, place, offset, True).wait_recv()

    def up_place(at):
        return r.ru.at[at, core]

    def bias_place(at):
        return r.rb.at[at, core]

    def down_place(at):
        return r.rd.at[core, at]

    def qkv_place(at):
        return r.rq.at[1, core, at]

    def out_place(at):
        return r.ro.at[1, core, at]

    def own_first(name, place_at):
        spread_first(name, place_at(chip), place_at(chip), name)

    def own_more(name, place_at):
        spread_more(name, place_at(chip), place_at(chip), name)

    key_ids = lax.broadcasted_iota(jnp.int32, (g.seq, g.seq), 0)
    query_ids = lax.broadcasted_iota(jnp.int32, (g.seq, g.seq), 1)
    scale = HEAD_DIM**-0.5
    micros = range(g.micro)

    def block_of(index):
        return lax.rem(index + sec, 3) if g.direct else index

    def head_slice(head):
        return slice(head * HEAD_DIM, (head + 1) * HEAD_DIM)

    def attention_forward(layer, stream, slot, micro):
        at = token_slice(micro)
        norm_into(stream, r.normed.at[2 * layer], 2 * layer, micro)
        packed = mm_nt(r.w_qkv[layer], r.normed[2 * layer, at, :]).astype(BF16)
        r.qkv[layer, :, :, at] = packed.reshape(3, head_cols, g.seq)
        allowed = (key_ids <= query_ids) & (key_ids < r.lens[:, micro : micro + 1])
        for head in range(g.heads):
            key = r.qkv[layer, block_of(1), head_slice(head), at]
            scores = mm_tn(key, r.qkv[layer, block_of(0), head_slice(head), at]) * scale
            scores = jnp.where(allowed, scores, MASKED)
            weight = jnp.exp(scores - jnp.max(scores, axis=0, keepdims=True))
            weight = weight / jnp.sum(weight, axis=0, keepdims=True)
            r.probs[layer, micro, head] = weight
            value = r.qkv[layer, block_of(2), head_slice(head), at]
            r.ctx[layer, head_slice(head), at] = mm(value, weight.astype(BF16)).astype(BF16)
        scatter_start(slot, micro, mm_tn(r.ctx[layer, :, at], r.w_out[layer]))

    def finish_forward(section, bias, stream, micro):
        total = scatter_sum(section, micro) + bias + stream[own(micro), :].astype(F32)
        r.xs[section, own(micro), :] = total.astype(BF16)
        gather_start(r.xs, section, section, micro)

    for micro in micros:
        attention_forward(0, r.x0, 0, micro)
        if g.direct and micro == 0:
            spread_more("up", r.wu, r.ru.at[chip, core])
    if g.direct:
        spread_pass("bias", bias_place, "bias")
        spread_pass("up", up_place, "up")
        plane_arrive("down", lambda at: r.rd.at[core, chip, at])
        own_first("down", down_place)
    for micro in micros:
        finish_forward(0, r.prm[8:9, :], r.x0, micro)
    if g.direct:
        own_more("down", down_place)
        spread_wait("bias", bias_place)
        spread_wait("up", up_place)
        pair_start("up", r.ru.at[:, core], r.ru.at[:, core], "up")
        pair_start("bias", r.rb.at[:, core], r.rb.at[:, core], "bias")
        pair_wait("up", r.ru.at[:, 1 - core])
        pair_wait("bias", r.rb.at[:, 1 - core])
        for at_dev in range(g.devices):
            row = r.rb[at_dev // 2, at_dev % 2, :, 0:shard_rows].astype(F32)
            r.b_up[:, at_dev * shard_rows : (at_dev + 1) * shard_rows] = row[0:TAIL]

    def up_rows(at):
        if g.direct:
            return r.ru[...].reshape(hidden, width)[at]
        return r.w_up[at, :]

    def hidden_blocks():
        return [slice(first, first + g.block) for first in range(0, hidden, g.block)]

    for micro in micros:
        rows = token_slice(micro)
        gather_wait(r.xs, 0, 0, micro)
        norm_into(r.xs.at[0], r.normed.at[1], 1, micro)
        for at in hidden_blocks():
            value, slope = gelu_parts(mm_nt(r.normed[1, rows, :], up_rows(at)) + r.b_up[0:1, at])
            r.act[rows, at] = value.astype(BF16)
            r.dgelu[rows, at] = slope
        if g.direct and micro == 0:
            spread_pass("down", down_place, "down")
            qkv_arrive(1, [0])
            own_first("qkv1", qkv_place)
            own_more("qkv1", qkv_place)
    if g.direct:
        spread_wait("down", down_place)
        pair_start("down", r.rd.at[core], r.rd.at[core], "down")
        plane_arrive("out1", lambda at: r.ro.at[1, core, chip, at])
        own_first("out1", out_place)
        own_more("out1", out_place)
        pair_wait("down", r.rd.at[1 - core])
        unfold_down()
    for micro in micros:
        scatter_start(1, micro, mm_nt(r.act[token_slice(micro), :], r.w_down[...]))
    if g.direct:
        spread_pass("qkv1", qkv_place, "qkv1")
    for micro in micros:
        finish_forward(1, r.prm[10:11, :], r.xs.at[0], micro)
        if g.direct and micro == 0:
            spread_pass("out1", out_place, "out1")
    if g.direct:
        spread_wait("qkv1", qkv_place)
        pair_start("qkv1", r.rq.at[1, core], r.rq.at[1, core], "qkv1")
        spread_wait("out1", out_place)
        pair_start("out1", r.ro.at[1, core], r.ro.at[1, core], "out1")

    def crow_at(part, side):
        return r.crow.at[:, part, side]

    def crow_line(offset, receiving):
        at_chip = from_chip(offset) if receiving else peer_chip(offset)
        place = r.crow.at[:, 0, core, rows_at(at_chip if receiving else chip, quarter)]
        return line_copy("crow", place if receiving else r.dispc.at[at_chip], place, offset, receiving)

    for offset in range(1, g.chips):
        launch(crow_line(offset, False))
    r.crow[:, 0, core, rows_at(chip, quarter), :] = r.dispc[chip]

    if g.direct:
        pair_wait("qkv1", r.rq.at[1, 1 - core])
        unfold_qkv(1)
        pair_wait("out1", r.ro.at[1, 1 - core])
        unfold_out(1)
    for micro in micros:
        gather_wait(r.xs, 1, 1, micro)
        attention_forward(1, r.xs.at[1], 2, micro)
    for micro in micros:
        finish_forward(2, r.prm[9:10, :], r.xs.at[1], micro)
    r.square[0 : g.micro, :] = jnp.concatenate(
        [place_row[:, token_slice(micro)] for micro in micros], axis=0
    ).astype(F32)
    columns = r.square[...].T

    wide = r.wide

    def gates(micro):
        at = token_slice(micro)
        norm_into(r.xs.at[2], wide.at[:, pl.ds(0, width)], 3, micro)
        logits = mm(wide[at, :width], r.w_router[...])
        lane = lax.broadcasted_iota(jnp.int32, logits.shape, 1) - g.router_lane
        place_col = columns[:, micro : micro + 1].astype(jnp.int32)
        chosen = (place_col >= lane * span) & (place_col < lane * span + span)
        score = jnp.sum(jnp.where(chosen, logits, 0.0), axis=-1, keepdims=True)
        gate = 1.0 / (1.0 + jnp.exp(-score))
        gate_high = gate.astype(BF16).astype(F32)
        lane = lax.broadcasted_iota(jnp.int32, (g.seq, LANES), 1)
        pair = jnp.where(lane == 0, gate_high, jnp.where(lane == 1, gate - gate_high, 0.0))
        wide[at, width:] = pair.astype(BF16)

    groups = range(g.groups)

    def rows_place(group, side):
        return lambda part: r.rows.at[group, part, side]

    def rows_line_start(group):
        name = "rows" + str(group)
        r.disp[group] = mm(r.table[group], wide[group_tokens(group), :]).astype(BF16)
        place = r.rows.at[group, 0, core, rows_at(chip, quarter)]
        line_start(name, lambda at: r.disp.at[group, rows_at(at, quarter)], place)
        r.rows[group, 0, core, rows_at(chip, quarter), :] = r.disp[group, rows_at(chip, quarter), :]

    def rows_line_wait(group):
        name = "rows" + str(group)
        mine = r.rows.at[group, 0, core]
        line_wait(name, lambda at, _: mine.at[rows_at(at, quarter)])
        rows_plane_start(name, rows_place(group, core), name)

    for micro in micros:
        gather_wait(r.xs, 2, 2, micro)
        if micro == 0:
            for offset in range(1, g.chips):
                crow_line(offset, True).wait_recv()
            rows_plane_start("crow", lambda part: crow_at(part, core), "crow")
        gates(micro)
        if g.groups > 1:
            rows_line_start(micro)
    if g.groups == 1:
        rows_line_start(0)
    for group in groups:
        rows_line_wait(group)
    loads["e_up"].wait()
    loads["e_down"].wait()

    own_router = FIRST_ROUTER + chip
    router_row = r.prm[pl.ds(own_router, 1), :]
    snd = dict(d=r.snd_d, y=r.snd_y)
    kept = dict(d=r.keep_d, y=r.keep_y)
    rcv = dict(d=r.rcv_d, y=r.rcv_y)

    def expert_block(wide_rows, cot_rows):
        row = wide_rows[:, :width]
        tail = wide_rows[:, width:].astype(F32)
        gate_row = tail[:, 0:1] + tail[:, 1:2]
        grad_row = (gate_row * cot_rows.astype(F32)).astype(BF16)
        value, slope = gelu_parts(mm(row, r.e_up[...]))
        value = value.astype(BF16)
        result = mm(value, r.e_down[...])
        total = jnp.sum(grad_row.astype(F32) * result, axis=-1, keepdims=True) * (1.0 - gate_row)
        inner = (slope * mm_nt(grad_row, r.e_down[...])).astype(BF16)
        back = mm_nt(inner, r.e_up[...]) + total * router_row
        r.small[pl.ds(own_router, 1), :] += jnp.sum(row.astype(F32) * total, axis=0, keepdims=True)
        return grad_row, value, inner, back, result * gate_row

    def expert_parts(group, first, count):
        parts = slice(first, first + count)
        each = 2 * block_rows
        if each <= g.block:
            lead = (count, 2, block_rows)
            found = expert_block(
                r.rows[group, parts].reshape(count * each, width + LANES),
                r.crow[group, parts].reshape(count * each, width),
            )
            for target, value in zip((r.grow, r.acte, r.dpree), found[:3], strict=True):
                target[group, parts] = value.reshape(*lead, value.shape[-1])
            r.both[0, parts] = found[3].reshape(*lead, width)
            r.both[1, parts] = found[4].reshape(*lead, width)
        else:
            for part in range(first, first + count):
                for side in range(2):

                    @pl.loop(0, block_rows // g.block)
                    def _(step, part=part, side=side):
                        at = rows_at(step, g.block)
                        found = expert_block(r.rows[group, part, side, at, :], r.crow[group, part, side, at, :])
                        for target, value in zip((r.grow, r.acte, r.dpree), found[:3], strict=True):
                            target[group, part, side, at, :] = value
                        r.both[0, part, side, at, :] = found[3]
                        r.both[1, part, side, at, :] = found[4]

        for which, value in (("d", r.both.at[0]), ("y", r.both.at[1])):
            for part in range(first, first + count):
                snd[which][group, part] = value[part, 1 - core].astype(BF16)
                place = rcv[which].at[group, part]
                pair_start(which + str(group) + str(part), snd[which].at[group, part], place)
                kept[which][group, part] = value[part, core]

    def merge(which, offset, group):
        pair_wait(which + str(group) + str(offset), rcv[which].at[group, offset])
        return kept[which][group, offset] + rcv[which][group, offset].astype(F32)

    def merge_send(offset, group):
        to = g.sections - offset
        r.out_d[offset - 1, group] = merge("d", offset, group).astype(BF16)
        name = "d" + str(group)
        launch(plane_copy(name, r.out_d.at[offset - 1, group], r.plane_d.at[to - 1, group], to, False))

    def parts_work(group, first, count):
        for part in range(first, first + count):
            if group == 0:
                pair_wait("crow" + str(part), crow_at(part, 1 - core))
            pair_wait("rows" + str(group) + str(part), rows_place(group, 1 - core)(part))
        expert_parts(group, first, count)

    def results_line(group):
        for offset in range(g.parts):
            r.ret_y[group, offset] = merge("y", offset, group).astype(BF16)
        name = "y" + str(group)
        line_start(name, lambda at: r.ret_y.at[group, :, rows_at(at, quarter)], r.back_y.at[chip, group])
        r.back_y[chip, group] = r.ret_y[group, :, rows_at(chip, quarter), :]

    def expert_back_line(group):
        name = "d" + str(group)
        total = merge("d", 0, group)
        if g.parts > 1:
            for offset in range(1, g.sections):
                place = r.plane_d.at[offset - 1, group]
                plane_copy(name, place, place, offset, True).wait_recv()
                total = total + place[...].astype(F32)
        r.ret_d[group] = total.astype(BF16)
        place = r.back_d.at[group, rows_at(chip, quarter)]
        line_start(name, lambda at: r.ret_d.at[group, rows_at(at, quarter)], place)
        r.back_d[group, rows_at(chip, quarter), :] = r.ret_d[group, rows_at(chip, quarter), :]

    def expert_combine(group):
        line_wait("d" + str(group), lambda at, _: r.back_d.at[group, rows_at(at, quarter)])
        value = mm_tn(r.table[group], r.back_d[group])
        if g.groups > 1:
            scatter_start(3, group, value)
        else:
            for micro in micros:
                scatter_start(3, micro, value[token_slice(micro)])

    def results_combine():
        for group in groups:
            line_wait("y" + str(group), lambda at, _: r.back_y.at[at, group])
        places = [(e, q, p) for e in range(g.chips) for q in groups for p in range(g.parts)]
        match = [slot_match(e, g.my_part(from_section(p)), q) for e, q, p in places]
        match = jnp.concatenate(match, axis=0)
        value = mm_tn(match, r.back_y[...].reshape(g.chips * span, width))
        for micro in micros:
            scatter_start(7, micro, value[token_slice(micro)])

    offsets = range(1, g.parts)
    for group in groups:
        parts_work(group, 0, 1)
    for offset in offsets:
        rows_plane_wait("crow", crow_at(offset, core), offset, "crow")
    for group in groups:
        name = "rows" + str(group)
        for offset in offsets:
            rows_plane_wait(name, rows_place(group, core)(offset), offset, name)
        if g.parts > 1:
            parts_work(group, 1, g.parts - 1)
        for offset in offsets:
            merge_send(offset, group)
        if group < g.groups - 1:
            results_line(group)
    for group in groups:
        expert_back_line(group)

    def expert_weights(left, right):
        rows = g.groups * g.parts * 2 * block_rows
        return mm_tn(left.reshape(rows, left.shape[-1]), right.reshape(rows, right.shape[-1]))

    r.g_eup[...] = expert_weights(r.rows[:, :, :, :, :width], r.dpree[...])
    r.g_edown[...] = expert_weights(r.acte[...], r.grow[...])
    store("g_eup", "g_edown")

    def add_small(index, micro, value):
        if micro == 0:
            r.small[index : index + 1, :] = value
        else:
            r.small[index : index + 1, :] += value

    def finish_backward(section, slot, stream, above, micro):
        grad = scatter_sum(slot, micro)
        unit, inverse = normalize(stream[own(micro), :].astype(F32))
        add_small(section, micro, jnp.sum(grad * unit, axis=0, keepdims=True))
        add_small(4 + section, micro, jnp.sum(grad, axis=0, keepdims=True))
        grad = grad * r.prm[section : section + 1, :]
        shared = jnp.mean(grad, axis=-1, keepdims=True)
        along = jnp.mean(grad * unit, axis=-1, keepdims=True)
        grad = inverse * (grad - shared - unit * along) + above[own(micro), :].astype(F32)
        r.gs[section, own(micro), :] = grad.astype(BF16)
        gather_start(r.gs, section, 4 + section, micro)

    for group in groups:
        expert_combine(group)
    results_line(g.groups - 1)
    for micro in micros:
        finish_backward(3, 3, r.xs.at[2], r.cot, micro)

    def bias_row(index, section):
        for micro in micros:
            value = r.gs[section, own(micro), :].astype(F32)
            add_small(index, micro, jnp.sum(value, axis=0, keepdims=True))

    def attention_backward(layer, section, slot, micro):
        at = token_slice(micro)
        dctx = mm_nt(r.w_out[layer], r.gs[section + 1, at, :]).astype(BF16)
        for head in range(g.heads):
            weight = r.probs[layer, micro, head]
            low = weight.astype(BF16)
            dhead = dctx[head_slice(head)]
            query = r.qkv[layer, block_of(0), head_slice(head), at]
            key = r.qkv[layer, block_of(1), head_slice(head), at]
            value = r.qkv[layer, block_of(2), head_slice(head), at]
            dprobs = mm_tn(value, dhead)
            delta = jnp.sum(weight * dprobs, axis=0, keepdims=True)
            dscores = (weight * (dprobs - delta)).astype(BF16)
            r.dqkv[block_of(0), head_slice(head), at] = (mm(key, dscores) * scale).astype(BF16)
            r.dqkv[block_of(1), head_slice(head), at] = (mm_nt(query, dscores) * scale).astype(BF16)
            r.dqkv[block_of(2), head_slice(head), at] = mm_nt(dhead, low).astype(BF16)
        flat_grad = r.dqkv[:, :, at].reshape(3 * head_cols, g.seq)
        scatter_start(slot, micro, mm_tn(flat_grad, r.w_qkv[layer]))

    def attention_weights(layer, section):
        grad_qkv = mm(r.dqkv[...].reshape(3 * head_cols, g.tokens), r.normed[2 * layer])
        if not g.direct:
            r.o_qkv[layer] = grad_qkv
            r.o_out[layer] = mm(r.ctx[layer], r.gs[section + 1])
            return
        r.tmp[0 : 3 * head_cols, :] = grad_qkv
        settle("qkv" + str(layer))
        for at_core, at_chip, index, first in chunk_places():
            r.rq[layer, at_core, at_chip, index] = pack_wide(r.tmp[first : first + cols, :])
        name = "gqkv" + str(layer)
        pair_start(name, r.rq.at[layer, 1 - core], r.hq.at[layer])
        r.tmp[:, 0:head_cols] = dot_as(r.gs[section + 1], r.ctx[layer], 0, 1)
        if layer:
            r.tmp[:, head_cols : head_cols + GROUP] = jnp.zeros((width, GROUP), F32)
            out_weights(1)

    def out_weights(layer):
        settle("out" + str(layer))
        for at_core, at_chip, at_sec, first in shard_places():
            block = r.tmp[first : first + cols, 0 : head_cols + GROUP]
            r.ro[layer, at_core, at_chip, at_sec] = pack_out(block)
        pair_start("gout" + str(layer), r.ro.at[layer, 1 - core], r.ho.at[layer])

    for micro in micros:
        gather_wait(r.gs, 3, 7, micro)
        attention_backward(1, 2, 4, micro)
    bias_row(9, 3)
    attention_weights(1, 2)
    if g.direct:
        grad_line("gqkv1", qkv_at(1), r.hq.at[1], r.aq.at[1], r.lq.at[1])
    finish_backward(2, 4, r.xs.at[1], r.gs.at[3], 0)
    if g.direct:
        grad_line("gout1", out_at(1), r.ho.at[1], r.ao.at[1], r.lo.at[1])
    for micro in micros[1:]:
        finish_backward(2, 4, r.xs.at[1], r.gs.at[3], micro)

    for micro in micros:
        rows = token_slice(micro)
        gather_wait(r.gs, 2, 6, micro)
        grad_two = r.gs[2, rows, :]
        for at in hidden_blocks():
            r.dpre[rows, at] = (r.dgelu[rows, at] * mm(grad_two, r.w_down[:, at])).astype(BF16)
        scatter_start(5, micro, mm(r.dpre[rows, :], up_rows(slice(None))))
    bias_row(10, 2)
    sum_up = jnp.sum(r.dpre[...].astype(F32), axis=0, keepdims=True)
    if g.direct:
        grad_relay("gqkv1", qkv_at(1), r.aq.at[1], r.lq.at[1])
        grad_relay("gout1", out_at(1), r.ao.at[1], r.lo.at[1])
        r.tmp[...] = mm_tn(r.gs[2], r.act[...])
        settle("down")
        for at_core, at_chip, at_sec, first in shard_places():
            r.rd[at_core, at_chip, at_sec] = pack_wide(r.tmp[first : first + cols, :])
        pair_start("gdown", r.rd.at[1 - core], r.hd)
        settle("up")
        settle("bias")
        r.ru[...] = mm_tn(r.dpre[...], r.normed[1]).astype(BF16).reshape(r.ru.shape)
        pair_start("gup", r.ru.at[:, 1 - core], r.hu)
        for at_dev in range(g.devices):
            row = sum_up[:, at_dev * shard_rows : (at_dev + 1) * shard_rows]
            row = jnp.broadcast_to(row, (r.pb.shape[0], shard_rows)).astype(BF16)
            r.rb[at_dev // 2, at_dev % 2, :, 0:shard_rows] = row
        pair_start("gbias", r.rb.at[:, 1 - core], r.hb)
        grad_line("gdown", down_at, r.hd, r.ad, r.ld)
    else:
        r.o_down[...] = mm_tn(r.gs[2], r.act[...])
        r.o_up[...] = mm_tn(r.dpre[...], r.normed[1])
        r.o_bup[...] = sum_up
    for micro in micros:
        finish_backward(1, 5, r.xs.at[0], r.gs.at[2], micro)
    if g.direct:
        grad_line("gbias", bias_at, r.hb, r.ab, r.lb)
        grad_relay("gdown", down_at, r.ad, r.ld)

    for micro in micros:
        gather_wait(r.gs, 1, 5, micro)
        attention_backward(0, 0, 6, micro)
    bias_row(8, 1)
    attention_weights(0, 0)
    finish_backward(0, 6, r.x0, r.gs.at[1], 0)
    if g.direct:
        grad_line("gqkv0", qkv_at(0), r.hq.at[0], r.aq.at[0], r.lq.at[0])
    for micro in micros[1:]:
        finish_backward(0, 6, r.x0, r.gs.at[1], micro)
    if g.direct:
        kinds = r.small[...]
        padded = jnp.concatenate([kinds, jnp.zeros((LANES - kinds.shape[0], width), F32)], axis=0)
        r.tmp[:, head_cols : head_cols + GROUP] = padded.T[:, 0:GROUP]
        out_weights(0)
        grad_line("gout0", out_at(0), r.ho.at[0], r.ao.at[0], r.lo.at[0])
        grad_line("gup", up_at, r.hu, r.au, r.lu)
        grad_relay("gbias", bias_at, r.ab, r.lb)
    results_combine()
    if g.direct:
        grad_qkv_plane(1)
        grad_plane("gout1", out_at(1), r.ao.at[1], r.mo.at[1], r.fo.at[1])
        grad_plane("gdown", down_at, r.ad, r.md, r.fd)
        grad_relay("gqkv0", qkv_at(0), r.aq.at[0], r.lq.at[0])
        grad_relay("gout0", out_at(0), r.ao.at[0], r.lo.at[0])
    for micro in micros:
        r.xs[3, own(micro), :] = (scatter_sum(7, micro) + r.xs[2, own(micro), :].astype(F32)).astype(BF16)
        gather_start(r.xs, 3, 3, micro)
    if g.direct:
        grad_relay("gup", up_at, r.au, r.lu)
    for micro in micros:
        gather_wait(r.xs, 3, 3, micro)
        gather_wait(r.gs, 0, 4, micro)
    r.sec_out[...] = r.xs[sec]
    r.sec_grad[...] = r.gs[sec]
    store("sec_out", "sec_grad")
    if g.direct:
        grad_qkv_plane(0)
        grad_plane("gout0", out_at(0), r.ao.at[0], r.mo.at[0], r.fo.at[0])
        grad_qkv_finish(1)
        grad_plane_wait("gdown", r.fd)
        for at_sec in range(g.sections):
            piece = r.fd[at_sec].astype(F32)
            unpack_wide(r.o_down.at[:, pl.ds(at_sec * hidden, hidden)], 0, piece)
        store("o_down")
        r.o_up[...] = grad_line_sum("gup", up_at, r.au)
        r.o_bup[...] = grad_line_sum("gbias", bias_at, r.ab)[0:1, 0:shard_rows]
        store("o_up", "o_bup")
        grad_plane_wait("gout1", r.fo.at[1])
        for at_sec in range(g.sections):
            unpack_out(r.o_out.at[1], 0, r.fo[1, at_sec].astype(F32), at_sec * head_cols)
        grad_qkv_finish(0)
        store("o_qkv")
        grad_plane_wait("gout0", r.fo.at[0])
        everyone = jnp.zeros((top, g.out_lanes), F32)
        for at_sec in range(g.sections):
            piece = r.fo[0, at_sec].astype(F32)
            unpack_out(r.o_out.at[0], 0, piece, at_sec * head_cols)
            everyone = everyone + piece
        r.square[...] = jnp.zeros_like(r.square)
        unpack_small(r.square, 0, everyone, 0)
        r.square[...] = r.square[...].T
        r.o_router[...] = r.square[FIRST_ROUTER : FIRST_ROUTER + g.experts, 0:cols]
        r.o_gain[...] = r.square[0:4, 0:cols]
        r.o_bias[...] = r.square[4:8, 0:cols]
        r.o_bout[...] = r.square[8:10, 0:cols]
        r.o_bdown[...] = r.square[10:11, 0:cols]
        store("o_out", "o_gain", "o_bias", "o_bout", "o_bdown", "o_router")
    else:
        r.o_small[...] = r.small[...]
        store("o_qkv", "o_out", "o_up", "o_down", "o_bup", "o_small")
    for copy in stores:
        copy.wait()
    exchanges_left()
    for copy, when in started:
        do_when(when, copy.wait_send)


def run_layers(g, operands):
    tokens, width, hidden, sections, chips = g.tokens, g.width, g.hidden, g.sections, g.chips
    part_rows = chips * g.quarter
    inner = operands["h_e_down"].shape[0]
    three = 3 * g.head_cols
    shape = jax.ShapeDtypeStruct
    vmem = pltpu.VMEM
    dma = pltpu.SemaphoreType.DMA
    top = g.cols - TAIL
    wide = width + width // 2
    up_rows = hidden // g.devices
    outs = dict(
        sec_out=shape((tokens, width), BF16),
        sec_grad=shape((tokens, width), BF16),
        g_eup=shape((width, inner), F32),
        g_edown=shape((inner, width), F32),
    )
    if g.direct:
        outs |= dict(
            o_qkv=shape((2, 3 * g.cols, width), F32),
            o_out=shape((2, g.cols, width), F32),
            o_up=shape((up_rows, width), F32),
            o_down=shape((g.cols, sections * hidden), F32),
            o_gain=shape((4, g.cols), F32),
            o_bias=shape((4, g.cols), F32),
            o_bout=shape((2, g.cols), F32),
            o_bdown=shape((1, g.cols), F32),
            o_router=shape((g.experts, g.cols), F32),
            o_bup=shape((1, up_rows), F32),
        )
    else:
        outs |= dict(
            o_qkv=shape((2, three, width), F32),
            o_out=shape((2, g.head_cols, width), F32),
            o_up=shape((hidden, width), F32),
            o_down=shape((width, hidden), F32),
            o_bup=shape((1, hidden), F32),
            o_small=shape((g.small, width), F32),
        )
    scratch = dict(
        xs=vmem((4, tokens, width), BF16),
        gs=vmem((4, tokens, width), BF16),
        normed=vmem((3, tokens, width), BF16),
        wide=vmem((tokens, width + LANES), BF16),
        qkv=vmem((2, 3, g.head_cols, tokens), BF16),
        probs=vmem((2, g.micro, g.heads, g.seq, g.seq), F32),
        ctx=vmem((2, g.head_cols, tokens), BF16),
        act=vmem((tokens, hidden), BF16),
        dgelu=vmem((tokens, hidden), F32),
        dpre=vmem((tokens, hidden), BF16),
        dqkv=vmem((3, g.head_cols, tokens), BF16),
        part=vmem((8, tokens, width), BF16),
        got=vmem((8, g.micro, sections - 1, g.piece, width), BF16),
        mine=vmem((tokens, width), F32),
        square=vmem((LANES, LANES), F32),
        table=vmem((g.groups, part_rows, tokens // g.groups), BF16),
        disp=vmem((g.groups, part_rows, width + LANES), BF16),
        dispc=vmem((chips, g.groups, g.quarter, width), BF16),
        rows=vmem((g.groups, g.parts, 2, part_rows, width + LANES), BF16),
        crow=vmem((g.groups, g.parts, 2, part_rows, width), BF16),
        grow=vmem((g.groups, g.parts, 2, part_rows, width), BF16),
        acte=vmem((g.groups, g.parts, 2, part_rows, inner), BF16),
        dpree=vmem((g.groups, g.parts, 2, part_rows, inner), BF16),
        both=vmem((2, g.parts, 2, part_rows, width), F32),
        small=vmem((g.small, width), F32),
        local_s=dma((len(g.loads) + len(outs),)),
    )
    g.stores = list(outs)
    for name, out in outs.items():
        scratch[name] = vmem(out.shape, out.dtype)
    for name in g.loads:
        scratch[name] = vmem(operands["h_" + name].shape, BF16)
    for which in ("d", "y"):
        scratch["keep_" + which] = vmem((g.groups, g.parts, part_rows, width), F32)
        for name in ("snd_", "rcv_"):
            scratch[name + which] = vmem((g.groups, g.parts, part_rows, width), BF16)
    scratch |= dict(
        out_d=vmem((sections - 1, g.groups, part_rows, width), BF16),
        plane_d=vmem((sections - 1, g.groups, part_rows, width), BF16),
        ret_d=vmem((g.groups, part_rows, width), BF16),
        back_d=vmem((g.groups, part_rows, width), BF16),
        ret_y=vmem((g.groups, g.parts, part_rows, width), BF16),
        back_y=vmem((chips, g.groups, g.parts, g.quarter, width), BF16),
    )
    scratch |= dict(scat_s=dma((1,)), gath_s=dma((1,)), scat_r=dma((8, g.micro)), gath_r=dma((8, g.micro)))
    for name, count, each in (("pair", len(g.pairs), 0), ("line", len(g.lines), chips), ("plane", len(g.planes), sections - 1)):
        sizes = (count, each) if each else (count,)
        scratch |= {name + "_s": dma(sizes), name + "_r": dma(sizes)}
    if g.direct:
        piece = (top, wide)
        out_piece = (top, g.out_lanes)
        up_piece = (up_rows, width)
        bias_piece = (2 * TAIL, LANES)
        scratch |= dict(
            pq=vmem((2, 3, *piece), BF16),
            po=vmem((2, sections, *out_piece), BF16),
            pb=vmem(bias_piece, BF16),
            rb=vmem((chips, 2, *bias_piece), BF16),
            hb=vmem((chips, *bias_piece), BF16),
            ab=vmem((chips - 1, *bias_piece), BF16),
            lb=vmem(bias_piece, BF16),
            lq=vmem((2, 3, *piece), BF16),
            lo=vmem((2, sections, *out_piece), BF16),
            lu=vmem(up_piece, BF16),
            ld=vmem((sections, *piece), BF16),
            pd=vmem((sections, *piece), BF16),
            rq=vmem((2, 2, chips, 3, *piece), BF16),
            ro=vmem((2, 2, chips, sections, *out_piece), BF16),
            ru=vmem((chips, 2, *up_piece), BF16),
            rd=vmem((2, chips, sections, *piece), BF16),
            w_qkv=vmem((2, three, width), BF16),
            w_out=vmem((2, g.head_cols, width), BF16),
            w_down=vmem((width, hidden), BF16),
            w_router=vmem((width, LANES), BF16),
            b_up=vmem((8, hidden), F32),
            prm=vmem((GROUP, width), F32),
            tmp=vmem((width, width), F32),
            hq=vmem((2, chips, 3, *piece), BF16),
            ho=vmem((2, chips, sections, *out_piece), BF16),
            hu=vmem((chips, *up_piece), BF16),
            hd=vmem((chips, sections, *piece), BF16),
            aq=vmem((2, chips - 1, 3, *piece), BF16),
            ao=vmem((2, chips - 1, sections, *out_piece), BF16),
            au=vmem((chips - 1, *up_piece), BF16),
            ad=vmem((chips - 1, sections, *piece), BF16),
            mq=vmem((2, 3, *piece), BF16),
            mo=vmem((2, sections, *out_piece), BF16),
            md=vmem((sections, *piece), BF16),
            fq=vmem((2, 3, *piece), BF16),
            fo=vmem((2, sections, *out_piece), BF16),
            fd=vmem((sections, *piece), BF16),
            wq_s=dma((3, chips + 1)),
            wq_r=dma((3, chips + 1)),
            wo_s=dma((sections, chips)),
            wo_r=dma((sections, chips)),
            gq_s=dma((2, 3)),
            gq_r=dma((2, 3)),
        )
    whole = pl.BlockSpec(memory_space=pltpu.VMEM)
    placed = pl.BlockSpec(memory_space=pl.ANY)
    apart = ["h_" + name for name in g.loads]
    names = (*operands, *("h_" + name for name in outs), *scratch)
    results = pl.pallas_call(
        functools.partial(layers_kernel, g, names),
        out_shape=tuple(outs.values()),
        in_specs=[placed if name in apart else whole for name in operands],
        out_specs=[placed] * len(outs),
        scratch_shapes=list(scratch.values()),
        compiler_params=pltpu.CompilerParams(
            collective_id=0, has_side_effects=True, vmem_limit_bytes=62 * 1024 * 1024
        ),
    )(*operands.values())
    return types.SimpleNamespace(**dict(zip(outs, results, strict=True)))


def finish_kernel(count, *refs):
    ins, outs, held = refs[:count], refs[count : 2 * count], refs[2 * count : 3 * count]
    wide, sems = refs[3 * count : 3 * count + 2], refs[-1]
    loads = [pltpu.make_async_copy(ins[i], held[i], sems.at[0, i]) for i in range(count)]
    stores = [pltpu.make_async_copy((wide[i] if i < 2 else held[i]), outs[i], sems.at[1, i]) for i in range(count)]
    for copy in loads:
        copy.start()
    for i in range(count):
        loads[i].wait()
        if i < 2:
            wide[i][...] = held[i][...].astype(F32)
        stores[i].start()
    for copy in stores:
        copy.wait()


def finish(arrays):
    count = len(arrays)
    placed = [pl.BlockSpec(memory_space=pl.ANY)] * count
    held = [pltpu.VMEM(array.shape, array.dtype) for array in arrays]
    wide = [pltpu.VMEM(array.shape, F32) for array in arrays[:2]]
    return pl.pallas_call(
        functools.partial(finish_kernel, count),
        out_shape=tuple(jax.ShapeDtypeStruct(array.shape, F32) for array in arrays),
        in_specs=placed,
        out_specs=placed,
        scratch_shapes=[*held, *wide, pltpu.SemaphoreType.DMA((2, count))],
        compiler_params=pltpu.CompilerParams(vmem_limit_bytes=62 * 1024 * 1024),
    )(*arrays)


BOTH = ("section", "dp")


def body(
    tokens, cotangent, lengths, routes, slots, norm_gain, norm_bias, attn_qkv, attn_out, attn_out_bias,
    ffn_up, ffn_up_bias, ffn_down, ffn_down_bias, router, expert_up, expert_down,
):
    sections, devices = lax.axis_size("section"), lax.axis_size("dp")
    sec = lax.axis_index("section")
    micro, _, seq, width = tokens.shape
    experts = router.shape[1]
    chips = devices // 2
    head_cols = width // sections
    hidden = ffn_up.shape[1] * devices
    cap = 2 * seq // experts
    span = micro * cap
    cols = ffn_down.shape[1]
    kinds = FIRST_ROUTER + experts
    direct = cols == 3 * TAIL and kinds <= GROUP and sections == 4 and ffn_up.shape[1] % 16 == 0
    parts = sections if span % (16 * sections) == 0 else 1
    groups = micro if cap % (16 * parts) == 0 else 1
    group_names = [str(group) for group in range(groups)]
    part_names = [str(part) for part in range(parts)]
    both_names = [a + b for a in group_names for b in part_names]
    g = types.SimpleNamespace(
        sections=sections, devices=devices, chips=chips, micro=micro, seq=seq, width=width, hidden=hidden, cap=cap,
        span=span, tokens=micro * seq, piece=seq // sections, heads=head_cols // HEAD_DIM,
        head_cols=head_cols, cols=cols, block=256, small=-(-kinds // 8) * 8, direct=direct, experts=experts,
        out_lanes=head_cols + 2 * GROUP + LANES, parts=parts, groups=groups, quarter=span // (parts * groups),
        loads=(["wo", "wq"] if direct else []) + ["x0", "cot"] + (["wu", "wd"] if direct else []) + ["e_up", "e_down"],
        relay=direct and chips == 4,
        my_part=(lambda section: section) if parts > 1 else (lambda section: 0),
        router_lane=FIRST_ROUTER + (LANES - 2 * GROUP if direct else 0),
        pairs=["crow" + a for a in part_names]
        + [name + a for name in ("rows", "d", "y") for a in both_names]
        + ([
            "out0", "qkv0", "up", "bias", "down", "qkv1", "out1",
            "gqkv0", "gqkv1", "gdown", "gup", "gbias", "gout0", "gout1",
        ] if direct else []),
        lines=["crow"]
        + [name + b for name in ("rows", "d", "y") for b in group_names]
        + ([
            "out0", "qkv0", "up", "bias", "down", "qkv1", "out1",
            "gqkv0", "gqkv1", "gdown", "gup", "gbias", "gout0", "gout1",
        ] if direct else []),
        planes=["crow"]
        + [name + b for name in ("rows", "d") for b in group_names] + (["down", "out1", "gdown", "gout0", "gout1"] if direct else []),
    )

    operands = dict(
        h_x0=tokens.reshape(g.tokens, width),
        h_cot=cotangent.reshape(g.tokens, width),
        lens=lengths.T,
        routes=routes[:, 0],
        slots=slots[:, 0],
        h_e_up=expert_up[0],
        h_e_down=expert_down[0],
    )
    if direct:
        operands |= dict(
            norm_gain=norm_gain,
            norm_bias=norm_bias,
            out_bias=attn_out_bias,
            down_bias=ffn_down_bias[None],
            up_bias=ffn_up_bias[None],
            router=router.T,
            h_wq=attn_qkv.transpose(0, 2, 1),
            h_wo=attn_out.transpose(0, 2, 1),
            h_wu=ffn_up.T,
            h_wd=ffn_down.T,
        )
    else:

        def every(array, axis):
            return lax.all_gather(array, BOTH, axis=axis, tiled=True)

        def part_of(array, axis, size):
            return lax.dynamic_slice_in_dim(array, sec * size, size, axis)

        rows = [norm_gain, norm_bias, attn_out_bias, ffn_down_bias[None], router.T]
        params = every(jnp.concatenate(rows, axis=0), 1)
        params = jnp.pad(params, ((0, LANES - kinds), (0, 0)))
        b_up = lax.all_gather(ffn_up_bias, "dp", axis=0, tiled=True).astype(F32)
        full = part_of(every(attn_qkv, 2).reshape(2, width, 3, width), 3, head_cols)
        operands |= dict(
            prm=params.astype(F32),
            w_router=params.T,
            b_up=b_up[None],
            w_qkv=full.transpose(0, 2, 3, 1).reshape(2, 3 * head_cols, width),
            w_out=part_of(every(attn_out, 2), 1, head_cols),
            w_up=lax.all_gather(ffn_up, "dp", axis=1, tiled=True).T,
            w_down=part_of(every(ffn_down, 1), 0, hidden).T,
        )
    res = run_layers(g, operands)

    if direct:
        names = list(vars(res))
        done = finish([getattr(res, name) for name in names])
        res = types.SimpleNamespace(**dict(zip(names, done, strict=True)))
        grads = (
            res.o_gain, res.o_bias, res.o_qkv.transpose(0, 2, 1), res.o_out.transpose(0, 2, 1), res.o_bout,
            res.o_up.T, res.o_bup[0], res.o_down.T, res.o_bdown[0], res.o_router.T,
        )
    else:

        def embed(array, shape, axis, size):
            return lax.dynamic_update_slice_in_dim(jnp.zeros(shape, F32), array, sec * size, axis)

        def share(array, axis, over=BOTH):
            return lax.psum_scatter(array, over, scatter_dimension=axis, tiled=True)

        small = share(res.o_small[:kinds], 1)
        g_qkv = res.o_qkv.reshape(2, 3, head_cols, width).transpose(0, 3, 1, 2)
        g_qkv = embed(g_qkv, (2, width, 3, width), 3, head_cols).reshape(2, width, 3 * width)
        g_out = embed(res.o_out, (2, width, width), 1, head_cols)
        g_down = embed(res.o_down.T, (hidden * sections, width), 0, hidden)
        grads = (
            small[0:4], small[4:8], share(g_qkv, 2), share(g_out, 2), small[8:10], share(res.o_up.T, 1, "dp"),
            share(res.o_bup[0], 0, "dp"), share(g_down, 1), small[10], small[FIRST_ROUTER:].T,
        )
    out_shape = (1, micro, 1, seq, width)
    return (
        res.sec_out.reshape(out_shape).astype(F32),
        res.sec_grad.reshape(out_shape).astype(F32),
        *grads,
        res.g_eup[None],
        res.g_edown[None],
    )


def solution(mesh):
    batch = P(None, "dp", None, None)
    table = P(None, "dp", None)
    in_specs = (
        batch, batch, P(None, "dp"), table, table,
        P(None, BOTH), P(None, BOTH), P(None, None, BOTH), P(None, None, BOTH), P(None, BOTH),
        P(None, BOTH), P(BOTH), P(None, BOTH), P(BOTH), P(BOTH, None),
        P("dp", None, "section"), P("dp", "section", None),
    )
    streams = P("section", None, "dp", None, None)
    out_specs = (
        streams, streams,
        P(None, BOTH), P(None, BOTH), P(None, None, BOTH), P(None, None, BOTH), P(None, BOTH),
        P(None, BOTH), P(BOTH), P(None, BOTH), P(BOTH), P(BOTH, None),
        P("dp", None, "section"), P("dp", "section", None),
    )
    return jax.shard_map(body, mesh=mesh, in_specs=in_specs, out_specs=out_specs, check_vma=False)
```

```python
import functools
import types

import jax
import jax.numpy as jnp
from jax import lax
from jax.experimental import pallas as pl
from jax.experimental.pallas import tpu as pltpu
from jax.sharding import PartitionSpec as P

HEADS = 12
HEAD_DIM = 64
EPS = 1e-05
MASKED = -1000000000.0
MESH = pl.DeviceIdType.MESH
F32 = jnp.float32
BF16 = jnp.bfloat16
LANES = 128


def dot_as(left, right, left_dim, right_dim):
    return lax.dot_general(
        left, right, (((left_dim,), (right_dim,)), ((), ())), preferred_element_type=F32
    )


def mm(left, right):
    return dot_as(left, right, 1, 0)


def mm_nt(left, right):
    return dot_as(left, right, 1, 1)


def mm_tn(left, right):
    return dot_as(left, right, 0, 0)


def normalize(values):
    center = values - jnp.mean(values, axis=-1, keepdims=True)
    spread = jnp.mean(center * center, axis=-1, keepdims=True)
    inverse = lax.rsqrt(spread + EPS)
    return center * inverse, inverse


def gelu_parts(pre):
    half = 0.5 + 0.5 * lax.erf(pre * 0.7071067811865476)
    density = jnp.exp(-0.5 * pre * pre) * 0.3989422804014327
    return pre * half, half + pre * density


TAIL = 8
GROUP = 32
FIRST_ROUTER = 11


def layers_kernel(g, names, *refs):
    r = types.SimpleNamespace(**dict(zip(names, refs, strict=True)))
    width, span, hidden, cols, head_cols = g.width, g.span, g.hidden, g.cols, g.head_cols
    sec = lax.axis_index("section")
    dev = lax.axis_index("dp")
    core = lax.rem(dev, 2)
    chip = lax.div(dev, 2)
    sib = dev + 1 - 2 * core
    quarter = g.quarter
    shard_rows = hidden // g.devices
    block_rows = g.chips * quarter

    def peer_section(offset):
        return lax.rem(sec + offset, g.sections)

    def from_section(offset):
        return lax.rem(sec + g.sections - offset, g.sections)

    def peer_chip(offset):
        return lax.rem(chip + offset, g.chips)

    def from_chip(offset):
        return lax.rem(chip + g.chips - offset, g.chips)

    def rows_at(index, size):
        return pl.ds(pl.multiple_of(index * size, size), size)

    def remote(source, target, send, arrive, where):
        return pltpu.make_async_remote_copy(
            src_ref=source, dst_ref=target, send_sem=send, recv_sem=arrive, device_id=where, device_id_type=MESH
        )

    def at_chip_core(index):
        return {"dp": 2 * index + core}

    started = []
    kept_back = {}

    def do_when(condition, action):
        if condition is None:
            action()
        else:
            pl.when(condition)(action)

    def launch(copy, buffer=None, when=None):
        do_when(when, copy.start)
        if buffer:
            kept_back.setdefault(buffer, []).append((copy, when))
        else:
            started.append((copy, when))

    def settle(buffer):
        for copy, when in kept_back.pop(buffer, []):
            do_when(when, copy.wait_send)

    barrier = pltpu.get_barrier_semaphore()
    partners = [(a, b) for a in range(g.sections) for b in range(g.chips) if a + b and (g.direct or a * b == 0)]
    for section_offset, chip_offset in partners:
        where = {"section": peer_section(section_offset), "dp": 2 * peer_chip(chip_offset) + core}
        pl.semaphore_signal(barrier, inc=1, device_id=where, device_id_type=MESH)
    pl.semaphore_signal(barrier, inc=1, device_id={"dp": sib}, device_id_type=MESH)

    def local(index, source, target):
        return pltpu.make_async_copy(source, target, r.local_s.at[index])

    held = vars(r)
    loads = {name: local(i, held["h_" + name], held[name]) for i, name in enumerate(g.loads)}
    stores = []

    def store(*some):
        for name in some:
            index = len(loads) + g.stores.index(name)
            stores.append(local(index, held[name], held["h_" + name]))
            stores[-1].start()

    for copy in loads.values():
        copy.start()

    def token_slice(micro):
        return slice(micro * g.seq, (micro + 1) * g.seq)

    def piece_at(micro, section):
        return pl.ds(pl.multiple_of(micro * g.seq + section * g.piece, g.piece), g.piece)

    def own(micro):
        return piece_at(micro, sec)

    def scatter_copy(slot, micro, offset):
        return remote(
            r.part.at[slot, piece_at(micro, peer_section(offset))], r.got.at[slot, micro, offset - 1],
            r.scat_s.at[0], r.scat_r.at[slot, micro], {"section": peer_section(offset)},
        )

    def all_pieces(slot, micro, arrive):
        place = r.got.at[slot, micro]
        remote(place, place, r.scat_s.at[0], arrive, {"section": peer_section(1)}).wait_recv()

    def scatter_start(slot, micro, value):
        r.part[slot, token_slice(micro), :] = value.astype(BF16)
        if slot != 7:
            r.mine[token_slice(micro), :] = value
        for offset in range(1, g.sections):
            scatter_copy(slot, micro, offset).start()

    def scatter_sum(slot, micro):
        at = own(micro)
        total = r.part[slot, at, :].astype(F32) if slot == 7 else r.mine[at, :]
        all_pieces(slot, micro, r.scat_r.at[slot, micro])
        for offset in range(1, g.sections):
            total = total + r.got[slot, micro, offset - 1].astype(F32)
        return total

    def gather_start(buffer, slot, sem, micro):
        place = buffer.at[slot, own(micro)]
        for offset in range(1, g.sections):
            remote(place, place, r.gath_s.at[0], r.gath_r.at[sem, micro], {"section": peer_section(offset)}).start()

    def gather_wait(buffer, slot, sem, micro):
        all_pieces(sem, micro, r.gath_r.at[sem, micro])

    def exchanges_left():
        for sem in (r.scat_s, r.gath_s):
            remote(r.got, r.got, sem.at[0], r.scat_r.at[0, 0], {"section": peer_section(1)}).wait_send()

    def pair_copy(name, source, target):
        index = g.pairs.index(name)
        return remote(source, target, r.pair_s.at[index], r.pair_r.at[index], {"dp": sib})

    def pair_start(name, source, target, buffer=None):
        launch(pair_copy(name, source, target), buffer)

    def pair_wait(name, target):
        pair_copy(name, target, target).wait_recv()

    def line_copy(name, source, target, offset, receiving):
        index = g.lines.index(name)
        where = from_chip(offset) if receiving else peer_chip(offset)
        return remote(
            source, target, r.line_s.at[index, offset - 1], r.line_r.at[index, offset - 1], at_chip_core(where)
        )

    last_chip = g.chips - 1
    is_end = lax.rem(chip, max(last_chip, 1)) == 0
    is_mid = lax.rem(chip, max(last_chip, 1)) != 0
    line_order = (2, 1, 3) if g.relay else range(1, g.chips)
    outward = jnp.clip(chip - 1, 0, 1)

    def near_to(offset):
        return {1: chip != last_chip, last_chip: chip != 0}.get(offset) if g.relay else None

    def near_from(offset):
        return {1: chip != 0, last_chip: chip != last_chip}.get(offset) if g.relay else None

    def spread_first(name, source, target, buffer=None):
        if g.relay:
            for offset, when in ((2, is_end), (1, chip == 2), (3, chip == 1)):
                launch(line_copy(name, source, target, offset, False), buffer, when)

    def spread_more(name, source, target, buffer=None):
        if g.relay:
            for offset, when in ((2, is_mid), (1, chip < 2), (3, chip > 1)):
                launch(line_copy(name, source, target, offset, False), buffer, when)
        else:
            for offset in line_order:
                launch(line_copy(name, source, target, offset, False), buffer)

    def spread_relay(name, place, buffer):
        index = g.lines.index(name)
        copy = remote(
            place, place, r.line_s.at[index, last_chip], r.line_r.at[index, outward * 2],
            at_chip_core(outward * last_chip),
        )
        launch(copy, buffer, is_mid)

    def spread_pass(name, place_at, buffer):
        if g.relay:
            place = place_at(from_chip(2))
            line_copy(name, place, place, 2, True).wait_recv()
            spread_relay(name, place, buffer)

    def spread_wait(name, place_at):
        for offset in (1, 3) if g.relay else line_order:
            place = place_at(from_chip(offset))
            line_copy(name, place, place, offset, True).wait_recv()

    def far_wait(name, place_at):
        for offset in (1, last_chip):
            place = place_at(from_chip(offset))
            copy = line_copy(name, place, place, offset, True)
            pl.when(jnp.logical_not(near_from(offset)))(copy.wait_recv)

    left = []

    def wait_all(place, send, arrive, sent):
        copy = remote(place, place, send, arrive, {"dp": sib})
        if sent:
            copy.wait_send()
        else:
            copy.wait_recv()

    def line_start(name, source_at, target, share):
        index = g.manys.index(name)
        for offset in range(1, g.chips):
            at = peer_chip(offset)
            remote(source_at(at), target, r.many_s.at[index], r.many_r.at[index], at_chip_core(at)).start()
        left.append((share, r.many_s.at[index], r.many_r.at[index]))

    def line_wait(name, share):
        index = g.manys.index(name)
        wait_all(share, r.many_s.at[index], r.many_r.at[index], False)

    def other_chips(size=1):
        return pl.ds(0, (g.chips - 1) * size)

    def rows_plane_start(name, place_at):
        if g.parts > 1:
            place = place_at(pl.ds(1, g.parts - 1))
            plane_start(name, lambda to, offset: place_at(0), place_at, place)
        pair_start(name + "0", place_at(0), place_at(0))

    def rows_plane_wait(name, place_at):
        place = place_at(pl.ds(1, g.parts - 1))
        plane_wait(name, place)
        pair_start(name + "1", place, place)

    top = cols - TAIL
    half = width // 2
    part_cols = head_cols // 2
    tail_lane = head_cols + 2 * GROUP

    def qkv_section(at_dev, index, section):
        return lax.rem(lax.div(3 * at_dev + index, g.devices) - section + g.sections, g.sections)

    def qkv_send(layer, offsets):
        for index in range(3):
            to = qkv_section(dev, index, sec)
            for offset in offsets:
                copy = remote(
                    r.pq.at[layer, index], r.rq.at[layer, core, chip, index],
                    r.wq_s.at[index, offset + layer * g.chips], r.wq_r.at[index, offset + layer * g.chips],
                    {"section": to, "dp": 2 * peer_chip(offset) + core},
                )
                if offset:
                    launch(copy, None, near_to(offset))
                else:
                    pl.when(to != sec)(copy.start)

                    @pl.when(to == sec)
                    def _(index=index):
                        r.rq[layer, core, chip, index] = r.pq[layer, index]

    def qkv_arrive(layer, offsets):
        for offset in offsets:
            for index in range(3):
                at_chip = from_chip(offset)
                target = r.rq.at[layer, core, at_chip, index]
                origin = qkv_section(2 * at_chip + core, index, sec)
                copy = remote(
                    target, target, r.wq_s.at[index, offset + layer * g.chips],
                    r.wq_r.at[index, offset + layer * g.chips],
                    {"section": origin, "dp": 2 * at_chip + core},
                )
                if offset:
                    do_when(near_from(offset), copy.wait_recv)
                else:

                    @pl.when(origin != sec)
                    def _(copy=copy):
                        copy.wait_recv()
                        copy.wait_send()

            if g.relay and offset == 2:
                spread_relay("qkv0", r.rq.at[0, core, from_chip(offset)], "qkv0")
        if g.relay and len(offsets) > 1:
            far_wait("qkv0", lambda at: r.rq.at[0, core, at])

    def out_copy(section_offset, offset, place, receiving):
        if receiving:
            to, at_chip = from_section(section_offset), from_chip(offset)
        else:
            to, at_chip = peer_section(section_offset), peer_chip(offset)
        source = place if receiving else r.po.at[0, to]
        return remote(
            source, place, r.wo_s.at[offset], r.wo_r.at[offset],
            {"section": to, "dp": 2 * at_chip + core},
        )

    def out_all(offset, sent):
        count = g.sections if offset else g.sections - 1
        wait_all(r.po.at[0, pl.ds(0, count)], r.wo_s.at[offset], r.wo_r.at[offset], sent)

    def out_offsets():
        return [(a, b) for b in (*line_order, 0) for a in range(g.sections) if a + b]

    def plane_start(name, source_at, target_at, share):
        index = g.planes.index(name)
        for offset in range(1, g.sections):
            to = peer_section(offset)
            sems = r.plane_s.at[index], r.plane_r.at[index]
            remote(source_at(to, offset), target_at(offset), *sems, {"section": to}).start()
        left.append((share, r.plane_s.at[index], r.plane_r.at[index]))

    def plane_wait(name, share):
        index = g.planes.index(name)
        wait_all(share, r.plane_s.at[index], r.plane_r.at[index], False)

    def others():
        return pl.ds(0, g.sections - 1)

    def pack_wide(block):
        tail = jnp.concatenate([block[top:, :half], block[top:, half:]], axis=0)
        return jnp.concatenate([block[:top], tail], axis=1).astype(BF16)

    def pack_out(block):
        small = jnp.concatenate([block[top:, head_cols:]] * 2, axis=0)
        tail = jnp.concatenate([block[top:, :part_cols], block[top:, part_cols:head_cols]], axis=0)
        empty = jnp.zeros((top, g.out_lanes - tail_lane - part_cols), F32)
        return jnp.concatenate([block[:top], small, tail, empty], axis=1).astype(BF16)

    def unpack_wide(target, first, piece):
        target[first : first + top, 0:width] = piece[:, 0:width]
        target[first + top : first + cols, 0:half] = piece[0:TAIL, width : width + half]
        target[first + top : first + cols, half:width] = piece[TAIL:, width : width + half]

    def unpack_out(target, first, piece, lane=0):
        last = slice(first + top, first + cols)
        tail = slice(tail_lane, tail_lane + part_cols)
        target[first : first + top, lane : lane + head_cols] = piece[:, 0:head_cols]
        target[last, lane : lane + part_cols] = piece[0:TAIL, tail]
        target[last, lane + part_cols : lane + head_cols] = piece[TAIL:, tail]

    def unpack_small(target, first, piece, lane):
        target[first : first + top, lane : lane + GROUP] = piece[:, head_cols : head_cols + GROUP]
        target[first + top : first + cols, lane : lane + GROUP] = piece[0:TAIL, head_cols + GROUP : tail_lane]

    def shard_places():
        for at_core in range(2):
            for at_chip in range(g.chips):
                for at_sec in range(g.sections):
                    yield at_core, at_chip, at_sec, (at_sec * g.devices + 2 * at_chip + at_core) * cols

    def chunk_places():
        for at_core in range(2):
            for at_chip in range(g.chips):
                for index in range(3):
                    yield at_core, at_chip, index, (3 * (2 * at_chip + at_core) + index) * cols

    def unfold_out(layer):
        for at_core, at_chip, at_sec, first in shard_places():
            piece = r.ro[layer, at_core, at_chip, at_sec].astype(F32)
            if layer == 0:
                unpack_small(r.tmp, first, piece, head_cols)
            unpack_out(r.tmp, first, piece)
        flipped = r.tmp[:, 0:tail_lane].T
        r.w_out[layer] = flipped[:head_cols].astype(BF16)
        if layer == 0:
            r.prm[...] = flipped[head_cols : head_cols + GROUP]
            r.w_router[...] = r.tmp[:, tail_lane - LANES : tail_lane].astype(BF16)

    def unfold_qkv(layer):
        for at_core, at_chip, index, first in chunk_places():
            unpack_wide(r.tmp, first, r.rq[layer, at_core, at_chip, index].astype(F32))
        r.w_qkv[layer] = r.tmp[0 : 3 * head_cols, 0:width].astype(BF16)

    def unfold_down():
        for at_core, at_chip, at_sec, first in shard_places():
            unpack_wide(r.tmp, first, r.rd[at_core, at_chip, at_sec].astype(F32))
        r.w_down[...] = r.tmp[...].astype(BF16)

    def grad_copy(name, buffer_at, target, offset):
        index, at = g.grads.index(name), peer_chip(offset)
        place = target.at[offset - 1]
        return remote(buffer_at(at), place, r.grad_s.at[index], r.grad_r.at[index], at_chip_core(at))

    def grad_line(name, buffer_at, landing, target, passed):
        pair_wait(name, landing)
        for at_chip in range(g.chips):
            block = buffer_at(at_chip)
            block[...] = (block[...].astype(F32) + landing[at_chip].astype(F32)).astype(BF16)
        if g.relay:
            index = g.grads.index(name)
            copy = remote(
                buffer_at(last_chip - chip), passed, r.grad_s.at[index], r.pass_r.at[index],
                at_chip_core(1 + lax.div(chip, last_chip)),
            )
            pl.when(is_end)(copy.start)
            for offset in (1, last_chip):

                @pl.when(jnp.logical_not(near_from(offset)))
                def _(offset=offset):
                    target[offset - 1] = jnp.zeros_like(target[offset - 1])

        for offset in line_order:
            copy = grad_copy(name, buffer_at, target, offset)
            do_when(is_end if g.relay and offset == 2 else near_to(offset), copy.start)
        index = g.grads.index(name)
        left.append((target, r.grad_s.at[index], r.grad_r.at[index]))

    def grad_relay(name, buffer_at, target, passed):
        if g.relay:
            index = g.grads.index(name)
            block = buffer_at(peer_chip(2))
            copy = grad_copy(name, buffer_at, target, 2)

            @pl.when(is_mid)
            def _():
                wait_all(passed, r.grad_s.at[index], r.pass_r.at[index], False)
                block[...] = (block[...].astype(F32) + passed[...].astype(F32)).astype(BF16)
                copy.start()

    def grad_line_sum(name, buffer_at, target):
        index = g.grads.index(name)

        def arrive(count):
            wait_all(target.at[pl.ds(0, count)], r.grad_s.at[index], r.grad_r.at[index], False)

        if g.relay:
            pl.when(is_end)(lambda: arrive(2))
            pl.when(is_mid)(lambda: arrive(3))
        else:
            arrive(g.chips - 1)
        total = buffer_at(chip)[...].astype(F32)
        for offset in range(1, g.chips):
            total = total + target[offset - 1].astype(F32)
        return total

    def qkv_at(layer):
        return lambda at: r.rq.at[layer, core, at]

    def down_at(at):
        return r.rd.at[core, at]

    def out_at(layer):
        return lambda at: r.ro.at[layer, core, at]

    def up_at(at):
        return r.ru.at[at, core]

    def bias_at(at):
        return r.rb.at[at, core]

    def grad_plane(name, buffer_at, target, summed, final):
        summed[...] = grad_line_sum(name, buffer_at, target).astype(BF16)
        plane_start(name, lambda to, _: summed.at[to], lambda _: final.at[sec], summed.at[others()])
        final[sec] = summed[sec]

    def grad_plane_wait(name, final):
        plane_wait(name, final.at[others()])

    def grad_qkv_copy(layer, index, place, where):
        return remote(
            r.mq.at[layer, index], place, r.gq_s.at[layer, index], r.gq_r.at[layer, index], {"section": where}
        )

    def grad_qkv_plane(layer):
        r.mq[layer] = grad_line_sum("gqkv" + str(layer), qkv_at(layer), r.aq.at[layer]).astype(BF16)
        for index in range(3):
            to = qkv_section(dev, index, sec)
            copy = grad_qkv_copy(layer, index, r.fq.at[layer, index], to)
            pl.when(to != sec)(copy.start)

            @pl.when(to == sec)
            def _(index=index):
                r.fq[layer, index] = r.mq[layer, index]

    def grad_qkv_finish(layer):
        for index in range(3):
            origin = qkv_section(dev, index, sec)
            copy = grad_qkv_copy(layer, index, r.fq.at[layer, index], origin)

            @pl.when(origin != sec)
            def _(copy=copy):
                copy.wait_recv()
                copy.wait_send()

            unpack_wide(r.o_qkv.at[layer], index * cols, r.fq[layer, index].astype(F32))

    def norm_into(source, target, index, micro):
        rows = g.seq // 2

        @pl.loop(0, 2)
        def _(step):
            at = rows_at(micro * 2 + step, rows)
            unit, _ = normalize(source[at, :].astype(F32))
            target[at, :] = (unit * r.prm[index : index + 1, :] + r.prm[4 + index : 5 + index, :]).astype(BF16)

    place_row = jnp.concatenate(
        [r.routes[m : m + 1] * span + m * g.cap + r.slots[m : m + 1] for m in range(g.micro)], axis=1
    )
    r.square[...] = jnp.zeros_like(r.square)
    if g.direct:
        r.square[0:4, 0:cols] = r.norm_gain[...].astype(F32)
        r.square[4:8, 0:cols] = r.norm_bias[...].astype(F32)
        r.square[8:10, 0:cols] = r.out_bias[...].astype(F32)
        r.square[10:11, 0:cols] = r.down_bias[...].astype(F32)
        r.pb[...] = jnp.zeros_like(r.pb)
        r.pb[:, 0:shard_rows] = jnp.broadcast_to(r.up_bias[...], (r.pb.shape[0], shard_rows))
        r.square[FIRST_ROUTER : FIRST_ROUTER + g.experts, 0:cols] = r.router[...].astype(F32)
        r.square[...] = r.square[...].T
        loads["wo"].wait()
        loads["wq"].wait()
        shard = r.wo[0].astype(F32)
        mine = r.square[0:cols, 0:GROUP]
        for at_sec in range(g.sections):
            block = shard[:, at_sec * head_cols : (at_sec + 1) * head_cols]
            r.po[0, at_sec] = pack_out(jnp.concatenate([block, mine], axis=1))
        shard = r.wq[0].astype(F32)
        for index in range(3):
            r.pq[0, index] = pack_wide(shard[index * cols : (index + 1) * cols])
    pl.semaphore_wait(barrier, len(partners) + 1)
    if g.direct:
        for section_offset, offset in out_offsets():
            copy = out_copy(section_offset, offset, r.ro.at[0, core, chip, sec], False)
            do_when(near_to(offset), copy.start)
        r.ro[0, core, chip, sec] = r.po[0, sec]
        qkv_send(0, (*line_order, 0))
        loads["wu"].wait()
        loads["wd"].wait()
        shard = r.wq[1].astype(F32)
        for index in range(3):
            r.pq[1, index] = pack_wide(shard[index * cols : (index + 1) * cols])
        shard, other = r.wd[...].astype(F32), r.wo[1].astype(F32)
        empty = jnp.zeros((cols, GROUP), F32)
        for at_sec in range(g.sections):
            r.pd[at_sec] = pack_wide(shard[:, at_sec * hidden : (at_sec + 1) * hidden])
            block = other[:, at_sec * head_cols : (at_sec + 1) * head_cols]
            r.po[1, at_sec] = pack_out(jnp.concatenate([block, empty], axis=1))

    loads["x0"].wait()
    loads["cot"].wait()
    slot_ids = lax.broadcasted_iota(jnp.int32, (quarter, g.tokens), 0)

    def slot_match(expert, part, group):
        first = expert * span + group * (span // g.groups) + part * quarter
        return jnp.where(slot_ids + first == place_row, 1.0, 0.0).astype(BF16)

    def group_tokens(group):
        count = g.tokens // g.groups
        return slice(group * count, (group + 1) * count)

    for group in range(g.groups):
        for expert in range(g.chips):
            match = slot_match(expert, g.my_part(sec), group)
            r.table[group, expert * quarter : (expert + 1) * quarter, :] = match[:, group_tokens(group)]
        sent = mm(r.table[group], r.cot[group_tokens(group), :]).astype(BF16)
        r.dispc[:, group] = sent.reshape(g.chips, quarter, width)
    r.small[...] = jnp.zeros_like(r.small)
    if g.direct:
        for offset in (*line_order, 0):
            do_when(near_from(offset), lambda offset=offset: out_all(offset, False))
            if g.relay and offset == 2:
                spread_relay("out0", r.ro.at[0, core, from_chip(offset)], "out0")
        if g.relay:
            far_wait("out0", lambda at: r.ro.at[0, core, at])
        pair_start("out0", r.ro.at[0, core], r.ro.at[0, core], "out0")
        qkv_arrive(0, (*line_order, 0))
        pair_start("qkv0", r.rq.at[0, core], r.rq.at[0, core], "qkv0")
        spread_first("bias", r.pb, r.rb.at[chip, core])
        spread_more("bias", r.pb, r.rb.at[chip, core])
        r.rb[chip, core] = r.pb[...]
        spread_first("up", r.wu, r.ru.at[chip, core])
        r.ru[chip, core] = r.wu[...]
        plane_start("down", lambda to, _: r.pd.at[to], lambda _: r.rd.at[core, chip, sec], r.pd.at[others()])
        r.rd[core, chip, sec] = r.pd[sec]
        qkv_send(1, [0])
        place = r.ro.at[1, core, chip, sec]
        plane_start("out1", lambda to, _: r.po.at[1, to], lambda _: place, r.po.at[1, others()])
        r.ro[1, core, chip, sec] = r.po[1, sec]
        pair_wait("out0", r.ro.at[0, 1 - core])
        unfold_out(0)
        pair_wait("qkv0", r.rq.at[0, 1 - core])
        unfold_qkv(0)

    def up_place(at):
        return r.ru.at[at, core]

    def bias_place(at):
        return r.rb.at[at, core]

    def down_place(at):
        return r.rd.at[core, at]

    def qkv_place(at):
        return r.rq.at[1, core, at]

    def out_place(at):
        return r.ro.at[1, core, at]

    def own_first(name, place_at):
        spread_first(name, place_at(chip), place_at(chip), name)

    def own_more(name, place_at):
        spread_more(name, place_at(chip), place_at(chip), name)

    key_ids = lax.broadcasted_iota(jnp.int32, (g.seq, g.seq), 0)
    query_ids = lax.broadcasted_iota(jnp.int32, (g.seq, g.seq), 1)
    scale = HEAD_DIM**-0.5
    micros = range(g.micro)

    def block_of(index):
        return lax.rem(index + sec, 3) if g.direct else index

    def head_slice(head):
        return slice(head * HEAD_DIM, (head + 1) * HEAD_DIM)

    def attention_forward(layer, stream, slot, micro):
        at = token_slice(micro)
        norm_into(stream, r.normed.at[2 * layer], 2 * layer, micro)
        packed = mm_nt(r.w_qkv[layer], r.normed[2 * layer, at, :]).astype(BF16)
        r.qkv[layer, :, :, at] = packed.reshape(3, head_cols, g.seq)
        allowed = (key_ids <= query_ids) & (key_ids < r.lens[:, micro : micro + 1])
        for head in range(g.heads):
            key = r.qkv[layer, block_of(1), head_slice(head), at]
            scores = mm_tn(key, r.qkv[layer, block_of(0), head_slice(head), at]) * scale
            scores = jnp.where(allowed, scores, MASKED)
            weight = jnp.exp(scores - jnp.max(scores, axis=0, keepdims=True))
            weight = weight / jnp.sum(weight, axis=0, keepdims=True)
            r.probs[layer, micro, head] = weight
            value = r.qkv[layer, block_of(2), head_slice(head), at]
            r.ctx[layer, head_slice(head), at] = mm(value, weight.astype(BF16)).astype(BF16)
        scatter_start(slot, micro, mm_tn(r.ctx[layer, :, at], r.w_out[layer]))

    def finish_forward(section, bias, stream, micro):
        total = scatter_sum(section, micro) + bias + stream[own(micro), :].astype(F32)
        r.xs[section, own(micro), :] = total.astype(BF16)
        gather_start(r.xs, section, section, micro)

    for micro in micros:
        attention_forward(0, r.x0, 0, micro)
        if g.direct and micro == 0:
            spread_more("up", r.wu, r.ru.at[chip, core])
    if g.direct:
        spread_pass("bias", bias_place, "bias")
        spread_pass("up", up_place, "up")
        plane_wait("down", r.pd.at[others()])
        own_first("down", down_place)
    for micro in micros:
        finish_forward(0, r.prm[8:9, :], r.x0, micro)
    if g.direct:
        own_more("down", down_place)
        spread_wait("bias", bias_place)
        spread_wait("up", up_place)
        pair_start("up", r.ru.at[:, core], r.ru.at[:, core], "up")
        pair_start("bias", r.rb.at[:, core], r.rb.at[:, core], "bias")
        pair_wait("up", r.ru.at[:, 1 - core])
        pair_wait("bias", r.rb.at[:, 1 - core])
        for at_dev in range(g.devices):
            row = r.rb[at_dev // 2, at_dev % 2, :, 0:shard_rows].astype(F32)
            r.b_up[:, at_dev * shard_rows : (at_dev + 1) * shard_rows] = row[0:TAIL]

    def up_rows(at):
        if g.direct:
            return r.ru[...].reshape(hidden, width)[at]
        return r.w_up[at, :]

    def hidden_blocks():
        return [slice(first, first + g.block) for first in range(0, hidden, g.block)]

    for micro in micros:
        rows = token_slice(micro)
        gather_wait(r.xs, 0, 0, micro)
        norm_into(r.xs.at[0], r.normed.at[1], 1, micro)
        for at in hidden_blocks():
            value, slope = gelu_parts(mm_nt(r.normed[1, rows, :], up_rows(at)) + r.b_up[0:1, at])
            r.act[rows, at] = value.astype(BF16)
            r.dgelu[rows, at] = slope
        if g.direct and micro == 0:
            spread_pass("down", down_place, "down")
            qkv_arrive(1, [0])
            own_first("qkv1", qkv_place)
            own_more("qkv1", qkv_place)
    if g.direct:
        spread_wait("down", down_place)
        pair_start("down", r.rd.at[core], r.rd.at[core], "down")
        plane_wait("out1", r.po.at[1, others()])
        own_first("out1", out_place)
        own_more("out1", out_place)
        pair_wait("down", r.rd.at[1 - core])
        unfold_down()
    for micro in micros:
        scatter_start(1, micro, mm_nt(r.act[token_slice(micro), :], r.w_down[...]))
    if g.direct:
        spread_pass("qkv1", qkv_place, "qkv1")
    for micro in micros:
        finish_forward(1, r.prm[10:11, :], r.xs.at[0], micro)
        if g.direct and micro == 0:
            spread_pass("out1", out_place, "out1")
    if g.direct:
        spread_wait("qkv1", qkv_place)
        pair_start("qkv1", r.rq.at[1, core], r.rq.at[1, core], "qkv1")
        spread_wait("out1", out_place)
        pair_start("out1", r.ro.at[1, core], r.ro.at[1, core], "out1")

    def crow_at(part, side):
        return r.crow.at[:, part, side]

    crow_share = r.dispc.at[other_chips()]
    place = r.crow.at[:, 0, core, rows_at(chip, quarter)]
    line_start("crow", lambda at: r.dispc.at[at], place, crow_share)
    r.crow[:, 0, core, rows_at(chip, quarter), :] = r.dispc[chip]

    if g.direct:
        pair_wait("qkv1", r.rq.at[1, 1 - core])
        unfold_qkv(1)
        pair_wait("out1", r.ro.at[1, 1 - core])
        unfold_out(1)
    for micro in micros:
        gather_wait(r.xs, 1, 1, micro)
        attention_forward(1, r.xs.at[1], 2, micro)
    for micro in micros:
        finish_forward(2, r.prm[9:10, :], r.xs.at[1], micro)
    r.square[0 : g.micro, :] = jnp.concatenate(
        [place_row[:, token_slice(micro)] for micro in micros], axis=0
    ).astype(F32)
    columns = r.square[...].T

    wide = r.wide

    def gates(micro):
        at = token_slice(micro)
        norm_into(r.xs.at[2], wide.at[:, pl.ds(0, width)], 3, micro)
        logits = mm(wide[at, :width], r.w_router[...])
        lane = lax.broadcasted_iota(jnp.int32, logits.shape, 1) - g.router_lane
        place_col = columns[:, micro : micro + 1].astype(jnp.int32)
        chosen = (place_col >= lane * span) & (place_col < lane * span + span)
        score = jnp.sum(jnp.where(chosen, logits, 0.0), axis=-1, keepdims=True)
        gate = 1.0 / (1.0 + jnp.exp(-score))
        gate_high = gate.astype(BF16).astype(F32)
        lane = lax.broadcasted_iota(jnp.int32, (g.seq, LANES), 1)
        pair = jnp.where(lane == 0, gate_high, jnp.where(lane == 1, gate - gate_high, 0.0))
        wide[at, width:] = pair.astype(BF16)

    groups = range(g.groups)

    def rows_place(group, side):
        return lambda part: r.rows.at[group, part, side]

    def rows_line_start(group):
        name = "rows" + str(group)
        r.disp[group] = mm(r.table[group], wide[group_tokens(group), :]).astype(BF16)
        place = r.rows.at[group, 0, core, rows_at(chip, quarter)]
        share = r.disp.at[group, other_chips(quarter)]
        line_start(name, lambda at: r.disp.at[group, rows_at(at, quarter)], place, share)
        r.rows[group, 0, core, rows_at(chip, quarter), :] = r.disp[group, rows_at(chip, quarter), :]

    def rows_line_wait(group):
        name = "rows" + str(group)
        line_wait(name, r.disp.at[group, other_chips(quarter)])
        place_at = rows_place(group, core)
        for offset in range(1, g.parts):
            sems = r.row_s.at[group], r.row_r.at[group, offset - 1]
            remote(place_at(0), place_at(offset), *sems, {"section": peer_section(offset)}).start()
        if g.parts > 1:
            left.append((place_at(pl.ds(1, g.parts - 1)), r.row_s.at[group], r.row_r.at[group, 0]))
        pair_start(name + "0", place_at(0), place_at(0))

    for micro in micros:
        gather_wait(r.xs, 2, 2, micro)
        if micro == 0:
            line_wait("crow", crow_share)
            rows_plane_start("crow", lambda part: crow_at(part, core))
        gates(micro)
        if g.groups > 1:
            rows_line_start(micro)
    if g.groups == 1:
        rows_line_start(0)
    for group in groups:
        rows_line_wait(group)
    loads["e_up"].wait()
    loads["e_down"].wait()

    own_router = FIRST_ROUTER + chip
    router_row = r.prm[pl.ds(own_router, 1), :]
    snd = dict(d=r.snd_d, y=r.snd_y)
    kept = dict(d=r.keep_d, y=r.keep_y)
    rcv = dict(d=r.rcv_d, y=r.rcv_y)

    def expert_block(wide_rows, cot_rows):
        row = wide_rows[:, :width]
        tail = wide_rows[:, width:].astype(F32)
        gate_row = tail[:, 0:1] + tail[:, 1:2]
        grad_row = (gate_row * cot_rows.astype(F32)).astype(BF16)
        value, slope = gelu_parts(mm(row, r.e_up[...]))
        value = value.astype(BF16)
        result = mm(value, r.e_down[...])
        total = jnp.sum(grad_row.astype(F32) * result, axis=-1, keepdims=True) * (1.0 - gate_row)
        inner = (slope * mm_nt(grad_row, r.e_down[...])).astype(BF16)
        back = mm_nt(inner, r.e_up[...]) + total * router_row
        r.small[pl.ds(own_router, 1), :] += jnp.sum(row.astype(F32) * total, axis=0, keepdims=True)
        return grad_row, value, inner, back, result * gate_row

    def expert_parts(group, first, count):
        parts = slice(first, first + count)
        each = 2 * block_rows
        if each <= g.block:
            lead = (count, 2, block_rows)
            found = expert_block(
                r.rows[group, parts].reshape(count * each, width + LANES),
                r.crow[group, parts].reshape(count * each, width),
            )
            for target, value in zip((r.grow, r.acte, r.dpree), found[:3], strict=True):
                target[group, parts] = value.reshape(*lead, value.shape[-1])
            r.both[0, parts] = found[3].reshape(*lead, width)
            r.both[1, parts] = found[4].reshape(*lead, width)
        else:
            for part in range(first, first + count):
                for side in range(2):

                    @pl.loop(0, block_rows // g.block)
                    def _(step, part=part, side=side):
                        at = rows_at(step, g.block)
                        found = expert_block(r.rows[group, part, side, at, :], r.crow[group, part, side, at, :])
                        for target, value in zip((r.grow, r.acte, r.dpree), found[:3], strict=True):
                            target[group, part, side, at, :] = value
                        r.both[0, part, side, at, :] = found[3]
                        r.both[1, part, side, at, :] = found[4]

        parts_send("d", r.both.at[0], group, first, count)

    def parts_send(which, value, group, first, count):
        for part in range(first, first + count):
            snd[which][group, part] = value[part, 1 - core].astype(BF16)
            if which == "d":
                pair_start(which + str(group) + str(part), snd[which].at[group, part], rcv[which].at[group, part])
        if which == "y":
            parts = pl.ds(first, count)
            name = which + str(group) + str(min(first, 1))
            pair_start(name, snd[which].at[group, parts], rcv[which].at[group, parts])
        for part in range(first, first + count):
            kept[which][group, part] = value[part, core]

    def results_pair(group, first, count):
        parts_send("y", r.both.at[1], group, first, count)

    def merge_ready(which, group, first, count):
        pair_wait(which + str(group) + str(min(first, 1)), rcv[which].at[group, pl.ds(first, count)])

    def merge(which, offset, group):
        return kept[which][group, offset] + rcv[which][group, offset].astype(F32)

    def merge_send(group):
        index = g.planes.index("d" + str(group))
        for offset in range(1, g.sections):
            to = g.sections - offset
            pair_wait("d" + str(group) + str(offset), rcv["d"].at[group, offset])
            r.out_d[offset - 1, group] = merge("d", offset, group).astype(BF16)
            sems = r.plane_s.at[index], r.plane_r.at[index]
            source, target = r.out_d.at[offset - 1, group], r.plane_d.at[to - 1, group]
            remote(source, target, *sems, {"section": peer_section(to)}).start()
        left.append((r.out_d.at[:, group], r.plane_s.at[index], r.plane_r.at[index]))

    def parts_work(group, first, count):
        parts, tag = pl.ds(first, count), str(min(first, 1))
        if group == 0:
            pair_wait("crow" + tag, crow_at(parts, 1 - core))
        for part in range(first, first + count):
            pair_wait("rows" + str(group) + str(part), rows_place(group, 1 - core)(part))
        expert_parts(group, first, count)

    def results_line(group):
        merge_ready("y", group, 0, 1)
        if g.parts > 1:
            merge_ready("y", group, 1, g.parts - 1)
        for offset in range(g.parts):
            r.ret_y[group, offset] = merge("y", offset, group).astype(BF16)
        name = "y" + str(group)
        place, share = r.back_y.at[chip, group], r.ret_y.at[group, :, other_chips(quarter)]
        line_start(name, lambda at: r.ret_y.at[group, :, rows_at(at, quarter)], place, share)
        r.back_y[chip, group] = r.ret_y[group, :, rows_at(chip, quarter), :]

    def expert_back_line(group):
        name = "d" + str(group)
        pair_wait("d" + str(group) + "0", rcv["d"].at[group, 0])
        total = merge("d", 0, group)
        if g.parts > 1:
            plane_wait(name, r.plane_d.at[:, group])
            for offset in range(1, g.sections):
                place = r.plane_d.at[offset - 1, group]
                total = total + place[...].astype(F32)
        r.ret_d[group] = total.astype(BF16)
        place = r.back_d.at[group, rows_at(chip, quarter)]
        share = r.ret_d.at[group, other_chips(quarter)]
        line_start(name, lambda at: r.ret_d.at[group, rows_at(at, quarter)], place, share)
        r.back_d[group, rows_at(chip, quarter), :] = r.ret_d[group, rows_at(chip, quarter), :]

    def expert_combine(group):
        line_wait("d" + str(group), r.ret_d.at[group, other_chips(quarter)])
        value = mm_tn(r.table[group], r.back_d[group])
        if g.groups > 1:
            scatter_start(3, group, value)
        else:
            for micro in micros:
                scatter_start(3, micro, value[token_slice(micro)])

    def results_combine():
        for group in groups:
            line_wait("y" + str(group), r.ret_y.at[group, :, other_chips(quarter)])
        places = [(e, q, p) for e in range(g.chips) for q in groups for p in range(g.parts)]
        match = [slot_match(e, g.my_part(from_section(p)), q) for e, q, p in places]
        match = jnp.concatenate(match, axis=0)
        value = mm_tn(match, r.back_y[...].reshape(g.chips * span, width))
        for micro in micros:
            scatter_start(7, micro, value[token_slice(micro)])

    for group in groups:
        parts_work(group, 0, 1)
        results_pair(group, 0, 1)
    if g.parts > 1:
        rows_plane_wait("crow", lambda part: crow_at(part, core))
    for group in groups:
        if g.parts > 1:
            for offset in range(1, g.parts):
                place = rows_place(group, core)(offset)
                wait_all(place, r.row_s.at[group], r.row_r.at[group, offset - 1], False)
                pair_start("rows" + str(group) + str(offset), place, place)
            parts_work(group, 1, g.parts - 1)
            merge_send(group)
            results_pair(group, 1, g.parts - 1)
        if group < g.groups - 1:
            results_line(group)
    for group in groups:
        expert_back_line(group)

    def expert_weights(left, right):
        rows = g.groups * g.parts * 2 * block_rows
        return mm_tn(left.reshape(rows, left.shape[-1]), right.reshape(rows, right.shape[-1]))

    r.g_eup[...] = expert_weights(r.rows[:, :, :, :, :width], r.dpree[...])
    r.g_edown[...] = expert_weights(r.acte[...], r.grow[...])
    store("g_eup", "g_edown")

    def add_small(index, micro, value):
        if micro == 0:
            r.small[index : index + 1, :] = value
        else:
            r.small[index : index + 1, :] += value

    def finish_backward(section, slot, stream, above, micro):
        grad = scatter_sum(slot, micro)
        unit, inverse = normalize(stream[own(micro), :].astype(F32))
        add_small(section, micro, jnp.sum(grad * unit, axis=0, keepdims=True))
        add_small(4 + section, micro, jnp.sum(grad, axis=0, keepdims=True))
        grad = grad * r.prm[section : section + 1, :]
        shared = jnp.mean(grad, axis=-1, keepdims=True)
        along = jnp.mean(grad * unit, axis=-1, keepdims=True)
        grad = inverse * (grad - shared - unit * along) + above[own(micro), :].astype(F32)
        r.gs[section, own(micro), :] = grad.astype(BF16)
        gather_start(r.gs, section, 4 + section, micro)

    for group in groups:
        expert_combine(group)
    results_line(g.groups - 1)
    for micro in micros:
        finish_backward(3, 3, r.xs.at[2], r.cot, micro)

    def bias_row(index, section):
        for micro in micros:
            value = r.gs[section, own(micro), :].astype(F32)
            add_small(index, micro, jnp.sum(value, axis=0, keepdims=True))

    def attention_backward(layer, section, slot, micro):
        at = token_slice(micro)
        dctx = mm_nt(r.w_out[layer], r.gs[section + 1, at, :]).astype(BF16)
        for head in range(g.heads):
            weight = r.probs[layer, micro, head]
            low = weight.astype(BF16)
            dhead = dctx[head_slice(head)]
            query = r.qkv[layer, block_of(0), head_slice(head), at]
            key = r.qkv[layer, block_of(1), head_slice(head), at]
            value = r.qkv[layer, block_of(2), head_slice(head), at]
            dprobs = mm_tn(value, dhead)
            delta = jnp.sum(weight * dprobs, axis=0, keepdims=True)
            dscores = (weight * (dprobs - delta)).astype(BF16)
            r.dqkv[block_of(0), head_slice(head), at] = (mm(key, dscores) * scale).astype(BF16)
            r.dqkv[block_of(1), head_slice(head), at] = (mm_nt(query, dscores) * scale).astype(BF16)
            r.dqkv[block_of(2), head_slice(head), at] = mm_nt(dhead, low).astype(BF16)
        flat_grad = r.dqkv[:, :, at].reshape(3 * head_cols, g.seq)
        scatter_start(slot, micro, mm_tn(flat_grad, r.w_qkv[layer]))

    def attention_weights(layer, section):
        grad_qkv = mm(r.dqkv[...].reshape(3 * head_cols, g.tokens), r.normed[2 * layer])
        if not g.direct:
            r.o_qkv[layer] = grad_qkv
            r.o_out[layer] = mm(r.ctx[layer], r.gs[section + 1])
            return
        r.tmp[0 : 3 * head_cols, :] = grad_qkv
        settle("qkv" + str(layer))
        for at_core, at_chip, index, first in chunk_places():
            r.rq[layer, at_core, at_chip, index] = pack_wide(r.tmp[first : first + cols, :])
        name = "gqkv" + str(layer)
        pair_start(name, r.rq.at[layer, 1 - core], r.hq.at[layer])
        r.tmp[:, 0:head_cols] = dot_as(r.gs[section + 1], r.ctx[layer], 0, 1)
        if layer:
            r.tmp[:, head_cols : head_cols + GROUP] = jnp.zeros((width, GROUP), F32)
            out_weights(1)

    def out_weights(layer):
        settle("out" + str(layer))
        for at_core, at_chip, at_sec, first in shard_places():
            block = r.tmp[first : first + cols, 0 : head_cols + GROUP]
            r.ro[layer, at_core, at_chip, at_sec] = pack_out(block)
        pair_start("gout" + str(layer), r.ro.at[layer, 1 - core], r.ho.at[layer])

    for micro in micros:
        gather_wait(r.gs, 3, 7, micro)
        attention_backward(1, 2, 4, micro)
    bias_row(9, 3)
    attention_weights(1, 2)
    if g.direct:
        grad_line("gqkv1", qkv_at(1), r.hq.at[1], r.aq.at[1], r.lq.at[1])
    finish_backward(2, 4, r.xs.at[1], r.gs.at[3], 0)
    if g.direct:
        grad_line("gout1", out_at(1), r.ho.at[1], r.ao.at[1], r.lo.at[1])
    for micro in micros[1:]:
        finish_backward(2, 4, r.xs.at[1], r.gs.at[3], micro)

    for micro in micros:
        rows = token_slice(micro)
        gather_wait(r.gs, 2, 6, micro)
        grad_two = r.gs[2, rows, :]
        for at in hidden_blocks():
            r.dpre[rows, at] = (r.dgelu[rows, at] * mm(grad_two, r.w_down[:, at])).astype(BF16)
        scatter_start(5, micro, mm(r.dpre[rows, :], up_rows(slice(None))))
    bias_row(10, 2)
    sum_up = jnp.sum(r.dpre[...].astype(F32), axis=0, keepdims=True)
    if g.direct:
        grad_relay("gqkv1", qkv_at(1), r.aq.at[1], r.lq.at[1])
        grad_relay("gout1", out_at(1), r.ao.at[1], r.lo.at[1])
        r.tmp[...] = mm_tn(r.gs[2], r.act[...])
        settle("down")
        for at_core, at_chip, at_sec, first in shard_places():
            r.rd[at_core, at_chip, at_sec] = pack_wide(r.tmp[first : first + cols, :])
        pair_start("gdown", r.rd.at[1 - core], r.hd)
        settle("up")
        settle("bias")
        r.ru[...] = mm_tn(r.dpre[...], r.normed[1]).astype(BF16).reshape(r.ru.shape)
        pair_start("gup", r.ru.at[:, 1 - core], r.hu)
        for at_dev in range(g.devices):
            row = sum_up[:, at_dev * shard_rows : (at_dev + 1) * shard_rows]
            row = jnp.broadcast_to(row, (r.pb.shape[0], shard_rows)).astype(BF16)
            r.rb[at_dev // 2, at_dev % 2, :, 0:shard_rows] = row
        pair_start("gbias", r.rb.at[:, 1 - core], r.hb)
        grad_line("gdown", down_at, r.hd, r.ad, r.ld)
    else:
        r.o_down[...] = mm_tn(r.gs[2], r.act[...])
        r.o_up[...] = mm_tn(r.dpre[...], r.normed[1])
        r.o_bup[...] = sum_up
    for micro in micros:
        finish_backward(1, 5, r.xs.at[0], r.gs.at[2], micro)
    if g.direct:
        grad_line("gbias", bias_at, r.hb, r.ab, r.lb)
        grad_relay("gdown", down_at, r.ad, r.ld)

    for micro in micros:
        gather_wait(r.gs, 1, 5, micro)
        attention_backward(0, 0, 6, micro)
    bias_row(8, 1)
    attention_weights(0, 0)
    finish_backward(0, 6, r.x0, r.gs.at[1], 0)
    if g.direct:
        grad_line("gqkv0", qkv_at(0), r.hq.at[0], r.aq.at[0], r.lq.at[0])
    for micro in micros[1:]:
        finish_backward(0, 6, r.x0, r.gs.at[1], micro)
    if g.direct:
        kinds = r.small[...]
        padded = jnp.concatenate([kinds, jnp.zeros((LANES - kinds.shape[0], width), F32)], axis=0)
        r.tmp[:, head_cols : head_cols + GROUP] = padded.T[:, 0:GROUP]
        out_weights(0)
        grad_line("gout0", out_at(0), r.ho.at[0], r.ao.at[0], r.lo.at[0])
        grad_line("gup", up_at, r.hu, r.au, r.lu)
        grad_relay("gbias", bias_at, r.ab, r.lb)
    results_combine()
    if g.direct:
        grad_qkv_plane(1)
        grad_plane("gout1", out_at(1), r.ao.at[1], r.mo.at[1], r.fo.at[1])
        grad_plane("gdown", down_at, r.ad, r.md, r.fd)
        grad_relay("gqkv0", qkv_at(0), r.aq.at[0], r.lq.at[0])
        grad_relay("gout0", out_at(0), r.ao.at[0], r.lo.at[0])
    for micro in micros:
        r.xs[3, own(micro), :] = (scatter_sum(7, micro) + r.xs[2, own(micro), :].astype(F32)).astype(BF16)
        gather_start(r.xs, 3, 3, micro)
    if g.direct:
        grad_relay("gup", up_at, r.au, r.lu)
    for micro in micros:
        gather_wait(r.xs, 3, 3, micro)
        gather_wait(r.gs, 0, 4, micro)
    r.sec_out[...] = r.xs[sec]
    r.sec_grad[...] = r.gs[sec]
    store("sec_out", "sec_grad")
    if g.direct:
        grad_qkv_plane(0)
        grad_plane("gout0", out_at(0), r.ao.at[0], r.mo.at[0], r.fo.at[0])
        grad_qkv_finish(1)
        grad_plane_wait("gdown", r.fd)
        for at_sec in range(g.sections):
            piece = r.fd[at_sec].astype(F32)
            unpack_wide(r.o_down.at[:, pl.ds(at_sec * hidden, hidden)], 0, piece)
        store("o_down")
        r.o_up[...] = grad_line_sum("gup", up_at, r.au)
        r.o_bup[...] = grad_line_sum("gbias", bias_at, r.ab)[0:1, 0:shard_rows]
        store("o_up", "o_bup")
        grad_plane_wait("gout1", r.fo.at[1])
        for at_sec in range(g.sections):
            unpack_out(r.o_out.at[1], 0, r.fo[1, at_sec].astype(F32), at_sec * head_cols)
        grad_qkv_finish(0)
        store("o_qkv")
        grad_plane_wait("gout0", r.fo.at[0])
        everyone = jnp.zeros((top, g.out_lanes), F32)
        for at_sec in range(g.sections):
            piece = r.fo[0, at_sec].astype(F32)
            unpack_out(r.o_out.at[0], 0, piece, at_sec * head_cols)
            everyone = everyone + piece
        r.square[...] = jnp.zeros_like(r.square)
        unpack_small(r.square, 0, everyone, 0)
        r.square[...] = r.square[...].T
        r.o_router[...] = r.square[FIRST_ROUTER : FIRST_ROUTER + g.experts, 0:cols]
        r.o_gain[...] = r.square[0:4, 0:cols]
        r.o_bias[...] = r.square[4:8, 0:cols]
        r.o_bout[...] = r.square[8:10, 0:cols]
        r.o_bdown[...] = r.square[10:11, 0:cols]
        store("o_out", "o_gain", "o_bias", "o_bout", "o_bdown", "o_router")
    else:
        r.o_small[...] = r.small[...]
        store("o_qkv", "o_out", "o_up", "o_down", "o_bup", "o_small")
    for copy in stores:
        copy.wait()
    exchanges_left()
    if g.direct:
        for offset in range(g.chips):
            do_when(near_to(offset), lambda offset=offset: out_all(offset, True))
    for share, send, arrive in left:
        wait_all(share, send, arrive, True)
    for copy, when in started:
        do_when(when, copy.wait_send)


def run_layers(g, operands):
    tokens, width, hidden, sections, chips = g.tokens, g.width, g.hidden, g.sections, g.chips
    part_rows = chips * g.quarter
    inner = operands["h_e_down"].shape[0]
    three = 3 * g.head_cols
    shape = jax.ShapeDtypeStruct
    vmem = pltpu.VMEM
    dma = pltpu.SemaphoreType.DMA
    top = g.cols - TAIL
    wide = width + width // 2
    up_rows = hidden // g.devices
    outs = dict(
        sec_out=shape((tokens, width), BF16),
        sec_grad=shape((tokens, width), BF16),
        g_eup=shape((width, inner), F32),
        g_edown=shape((inner, width), F32),
    )
    if g.direct:
        outs |= dict(
            o_qkv=shape((2, 3 * g.cols, width), F32),
            o_out=shape((2, g.cols, width), F32),
            o_up=shape((up_rows, width), F32),
            o_down=shape((g.cols, sections * hidden), F32),
            o_gain=shape((4, g.cols), F32),
            o_bias=shape((4, g.cols), F32),
            o_bout=shape((2, g.cols), F32),
            o_bdown=shape((1, g.cols), F32),
            o_router=shape((g.experts, g.cols), F32),
            o_bup=shape((1, up_rows), F32),
        )
    else:
        outs |= dict(
            o_qkv=shape((2, three, width), F32),
            o_out=shape((2, g.head_cols, width), F32),
            o_up=shape((hidden, width), F32),
            o_down=shape((width, hidden), F32),
            o_bup=shape((1, hidden), F32),
            o_small=shape((g.small, width), F32),
        )
    scratch = dict(
        xs=vmem((4, tokens, width), BF16),
        gs=vmem((4, tokens, width), BF16),
        normed=vmem((3, tokens, width), BF16),
        wide=vmem((tokens, width + LANES), BF16),
        qkv=vmem((2, 3, g.head_cols, tokens), BF16),
        probs=vmem((2, g.micro, g.heads, g.seq, g.seq), F32),
        ctx=vmem((2, g.head_cols, tokens), BF16),
        act=vmem((tokens, hidden), BF16),
        dgelu=vmem((tokens, hidden), F32),
        dpre=vmem((tokens, hidden), BF16),
        dqkv=vmem((3, g.head_cols, tokens), BF16),
        part=vmem((8, tokens, width), BF16),
        got=vmem((8, g.micro, sections - 1, g.piece, width), BF16),
        mine=vmem((tokens, width), F32),
        square=vmem((LANES, LANES), F32),
        table=vmem((g.groups, part_rows, tokens // g.groups), BF16),
        disp=vmem((g.groups, part_rows, width + LANES), BF16),
        dispc=vmem((chips, g.groups, g.quarter, width), BF16),
        rows=vmem((g.groups, g.parts, 2, part_rows, width + LANES), BF16),
        crow=vmem((g.groups, g.parts, 2, part_rows, width), BF16),
        grow=vmem((g.groups, g.parts, 2, part_rows, width), BF16),
        acte=vmem((g.groups, g.parts, 2, part_rows, inner), BF16),
        dpree=vmem((g.groups, g.parts, 2, part_rows, inner), BF16),
        both=vmem((2, g.parts, 2, part_rows, width), F32),
        small=vmem((g.small, width), F32),
        local_s=dma((len(g.loads) + len(outs),)),
    )
    g.stores = list(outs)
    for name, out in outs.items():
        scratch[name] = vmem(out.shape, out.dtype)
    for name in g.loads:
        scratch[name] = vmem(operands["h_" + name].shape, BF16)
    for which in ("d", "y"):
        scratch["keep_" + which] = vmem((g.groups, g.parts, part_rows, width), F32)
        for name in ("snd_", "rcv_"):
            scratch[name + which] = vmem((g.groups, g.parts, part_rows, width), BF16)
    scratch |= dict(
        out_d=vmem((sections - 1, g.groups, part_rows, width), BF16),
        plane_d=vmem((sections - 1, g.groups, part_rows, width), BF16),
        ret_d=vmem((g.groups, part_rows, width), BF16),
        back_d=vmem((g.groups, part_rows, width), BF16),
        ret_y=vmem((g.groups, g.parts, part_rows, width), BF16),
        back_y=vmem((chips, g.groups, g.parts, g.quarter, width), BF16),
    )
    scratch |= dict(row_s=dma((g.groups,)), row_r=dma((g.groups, max(g.parts - 1, 1))))
    scratch |= dict(scat_s=dma((1,)), gath_s=dma((1,)), scat_r=dma((8, g.micro)), gath_r=dma((8, g.micro)))
    for name, sizes in (
        ("pair", (len(g.pairs),)), ("plane", (len(g.planes),)), ("many", (len(g.manys),)),
        ("line", (len(g.lines), chips)), ("grad", (len(g.grads),)), ("pass", (len(g.grads),)),
    ):
        if sizes[0]:
            scratch |= {name + "_s": dma(sizes), name + "_r": dma(sizes)}
    if g.direct:
        del scratch["pass_s"]
    if g.direct:
        piece = (top, wide)
        out_piece = (top, g.out_lanes)
        up_piece = (up_rows, width)
        bias_piece = (2 * TAIL, LANES)
        scratch |= dict(
            pq=vmem((2, 3, *piece), BF16),
            po=vmem((2, sections, *out_piece), BF16),
            pb=vmem(bias_piece, BF16),
            rb=vmem((chips, 2, *bias_piece), BF16),
            hb=vmem((chips, *bias_piece), BF16),
            ab=vmem((chips - 1, *bias_piece), BF16),
            lb=vmem(bias_piece, BF16),
            lq=vmem((2, 3, *piece), BF16),
            lo=vmem((2, sections, *out_piece), BF16),
            lu=vmem(up_piece, BF16),
            ld=vmem((sections, *piece), BF16),
            pd=vmem((sections, *piece), BF16),
            rq=vmem((2, 2, chips, 3, *piece), BF16),
            ro=vmem((2, 2, chips, sections, *out_piece), BF16),
            ru=vmem((chips, 2, *up_piece), BF16),
            rd=vmem((2, chips, sections, *piece), BF16),
            w_qkv=vmem((2, three, width), BF16),
            w_out=vmem((2, g.head_cols, width), BF16),
            w_down=vmem((width, hidden), BF16),
            w_router=vmem((width, LANES), BF16),
            b_up=vmem((8, hidden), F32),
            prm=vmem((GROUP, width), F32),
            tmp=vmem((width, width), F32),
            hq=vmem((2, chips, 3, *piece), BF16),
            ho=vmem((2, chips, sections, *out_piece), BF16),
            hu=vmem((chips, *up_piece), BF16),
            hd=vmem((chips, sections, *piece), BF16),
            aq=vmem((2, chips - 1, 3, *piece), BF16),
            ao=vmem((2, chips - 1, sections, *out_piece), BF16),
            au=vmem((chips - 1, *up_piece), BF16),
            ad=vmem((chips - 1, sections, *piece), BF16),
            mq=vmem((2, 3, *piece), BF16),
            mo=vmem((2, sections, *out_piece), BF16),
            md=vmem((sections, *piece), BF16),
            fq=vmem((2, 3, *piece), BF16),
            fo=vmem((2, sections, *out_piece), BF16),
            fd=vmem((sections, *piece), BF16),
            wq_s=dma((3, chips + 1)),
            wq_r=dma((3, chips + 1)),
            wo_s=dma((chips,)),
            wo_r=dma((chips,)),
            gq_s=dma((2, 3)),
            gq_r=dma((2, 3)),
        )
    whole = pl.BlockSpec(memory_space=pltpu.VMEM)
    placed = pl.BlockSpec(memory_space=pl.ANY)
    apart = ["h_" + name for name in g.loads]
    names = (*operands, *("h_" + name for name in outs), *scratch)
    results = pl.pallas_call(
        functools.partial(layers_kernel, g, names),
        out_shape=tuple(outs.values()),
        in_specs=[placed if name in apart else whole for name in operands],
        out_specs=[placed] * len(outs),
        scratch_shapes=list(scratch.values()),
        compiler_params=pltpu.CompilerParams(
            collective_id=0, has_side_effects=True, vmem_limit_bytes=62 * 1024 * 1024
        ),
    )(*operands.values())
    return types.SimpleNamespace(**dict(zip(outs, results, strict=True)))


def finish_kernel(count, *refs):
    ins, outs, held = refs[:count], refs[count : 2 * count], refs[2 * count : 3 * count]
    wide, sems = refs[3 * count : 3 * count + 2], refs[-1]
    loads = [pltpu.make_async_copy(ins[i], held[i], sems.at[0, i]) for i in range(count)]
    stores = [pltpu.make_async_copy((wide[i] if i < 2 else held[i]), outs[i], sems.at[1, i]) for i in range(count)]
    for copy in loads:
        copy.start()
    for i in range(count):
        loads[i].wait()
        if i < 2:
            wide[i][...] = held[i][...].astype(F32)
        stores[i].start()
    for copy in stores:
        copy.wait()


def finish(arrays):
    count = len(arrays)
    placed = [pl.BlockSpec(memory_space=pl.ANY)] * count
    held = [pltpu.VMEM(array.shape, array.dtype) for array in arrays]
    wide = [pltpu.VMEM(array.shape, F32) for array in arrays[:2]]
    return pl.pallas_call(
        functools.partial(finish_kernel, count),
        out_shape=tuple(jax.ShapeDtypeStruct(array.shape, F32) for array in arrays),
        in_specs=placed,
        out_specs=placed,
        scratch_shapes=[*held, *wide, pltpu.SemaphoreType.DMA((2, count))],
        compiler_params=pltpu.CompilerParams(vmem_limit_bytes=62 * 1024 * 1024),
    )(*arrays)


BOTH = ("section", "dp")


def body(
    tokens, cotangent, lengths, routes, slots, norm_gain, norm_bias, attn_qkv, attn_out, attn_out_bias,
    ffn_up, ffn_up_bias, ffn_down, ffn_down_bias, router, expert_up, expert_down,
):
    sections, devices = lax.axis_size("section"), lax.axis_size("dp")
    sec = lax.axis_index("section")
    micro, _, seq, width = tokens.shape
    experts = router.shape[1]
    chips = devices // 2
    head_cols = width // sections
    hidden = ffn_up.shape[1] * devices
    cap = 2 * seq // experts
    span = micro * cap
    cols = ffn_down.shape[1]
    kinds = FIRST_ROUTER + experts
    direct = cols == 3 * TAIL and kinds <= GROUP and sections == 4 and ffn_up.shape[1] % 16 == 0
    parts = sections if span % (16 * sections) == 0 else 1
    groups = micro if cap % (16 * parts) == 0 else 1
    group_names = [str(group) for group in range(groups)]
    part_names = [str(part) for part in range(parts)]
    half_names = part_names[:2]
    g = types.SimpleNamespace(
        sections=sections, devices=devices, chips=chips, micro=micro, seq=seq, width=width, hidden=hidden, cap=cap,
        span=span, tokens=micro * seq, piece=seq // sections, heads=head_cols // HEAD_DIM,
        head_cols=head_cols, cols=cols, block=256, small=-(-kinds // 8) * 8, direct=direct, experts=experts,
        out_lanes=head_cols + 2 * GROUP + LANES, parts=parts, groups=groups, quarter=span // (parts * groups),
        loads=(["wo", "wq"] if direct else []) + ["x0", "cot"] + (["wu", "wd"] if direct else []) + ["e_up", "e_down"],
        relay=direct and chips == 4,
        my_part=(lambda section: section) if parts > 1 else (lambda section: 0),
        router_lane=FIRST_ROUTER + (LANES - 2 * GROUP if direct else 0),
        pairs=["crow" + a for a in half_names]
        + [name + a + b for name in ("rows", "d") for a in group_names for b in part_names]
        + ["y" + a + b for a in group_names for b in half_names]
        + ([
            "out0", "qkv0", "up", "bias", "down", "qkv1", "out1",
            "gqkv0", "gqkv1", "gdown", "gup", "gbias", "gout0", "gout1",
        ] if direct else []),
        lines=["out0", "qkv0", "up", "bias", "down", "qkv1", "out1"] if direct else [],
        grads=["gqkv0", "gqkv1", "gdown", "gup", "gbias", "gout0", "gout1"] if direct else [],
        manys=["crow"] + [name + b for name in ("rows", "d", "y") for b in group_names],
        planes=["crow"]
        + ["d" + b for b in group_names]
        + (["down", "out1", "gdown", "gout0", "gout1"] if direct else []),
    )

    operands = dict(
        h_x0=tokens.reshape(g.tokens, width),
        h_cot=cotangent.reshape(g.tokens, width),
        lens=lengths.T,
        routes=routes[:, 0],
        slots=slots[:, 0],
        h_e_up=expert_up[0],
        h_e_down=expert_down[0],
    )
    if direct:
        operands |= dict(
            norm_gain=norm_gain,
            norm_bias=norm_bias,
            out_bias=attn_out_bias,
            down_bias=ffn_down_bias[None],
            up_bias=ffn_up_bias[None],
            router=router.T,
            h_wq=attn_qkv.transpose(0, 2, 1),
            h_wo=attn_out.transpose(0, 2, 1),
            h_wu=ffn_up.T,
            h_wd=ffn_down.T,
        )
    else:

        def every(array, axis):
            return lax.all_gather(array, BOTH, axis=axis, tiled=True)

        def part_of(array, axis, size):
            return lax.dynamic_slice_in_dim(array, sec * size, size, axis)

        rows = [norm_gain, norm_bias, attn_out_bias, ffn_down_bias[None], router.T]
        params = every(jnp.concatenate(rows, axis=0), 1)
        params = jnp.pad(params, ((0, LANES - kinds), (0, 0)))
        b_up = lax.all_gather(ffn_up_bias, "dp", axis=0, tiled=True).astype(F32)
        full = part_of(every(attn_qkv, 2).reshape(2, width, 3, width), 3, head_cols)
        operands |= dict(
            prm=params.astype(F32),
            w_router=params.T,
            b_up=b_up[None],
            w_qkv=full.transpose(0, 2, 3, 1).reshape(2, 3 * head_cols, width),
            w_out=part_of(every(attn_out, 2), 1, head_cols),
            w_up=lax.all_gather(ffn_up, "dp", axis=1, tiled=True).T,
            w_down=part_of(every(ffn_down, 1), 0, hidden).T,
        )
    res = run_layers(g, operands)

    if direct:
        names = list(vars(res))
        done = finish([getattr(res, name) for name in names])
        res = types.SimpleNamespace(**dict(zip(names, done, strict=True)))
        grads = (
            res.o_gain, res.o_bias, res.o_qkv.transpose(0, 2, 1), res.o_out.transpose(0, 2, 1), res.o_bout,
            res.o_up.T, res.o_bup[0], res.o_down.T, res.o_bdown[0], res.o_router.T,
        )
    else:

        def embed(array, shape, axis, size):
            return lax.dynamic_update_slice_in_dim(jnp.zeros(shape, F32), array, sec * size, axis)

        def share(array, axis, over=BOTH):
            return lax.psum_scatter(array, over, scatter_dimension=axis, tiled=True)

        small = share(res.o_small[:kinds], 1)
        g_qkv = res.o_qkv.reshape(2, 3, head_cols, width).transpose(0, 3, 1, 2)
        g_qkv = embed(g_qkv, (2, width, 3, width), 3, head_cols).reshape(2, width, 3 * width)
        g_out = embed(res.o_out, (2, width, width), 1, head_cols)
        g_down = embed(res.o_down.T, (hidden * sections, width), 0, hidden)
        grads = (
            small[0:4], small[4:8], share(g_qkv, 2), share(g_out, 2), small[8:10], share(res.o_up.T, 1, "dp"),
            share(res.o_bup[0], 0, "dp"), share(g_down, 1), small[10], small[FIRST_ROUTER:].T,
        )
    out_shape = (1, micro, 1, seq, width)
    return (
        res.sec_out.reshape(out_shape).astype(F32),
        res.sec_grad.reshape(out_shape).astype(F32),
        *grads,
        res.g_eup[None],
        res.g_edown[None],
    )


def solution(mesh):
    batch = P(None, "dp", None, None)
    table = P(None, "dp", None)
    in_specs = (
        batch, batch, P(None, "dp"), table, table,
        P(None, BOTH), P(None, BOTH), P(None, None, BOTH), P(None, None, BOTH), P(None, BOTH),
        P(None, BOTH), P(BOTH), P(None, BOTH), P(BOTH), P(BOTH, None),
        P("dp", None, "section"), P("dp", "section", None),
    )
    streams = P("section", None, "dp", None, None)
    out_specs = (
        streams, streams,
        P(None, BOTH), P(None, BOTH), P(None, None, BOTH), P(None, None, BOTH), P(None, BOTH),
        P(None, BOTH), P(BOTH), P(None, BOTH), P(BOTH), P(BOTH, None),
        P("dp", None, "section"), P("dp", "section", None),
    )
    return jax.shard_map(body, mesh=mesh, in_specs=in_specs, out_specs=out_specs, check_vma=False)
```

```python
import functools
import types

import jax
import jax.numpy as jnp
from jax import lax
from jax.experimental import pallas as pl
from jax.experimental.pallas import tpu as pltpu
from jax.sharding import PartitionSpec as P

HEADS = 12
HEAD_DIM = 64
EPS = 1e-05
MASKED = -1000000000.0
MESH = pl.DeviceIdType.MESH
F32 = jnp.float32
BF16 = jnp.bfloat16
LANES = 128


def dot_as(left, right, left_dim, right_dim):
    return lax.dot_general(
        left, right, (((left_dim,), (right_dim,)), ((), ())), preferred_element_type=F32
    )


def mm(left, right):
    return dot_as(left, right, 1, 0)


def mm_nt(left, right):
    return dot_as(left, right, 1, 1)


def mm_tn(left, right):
    return dot_as(left, right, 0, 0)


def normalize(values):
    center = values - jnp.mean(values, axis=-1, keepdims=True)
    spread = jnp.mean(center * center, axis=-1, keepdims=True)
    inverse = lax.rsqrt(spread + EPS)
    return center * inverse, inverse


def gelu_parts(pre):
    half = 0.5 + 0.5 * lax.erf(pre * 0.7071067811865476)
    density = jnp.exp(-0.5 * pre * pre) * 0.3989422804014327
    return pre * half, half + pre * density


TAIL = 8
GROUP = 32
FIRST_ROUTER = 11


def layers_kernel(g, names, *refs):
    r = types.SimpleNamespace(**dict(zip(names, refs, strict=True)))
    width, span, hidden, cols, head_cols = g.width, g.span, g.hidden, g.cols, g.head_cols
    sec = lax.axis_index("section")
    dev = lax.axis_index("dp")
    core = lax.rem(dev, 2)
    chip = lax.div(dev, 2)
    sib = dev + 1 - 2 * core
    quarter = g.quarter
    shard_rows = hidden // g.devices
    block_rows = g.chips * quarter

    def peer_section(offset):
        return lax.rem(sec + offset, g.sections)

    def from_section(offset):
        return lax.rem(sec + g.sections - offset, g.sections)

    def peer_chip(offset):
        return lax.rem(chip + offset, g.chips)

    def from_chip(offset):
        return lax.rem(chip + g.chips - offset, g.chips)

    def rows_at(index, size):
        return pl.ds(pl.multiple_of(index * size, size), size)

    def remote(source, target, send, arrive, where):
        return pltpu.make_async_remote_copy(
            src_ref=source, dst_ref=target, send_sem=send, recv_sem=arrive, device_id=where, device_id_type=MESH
        )

    def at_chip_core(index):
        return {"dp": 2 * index + core}

    started = []
    kept_back = {}

    def do_when(condition, action):
        if condition is None:
            action()
        else:
            pl.when(condition)(action)

    def launch(copy, buffer=None, when=None):
        do_when(when, copy.start)
        if buffer:
            kept_back.setdefault(buffer, []).append((copy, when))
        else:
            started.append((copy, when))

    def settle(buffer):
        for copy, when in kept_back.pop(buffer, []):
            do_when(when, copy.wait_send)

    barrier = pltpu.get_barrier_semaphore()
    partners = [(a, b) for a in range(g.sections) for b in range(g.chips) if a + b and (g.direct or a * b == 0)]
    for section_offset, chip_offset in partners:
        where = {"section": peer_section(section_offset), "dp": 2 * peer_chip(chip_offset) + core}
        pl.semaphore_signal(barrier, inc=1, device_id=where, device_id_type=MESH)
    pl.semaphore_signal(barrier, inc=1, device_id={"dp": sib}, device_id_type=MESH)

    def local(index, source, target):
        return pltpu.make_async_copy(source, target, r.local_s.at[index])

    held = vars(r)
    loads = {name: local(i, held["h_" + name], held[name]) for i, name in enumerate(g.loads)}
    stores = []

    def store(*some):
        for name in some:
            index = len(loads) + g.stores.index(name)
            stores.append(local(index, held[name], held["h_" + name]))
            stores[-1].start()

    for copy in loads.values():
        copy.start()

    def token_slice(micro):
        return slice(micro * g.seq, (micro + 1) * g.seq)

    def piece_at(micro, section):
        return pl.ds(pl.multiple_of(micro * g.seq + section * g.piece, g.piece), g.piece)

    def own(micro):
        return piece_at(micro, sec)

    def scatter_copy(slot, micro, offset):
        return remote(
            r.part.at[slot, piece_at(micro, peer_section(offset))], r.got.at[slot, micro, offset - 1],
            r.scat_s.at[0], r.scat_r.at[slot, micro], {"section": peer_section(offset)},
        )

    def all_pieces(slot, micro, arrive):
        place = r.got.at[slot, micro]
        remote(place, place, r.scat_s.at[0], arrive, {"section": peer_section(1)}).wait_recv()

    def scatter_start(slot, micro, value):
        r.part[slot, token_slice(micro), :] = value.astype(BF16)
        if slot != 7:
            r.mine[token_slice(micro), :] = value
        for offset in range(1, g.sections):
            scatter_copy(slot, micro, offset).start()

    def scatter_sum(slot, micro):
        at = own(micro)
        total = r.part[slot, at, :].astype(F32) if slot == 7 else r.mine[at, :]
        all_pieces(slot, micro, r.scat_r.at[slot, micro])
        for offset in range(1, g.sections):
            total = total + r.got[slot, micro, offset - 1].astype(F32)
        return total

    def gather_start(buffer, slot, sem, micro):
        place = buffer.at[slot, own(micro)]
        for offset in range(1, g.sections):
            remote(place, place, r.gath_s.at[0], r.gath_r.at[sem, micro], {"section": peer_section(offset)}).start()

    def gather_wait(buffer, slot, sem, micro):
        all_pieces(sem, micro, r.gath_r.at[sem, micro])

    def exchanges_left():
        for sem in (r.scat_s, r.gath_s):
            remote(r.got, r.got, sem.at[0], r.scat_r.at[0, 0], {"section": peer_section(1)}).wait_send()

    def pair_copy(name, source, target):
        index = g.pairs.index(name)
        return remote(source, target, r.pair_s.at[index], r.pair_r.at[index], {"dp": sib})

    def pair_start(name, source, target, buffer=None):
        launch(pair_copy(name, source, target), buffer)

    def pair_wait(name, target):
        pair_copy(name, target, target).wait_recv()

    def line_copy(name, source, target, offset, receiving):
        index = g.lines.index(name)
        where = from_chip(offset) if receiving else peer_chip(offset)
        return remote(
            source, target, r.line_s.at[index, offset - 1], r.line_r.at[index, offset - 1], at_chip_core(where)
        )

    last_chip = g.chips - 1
    is_end = lax.rem(chip, max(last_chip, 1)) == 0
    is_mid = lax.rem(chip, max(last_chip, 1)) != 0
    line_order = (2, 1, 3) if g.relay else range(1, g.chips)
    outward = jnp.clip(chip - 1, 0, 1)

    def near_to(offset):
        return {1: chip != last_chip, last_chip: chip != 0}.get(offset) if g.relay else None

    def near_from(offset):
        return {1: chip != 0, last_chip: chip != last_chip}.get(offset) if g.relay else None

    def spread_first(name, source, target, buffer=None):
        if g.relay:
            for offset, when in ((2, is_end), (1, chip == 2), (3, chip == 1)):
                launch(line_copy(name, source, target, offset, False), buffer, when)

    def spread_more(name, source, target, buffer=None):
        if g.relay:
            for offset, when in ((2, is_mid), (1, chip < 2), (3, chip > 1)):
                launch(line_copy(name, source, target, offset, False), buffer, when)
        else:
            for offset in line_order:
                launch(line_copy(name, source, target, offset, False), buffer)

    def spread_relay(name, place, buffer):
        index = g.lines.index(name)
        copy = remote(
            place, place, r.line_s.at[index, last_chip], r.line_r.at[index, outward * 2],
            at_chip_core(outward * last_chip),
        )
        launch(copy, buffer, is_mid)

    def spread_pass(name, place_at, buffer):
        if g.relay:
            place = place_at(from_chip(2))
            line_copy(name, place, place, 2, True).wait_recv()
            spread_relay(name, place, buffer)

    def spread_wait(name, place_at):
        for offset in (1, 3) if g.relay else line_order:
            place = place_at(from_chip(offset))
            line_copy(name, place, place, offset, True).wait_recv()

    def far_wait(name, place_at):
        for offset in (1, last_chip):
            place = place_at(from_chip(offset))
            copy = line_copy(name, place, place, offset, True)
            pl.when(jnp.logical_not(near_from(offset)))(copy.wait_recv)

    left = []

    def wait_all(place, send, arrive, sent):
        copy = remote(place, place, send, arrive, {"dp": sib})
        if sent:
            copy.wait_send()
        else:
            copy.wait_recv()

    def line_start(name, source_at, target, share):
        index = g.manys.index(name)
        for offset in range(1, g.chips):
            at = peer_chip(offset)
            remote(source_at(at), target, r.many_s.at[index], r.many_r.at[index], at_chip_core(at)).start()
        left.append((share, r.many_s.at[index], r.many_r.at[index]))

    def line_wait(name, share):
        index = g.manys.index(name)
        wait_all(share, r.many_s.at[index], r.many_r.at[index], False)

    def other_chips(size=1):
        return pl.ds(0, (g.chips - 1) * size)

    def rows_plane_start(name, place_at):
        if g.parts > 1:
            place = place_at(pl.ds(1, g.parts - 1))
            plane_start(name, lambda to, offset: place_at(0), place_at, place)
        pair_start(name + "0", place_at(0), place_at(0))

    def rows_plane_wait(name, place_at):
        place = place_at(pl.ds(1, g.parts - 1))
        plane_wait(name, place)
        pair_start(name + "1", place, place)

    top = cols - TAIL
    half = width // 2
    part_cols = head_cols // 2
    tail_lane = head_cols + 2 * GROUP

    def qkv_section(at_dev, index, section):
        return lax.rem(lax.div(3 * at_dev + index, g.devices) - section + g.sections, g.sections)

    def qkv_send(layer, offsets):
        for index in range(3):
            to = qkv_section(dev, index, sec)
            for offset in offsets:
                copy = remote(
                    r.pq.at[layer, index], r.rq.at[layer, core, chip, index],
                    r.wq_s.at[index, offset + layer * g.chips], r.wq_r.at[index, offset + layer * g.chips],
                    {"section": to, "dp": 2 * peer_chip(offset) + core},
                )
                if offset:
                    launch(copy, None, near_to(offset))
                else:
                    pl.when(to != sec)(copy.start)

                    @pl.when(to == sec)
                    def _(index=index):
                        r.rq[layer, core, chip, index] = r.pq[layer, index]

    def qkv_arrive(layer, offsets):
        for offset in offsets:
            for index in range(3):
                at_chip = from_chip(offset)
                target = r.rq.at[layer, core, at_chip, index]
                origin = qkv_section(2 * at_chip + core, index, sec)
                copy = remote(
                    target, target, r.wq_s.at[index, offset + layer * g.chips],
                    r.wq_r.at[index, offset + layer * g.chips],
                    {"section": origin, "dp": 2 * at_chip + core},
                )
                if offset:
                    do_when(near_from(offset), copy.wait_recv)
                else:

                    @pl.when(origin != sec)
                    def _(copy=copy):
                        copy.wait_recv()
                        copy.wait_send()

            if g.relay and offset == 2:
                spread_relay("qkv0", r.rq.at[0, core, from_chip(offset)], "qkv0")
        if g.relay and len(offsets) > 1:
            far_wait("qkv0", lambda at: r.rq.at[0, core, at])

    def out_copy(section_offset, offset, place, receiving):
        if receiving:
            to, at_chip = from_section(section_offset), from_chip(offset)
        else:
            to, at_chip = peer_section(section_offset), peer_chip(offset)
        source = place if receiving else r.po.at[0, to]
        return remote(
            source, place, r.wo_s.at[offset], r.wo_r.at[offset],
            {"section": to, "dp": 2 * at_chip + core},
        )

    def out_all(offset, sent):
        count = g.sections if offset else g.sections - 1
        wait_all(r.po.at[0, pl.ds(0, count)], r.wo_s.at[offset], r.wo_r.at[offset], sent)

    def out_offsets():
        return [(a, b) for b in (*line_order, 0) for a in range(g.sections) if a + b]

    def plane_start(name, source_at, target_at, share):
        index = g.planes.index(name)
        for offset in range(1, g.sections):
            to = peer_section(offset)
            sems = r.plane_s.at[index], r.plane_r.at[index]
            remote(source_at(to, offset), target_at(offset), *sems, {"section": to}).start()
        left.append((share, r.plane_s.at[index], r.plane_r.at[index]))

    def plane_wait(name, share):
        index = g.planes.index(name)
        wait_all(share, r.plane_s.at[index], r.plane_r.at[index], False)

    def others():
        return pl.ds(0, g.sections - 1)

    def pack_wide(block):
        tail = jnp.concatenate([block[top:, :half], block[top:, half:]], axis=0)
        return jnp.concatenate([block[:top], tail], axis=1).astype(BF16)

    def pack_out(block):
        small = jnp.concatenate([block[top:, head_cols:]] * 2, axis=0)
        tail = jnp.concatenate([block[top:, :part_cols], block[top:, part_cols:head_cols]], axis=0)
        empty = jnp.zeros((top, g.out_lanes - tail_lane - part_cols), F32)
        return jnp.concatenate([block[:top], small, tail, empty], axis=1).astype(BF16)

    def unpack_wide(target, first, piece):
        target[first : first + top, 0:width] = piece[:, 0:width]
        target[first + top : first + cols, 0:half] = piece[0:TAIL, width : width + half]
        target[first + top : first + cols, half:width] = piece[TAIL:, width : width + half]

    def unpack_out(target, first, piece, lane=0):
        last = slice(first + top, first + cols)
        tail = slice(tail_lane, tail_lane + part_cols)
        target[first : first + top, lane : lane + head_cols] = piece[:, 0:head_cols]
        target[last, lane : lane + part_cols] = piece[0:TAIL, tail]
        target[last, lane + part_cols : lane + head_cols] = piece[TAIL:, tail]

    def unpack_small(target, first, piece, lane):
        target[first : first + top, lane : lane + GROUP] = piece[:, head_cols : head_cols + GROUP]
        target[first + top : first + cols, lane : lane + GROUP] = piece[0:TAIL, head_cols + GROUP : tail_lane]

    def shard_places():
        for at_core in range(2):
            for at_chip in range(g.chips):
                for at_sec in range(g.sections):
                    yield at_core, at_chip, at_sec, (at_sec * g.devices + 2 * at_chip + at_core) * cols

    def chunk_places():
        for at_core in range(2):
            for at_chip in range(g.chips):
                for index in range(3):
                    yield at_core, at_chip, index, (3 * (2 * at_chip + at_core) + index) * cols

    def unfold_out(layer):
        for at_core, at_chip, at_sec, first in shard_places():
            piece = r.ro[layer, at_core, at_chip, at_sec].astype(F32)
            if layer == 0:
                unpack_small(r.tmp, first, piece, head_cols)
            unpack_out(r.tmp, first, piece)
        flipped = r.tmp[:, 0:tail_lane].T
        r.w_out[layer] = flipped[:head_cols].astype(BF16)
        if layer == 0:
            r.prm[...] = flipped[head_cols : head_cols + GROUP]
            r.w_router[...] = r.tmp[:, tail_lane - LANES : tail_lane].astype(BF16)

    def unfold_qkv(layer):
        for at_core, at_chip, index, first in chunk_places():
            unpack_wide(r.tmp, first, r.rq[layer, at_core, at_chip, index].astype(F32))
        r.w_qkv[layer] = r.tmp[0 : 3 * head_cols, 0:width].astype(BF16)

    def unfold_down():
        for at_core, at_chip, at_sec, first in shard_places():
            unpack_wide(r.tmp, first, r.rd[at_core, at_chip, at_sec].astype(F32))
        r.w_down[...] = r.tmp[...].astype(BF16)

    def grad_copy(name, buffer_at, target, offset):
        index, at = g.grads.index(name), peer_chip(offset)
        place = target.at[offset - 1]
        return remote(buffer_at(at), place, r.grad_s.at[index], r.grad_r.at[index], at_chip_core(at))

    def grad_line(name, buffer_at, landing, target, passed):
        pair_wait(name, landing)
        for at_chip in range(g.chips):
            block = buffer_at(at_chip)
            block[...] = (block[...].astype(F32) + landing[at_chip].astype(F32)).astype(BF16)
        if g.relay:
            index = g.grads.index(name)
            copy = remote(
                buffer_at(last_chip - chip), passed, r.grad_s.at[index], r.pass_r.at[index],
                at_chip_core(1 + lax.div(chip, last_chip)),
            )
            pl.when(is_end)(copy.start)
            for offset in (1, last_chip):

                @pl.when(jnp.logical_not(near_from(offset)))
                def _(offset=offset):
                    target[offset - 1] = jnp.zeros_like(target[offset - 1])

        for offset in line_order:
            copy = grad_copy(name, buffer_at, target, offset)
            do_when(is_end if g.relay and offset == 2 else near_to(offset), copy.start)
        index = g.grads.index(name)
        left.append((target, r.grad_s.at[index], r.grad_r.at[index]))

    def grad_relay(name, buffer_at, target, passed):
        if g.relay:
            index = g.grads.index(name)
            block = buffer_at(peer_chip(2))
            copy = grad_copy(name, buffer_at, target, 2)

            @pl.when(is_mid)
            def _():
                wait_all(passed, r.grad_s.at[index], r.pass_r.at[index], False)
                block[...] = (block[...].astype(F32) + passed[...].astype(F32)).astype(BF16)
                copy.start()

    def grad_line_sum(name, buffer_at, target):
        index = g.grads.index(name)

        def arrive(count):
            wait_all(target.at[pl.ds(0, count)], r.grad_s.at[index], r.grad_r.at[index], False)

        if g.relay:
            pl.when(is_end)(lambda: arrive(2))
            pl.when(is_mid)(lambda: arrive(3))
        else:
            arrive(g.chips - 1)
        total = buffer_at(chip)[...].astype(F32)
        for offset in range(1, g.chips):
            total = total + target[offset - 1].astype(F32)
        return total

    def qkv_at(layer):
        return lambda at: r.rq.at[layer, core, at]

    def down_at(at):
        return r.rd.at[core, at]

    def out_at(layer):
        return lambda at: r.ro.at[layer, core, at]

    def up_at(at):
        return r.ru.at[at, core]

    def bias_at(at):
        return r.rb.at[at, core]

    def grad_plane(name, buffer_at, target, summed, final):
        summed[...] = grad_line_sum(name, buffer_at, target).astype(BF16)
        plane_start(name, lambda to, _: summed.at[to], lambda _: final.at[sec], summed.at[others()])
        final[sec] = summed[sec]

    def grad_plane_wait(name, final):
        plane_wait(name, final.at[others()])

    def grad_qkv_copy(layer, index, place, where):
        return remote(
            r.mq.at[layer, index], place, r.gq_s.at[layer, index], r.gq_r.at[layer, index], {"section": where}
        )

    def grad_qkv_plane(layer):
        r.mq[layer] = grad_line_sum("gqkv" + str(layer), qkv_at(layer), r.aq.at[layer]).astype(BF16)
        for index in range(3):
            to = qkv_section(dev, index, sec)
            copy = grad_qkv_copy(layer, index, r.fq.at[layer, index], to)
            pl.when(to != sec)(copy.start)

            @pl.when(to == sec)
            def _(index=index):
                r.fq[layer, index] = r.mq[layer, index]

    def grad_qkv_finish(layer):
        for index in range(3):
            origin = qkv_section(dev, index, sec)
            copy = grad_qkv_copy(layer, index, r.fq.at[layer, index], origin)

            @pl.when(origin != sec)
            def _(copy=copy):
                copy.wait_recv()
                copy.wait_send()

            unpack_wide(r.o_qkv.at[layer], index * cols, r.fq[layer, index].astype(F32))

    def norm_into(source, target, index, micro):
        rows = g.seq // 2

        @pl.loop(0, 2)
        def _(step):
            at = rows_at(micro * 2 + step, rows)
            unit, _ = normalize(source[at, :].astype(F32))
            target[at, :] = (unit * r.prm[index : index + 1, :] + r.prm[4 + index : 5 + index, :]).astype(BF16)

    place_row = jnp.concatenate(
        [r.routes[m : m + 1] * span + m * g.cap + r.slots[m : m + 1] for m in range(g.micro)], axis=1
    )
    r.square[...] = jnp.zeros_like(r.square)
    if g.direct:
        r.square[0:4, 0:cols] = r.norm_gain[...].astype(F32)
        r.square[4:8, 0:cols] = r.norm_bias[...].astype(F32)
        r.square[8:10, 0:cols] = r.out_bias[...].astype(F32)
        r.square[10:11, 0:cols] = r.down_bias[...].astype(F32)
        r.pb[...] = jnp.zeros_like(r.pb)
        r.pb[:, 0:shard_rows] = jnp.broadcast_to(r.up_bias[...], (r.pb.shape[0], shard_rows))
        r.square[FIRST_ROUTER : FIRST_ROUTER + g.experts, 0:cols] = r.router[...].astype(F32)
        r.square[...] = r.square[...].T
        loads["wo"].wait()
        loads["wq"].wait()
        shard = r.wo[0].astype(F32)
        mine = r.square[0:cols, 0:GROUP]
        for at_sec in range(g.sections):
            block = shard[:, at_sec * head_cols : (at_sec + 1) * head_cols]
            r.po[0, at_sec] = pack_out(jnp.concatenate([block, mine], axis=1))
        shard = r.wq[0].astype(F32)
        for index in range(3):
            r.pq[0, index] = pack_wide(shard[index * cols : (index + 1) * cols])
    pl.semaphore_wait(barrier, len(partners) + 1)
    if g.direct:
        for section_offset, offset in out_offsets():
            copy = out_copy(section_offset, offset, r.ro.at[0, core, chip, sec], False)
            do_when(near_to(offset), copy.start)
        r.ro[0, core, chip, sec] = r.po[0, sec]
        qkv_send(0, (*line_order, 0))
        loads["wu"].wait()
        loads["wd"].wait()
        shard = r.wq[1].astype(F32)
        for index in range(3):
            r.pq[1, index] = pack_wide(shard[index * cols : (index + 1) * cols])
        shard, other = r.wd[...].astype(F32), r.wo[1].astype(F32)
        empty = jnp.zeros((cols, GROUP), F32)
        for at_sec in range(g.sections):
            r.pd[at_sec] = pack_wide(shard[:, at_sec * hidden : (at_sec + 1) * hidden])
            block = other[:, at_sec * head_cols : (at_sec + 1) * head_cols]
            r.po[1, at_sec] = pack_out(jnp.concatenate([block, empty], axis=1))

    loads["x0"].wait()
    loads["cot"].wait()
    slot_ids = lax.broadcasted_iota(jnp.int32, (quarter, g.tokens), 0)

    def slot_match(expert, part, group):
        first = expert * span + group * (span // g.groups) + part * quarter
        return jnp.where(slot_ids + first == place_row, 1.0, 0.0).astype(BF16)

    def group_tokens(group):
        count = g.tokens // g.groups
        return slice(group * count, (group + 1) * count)

    for group in range(g.groups):
        for expert in range(g.chips):
            match = slot_match(expert, g.my_part(sec), group)
            r.table[group, expert * quarter : (expert + 1) * quarter, :] = match[:, group_tokens(group)]
        sent = mm(r.table[group], r.cot[group_tokens(group), :]).astype(BF16)
        r.dispc[:, group] = sent.reshape(g.chips, quarter, width)
    r.small[...] = jnp.zeros_like(r.small)
    if g.direct:
        for offset in (*line_order, 0):
            do_when(near_from(offset), lambda offset=offset: out_all(offset, False))
            if g.relay and offset == 2:
                spread_relay("out0", r.ro.at[0, core, from_chip(offset)], "out0")
        if g.relay:
            far_wait("out0", lambda at: r.ro.at[0, core, at])
        pair_start("out0", r.ro.at[0, core], r.ro.at[0, core], "out0")
        qkv_arrive(0, (*line_order, 0))
        pair_start("qkv0", r.rq.at[0, core], r.rq.at[0, core], "qkv0")
        spread_first("bias", r.pb, r.rb.at[chip, core])
        spread_more("bias", r.pb, r.rb.at[chip, core])
        r.rb[chip, core] = r.pb[...]
        spread_first("up", r.wu, r.ru.at[chip, core])
        r.ru[chip, core] = r.wu[...]
        plane_start("down", lambda to, _: r.pd.at[to], lambda _: r.rd.at[core, chip, sec], r.pd.at[others()])
        r.rd[core, chip, sec] = r.pd[sec]
        qkv_send(1, [0])
        place = r.ro.at[1, core, chip, sec]
        plane_start("out1", lambda to, _: r.po.at[1, to], lambda _: place, r.po.at[1, others()])
        r.ro[1, core, chip, sec] = r.po[1, sec]
        pair_wait("out0", r.ro.at[0, 1 - core])
        unfold_out(0)
        pair_wait("qkv0", r.rq.at[0, 1 - core])
        unfold_qkv(0)

    def up_place(at):
        return r.ru.at[at, core]

    def bias_place(at):
        return r.rb.at[at, core]

    def down_place(at):
        return r.rd.at[core, at]

    def qkv_place(at):
        return r.rq.at[1, core, at]

    def out_place(at):
        return r.ro.at[1, core, at]

    def own_first(name, place_at):
        spread_first(name, place_at(chip), place_at(chip), name)

    def own_more(name, place_at):
        spread_more(name, place_at(chip), place_at(chip), name)

    key_ids = lax.broadcasted_iota(jnp.int32, (g.seq, g.seq), 0)
    query_ids = lax.broadcasted_iota(jnp.int32, (g.seq, g.seq), 1)
    scale = HEAD_DIM**-0.5
    micros = range(g.micro)

    def block_of(index):
        return lax.rem(index + sec, 3) if g.direct else index

    def head_slice(head):
        return slice(head * HEAD_DIM, (head + 1) * HEAD_DIM)

    def attention_forward(layer, stream, slot, micro):
        at = token_slice(micro)
        norm_into(stream, r.normed.at[2 * layer], 2 * layer, micro)
        packed = mm_nt(r.w_qkv[layer], r.normed[2 * layer, at, :]).astype(BF16)
        r.qkv[layer, :, :, at] = packed.reshape(3, head_cols, g.seq)
        allowed = (key_ids <= query_ids) & (key_ids < r.lens[:, micro : micro + 1])
        for head in range(g.heads):
            key = r.qkv[layer, block_of(1), head_slice(head), at]
            scores = mm_tn(key, r.qkv[layer, block_of(0), head_slice(head), at]) * scale
            scores = jnp.where(allowed, scores, MASKED)
            weight = jnp.exp(scores - jnp.max(scores, axis=0, keepdims=True))
            weight = weight / jnp.sum(weight, axis=0, keepdims=True)
            r.probs[layer, micro, head] = weight
            value = r.qkv[layer, block_of(2), head_slice(head), at]
            r.ctx[layer, head_slice(head), at] = mm(value, weight.astype(BF16)).astype(BF16)
        scatter_start(slot, micro, mm_tn(r.ctx[layer, :, at], r.w_out[layer]))

    def finish_forward(section, bias, stream, micro):
        total = scatter_sum(section, micro) + bias + stream[own(micro), :].astype(F32)
        r.xs[section, own(micro), :] = total.astype(BF16)
        gather_start(r.xs, section, section, micro)

    for micro in micros:
        attention_forward(0, r.x0, 0, micro)
        if g.direct and micro == 0:
            spread_more("up", r.wu, r.ru.at[chip, core])
    if g.direct:
        spread_pass("bias", bias_place, "bias")
        spread_pass("up", up_place, "up")
        plane_wait("down", r.pd.at[others()])
        own_first("down", down_place)
    for micro in micros:
        finish_forward(0, r.prm[8:9, :], r.x0, micro)
    if g.direct:
        own_more("down", down_place)
        spread_wait("bias", bias_place)
        spread_wait("up", up_place)
        pair_start("up", r.ru.at[:, core], r.ru.at[:, core], "up")
        pair_start("bias", r.rb.at[:, core], r.rb.at[:, core], "bias")
        pair_wait("up", r.ru.at[:, 1 - core])
        pair_wait("bias", r.rb.at[:, 1 - core])
        for at_dev in range(g.devices):
            row = r.rb[at_dev // 2, at_dev % 2, :, 0:shard_rows].astype(F32)
            r.b_up[:, at_dev * shard_rows : (at_dev + 1) * shard_rows] = row[0:TAIL]

    def up_rows(at):
        if g.direct:
            return r.ru[...].reshape(hidden, width)[at]
        return r.w_up[at, :]

    def hidden_blocks():
        return [slice(first, first + g.block) for first in range(0, hidden, g.block)]

    for micro in micros:
        rows = token_slice(micro)
        gather_wait(r.xs, 0, 0, micro)
        norm_into(r.xs.at[0], r.normed.at[1], 1, micro)
        for at in hidden_blocks():
            value, slope = gelu_parts(mm_nt(r.normed[1, rows, :], up_rows(at)) + r.b_up[0:1, at])
            r.act[rows, at] = value.astype(BF16)
            r.dgelu[rows, at] = slope
        if g.direct and micro == 0:
            spread_pass("down", down_place, "down")
            qkv_arrive(1, [0])
            own_first("qkv1", qkv_place)
            own_more("qkv1", qkv_place)
    if g.direct:
        spread_wait("down", down_place)
        pair_start("down", r.rd.at[core], r.rd.at[core], "down")
        plane_wait("out1", r.po.at[1, others()])
        own_first("out1", out_place)
        own_more("out1", out_place)
        pair_wait("down", r.rd.at[1 - core])
        unfold_down()
    for micro in micros:
        scatter_start(1, micro, mm_nt(r.act[token_slice(micro), :], r.w_down[...]))
    if g.direct:
        spread_pass("qkv1", qkv_place, "qkv1")
    for micro in micros:
        finish_forward(1, r.prm[10:11, :], r.xs.at[0], micro)
        if g.direct and micro == 0:
            spread_pass("out1", out_place, "out1")
    if g.direct:
        spread_wait("qkv1", qkv_place)
        pair_start("qkv1", r.rq.at[1, core], r.rq.at[1, core], "qkv1")
        spread_wait("out1", out_place)
        pair_start("out1", r.ro.at[1, core], r.ro.at[1, core], "out1")

    def crow_at(part, side):
        return r.crow.at[:, part, side]

    crow_share = r.dispc.at[other_chips()]
    place = r.crow.at[:, 0, core, rows_at(chip, quarter)]
    line_start("crow", lambda at: r.dispc.at[at], place, crow_share)
    r.crow[:, 0, core, rows_at(chip, quarter), :] = r.dispc[chip]

    if g.direct:
        pair_wait("qkv1", r.rq.at[1, 1 - core])
        unfold_qkv(1)
        pair_wait("out1", r.ro.at[1, 1 - core])
        unfold_out(1)
    for micro in micros:
        gather_wait(r.xs, 1, 1, micro)
        attention_forward(1, r.xs.at[1], 2, micro)
    for micro in micros:
        finish_forward(2, r.prm[9:10, :], r.xs.at[1], micro)
    r.square[0 : g.micro, :] = jnp.concatenate(
        [place_row[:, token_slice(micro)] for micro in micros], axis=0
    ).astype(F32)
    columns = r.square[...].T

    wide = r.wide

    def gates(micro):
        at = token_slice(micro)
        norm_into(r.xs.at[2], wide.at[:, pl.ds(0, width)], 3, micro)
        logits = mm(wide[at, :width], r.w_router[...])
        lane = lax.broadcasted_iota(jnp.int32, logits.shape, 1) - g.router_lane
        place_col = columns[:, micro : micro + 1].astype(jnp.int32)
        chosen = (place_col >= lane * span) & (place_col < lane * span + span)
        score = jnp.sum(jnp.where(chosen, logits, 0.0), axis=-1, keepdims=True)
        gate = 1.0 / (1.0 + jnp.exp(-score))
        gate_high = gate.astype(BF16).astype(F32)
        lane = lax.broadcasted_iota(jnp.int32, (g.seq, LANES), 1)
        pair = jnp.where(lane == 0, gate_high, jnp.where(lane == 1, gate - gate_high, 0.0))
        wide[at, width:] = pair.astype(BF16)

    groups = range(g.groups)

    def rows_place(group, side):
        return lambda part: r.rows.at[group, part, side]

    def rows_line_start(group):
        name = "rows" + str(group)
        r.disp[group] = mm(r.table[group], wide[group_tokens(group), :]).astype(BF16)
        place = r.rows.at[group, 0, core, rows_at(chip, quarter)]
        share = r.disp.at[group, other_chips(quarter)]
        line_start(name, lambda at: r.disp.at[group, rows_at(at, quarter)], place, share)
        r.rows[group, 0, core, rows_at(chip, quarter), :] = r.disp[group, rows_at(chip, quarter), :]

    def rows_line_wait(group):
        name = "rows" + str(group)
        line_wait(name, r.disp.at[group, other_chips(quarter)])
        place_at = rows_place(group, core)
        for offset in range(1, g.parts):
            sems = r.row_s.at[group], r.row_r.at[group, offset - 1]
            remote(place_at(0), place_at(offset), *sems, {"section": peer_section(offset)}).start()
        if g.parts > 1:
            left.append((place_at(pl.ds(1, g.parts - 1)), r.row_s.at[group], r.row_r.at[group, 0]))
        pair_start(name + "0", place_at(0), place_at(0))

    for micro in micros:
        gather_wait(r.xs, 2, 2, micro)
        if micro == 0:
            line_wait("crow", crow_share)
            rows_plane_start("crow", lambda part: crow_at(part, core))
        gates(micro)
        if g.groups > 1:
            rows_line_start(micro)
    if g.groups == 1:
        rows_line_start(0)
    for group in groups:
        rows_line_wait(group)
    loads["e_up"].wait()
    loads["e_down"].wait()

    own_router = FIRST_ROUTER + chip
    router_row = r.prm[pl.ds(own_router, 1), :]
    snd = dict(d=r.snd_d, y=r.snd_y)
    kept = dict(d=r.keep_d, y=r.keep_y)
    rcv = dict(d=r.rcv_d, y=r.rcv_y)

    def expert_block(wide_rows, cot_rows):
        row = wide_rows[:, :width]
        tail = wide_rows[:, width:].astype(F32)
        gate_row = tail[:, 0:1] + tail[:, 1:2]
        grad_row = (gate_row * cot_rows.astype(F32)).astype(BF16)
        value, slope = gelu_parts(mm(row, r.e_up[...]))
        value = value.astype(BF16)
        result = mm(value, r.e_down[...])
        total = jnp.sum(grad_row.astype(F32) * result, axis=-1, keepdims=True) * (1.0 - gate_row)
        inner = (slope * mm_nt(grad_row, r.e_down[...])).astype(BF16)
        back = mm_nt(inner, r.e_up[...]) + total * router_row
        r.small[pl.ds(own_router, 1), :] += jnp.sum(row.astype(F32) * total, axis=0, keepdims=True)
        return grad_row, value, inner, back, result * gate_row

    def expert_parts(group, first, count):
        parts = slice(first, first + count)
        each = 2 * block_rows
        if each <= g.block:
            lead = (count, 2, block_rows)
            found = expert_block(
                r.rows[group, parts].reshape(count * each, width + LANES),
                r.crow[group, parts].reshape(count * each, width),
            )
            for target, value in zip((r.grow, r.acte, r.dpree), found[:3], strict=True):
                target[group, parts] = value.reshape(*lead, value.shape[-1])
            r.both[0, parts] = found[3].reshape(*lead, width)
            r.both[1, parts] = found[4].reshape(*lead, width)
        else:
            for part in range(first, first + count):
                for side in range(2):

                    @pl.loop(0, block_rows // g.block)
                    def _(step, part=part, side=side):
                        at = rows_at(step, g.block)
                        found = expert_block(r.rows[group, part, side, at, :], r.crow[group, part, side, at, :])
                        for target, value in zip((r.grow, r.acte, r.dpree), found[:3], strict=True):
                            target[group, part, side, at, :] = value
                        r.both[0, part, side, at, :] = found[3]
                        r.both[1, part, side, at, :] = found[4]

        parts_send("d", r.both.at[0], group, first, count)

    def parts_send(which, value, group, first, count):
        for part in range(first, first + count):
            snd[which][group, part] = value[part, 1 - core].astype(BF16)
            if which == "d":
                pair_start(which + str(group) + str(part), snd[which].at[group, part], rcv[which].at[group, part])
        if which == "y":
            parts = pl.ds(first, count)
            name = which + str(group) + str(min(first, 1))
            pair_start(name, snd[which].at[group, parts], rcv[which].at[group, parts])
        for part in range(first, first + count):
            kept[which][group, part] = value[part, core]

    def results_pair(group, first, count):
        parts_send("y", r.both.at[1], group, first, count)

    def merge_ready(which, group, first, count):
        pair_wait(which + str(group) + str(min(first, 1)), rcv[which].at[group, pl.ds(first, count)])

    def merge(which, offset, group):
        return kept[which][group, offset] + rcv[which][group, offset].astype(F32)

    def merge_send(group):
        index = g.planes.index("d" + str(group))
        for offset in range(1, g.sections):
            to = g.sections - offset
            pair_wait("d" + str(group) + str(offset), rcv["d"].at[group, offset])
            r.out_d[offset - 1, group] = merge("d", offset, group).astype(BF16)
            sems = r.plane_s.at[index], r.plane_r.at[index]
            source, target = r.out_d.at[offset - 1, group], r.plane_d.at[to - 1, group]
            remote(source, target, *sems, {"section": peer_section(to)}).start()
        left.append((r.out_d.at[:, group], r.plane_s.at[index], r.plane_r.at[index]))

    def parts_work(group, first, count):
        parts, tag = pl.ds(first, count), str(min(first, 1))
        if group == 0:
            pair_wait("crow" + tag, crow_at(parts, 1 - core))
        for part in range(first, first + count):
            pair_wait("rows" + str(group) + str(part), rows_place(group, 1 - core)(part))
        expert_parts(group, first, count)

    def results_line(group):
        merge_ready("y", group, 0, 1)
        if g.parts > 1:
            merge_ready("y", group, 1, g.parts - 1)
        for offset in range(g.parts):
            r.ret_y[group, offset] = merge("y", offset, group).astype(BF16)
        name = "y" + str(group)
        place, share = r.back_y.at[chip, group], r.ret_y.at[group, :, other_chips(quarter)]
        line_start(name, lambda at: r.ret_y.at[group, :, rows_at(at, quarter)], place, share)
        r.back_y[chip, group] = r.ret_y[group, :, rows_at(chip, quarter), :]

    def expert_back_line(group):
        name = "d" + str(group)
        pair_wait("d" + str(group) + "0", rcv["d"].at[group, 0])
        total = merge("d", 0, group)
        if g.parts > 1:
            plane_wait(name, r.plane_d.at[:, group])
            for offset in range(1, g.sections):
                place = r.plane_d.at[offset - 1, group]
                total = total + place[...].astype(F32)
        r.ret_d[group] = total.astype(BF16)
        place = r.back_d.at[group, rows_at(chip, quarter)]
        share = r.ret_d.at[group, other_chips(quarter)]
        line_start(name, lambda at: r.ret_d.at[group, rows_at(at, quarter)], place, share)
        r.back_d[group, rows_at(chip, quarter), :] = r.ret_d[group, rows_at(chip, quarter), :]

    def expert_combine(group):
        line_wait("d" + str(group), r.ret_d.at[group, other_chips(quarter)])
        value = mm_tn(r.table[group], r.back_d[group])
        if g.groups > 1:
            scatter_start(3, group, value)
        else:
            for micro in micros:
                scatter_start(3, micro, value[token_slice(micro)])

    def results_combine():
        for group in groups:
            line_wait("y" + str(group), r.ret_y.at[group, :, other_chips(quarter)])
        places = [(e, q, p) for e in range(g.chips) for q in groups for p in range(g.parts)]
        match = [slot_match(e, g.my_part(from_section(p)), q) for e, q, p in places]
        match = jnp.concatenate(match, axis=0)
        value = mm_tn(match, r.back_y[...].reshape(g.chips * span, width))
        for micro in micros:
            scatter_start(7, micro, value[token_slice(micro)])

    for group in groups:
        parts_work(group, 0, 1)
        results_pair(group, 0, 1)
    if g.parts > 1:
        rows_plane_wait("crow", lambda part: crow_at(part, core))
    for group in groups:
        if g.parts > 1:
            for offset in range(1, g.parts):
                place = rows_place(group, core)(offset)
                wait_all(place, r.row_s.at[group], r.row_r.at[group, offset - 1], False)
                pair_start("rows" + str(group) + str(offset), place, place)
            parts_work(group, 1, g.parts - 1)
            merge_send(group)
            results_pair(group, 1, g.parts - 1)
        if group < g.groups - 1:
            results_line(group)
    for group in groups:
        expert_back_line(group)

    def expert_weights(left, right):
        rows = g.groups * g.parts * 2 * block_rows
        return mm_tn(left.reshape(rows, left.shape[-1]), right.reshape(rows, right.shape[-1]))

    r.g_eup[...] = expert_weights(r.rows[:, :, :, :, :width], r.dpree[...])
    r.g_edown[...] = expert_weights(r.acte[...], r.grow[...])
    store("g_eup", "g_edown")

    def add_small(index, micro, value):
        if micro == 0:
            r.small[index : index + 1, :] = value
        else:
            r.small[index : index + 1, :] += value

    def finish_backward(section, slot, stream, above, micro):
        grad = scatter_sum(slot, micro)
        unit, inverse = normalize(stream[own(micro), :].astype(F32))
        add_small(section, micro, jnp.sum(grad * unit, axis=0, keepdims=True))
        add_small(4 + section, micro, jnp.sum(grad, axis=0, keepdims=True))
        grad = grad * r.prm[section : section + 1, :]
        shared = jnp.mean(grad, axis=-1, keepdims=True)
        along = jnp.mean(grad * unit, axis=-1, keepdims=True)
        grad = inverse * (grad - shared - unit * along) + above[own(micro), :].astype(F32)
        r.gs[section, own(micro), :] = grad.astype(BF16)
        gather_start(r.gs, section, 4 + section, micro)

    for group in groups:
        expert_combine(group)
    results_line(g.groups - 1)
    for micro in micros:
        finish_backward(3, 3, r.xs.at[2], r.cot, micro)

    def bias_row(index, section):
        for micro in micros:
            value = r.gs[section, own(micro), :].astype(F32)
            add_small(index, micro, jnp.sum(value, axis=0, keepdims=True))

    def attention_backward(layer, section, slot, micro):
        at = token_slice(micro)
        dctx = mm_nt(r.w_out[layer], r.gs[section + 1, at, :]).astype(BF16)
        for head in range(g.heads):
            weight = r.probs[layer, micro, head]
            low = weight.astype(BF16)
            dhead = dctx[head_slice(head)]
            query = r.qkv[layer, block_of(0), head_slice(head), at]
            key = r.qkv[layer, block_of(1), head_slice(head), at]
            value = r.qkv[layer, block_of(2), head_slice(head), at]
            dprobs = mm_tn(value, dhead)
            delta = jnp.sum(weight * dprobs, axis=0, keepdims=True)
            dscores = (weight * (dprobs - delta)).astype(BF16)
            r.dqkv[block_of(0), head_slice(head), at] = (mm(key, dscores) * scale).astype(BF16)
            r.dqkv[block_of(1), head_slice(head), at] = (mm_nt(query, dscores) * scale).astype(BF16)
            r.dqkv[block_of(2), head_slice(head), at] = mm_nt(dhead, low).astype(BF16)
        flat_grad = r.dqkv[:, :, at].reshape(3 * head_cols, g.seq)
        scatter_start(slot, micro, mm_tn(flat_grad, r.w_qkv[layer]))

    def attention_weights(layer, section):
        grad_qkv = mm(r.dqkv[...].reshape(3 * head_cols, g.tokens), r.normed[2 * layer])
        if not g.direct:
            r.o_qkv[layer] = grad_qkv
            r.o_out[layer] = mm(r.ctx[layer], r.gs[section + 1])
            return
        r.tmp[0 : 3 * head_cols, :] = grad_qkv
        settle("qkv" + str(layer))
        for at_core, at_chip, index, first in chunk_places():
            r.rq[layer, at_core, at_chip, index] = pack_wide(r.tmp[first : first + cols, :])
        name = "gqkv" + str(layer)
        pair_start(name, r.rq.at[layer, 1 - core], r.hq.at[layer])
        if layer == 0:
            r.tmp[:, 0:head_cols] = dot_as(r.gs[1], r.ctx[0], 0, 1)

    def out_weights_ahead():
        r.tmp[:, 0:head_cols] = dot_as(r.gs[3], r.ctx[1], 0, 1)
        r.tmp[:, head_cols : head_cols + GROUP] = jnp.zeros((width, GROUP), F32)
        out_weights(1)

    def down_weights_ahead():
        r.tmp[...] = mm_tn(r.gs[2], r.act[...])
        settle("down")
        for at_core, at_chip, at_sec, first in shard_places():
            r.rd[at_core, at_chip, at_sec] = pack_wide(r.tmp[first : first + cols, :])
        pair_start("gdown", r.rd.at[1 - core], r.hd)

    def out_weights(layer):
        settle("out" + str(layer))
        for at_core, at_chip, at_sec, first in shard_places():
            block = r.tmp[first : first + cols, 0 : head_cols + GROUP]
            r.ro[layer, at_core, at_chip, at_sec] = pack_out(block)
        pair_start("gout" + str(layer), r.ro.at[layer, 1 - core], r.ho.at[layer])

    for micro in micros:
        gather_wait(r.gs, 3, 7, micro)
        if g.direct and micro == g.micro - 1:
            out_weights_ahead()
        attention_backward(1, 2, 4, micro)
    bias_row(9, 3)
    if g.direct:
        grad_line("gout1", out_at(1), r.ho.at[1], r.ao.at[1], r.lo.at[1])
    attention_weights(1, 2)
    if g.direct:
        grad_line("gqkv1", qkv_at(1), r.hq.at[1], r.aq.at[1], r.lq.at[1])
    finish_backward(2, 4, r.xs.at[1], r.gs.at[3], 0)
    for micro in micros[1:]:
        finish_backward(2, 4, r.xs.at[1], r.gs.at[3], micro)

    for micro in micros:
        rows = token_slice(micro)
        gather_wait(r.gs, 2, 6, micro)
        if g.direct and micro == g.micro - 1:
            down_weights_ahead()
        grad_two = r.gs[2, rows, :]
        for at in hidden_blocks():
            r.dpre[rows, at] = (r.dgelu[rows, at] * mm(grad_two, r.w_down[:, at])).astype(BF16)
        scatter_start(5, micro, mm(r.dpre[rows, :], up_rows(slice(None))))
    bias_row(10, 2)
    sum_up = jnp.sum(r.dpre[...].astype(F32), axis=0, keepdims=True)
    if g.direct:
        grad_relay("gqkv1", qkv_at(1), r.aq.at[1], r.lq.at[1])
        grad_relay("gout1", out_at(1), r.ao.at[1], r.lo.at[1])
        grad_line("gdown", down_at, r.hd, r.ad, r.ld)
        settle("up")
        settle("bias")
        r.ru[...] = mm_tn(r.dpre[...], r.normed[1]).astype(BF16).reshape(r.ru.shape)
        pair_start("gup", r.ru.at[:, 1 - core], r.hu)
        for at_dev in range(g.devices):
            row = sum_up[:, at_dev * shard_rows : (at_dev + 1) * shard_rows]
            row = jnp.broadcast_to(row, (r.pb.shape[0], shard_rows)).astype(BF16)
            r.rb[at_dev // 2, at_dev % 2, :, 0:shard_rows] = row
        pair_start("gbias", r.rb.at[:, 1 - core], r.hb)
    else:
        r.o_down[...] = mm_tn(r.gs[2], r.act[...])
        r.o_up[...] = mm_tn(r.dpre[...], r.normed[1])
        r.o_bup[...] = sum_up
    for micro in micros:
        finish_backward(1, 5, r.xs.at[0], r.gs.at[2], micro)
    if g.direct:
        grad_line("gbias", bias_at, r.hb, r.ab, r.lb)
        grad_relay("gdown", down_at, r.ad, r.ld)

    for micro in micros:
        gather_wait(r.gs, 1, 5, micro)
        attention_backward(0, 0, 6, micro)
    bias_row(8, 1)
    attention_weights(0, 0)
    finish_backward(0, 6, r.x0, r.gs.at[1], 0)
    if g.direct:
        grad_line("gqkv0", qkv_at(0), r.hq.at[0], r.aq.at[0], r.lq.at[0])
    for micro in micros[1:]:
        finish_backward(0, 6, r.x0, r.gs.at[1], micro)
    if g.direct:
        kinds = r.small[...]
        padded = jnp.concatenate([kinds, jnp.zeros((LANES - kinds.shape[0], width), F32)], axis=0)
        r.tmp[:, head_cols : head_cols + GROUP] = padded.T[:, 0:GROUP]
        out_weights(0)
        grad_line("gout0", out_at(0), r.ho.at[0], r.ao.at[0], r.lo.at[0])
        grad_line("gup", up_at, r.hu, r.au, r.lu)
        grad_relay("gbias", bias_at, r.ab, r.lb)
    results_combine()
    if g.direct:
        grad_qkv_plane(1)
        grad_plane("gout1", out_at(1), r.ao.at[1], r.mo.at[1], r.fo.at[1])
        grad_plane("gdown", down_at, r.ad, r.md, r.fd)
        grad_relay("gqkv0", qkv_at(0), r.aq.at[0], r.lq.at[0])
        grad_relay("gout0", out_at(0), r.ao.at[0], r.lo.at[0])
    for micro in micros:
        r.xs[3, own(micro), :] = (scatter_sum(7, micro) + r.xs[2, own(micro), :].astype(F32)).astype(BF16)
        gather_start(r.xs, 3, 3, micro)
    if g.direct:
        grad_relay("gup", up_at, r.au, r.lu)
    for micro in micros:
        gather_wait(r.xs, 3, 3, micro)
        gather_wait(r.gs, 0, 4, micro)
    r.sec_out[...] = r.xs[sec]
    r.sec_grad[...] = r.gs[sec]
    store("sec_out", "sec_grad")
    if g.direct:
        grad_qkv_plane(0)
        grad_plane("gout0", out_at(0), r.ao.at[0], r.mo.at[0], r.fo.at[0])
        grad_qkv_finish(1)
        grad_plane_wait("gdown", r.fd)
        for at_sec in range(g.sections):
            piece = r.fd[at_sec].astype(F32)
            unpack_wide(r.o_down.at[:, pl.ds(at_sec * hidden, hidden)], 0, piece)
        store("o_down")
        r.o_up[...] = grad_line_sum("gup", up_at, r.au)
        r.o_bup[...] = grad_line_sum("gbias", bias_at, r.ab)[0:1, 0:shard_rows]
        store("o_up", "o_bup")
        grad_plane_wait("gout1", r.fo.at[1])
        for at_sec in range(g.sections):
            unpack_out(r.o_out.at[1], 0, r.fo[1, at_sec].astype(F32), at_sec * head_cols)
        grad_qkv_finish(0)
        store("o_qkv")
        grad_plane_wait("gout0", r.fo.at[0])
        everyone = jnp.zeros((top, g.out_lanes), F32)
        for at_sec in range(g.sections):
            piece = r.fo[0, at_sec].astype(F32)
            unpack_out(r.o_out.at[0], 0, piece, at_sec * head_cols)
            everyone = everyone + piece
        r.square[...] = jnp.zeros_like(r.square)
        unpack_small(r.square, 0, everyone, 0)
        r.square[...] = r.square[...].T
        r.o_router[...] = r.square[FIRST_ROUTER : FIRST_ROUTER + g.experts, 0:cols]
        r.o_gain[...] = r.square[0:4, 0:cols]
        r.o_bias[...] = r.square[4:8, 0:cols]
        r.o_bout[...] = r.square[8:10, 0:cols]
        r.o_bdown[...] = r.square[10:11, 0:cols]
        store("o_out", "o_gain", "o_bias", "o_bout", "o_bdown", "o_router")
    else:
        r.o_small[...] = r.small[...]
        store("o_qkv", "o_out", "o_up", "o_down", "o_bup", "o_small")
    for copy in stores:
        copy.wait()
    exchanges_left()
    if g.direct:
        for offset in range(g.chips):
            do_when(near_to(offset), lambda offset=offset: out_all(offset, True))
    for share, send, arrive in left:
        wait_all(share, send, arrive, True)
    for copy, when in started:
        do_when(when, copy.wait_send)


def run_layers(g, operands):
    tokens, width, hidden, sections, chips = g.tokens, g.width, g.hidden, g.sections, g.chips
    part_rows = chips * g.quarter
    inner = operands["h_e_down"].shape[0]
    three = 3 * g.head_cols
    shape = jax.ShapeDtypeStruct
    vmem = pltpu.VMEM
    dma = pltpu.SemaphoreType.DMA
    top = g.cols - TAIL
    wide = width + width // 2
    up_rows = hidden // g.devices
    outs = dict(
        sec_out=shape((tokens, width), BF16),
        sec_grad=shape((tokens, width), BF16),
        g_eup=shape((width, inner), F32),
        g_edown=shape((inner, width), F32),
    )
    if g.direct:
        outs |= dict(
            o_qkv=shape((2, 3 * g.cols, width), F32),
            o_out=shape((2, g.cols, width), F32),
            o_up=shape((up_rows, width), F32),
            o_down=shape((g.cols, sections * hidden), F32),
            o_gain=shape((4, g.cols), F32),
            o_bias=shape((4, g.cols), F32),
            o_bout=shape((2, g.cols), F32),
            o_bdown=shape((1, g.cols), F32),
            o_router=shape((g.experts, g.cols), F32),
            o_bup=shape((1, up_rows), F32),
        )
    else:
        outs |= dict(
            o_qkv=shape((2, three, width), F32),
            o_out=shape((2, g.head_cols, width), F32),
            o_up=shape((hidden, width), F32),
            o_down=shape((width, hidden), F32),
            o_bup=shape((1, hidden), F32),
            o_small=shape((g.small, width), F32),
        )
    scratch = dict(
        xs=vmem((4, tokens, width), BF16),
        gs=vmem((4, tokens, width), BF16),
        normed=vmem((3, tokens, width), BF16),
        wide=vmem((tokens, width + LANES), BF16),
        qkv=vmem((2, 3, g.head_cols, tokens), BF16),
        probs=vmem((2, g.micro, g.heads, g.seq, g.seq), F32),
        ctx=vmem((2, g.head_cols, tokens), BF16),
        act=vmem((tokens, hidden), BF16),
        dgelu=vmem((tokens, hidden), F32),
        dpre=vmem((tokens, hidden), BF16),
        dqkv=vmem((3, g.head_cols, tokens), BF16),
        part=vmem((8, tokens, width), BF16),
        got=vmem((8, g.micro, sections - 1, g.piece, width), BF16),
        mine=vmem((tokens, width), F32),
        square=vmem((LANES, LANES), F32),
        table=vmem((g.groups, part_rows, tokens // g.groups), BF16),
        disp=vmem((g.groups, part_rows, width + LANES), BF16),
        dispc=vmem((chips, g.groups, g.quarter, width), BF16),
        rows=vmem((g.groups, g.parts, 2, part_rows, width + LANES), BF16),
        crow=vmem((g.groups, g.parts, 2, part_rows, width), BF16),
        grow=vmem((g.groups, g.parts, 2, part_rows, width), BF16),
        acte=vmem((g.groups, g.parts, 2, part_rows, inner), BF16),
        dpree=vmem((g.groups, g.parts, 2, part_rows, inner), BF16),
        both=vmem((2, g.parts, 2, part_rows, width), F32),
        small=vmem((g.small, width), F32),
        local_s=dma((len(g.loads) + len(outs),)),
    )
    g.stores = list(outs)
    for name, out in outs.items():
        scratch[name] = vmem(out.shape, out.dtype)
    for name in g.loads:
        scratch[name] = vmem(operands["h_" + name].shape, BF16)
    for which in ("d", "y"):
        scratch["keep_" + which] = vmem((g.groups, g.parts, part_rows, width), F32)
        for name in ("snd_", "rcv_"):
            scratch[name + which] = vmem((g.groups, g.parts, part_rows, width), BF16)
    scratch |= dict(
        out_d=vmem((sections - 1, g.groups, part_rows, width), BF16),
        plane_d=vmem((sections - 1, g.groups, part_rows, width), BF16),
        ret_d=vmem((g.groups, part_rows, width), BF16),
        back_d=vmem((g.groups, part_rows, width), BF16),
        ret_y=vmem((g.groups, g.parts, part_rows, width), BF16),
        back_y=vmem((chips, g.groups, g.parts, g.quarter, width), BF16),
    )
    scratch |= dict(row_s=dma((g.groups,)), row_r=dma((g.groups, max(g.parts - 1, 1))))
    scratch |= dict(scat_s=dma((1,)), gath_s=dma((1,)), scat_r=dma((8, g.micro)), gath_r=dma((8, g.micro)))
    for name, sizes in (
        ("pair", (len(g.pairs),)), ("plane", (len(g.planes),)), ("many", (len(g.manys),)),
        ("line", (len(g.lines), chips)), ("grad", (len(g.grads),)), ("pass", (len(g.grads),)),
    ):
        if sizes[0]:
            scratch |= {name + "_s": dma(sizes), name + "_r": dma(sizes)}
    if g.direct:
        del scratch["pass_s"]
    if g.direct:
        piece = (top, wide)
        out_piece = (top, g.out_lanes)
        up_piece = (up_rows, width)
        bias_piece = (2 * TAIL, LANES)
        scratch |= dict(
            pq=vmem((2, 3, *piece), BF16),
            po=vmem((2, sections, *out_piece), BF16),
            pb=vmem(bias_piece, BF16),
            rb=vmem((chips, 2, *bias_piece), BF16),
            hb=vmem((chips, *bias_piece), BF16),
            ab=vmem((chips - 1, *bias_piece), BF16),
            lb=vmem(bias_piece, BF16),
            lq=vmem((2, 3, *piece), BF16),
            lo=vmem((2, sections, *out_piece), BF16),
            lu=vmem(up_piece, BF16),
            ld=vmem((sections, *piece), BF16),
            pd=vmem((sections, *piece), BF16),
            rq=vmem((2, 2, chips, 3, *piece), BF16),
            ro=vmem((2, 2, chips, sections, *out_piece), BF16),
            ru=vmem((chips, 2, *up_piece), BF16),
            rd=vmem((2, chips, sections, *piece), BF16),
            w_qkv=vmem((2, three, width), BF16),
            w_out=vmem((2, g.head_cols, width), BF16),
            w_down=vmem((width, hidden), BF16),
            w_router=vmem((width, LANES), BF16),
            b_up=vmem((8, hidden), F32),
            prm=vmem((GROUP, width), F32),
            tmp=vmem((width, width), F32),
            hq=vmem((2, chips, 3, *piece), BF16),
            ho=vmem((2, chips, sections, *out_piece), BF16),
            hu=vmem((chips, *up_piece), BF16),
            hd=vmem((chips, sections, *piece), BF16),
            aq=vmem((2, chips - 1, 3, *piece), BF16),
            ao=vmem((2, chips - 1, sections, *out_piece), BF16),
            au=vmem((chips - 1, *up_piece), BF16),
            ad=vmem((chips - 1, sections, *piece), BF16),
            mq=vmem((2, 3, *piece), BF16),
            mo=vmem((2, sections, *out_piece), BF16),
            md=vmem((sections, *piece), BF16),
            fq=vmem((2, 3, *piece), BF16),
            fo=vmem((2, sections, *out_piece), BF16),
            fd=vmem((sections, *piece), BF16),
            wq_s=dma((3, chips + 1)),
            wq_r=dma((3, chips + 1)),
            wo_s=dma((chips,)),
            wo_r=dma((chips,)),
            gq_s=dma((2, 3)),
            gq_r=dma((2, 3)),
        )
    whole = pl.BlockSpec(memory_space=pltpu.VMEM)
    placed = pl.BlockSpec(memory_space=pl.ANY)
    apart = ["h_" + name for name in g.loads]
    names = (*operands, *("h_" + name for name in outs), *scratch)
    results = pl.pallas_call(
        functools.partial(layers_kernel, g, names),
        out_shape=tuple(outs.values()),
        in_specs=[placed if name in apart else whole for name in operands],
        out_specs=[placed] * len(outs),
        scratch_shapes=list(scratch.values()),
        compiler_params=pltpu.CompilerParams(
            collective_id=0, has_side_effects=True, vmem_limit_bytes=62 * 1024 * 1024
        ),
    )(*operands.values())
    return types.SimpleNamespace(**dict(zip(outs, results, strict=True)))


def finish_kernel(count, *refs):
    ins, outs, held = refs[:count], refs[count : 2 * count], refs[2 * count : 3 * count]
    wide, sems = refs[3 * count : 3 * count + 2], refs[-1]
    loads = [pltpu.make_async_copy(ins[i], held[i], sems.at[0, i]) for i in range(count)]
    stores = [pltpu.make_async_copy((wide[i] if i < 2 else held[i]), outs[i], sems.at[1, i]) for i in range(count)]
    for copy in loads:
        copy.start()
    for i in range(count):
        loads[i].wait()
        if i < 2:
            wide[i][...] = held[i][...].astype(F32)
        stores[i].start()
    for copy in stores:
        copy.wait()


def finish(arrays):
    count = len(arrays)
    placed = [pl.BlockSpec(memory_space=pl.ANY)] * count
    held = [pltpu.VMEM(array.shape, array.dtype) for array in arrays]
    wide = [pltpu.VMEM(array.shape, F32) for array in arrays[:2]]
    return pl.pallas_call(
        functools.partial(finish_kernel, count),
        out_shape=tuple(jax.ShapeDtypeStruct(array.shape, F32) for array in arrays),
        in_specs=placed,
        out_specs=placed,
        scratch_shapes=[*held, *wide, pltpu.SemaphoreType.DMA((2, count))],
        compiler_params=pltpu.CompilerParams(vmem_limit_bytes=62 * 1024 * 1024),
    )(*arrays)


BOTH = ("section", "dp")


def body(
    tokens, cotangent, lengths, routes, slots, norm_gain, norm_bias, attn_qkv, attn_out, attn_out_bias,
    ffn_up, ffn_up_bias, ffn_down, ffn_down_bias, router, expert_up, expert_down,
):
    sections, devices = lax.axis_size("section"), lax.axis_size("dp")
    sec = lax.axis_index("section")
    micro, _, seq, width = tokens.shape
    experts = router.shape[1]
    chips = devices // 2
    head_cols = width // sections
    hidden = ffn_up.shape[1] * devices
    cap = 2 * seq // experts
    span = micro * cap
    cols = ffn_down.shape[1]
    kinds = FIRST_ROUTER + experts
    direct = cols == 3 * TAIL and kinds <= GROUP and sections == 4 and ffn_up.shape[1] % 16 == 0
    parts = sections if span % (16 * sections) == 0 else 1
    groups = micro if cap % (16 * parts) == 0 else 1
    group_names = [str(group) for group in range(groups)]
    part_names = [str(part) for part in range(parts)]
    half_names = part_names[:2]
    g = types.SimpleNamespace(
        sections=sections, devices=devices, chips=chips, micro=micro, seq=seq, width=width, hidden=hidden, cap=cap,
        span=span, tokens=micro * seq, piece=seq // sections, heads=head_cols // HEAD_DIM,
        head_cols=head_cols, cols=cols, block=256, small=-(-kinds // 8) * 8, direct=direct, experts=experts,
        out_lanes=head_cols + 2 * GROUP + LANES, parts=parts, groups=groups, quarter=span // (parts * groups),
        loads=(["wo", "wq"] if direct else []) + ["x0", "cot"] + (["wu", "wd"] if direct else []) + ["e_up", "e_down"],
        relay=direct and chips == 4,
        my_part=(lambda section: section) if parts > 1 else (lambda section: 0),
        router_lane=FIRST_ROUTER + (LANES - 2 * GROUP if direct else 0),
        pairs=["crow" + a for a in half_names]
        + [name + a + b for name in ("rows", "d") for a in group_names for b in part_names]
        + ["y" + a + b for a in group_names for b in half_names]
        + ([
            "out0", "qkv0", "up", "bias", "down", "qkv1", "out1",
            "gqkv0", "gqkv1", "gdown", "gup", "gbias", "gout0", "gout1",
        ] if direct else []),
        lines=["out0", "qkv0", "up", "bias", "down", "qkv1", "out1"] if direct else [],
        grads=["gqkv0", "gqkv1", "gdown", "gup", "gbias", "gout0", "gout1"] if direct else [],
        manys=["crow"] + [name + b for name in ("rows", "d", "y") for b in group_names],
        planes=["crow"]
        + ["d" + b for b in group_names]
        + (["down", "out1", "gdown", "gout0", "gout1"] if direct else []),
    )

    operands = dict(
        h_x0=tokens.reshape(g.tokens, width),
        h_cot=cotangent.reshape(g.tokens, width),
        lens=lengths.T,
        routes=routes[:, 0],
        slots=slots[:, 0],
        h_e_up=expert_up[0],
        h_e_down=expert_down[0],
    )
    if direct:
        operands |= dict(
            norm_gain=norm_gain,
            norm_bias=norm_bias,
            out_bias=attn_out_bias,
            down_bias=ffn_down_bias[None],
            up_bias=ffn_up_bias[None],
            router=router.T,
            h_wq=attn_qkv.transpose(0, 2, 1),
            h_wo=attn_out.transpose(0, 2, 1),
            h_wu=ffn_up.T,
            h_wd=ffn_down.T,
        )
    else:

        def every(array, axis):
            return lax.all_gather(array, BOTH, axis=axis, tiled=True)

        def part_of(array, axis, size):
            return lax.dynamic_slice_in_dim(array, sec * size, size, axis)

        rows = [norm_gain, norm_bias, attn_out_bias, ffn_down_bias[None], router.T]
        params = every(jnp.concatenate(rows, axis=0), 1)
        params = jnp.pad(params, ((0, LANES - kinds), (0, 0)))
        b_up = lax.all_gather(ffn_up_bias, "dp", axis=0, tiled=True).astype(F32)
        full = part_of(every(attn_qkv, 2).reshape(2, width, 3, width), 3, head_cols)
        operands |= dict(
            prm=params.astype(F32),
            w_router=params.T,
            b_up=b_up[None],
            w_qkv=full.transpose(0, 2, 3, 1).reshape(2, 3 * head_cols, width),
            w_out=part_of(every(attn_out, 2), 1, head_cols),
            w_up=lax.all_gather(ffn_up, "dp", axis=1, tiled=True).T,
            w_down=part_of(every(ffn_down, 1), 0, hidden).T,
        )
    res = run_layers(g, operands)

    if direct:
        names = list(vars(res))
        done = finish([getattr(res, name) for name in names])
        res = types.SimpleNamespace(**dict(zip(names, done, strict=True)))
        grads = (
            res.o_gain, res.o_bias, res.o_qkv.transpose(0, 2, 1), res.o_out.transpose(0, 2, 1), res.o_bout,
            res.o_up.T, res.o_bup[0], res.o_down.T, res.o_bdown[0], res.o_router.T,
        )
    else:

        def embed(array, shape, axis, size):
            return lax.dynamic_update_slice_in_dim(jnp.zeros(shape, F32), array, sec * size, axis)

        def share(array, axis, over=BOTH):
            return lax.psum_scatter(array, over, scatter_dimension=axis, tiled=True)

        small = share(res.o_small[:kinds], 1)
        g_qkv = res.o_qkv.reshape(2, 3, head_cols, width).transpose(0, 3, 1, 2)
        g_qkv = embed(g_qkv, (2, width, 3, width), 3, head_cols).reshape(2, width, 3 * width)
        g_out = embed(res.o_out, (2, width, width), 1, head_cols)
        g_down = embed(res.o_down.T, (hidden * sections, width), 0, hidden)
        grads = (
            small[0:4], small[4:8], share(g_qkv, 2), share(g_out, 2), small[8:10], share(res.o_up.T, 1, "dp"),
            share(res.o_bup[0], 0, "dp"), share(g_down, 1), small[10], small[FIRST_ROUTER:].T,
        )
    out_shape = (1, micro, 1, seq, width)
    return (
        res.sec_out.reshape(out_shape).astype(F32),
        res.sec_grad.reshape(out_shape).astype(F32),
        *grads,
        res.g_eup[None],
        res.g_edown[None],
    )


def solution(mesh):
    batch = P(None, "dp", None, None)
    table = P(None, "dp", None)
    in_specs = (
        batch, batch, P(None, "dp"), table, table,
        P(None, BOTH), P(None, BOTH), P(None, None, BOTH), P(None, None, BOTH), P(None, BOTH),
        P(None, BOTH), P(BOTH), P(None, BOTH), P(BOTH), P(BOTH, None),
        P("dp", None, "section"), P("dp", "section", None),
    )
    streams = P("section", None, "dp", None, None)
    out_specs = (
        streams, streams,
        P(None, BOTH), P(None, BOTH), P(None, None, BOTH), P(None, None, BOTH), P(None, BOTH),
        P(None, BOTH), P(BOTH), P(None, BOTH), P(BOTH), P(BOTH, None),
        P("dp", None, "section"), P("dp", "section", None),
    )
    return jax.shard_map(body, mesh=mesh, in_specs=in_specs, out_specs=out_specs, check_vma=False)
```

```python
import functools
import types

import jax
import jax.numpy as jnp
from jax import lax
from jax.experimental import pallas as pl
from jax.experimental.pallas import tpu as pltpu
from jax.sharding import PartitionSpec as P

HEADS = 12
HEAD_DIM = 64
EPS = 1e-05
MASKED = -1000000000.0
MESH = pl.DeviceIdType.MESH
F32 = jnp.float32
BF16 = jnp.bfloat16
LANES = 128


def dot_as(left, right, left_dim, right_dim):
    return lax.dot_general(
        left, right, (((left_dim,), (right_dim,)), ((), ())), preferred_element_type=F32
    )


def mm(left, right):
    return dot_as(left, right, 1, 0)


def mm_nt(left, right):
    return dot_as(left, right, 1, 1)


def mm_tn(left, right):
    return dot_as(left, right, 0, 0)


def normalize(values):
    center = values - jnp.mean(values, axis=-1, keepdims=True)
    spread = jnp.mean(center * center, axis=-1, keepdims=True)
    inverse = lax.rsqrt(spread + EPS)
    return center * inverse, inverse


def gelu_parts(pre):
    half = 0.5 + 0.5 * lax.erf(pre * 0.7071067811865476)
    density = jnp.exp(-0.5 * pre * pre) * 0.3989422804014327
    return pre * half, half + pre * density


TAIL = 8
GROUP = 32
FIRST_ROUTER = 11


def layers_kernel(g, names, *refs):
    r = types.SimpleNamespace(**dict(zip(names, refs, strict=True)))
    width, span, hidden, cols, head_cols = g.width, g.span, g.hidden, g.cols, g.head_cols
    sec = lax.axis_index("section")
    dev = lax.axis_index("dp")
    core = lax.rem(dev, 2)
    chip = lax.div(dev, 2)
    sib = dev + 1 - 2 * core
    quarter = g.quarter
    shard_rows = hidden // g.devices
    block_rows = g.chips * quarter

    def peer_section(offset):
        return lax.rem(sec + offset, g.sections)

    def from_section(offset):
        return lax.rem(sec + g.sections - offset, g.sections)

    def peer_chip(offset):
        return lax.rem(chip + offset, g.chips)

    def from_chip(offset):
        return lax.rem(chip + g.chips - offset, g.chips)

    def rows_at(index, size):
        return pl.ds(pl.multiple_of(index * size, size), size)

    def remote(source, target, send, arrive, where):
        return pltpu.make_async_remote_copy(
            src_ref=source, dst_ref=target, send_sem=send, recv_sem=arrive, device_id=where, device_id_type=MESH
        )

    def at_chip_core(index):
        return {"dp": 2 * index + core}

    started = []
    kept_back = {}

    def do_when(condition, action):
        if condition is None:
            action()
        else:
            pl.when(condition)(action)

    def launch(copy, buffer=None, when=None):
        do_when(when, copy.start)
        if buffer:
            kept_back.setdefault(buffer, []).append((copy, when))
        else:
            started.append((copy, when))

    def settle(buffer):
        for copy, when in kept_back.pop(buffer, []):
            do_when(when, copy.wait_send)

    barrier = pltpu.get_barrier_semaphore()
    partners = [(a, b) for a in range(g.sections) for b in range(g.chips) if a + b and (g.direct or a * b == 0)]
    for section_offset, chip_offset in partners:
        where = {"section": peer_section(section_offset), "dp": 2 * peer_chip(chip_offset) + core}
        pl.semaphore_signal(barrier, inc=1, device_id=where, device_id_type=MESH)
    pl.semaphore_signal(barrier, inc=1, device_id={"dp": sib}, device_id_type=MESH)

    def local(index, source, target):
        return pltpu.make_async_copy(source, target, r.local_s.at[index])

    held = vars(r)
    loads = {name: local(i, held["h_" + name], held[name]) for i, name in enumerate(g.loads)}
    stores = []

    def store(*some):
        for name in some:
            index = len(loads) + g.stores.index(name)
            stores.append(local(index, held[name], held["h_" + name]))
            stores[-1].start()

    for copy in loads.values():
        copy.start()

    def token_slice(micro):
        return slice(micro * g.seq, (micro + 1) * g.seq)

    def piece_at(micro, section):
        return pl.ds(pl.multiple_of(micro * g.seq + section * g.piece, g.piece), g.piece)

    def own(micro):
        return piece_at(micro, sec)

    def scatter_copy(slot, micro, offset):
        return remote(
            r.part.at[slot, piece_at(micro, peer_section(offset))], r.got.at[slot, micro, offset - 1],
            r.scat_s.at[0], r.scat_r.at[slot, micro], {"section": peer_section(offset)},
        )

    def all_pieces(slot, micro, arrive):
        place = r.got.at[slot, micro]
        remote(place, place, r.scat_s.at[0], arrive, {"section": peer_section(1)}).wait_recv()

    def scatter_start(slot, micro, value):
        r.part[slot, token_slice(micro), :] = value.astype(BF16)
        if slot != 7:
            r.mine[token_slice(micro), :] = value
        for offset in range(1, g.sections):
            scatter_copy(slot, micro, offset).start()

    def scatter_sum(slot, micro):
        at = own(micro)
        total = r.part[slot, at, :].astype(F32) if slot == 7 else r.mine[at, :]
        all_pieces(slot, micro, r.scat_r.at[slot, micro])
        for offset in range(1, g.sections):
            total = total + r.got[slot, micro, offset - 1].astype(F32)
        return total

    def gather_start(buffer, slot, sem, micro):
        place = buffer.at[slot, own(micro)]
        for offset in range(1, g.sections):
            remote(place, place, r.gath_s.at[0], r.gath_r.at[sem, micro], {"section": peer_section(offset)}).start()

    def gather_wait(buffer, slot, sem, micro):
        all_pieces(sem, micro, r.gath_r.at[sem, micro])

    def exchanges_left():
        for sem in (r.scat_s, r.gath_s):
            remote(r.got, r.got, sem.at[0], r.scat_r.at[0, 0], {"section": peer_section(1)}).wait_send()

    def pair_copy(name, source, target):
        index = g.pairs.index(name)
        return remote(source, target, r.pair_s.at[index], r.pair_r.at[index], {"dp": sib})

    def pair_start(name, source, target, buffer=None):
        launch(pair_copy(name, source, target), buffer)

    def pair_wait(name, target):
        pair_copy(name, target, target).wait_recv()

    def line_copy(name, source, target, offset, receiving):
        index = g.lines.index(name)
        where = from_chip(offset) if receiving else peer_chip(offset)
        return remote(
            source, target, r.line_s.at[index, offset - 1], r.line_r.at[index, offset - 1], at_chip_core(where)
        )

    last_chip = g.chips - 1
    is_end = lax.rem(chip, max(last_chip, 1)) == 0
    is_mid = lax.rem(chip, max(last_chip, 1)) != 0
    line_order = (2, 1, 3) if g.relay else range(1, g.chips)
    outward = jnp.clip(chip - 1, 0, 1)

    def near_to(offset):
        return {1: chip != last_chip, last_chip: chip != 0}.get(offset) if g.relay else None

    def near_from(offset):
        return {1: chip != 0, last_chip: chip != last_chip}.get(offset) if g.relay else None

    def spread_first(name, source, target, buffer=None):
        if g.relay:
            for offset, when in ((2, is_end), (1, chip == 2), (3, chip == 1)):
                launch(line_copy(name, source, target, offset, False), buffer, when)

    def spread_more(name, source, target, buffer=None):
        if g.relay:
            for offset, when in ((2, is_mid), (1, chip < 2), (3, chip > 1)):
                launch(line_copy(name, source, target, offset, False), buffer, when)
        else:
            for offset in line_order:
                launch(line_copy(name, source, target, offset, False), buffer)

    def spread_relay(name, place, buffer):
        index = g.lines.index(name)
        copy = remote(
            place, place, r.line_s.at[index, last_chip], r.line_r.at[index, outward * 2],
            at_chip_core(outward * last_chip),
        )
        launch(copy, buffer, is_mid)

    def spread_pass(name, place_at, buffer):
        if g.relay:
            place = place_at(from_chip(2))
            line_copy(name, place, place, 2, True).wait_recv()
            spread_relay(name, place, buffer)

    def spread_wait(name, place_at):
        for offset in (1, 3) if g.relay else line_order:
            place = place_at(from_chip(offset))
            line_copy(name, place, place, offset, True).wait_recv()

    def far_wait(name, place_at):
        for offset in (1, last_chip):
            place = place_at(from_chip(offset))
            copy = line_copy(name, place, place, offset, True)
            pl.when(jnp.logical_not(near_from(offset)))(copy.wait_recv)

    left = []

    def wait_all(place, send, arrive, sent):
        copy = remote(place, place, send, arrive, {"dp": sib})
        if sent:
            copy.wait_send()
        else:
            copy.wait_recv()

    def line_start(name, source_at, target, share):
        index = g.manys.index(name)
        for offset in range(1, g.chips):
            at = peer_chip(offset)
            remote(source_at(at), target, r.many_s.at[index], r.many_r.at[index], at_chip_core(at)).start()
        left.append((share, r.many_s.at[index], r.many_r.at[index]))

    def line_wait(name, share):
        index = g.manys.index(name)
        wait_all(share, r.many_s.at[index], r.many_r.at[index], False)

    def other_chips(size=1):
        return pl.ds(0, (g.chips - 1) * size)

    def rows_plane_start(name, place_at):
        if g.parts > 1:
            place = place_at(pl.ds(1, g.parts - 1))
            plane_start(name, lambda to, offset: place_at(0), place_at, place)
        pair_start(name + "0", place_at(0), place_at(0))

    def rows_plane_wait(name, place_at):
        place = place_at(pl.ds(1, g.parts - 1))
        plane_wait(name, place)
        pair_start(name + "1", place, place)

    top = cols - TAIL
    half = width // 2
    part_cols = head_cols // 2
    tail_lane = head_cols + 2 * GROUP

    def qkv_section(at_dev, index, section):
        return lax.rem(lax.div(3 * at_dev + index, g.devices) - section + g.sections, g.sections)

    def qkv_send(layer, offsets):
        for index in range(3):
            to = qkv_section(dev, index, sec)
            for offset in offsets:
                copy = remote(
                    r.pq.at[layer, index], r.rq.at[layer, core, chip, index],
                    r.wq_s.at[index, offset + layer * g.chips], r.wq_r.at[index, offset + layer * g.chips],
                    {"section": to, "dp": 2 * peer_chip(offset) + core},
                )
                if offset:
                    launch(copy, None, near_to(offset))
                else:
                    pl.when(to != sec)(copy.start)

                    @pl.when(to == sec)
                    def _(index=index):
                        r.rq[layer, core, chip, index] = r.pq[layer, index]

    def qkv_arrive(layer, offsets):
        for offset in offsets:
            for index in range(3):
                at_chip = from_chip(offset)
                target = r.rq.at[layer, core, at_chip, index]
                origin = qkv_section(2 * at_chip + core, index, sec)
                copy = remote(
                    target, target, r.wq_s.at[index, offset + layer * g.chips],
                    r.wq_r.at[index, offset + layer * g.chips],
                    {"section": origin, "dp": 2 * at_chip + core},
                )
                if offset:
                    do_when(near_from(offset), copy.wait_recv)
                else:

                    @pl.when(origin != sec)
                    def _(copy=copy):
                        copy.wait_recv()
                        copy.wait_send()

            if g.relay and offset == 2:
                spread_relay("qkv0", r.rq.at[0, core, from_chip(offset)], "qkv0")
        if g.relay and len(offsets) > 1:
            far_wait("qkv0", lambda at: r.rq.at[0, core, at])

    def out_copy(section_offset, offset, place, receiving):
        if receiving:
            to, at_chip = from_section(section_offset), from_chip(offset)
        else:
            to, at_chip = peer_section(section_offset), peer_chip(offset)
        source = place if receiving else r.po.at[0, to]
        return remote(
            source, place, r.wo_s.at[offset], r.wo_r.at[offset],
            {"section": to, "dp": 2 * at_chip + core},
        )

    def out_all(offset, sent):
        count = g.sections if offset else g.sections - 1
        wait_all(r.po.at[0, pl.ds(0, count)], r.wo_s.at[offset], r.wo_r.at[offset], sent)

    def out_offsets():
        return [(a, b) for b in (*line_order, 0) for a in range(g.sections) if a + b]

    def plane_start(name, source_at, target_at, share):
        index = g.planes.index(name)
        for offset in range(1, g.sections):
            to = peer_section(offset)
            sems = r.plane_s.at[index], r.plane_r.at[index]
            remote(source_at(to, offset), target_at(offset), *sems, {"section": to}).start()
        left.append((share, r.plane_s.at[index], r.plane_r.at[index]))

    def plane_wait(name, share):
        index = g.planes.index(name)
        wait_all(share, r.plane_s.at[index], r.plane_r.at[index], False)

    def others():
        return pl.ds(0, g.sections - 1)

    def pack_wide(block):
        tail = jnp.concatenate([block[top:, :half], block[top:, half:]], axis=0)
        return jnp.concatenate([block[:top], tail], axis=1).astype(BF16)

    def pack_out(block):
        small = jnp.concatenate([block[top:, head_cols:]] * 2, axis=0)
        tail = jnp.concatenate([block[top:, :part_cols], block[top:, part_cols:head_cols]], axis=0)
        empty = jnp.zeros((top, g.out_lanes - tail_lane - part_cols), F32)
        return jnp.concatenate([block[:top], small, tail, empty], axis=1).astype(BF16)

    def unpack_wide(target, first, piece):
        target[first : first + top, 0:width] = piece[:, 0:width]
        target[first + top : first + cols, 0:half] = piece[0:TAIL, width : width + half]
        target[first + top : first + cols, half:width] = piece[TAIL:, width : width + half]

    def unpack_out(target, first, piece, lane=0):
        last = slice(first + top, first + cols)
        tail = slice(tail_lane, tail_lane + part_cols)
        target[first : first + top, lane : lane + head_cols] = piece[:, 0:head_cols]
        target[last, lane : lane + part_cols] = piece[0:TAIL, tail]
        target[last, lane + part_cols : lane + head_cols] = piece[TAIL:, tail]

    def unpack_small(target, first, piece, lane):
        target[first : first + top, lane : lane + GROUP] = piece[:, head_cols : head_cols + GROUP]
        target[first + top : first + cols, lane : lane + GROUP] = piece[0:TAIL, head_cols + GROUP : tail_lane]

    def shard_places():
        for at_core in range(2):
            for at_chip in range(g.chips):
                for at_sec in range(g.sections):
                    yield at_core, at_chip, at_sec, (at_sec * g.devices + 2 * at_chip + at_core) * cols

    def chunk_places():
        for at_core in range(2):
            for at_chip in range(g.chips):
                for index in range(3):
                    yield at_core, at_chip, index, (3 * (2 * at_chip + at_core) + index) * cols

    def unfold_out(layer):
        for at_core, at_chip, at_sec, first in shard_places():
            piece = r.ro[layer, at_core, at_chip, at_sec].astype(F32)
            if layer == 0:
                unpack_small(r.tmp, first, piece, head_cols)
            unpack_out(r.tmp, first, piece)
        flipped = r.tmp[:, 0:tail_lane].T
        r.w_out[layer] = flipped[:head_cols].astype(BF16)
        if layer == 0:
            r.prm[...] = flipped[head_cols : head_cols + GROUP]
            r.w_router[...] = r.tmp[:, tail_lane - LANES : tail_lane].astype(BF16)

    def unfold_qkv(layer):
        for at_core, at_chip, index, first in chunk_places():
            unpack_wide(r.tmp, first, r.rq[layer, at_core, at_chip, index].astype(F32))
        r.w_qkv[layer] = r.tmp[0 : 3 * head_cols, 0:width].astype(BF16)

    def unfold_down():
        for at_core, at_chip, at_sec, first in shard_places():
            unpack_wide(r.tmp, first, r.rd[at_core, at_chip, at_sec].astype(F32))
        r.w_down[...] = r.tmp[...].astype(BF16)

    def grad_copy(name, buffer_at, target, offset):
        index, at = g.grads.index(name), peer_chip(offset)
        place = target.at[offset - 1]
        return remote(buffer_at(at), place, r.grad_s.at[index], r.grad_r.at[index], at_chip_core(at))

    def grad_line(name, buffer_at, landing, target, passed):
        pair_wait(name, landing)
        for at_chip in range(g.chips):
            block = buffer_at(at_chip)
            block[...] = (block[...].astype(F32) + landing[at_chip].astype(F32)).astype(BF16)
        if g.relay:
            index = g.grads.index(name)
            copy = remote(
                buffer_at(last_chip - chip), passed, r.grad_s.at[index], r.pass_r.at[index],
                at_chip_core(1 + lax.div(chip, last_chip)),
            )
            pl.when(is_end)(copy.start)
            for offset in (1, last_chip):

                @pl.when(jnp.logical_not(near_from(offset)))
                def _(offset=offset):
                    target[offset - 1] = jnp.zeros_like(target[offset - 1])

        for offset in line_order:
            copy = grad_copy(name, buffer_at, target, offset)
            do_when(is_end if g.relay and offset == 2 else near_to(offset), copy.start)
        index = g.grads.index(name)
        left.append((target, r.grad_s.at[index], r.grad_r.at[index]))

    def grad_relay(name, buffer_at, target, passed):
        if g.relay:
            index = g.grads.index(name)
            block = buffer_at(peer_chip(2))
            copy = grad_copy(name, buffer_at, target, 2)

            @pl.when(is_mid)
            def _():
                wait_all(passed, r.grad_s.at[index], r.pass_r.at[index], False)
                block[...] = (block[...].astype(F32) + passed[...].astype(F32)).astype(BF16)
                copy.start()

    def grad_line_sum(name, buffer_at, target):
        index = g.grads.index(name)

        def arrive(count):
            wait_all(target.at[pl.ds(0, count)], r.grad_s.at[index], r.grad_r.at[index], False)

        if g.relay:
            pl.when(is_end)(lambda: arrive(2))
            pl.when(is_mid)(lambda: arrive(3))
        else:
            arrive(g.chips - 1)
        total = buffer_at(chip)[...].astype(F32)
        for offset in range(1, g.chips):
            total = total + target[offset - 1].astype(F32)
        return total

    def qkv_at(layer):
        return lambda at: r.rq.at[layer, core, at]

    def down_at(at):
        return r.rd.at[core, at]

    def out_at(layer):
        return lambda at: r.ro.at[layer, core, at]

    def up_at(at):
        return r.ru.at[at, core]

    def bias_at(at):
        return r.rb.at[at, core]

    def grad_plane(name, buffer_at, target, summed, final):
        summed[...] = grad_line_sum(name, buffer_at, target).astype(BF16)
        plane_start(name, lambda to, _: summed.at[to], lambda _: final.at[sec], summed.at[others()])
        final[sec] = summed[sec]

    def grad_plane_wait(name, final):
        plane_wait(name, final.at[others()])

    def grad_qkv_copy(layer, index, place, where):
        return remote(
            r.mq.at[layer, index], place, r.gq_s.at[layer, index], r.gq_r.at[layer, index], {"section": where}
        )

    def grad_qkv_plane(layer):
        r.mq[layer] = grad_line_sum("gqkv" + str(layer), qkv_at(layer), r.aq.at[layer]).astype(BF16)
        for index in range(3):
            to = qkv_section(dev, index, sec)
            copy = grad_qkv_copy(layer, index, r.fq.at[layer, index], to)
            pl.when(to != sec)(copy.start)

            @pl.when(to == sec)
            def _(index=index):
                r.fq[layer, index] = r.mq[layer, index]

    def grad_qkv_finish(layer):
        for index in range(3):
            origin = qkv_section(dev, index, sec)
            copy = grad_qkv_copy(layer, index, r.fq.at[layer, index], origin)

            @pl.when(origin != sec)
            def _(copy=copy):
                copy.wait_recv()
                copy.wait_send()

            unpack_wide(r.o_qkv.at[layer], index * cols, r.fq[layer, index].astype(F32))

    def norm_into(source, target, index, micro):
        rows = g.seq // 2

        @pl.loop(0, 2)
        def _(step):
            at = rows_at(micro * 2 + step, rows)
            unit, _ = normalize(source[at, :].astype(F32))
            target[at, :] = (unit * r.prm[index : index + 1, :] + r.prm[4 + index : 5 + index, :]).astype(BF16)

    place_row = jnp.concatenate(
        [r.routes[m : m + 1] * span + m * g.cap + r.slots[m : m + 1] for m in range(g.micro)], axis=1
    )
    r.square[...] = jnp.zeros_like(r.square)
    if g.direct:
        r.square[0:4, 0:cols] = r.norm_gain[...].astype(F32)
        r.square[4:8, 0:cols] = r.norm_bias[...].astype(F32)
        r.square[8:10, 0:cols] = r.out_bias[...].astype(F32)
        r.square[10:11, 0:cols] = r.down_bias[...].astype(F32)
        r.pb[...] = jnp.zeros_like(r.pb)
        r.pb[:, 0:shard_rows] = jnp.broadcast_to(r.up_bias[...], (r.pb.shape[0], shard_rows))
        r.square[FIRST_ROUTER : FIRST_ROUTER + g.experts, 0:cols] = r.router[...].astype(F32)
        r.square[...] = r.square[...].T
        loads["wo"].wait()
        loads["wq"].wait()
        shard = r.wo[0].astype(F32)
        mine = r.square[0:cols, 0:GROUP]
        for at_sec in range(g.sections):
            block = shard[:, at_sec * head_cols : (at_sec + 1) * head_cols]
            r.po[0, at_sec] = pack_out(jnp.concatenate([block, mine], axis=1))
        shard = r.wq[0].astype(F32)
        for index in range(3):
            r.pq[0, index] = pack_wide(shard[index * cols : (index + 1) * cols])
    pl.semaphore_wait(barrier, len(partners) + 1)
    if g.direct:
        for section_offset, offset in out_offsets():
            copy = out_copy(section_offset, offset, r.ro.at[0, core, chip, sec], False)
            do_when(near_to(offset), copy.start)
        r.ro[0, core, chip, sec] = r.po[0, sec]
        qkv_send(0, (*line_order, 0))
        loads["wu"].wait()
        loads["wd"].wait()
        shard = r.wq[1].astype(F32)
        for index in range(3):
            r.pq[1, index] = pack_wide(shard[index * cols : (index + 1) * cols])
        shard, other = r.wd[...].astype(F32), r.wo[1].astype(F32)
        empty = jnp.zeros((cols, GROUP), F32)
        for at_sec in range(g.sections):
            r.pd[at_sec] = pack_wide(shard[:, at_sec * hidden : (at_sec + 1) * hidden])
            block = other[:, at_sec * head_cols : (at_sec + 1) * head_cols]
            r.po[1, at_sec] = pack_out(jnp.concatenate([block, empty], axis=1))

    loads["x0"].wait()
    loads["cot"].wait()
    slot_ids = lax.broadcasted_iota(jnp.int32, (quarter, g.tokens), 0)

    def slot_match(expert, part, group):
        first = expert * span + group * (span // g.groups) + part * quarter
        return jnp.where(slot_ids + first == place_row, 1.0, 0.0).astype(BF16)

    def group_tokens(group):
        count = g.tokens // g.groups
        return slice(group * count, (group + 1) * count)

    for group in range(g.groups):
        for expert in range(g.chips):
            match = slot_match(expert, g.my_part(sec), group)
            r.table[group, expert * quarter : (expert + 1) * quarter, :] = match[:, group_tokens(group)]
        sent = mm(r.table[group], r.cot[group_tokens(group), :]).astype(BF16)
        r.dispc[:, group] = sent.reshape(g.chips, quarter, width)
    r.small[...] = jnp.zeros_like(r.small)
    if g.direct:
        for offset in (*line_order, 0):
            do_when(near_from(offset), lambda offset=offset: out_all(offset, False))
            if g.relay and offset == 2:
                spread_relay("out0", r.ro.at[0, core, from_chip(offset)], "out0")
        if g.relay:
            far_wait("out0", lambda at: r.ro.at[0, core, at])
        pair_start("out0", r.ro.at[0, core], r.ro.at[0, core], "out0")
        qkv_arrive(0, (*line_order, 0))
        pair_start("qkv0", r.rq.at[0, core], r.rq.at[0, core], "qkv0")
        spread_first("bias", r.pb, r.rb.at[chip, core])
        spread_more("bias", r.pb, r.rb.at[chip, core])
        r.rb[chip, core] = r.pb[...]
        spread_first("up", r.wu, r.ru.at[chip, core])
        r.ru[chip, core] = r.wu[...]
        plane_start("down", lambda to, _: r.pd.at[to], lambda _: r.rd.at[core, chip, sec], r.pd.at[others()])
        r.rd[core, chip, sec] = r.pd[sec]
        qkv_send(1, [0])
        place = r.ro.at[1, core, chip, sec]
        plane_start("out1", lambda to, _: r.po.at[1, to], lambda _: place, r.po.at[1, others()])
        r.ro[1, core, chip, sec] = r.po[1, sec]
        pair_wait("out0", r.ro.at[0, 1 - core])
        unfold_out(0)
        pair_wait("qkv0", r.rq.at[0, 1 - core])
        unfold_qkv(0)

    def up_place(at):
        return r.ru.at[at, core]

    def bias_place(at):
        return r.rb.at[at, core]

    def down_place(at):
        return r.rd.at[core, at]

    def qkv_place(at):
        return r.rq.at[1, core, at]

    def out_place(at):
        return r.ro.at[1, core, at]

    def own_first(name, place_at):
        spread_first(name, place_at(chip), place_at(chip), name)

    def own_more(name, place_at):
        spread_more(name, place_at(chip), place_at(chip), name)

    key_ids = lax.broadcasted_iota(jnp.int32, (g.seq, g.seq), 0)
    query_ids = lax.broadcasted_iota(jnp.int32, (g.seq, g.seq), 1)
    scale = HEAD_DIM**-0.5
    micros = range(g.micro)

    def block_of(index):
        return lax.rem(index + sec, 3) if g.direct else index

    def head_slice(head):
        return slice(head * HEAD_DIM, (head + 1) * HEAD_DIM)

    def attention_forward(layer, stream, slot, micro, before_out=None):
        at = token_slice(micro)
        norm_into(stream, r.normed.at[2 * layer], 2 * layer, micro)
        packed = mm_nt(r.w_qkv[layer], r.normed[2 * layer, at, :]).astype(BF16)
        r.qkv[layer, :, :, at] = packed.reshape(3, head_cols, g.seq)
        allowed = (key_ids <= query_ids) & (key_ids < r.lens[:, micro : micro + 1])
        for head in range(g.heads):
            key = r.qkv[layer, block_of(1), head_slice(head), at]
            scores = mm_tn(key, r.qkv[layer, block_of(0), head_slice(head), at]) * scale
            scores = jnp.where(allowed, scores, MASKED)
            weight = jnp.exp(scores - jnp.max(scores, axis=0, keepdims=True))
            weight = weight / jnp.sum(weight, axis=0, keepdims=True)
            r.probs[layer, micro, head] = weight
            value = r.qkv[layer, block_of(2), head_slice(head), at]
            r.ctx[layer, head_slice(head), at] = mm(value, weight.astype(BF16)).astype(BF16)
        if before_out:
            before_out()
        scatter_start(slot, micro, mm_tn(r.ctx[layer, :, at], r.w_out[layer]))

    def finish_forward(section, bias, stream, micro):
        total = scatter_sum(section, micro) + bias + stream[own(micro), :].astype(F32)
        r.xs[section, own(micro), :] = total.astype(BF16)
        gather_start(r.xs, section, section, micro)

    for micro in micros:
        attention_forward(0, r.x0, 0, micro)
        if g.direct and micro == 0:
            spread_more("up", r.wu, r.ru.at[chip, core])
    if g.direct:
        spread_pass("bias", bias_place, "bias")
        spread_pass("up", up_place, "up")
        plane_wait("down", r.pd.at[others()])
        own_first("down", down_place)
    for micro in micros:
        finish_forward(0, r.prm[8:9, :], r.x0, micro)
    if g.direct:
        own_more("down", down_place)
        spread_wait("bias", bias_place)
        spread_wait("up", up_place)
        pair_start("up", r.ru.at[:, core], r.ru.at[:, core], "up")
        pair_start("bias", r.rb.at[:, core], r.rb.at[:, core], "bias")
        pair_wait("up", r.ru.at[:, 1 - core])
        pair_wait("bias", r.rb.at[:, 1 - core])
        for at_dev in range(g.devices):
            row = r.rb[at_dev // 2, at_dev % 2, :, 0:shard_rows].astype(F32)
            r.b_up[:, at_dev * shard_rows : (at_dev + 1) * shard_rows] = row[0:TAIL]

    def up_rows(at):
        if g.direct:
            return r.ru[...].reshape(hidden, width)[at]
        return r.w_up[at, :]

    def hidden_blocks():
        return [slice(first, first + g.block) for first in range(0, hidden, g.block)]

    for micro in micros:
        rows = token_slice(micro)
        gather_wait(r.xs, 0, 0, micro)
        norm_into(r.xs.at[0], r.normed.at[1], 1, micro)
        for at in hidden_blocks():
            value, slope = gelu_parts(mm_nt(r.normed[1, rows, :], up_rows(at)) + r.b_up[0:1, at])
            r.act[rows, at] = value.astype(BF16)
            r.dgelu[rows, at] = slope
        if g.direct and micro == 0:
            spread_pass("down", down_place, "down")
            qkv_arrive(1, [0])
            own_first("qkv1", qkv_place)
            own_more("qkv1", qkv_place)
    if g.direct:
        spread_wait("down", down_place)
        pair_start("down", r.rd.at[core], r.rd.at[core], "down")
        plane_wait("out1", r.po.at[1, others()])
        own_first("out1", out_place)
        own_more("out1", out_place)
        pair_wait("down", r.rd.at[1 - core])
        unfold_down()
    for micro in micros:
        scatter_start(1, micro, mm_nt(r.act[token_slice(micro), :], r.w_down[...]))
    if g.direct:
        spread_pass("qkv1", qkv_place, "qkv1")
    for micro in micros:
        finish_forward(1, r.prm[10:11, :], r.xs.at[0], micro)
        if g.direct and micro == 0:
            spread_pass("out1", out_place, "out1")
    if g.direct:
        spread_wait("qkv1", qkv_place)
        pair_start("qkv1", r.rq.at[1, core], r.rq.at[1, core], "qkv1")

    def crow_at(part, side):
        return r.crow.at[:, part, side]

    crow_share = r.dispc.at[other_chips()]

    def output_weights():
        if g.direct:
            spread_wait("out1", out_place)
            pair_start("out1", r.ro.at[1, core], r.ro.at[1, core], "out1")
        place = r.crow.at[:, 0, core, rows_at(chip, quarter)]
        line_start("crow", lambda at: r.dispc.at[at], place, crow_share)
        r.crow[:, 0, core, rows_at(chip, quarter), :] = r.dispc[chip]
        if g.direct:
            pair_wait("out1", r.ro.at[1, 1 - core])
            unfold_out(1)

    if g.direct:
        pair_wait("qkv1", r.rq.at[1, 1 - core])
        unfold_qkv(1)
    for micro in micros:
        gather_wait(r.xs, 1, 1, micro)
        attention_forward(1, r.xs.at[1], 2, micro, None if micro else output_weights)
    for micro in micros:
        finish_forward(2, r.prm[9:10, :], r.xs.at[1], micro)
    r.square[0 : g.micro, :] = jnp.concatenate(
        [place_row[:, token_slice(micro)] for micro in micros], axis=0
    ).astype(F32)
    columns = r.square[...].T

    wide = r.wide

    def gates(micro):
        at = token_slice(micro)
        norm_into(r.xs.at[2], wide.at[:, pl.ds(0, width)], 3, micro)
        logits = mm(wide[at, :width], r.w_router[...])
        lane = lax.broadcasted_iota(jnp.int32, logits.shape, 1) - g.router_lane
        place_col = columns[:, micro : micro + 1].astype(jnp.int32)
        chosen = (place_col >= lane * span) & (place_col < lane * span + span)
        score = jnp.sum(jnp.where(chosen, logits, 0.0), axis=-1, keepdims=True)
        gate = 1.0 / (1.0 + jnp.exp(-score))
        gate_high = gate.astype(BF16).astype(F32)
        lane = lax.broadcasted_iota(jnp.int32, (g.seq, LANES), 1)
        pair = jnp.where(lane == 0, gate_high, jnp.where(lane == 1, gate - gate_high, 0.0))
        wide[at, width:] = pair.astype(BF16)

    groups = range(g.groups)

    def rows_place(group, side):
        return lambda part: r.rows.at[group, part, side]

    def rows_line_start(group):
        name = "rows" + str(group)
        r.disp[group] = mm(r.table[group], wide[group_tokens(group), :]).astype(BF16)
        place = r.rows.at[group, 0, core, rows_at(chip, quarter)]
        share = r.disp.at[group, other_chips(quarter)]
        line_start(name, lambda at: r.disp.at[group, rows_at(at, quarter)], place, share)
        r.rows[group, 0, core, rows_at(chip, quarter), :] = r.disp[group, rows_at(chip, quarter), :]

    def rows_line_wait(group):
        name = "rows" + str(group)
        line_wait(name, r.disp.at[group, other_chips(quarter)])
        place_at = rows_place(group, core)
        for offset in range(1, g.parts):
            sems = r.row_s.at[group], r.row_r.at[group, offset - 1]
            remote(place_at(0), place_at(offset), *sems, {"section": peer_section(offset)}).start()
        if g.parts > 1:
            left.append((place_at(pl.ds(1, g.parts - 1)), r.row_s.at[group], r.row_r.at[group, 0]))
        pair_start(name + "0", place_at(0), place_at(0))

    for micro in micros:
        gather_wait(r.xs, 2, 2, micro)
        if micro == 0:
            line_wait("crow", crow_share)
            rows_plane_start("crow", lambda part: crow_at(part, core))
        gates(micro)
        if g.groups > 1:
            rows_line_start(micro)
    if g.groups == 1:
        rows_line_start(0)
    for group in groups:
        rows_line_wait(group)
    loads["e_up"].wait()
    loads["e_down"].wait()

    own_router = FIRST_ROUTER + chip
    router_row = r.prm[pl.ds(own_router, 1), :]
    snd = dict(d=r.snd_d, y=r.snd_y)
    kept = dict(d=r.keep_d, y=r.keep_y)
    rcv = dict(d=r.rcv_d, y=r.rcv_y)

    def expert_block(wide_rows, cot_rows):
        row = wide_rows[:, :width]
        tail = wide_rows[:, width:].astype(F32)
        gate_row = tail[:, 0:1] + tail[:, 1:2]
        grad_row = (gate_row * cot_rows.astype(F32)).astype(BF16)
        value, slope = gelu_parts(mm(row, r.e_up[...]))
        value = value.astype(BF16)
        result = mm(value, r.e_down[...])
        total = jnp.sum(grad_row.astype(F32) * result, axis=-1, keepdims=True) * (1.0 - gate_row)
        inner = (slope * mm_nt(grad_row, r.e_down[...])).astype(BF16)
        back = mm_nt(inner, r.e_up[...]) + total * router_row
        r.small[pl.ds(own_router, 1), :] += jnp.sum(row.astype(F32) * total, axis=0, keepdims=True)
        return grad_row, value, inner, back, result * gate_row

    def expert_parts(group, first, count):
        parts = slice(first, first + count)
        each = 2 * block_rows
        if each <= g.block:
            lead = (count, 2, block_rows)
            found = expert_block(
                r.rows[group, parts].reshape(count * each, width + LANES),
                r.crow[group, parts].reshape(count * each, width),
            )
            for target, value in zip((r.grow, r.acte, r.dpree), found[:3], strict=True):
                target[group, parts] = value.reshape(*lead, value.shape[-1])
            r.both[0, parts] = found[3].reshape(*lead, width)
            r.both[1, parts] = found[4].reshape(*lead, width)
        else:
            for part in range(first, first + count):
                for side in range(2):

                    @pl.loop(0, block_rows // g.block)
                    def _(step, part=part, side=side):
                        at = rows_at(step, g.block)
                        found = expert_block(r.rows[group, part, side, at, :], r.crow[group, part, side, at, :])
                        for target, value in zip((r.grow, r.acte, r.dpree), found[:3], strict=True):
                            target[group, part, side, at, :] = value
                        r.both[0, part, side, at, :] = found[3]
                        r.both[1, part, side, at, :] = found[4]

        parts_send("d", r.both.at[0], group, first, count)

    def parts_send(which, value, group, first, count):
        for part in range(first, first + count):
            snd[which][group, part] = value[part, 1 - core].astype(BF16)
            if which == "d":
                pair_start(which + str(group) + str(part), snd[which].at[group, part], rcv[which].at[group, part])
        if which == "y":
            parts = pl.ds(first, count)
            name = which + str(group) + str(min(first, 1))
            pair_start(name, snd[which].at[group, parts], rcv[which].at[group, parts])
        for part in range(first, first + count):
            kept[which][group, part] = value[part, core]

    def results_pair(group, first, count):
        parts_send("y", r.both.at[1], group, first, count)

    def merge_ready(which, group, first, count):
        pair_wait(which + str(group) + str(min(first, 1)), rcv[which].at[group, pl.ds(first, count)])

    def merge(which, offset, group):
        return kept[which][group, offset] + rcv[which][group, offset].astype(F32)

    def merge_send(group):
        index = g.planes.index("d" + str(group))
        for offset in range(1, g.sections):
            to = g.sections - offset
            pair_wait("d" + str(group) + str(offset), rcv["d"].at[group, offset])
            r.out_d[offset - 1, group] = merge("d", offset, group).astype(BF16)
            sems = r.plane_s.at[index], r.plane_r.at[index]
            source, target = r.out_d.at[offset - 1, group], r.plane_d.at[to - 1, group]
            remote(source, target, *sems, {"section": peer_section(to)}).start()
        left.append((r.out_d.at[:, group], r.plane_s.at[index], r.plane_r.at[index]))

    def parts_work(group, first, count):
        parts, tag = pl.ds(first, count), str(min(first, 1))
        if group == 0:
            pair_wait("crow" + tag, crow_at(parts, 1 - core))
        for part in range(first, first + count):
            pair_wait("rows" + str(group) + str(part), rows_place(group, 1 - core)(part))
        expert_parts(group, first, count)

    def results_line(group):
        merge_ready("y", group, 0, 1)
        if g.parts > 1:
            merge_ready("y", group, 1, g.parts - 1)
        for offset in range(g.parts):
            r.ret_y[group, offset] = merge("y", offset, group).astype(BF16)
        name = "y" + str(group)
        place, share = r.back_y.at[chip, group], r.ret_y.at[group, :, other_chips(quarter)]
        line_start(name, lambda at: r.ret_y.at[group, :, rows_at(at, quarter)], place, share)
        r.back_y[chip, group] = r.ret_y[group, :, rows_at(chip, quarter), :]

    def expert_back_line(group):
        name = "d" + str(group)
        pair_wait("d" + str(group) + "0", rcv["d"].at[group, 0])
        total = merge("d", 0, group)
        if g.parts > 1:
            plane_wait(name, r.plane_d.at[:, group])
            for offset in range(1, g.sections):
                place = r.plane_d.at[offset - 1, group]
                total = total + place[...].astype(F32)
        r.ret_d[group] = total.astype(BF16)
        place = r.back_d.at[group, rows_at(chip, quarter)]
        share = r.ret_d.at[group, other_chips(quarter)]
        line_start(name, lambda at: r.ret_d.at[group, rows_at(at, quarter)], place, share)
        r.back_d[group, rows_at(chip, quarter), :] = r.ret_d[group, rows_at(chip, quarter), :]

    def expert_combine(group):
        line_wait("d" + str(group), r.ret_d.at[group, other_chips(quarter)])
        value = mm_tn(r.table[group], r.back_d[group])
        if g.groups > 1:
            scatter_start(3, group, value)
        else:
            for micro in micros:
                scatter_start(3, micro, value[token_slice(micro)])

    def results_combine():
        for group in groups:
            line_wait("y" + str(group), r.ret_y.at[group, :, other_chips(quarter)])
        places = [(e, q, p) for e in range(g.chips) for q in groups for p in range(g.parts)]
        match = [slot_match(e, g.my_part(from_section(p)), q) for e, q, p in places]
        match = jnp.concatenate(match, axis=0)
        value = mm_tn(match, r.back_y[...].reshape(g.chips * span, width))
        for micro in micros:
            scatter_start(7, micro, value[token_slice(micro)])

    for group in groups:
        parts_work(group, 0, 1)
        results_pair(group, 0, 1)
    if g.parts > 1:
        rows_plane_wait("crow", lambda part: crow_at(part, core))
    for group in groups:
        if g.parts > 1:
            for offset in range(1, g.parts):
                place = rows_place(group, core)(offset)
                wait_all(place, r.row_s.at[group], r.row_r.at[group, offset - 1], False)
                pair_start("rows" + str(group) + str(offset), place, place)
            parts_work(group, 1, g.parts - 1)
            merge_send(group)
            results_pair(group, 1, g.parts - 1)
        if group < g.groups - 1:
            results_line(group)
    for group in groups:
        expert_back_line(group)

    def expert_weights(left, right):
        rows = g.groups * g.parts * 2 * block_rows
        return mm_tn(left.reshape(rows, left.shape[-1]), right.reshape(rows, right.shape[-1]))

    r.g_eup[...] = expert_weights(r.rows[:, :, :, :, :width], r.dpree[...])
    r.g_edown[...] = expert_weights(r.acte[...], r.grow[...])
    store("g_eup", "g_edown")

    def add_small(index, micro, value):
        if micro == 0:
            r.small[index : index + 1, :] = value
        else:
            r.small[index : index + 1, :] += value

    def finish_backward(section, slot, stream, above, micro):
        grad = scatter_sum(slot, micro)
        unit, inverse = normalize(stream[own(micro), :].astype(F32))
        add_small(section, micro, jnp.sum(grad * unit, axis=0, keepdims=True))
        add_small(4 + section, micro, jnp.sum(grad, axis=0, keepdims=True))
        grad = grad * r.prm[section : section + 1, :]
        shared = jnp.mean(grad, axis=-1, keepdims=True)
        along = jnp.mean(grad * unit, axis=-1, keepdims=True)
        grad = inverse * (grad - shared - unit * along) + above[own(micro), :].astype(F32)
        r.gs[section, own(micro), :] = grad.astype(BF16)
        gather_start(r.gs, section, 4 + section, micro)

    for group in groups:
        expert_combine(group)
    results_line(g.groups - 1)
    for micro in micros:
        finish_backward(3, 3, r.xs.at[2], r.cot, micro)

    def bias_row(index, section):
        for micro in micros:
            value = r.gs[section, own(micro), :].astype(F32)
            add_small(index, micro, jnp.sum(value, axis=0, keepdims=True))

    def attention_backward(layer, section, slot, micro):
        at = token_slice(micro)
        dctx = mm_nt(r.w_out[layer], r.gs[section + 1, at, :]).astype(BF16)
        for head in range(g.heads):
            weight = r.probs[layer, micro, head]
            low = weight.astype(BF16)
            dhead = dctx[head_slice(head)]
            query = r.qkv[layer, block_of(0), head_slice(head), at]
            key = r.qkv[layer, block_of(1), head_slice(head), at]
            value = r.qkv[layer, block_of(2), head_slice(head), at]
            dprobs = mm_tn(value, dhead)
            delta = jnp.sum(weight * dprobs, axis=0, keepdims=True)
            dscores = (weight * (dprobs - delta)).astype(BF16)
            r.dqkv[block_of(0), head_slice(head), at] = (mm(key, dscores) * scale).astype(BF16)
            r.dqkv[block_of(1), head_slice(head), at] = (mm_nt(query, dscores) * scale).astype(BF16)
            r.dqkv[block_of(2), head_slice(head), at] = mm_nt(dhead, low).astype(BF16)
        flat_grad = r.dqkv[:, :, at].reshape(3 * head_cols, g.seq)
        scatter_start(slot, micro, mm_tn(flat_grad, r.w_qkv[layer]))

    def attention_weights(layer, section):
        grad_qkv = mm(r.dqkv[...].reshape(3 * head_cols, g.tokens), r.normed[2 * layer])
        if not g.direct:
            r.o_qkv[layer] = grad_qkv
            r.o_out[layer] = mm(r.ctx[layer], r.gs[section + 1])
            return
        r.tmp[0 : 3 * head_cols, :] = grad_qkv
        settle("qkv" + str(layer))
        for at_core, at_chip, index, first in chunk_places():
            r.rq[layer, at_core, at_chip, index] = pack_wide(r.tmp[first : first + cols, :])
        name = "gqkv" + str(layer)
        pair_start(name, r.rq.at[layer, 1 - core], r.hq.at[layer])
        if layer == 0:
            r.tmp[:, 0:head_cols] = dot_as(r.gs[1], r.ctx[0], 0, 1)

    def out_weights_ahead():
        r.tmp[:, 0:head_cols] = dot_as(r.gs[3], r.ctx[1], 0, 1)
        r.tmp[:, head_cols : head_cols + GROUP] = jnp.zeros((width, GROUP), F32)
        out_weights(1)

    def down_weights_ahead():
        r.tmp[...] = mm_tn(r.gs[2], r.act[...])
        settle("down")
        for at_core, at_chip, at_sec, first in shard_places():
            r.rd[at_core, at_chip, at_sec] = pack_wide(r.tmp[first : first + cols, :])
        pair_start("gdown", r.rd.at[1 - core], r.hd)

    def out_weights(layer):
        settle("out" + str(layer))
        for at_core, at_chip, at_sec, first in shard_places():
            block = r.tmp[first : first + cols, 0 : head_cols + GROUP]
            r.ro[layer, at_core, at_chip, at_sec] = pack_out(block)
        pair_start("gout" + str(layer), r.ro.at[layer, 1 - core], r.ho.at[layer])

    for micro in micros:
        gather_wait(r.gs, 3, 7, micro)
        if g.direct and micro == g.micro - 1:
            out_weights_ahead()
        attention_backward(1, 2, 4, micro)
    bias_row(9, 3)
    if g.direct:
        grad_line("gout1", out_at(1), r.ho.at[1], r.ao.at[1], r.lo.at[1])
    attention_weights(1, 2)
    if g.direct:
        grad_line("gqkv1", qkv_at(1), r.hq.at[1], r.aq.at[1], r.lq.at[1])
    finish_backward(2, 4, r.xs.at[1], r.gs.at[3], 0)
    for micro in micros[1:]:
        finish_backward(2, 4, r.xs.at[1], r.gs.at[3], micro)

    for micro in micros:
        rows = token_slice(micro)
        gather_wait(r.gs, 2, 6, micro)
        if g.direct and micro == g.micro - 1:
            down_weights_ahead()
        grad_two = r.gs[2, rows, :]
        for at in hidden_blocks():
            r.dpre[rows, at] = (r.dgelu[rows, at] * mm(grad_two, r.w_down[:, at])).astype(BF16)
        scatter_start(5, micro, mm(r.dpre[rows, :], up_rows(slice(None))))
    bias_row(10, 2)
    sum_up = jnp.sum(r.dpre[...].astype(F32), axis=0, keepdims=True)
    if g.direct:
        grad_relay("gqkv1", qkv_at(1), r.aq.at[1], r.lq.at[1])
        grad_relay("gout1", out_at(1), r.ao.at[1], r.lo.at[1])
        grad_line("gdown", down_at, r.hd, r.ad, r.ld)
        settle("up")
        settle("bias")
        r.ru[...] = mm_tn(r.dpre[...], r.normed[1]).astype(BF16).reshape(r.ru.shape)
        pair_start("gup", r.ru.at[:, 1 - core], r.hu)
        for at_dev in range(g.devices):
            row = sum_up[:, at_dev * shard_rows : (at_dev + 1) * shard_rows]
            row = jnp.broadcast_to(row, (r.pb.shape[0], shard_rows)).astype(BF16)
            r.rb[at_dev // 2, at_dev % 2, :, 0:shard_rows] = row
        pair_start("gbias", r.rb.at[:, 1 - core], r.hb)
    else:
        r.o_down[...] = mm_tn(r.gs[2], r.act[...])
        r.o_up[...] = mm_tn(r.dpre[...], r.normed[1])
        r.o_bup[...] = sum_up
    for micro in micros:
        finish_backward(1, 5, r.xs.at[0], r.gs.at[2], micro)
    if g.direct:
        grad_line("gbias", bias_at, r.hb, r.ab, r.lb)
        grad_relay("gdown", down_at, r.ad, r.ld)

    for micro in micros:
        gather_wait(r.gs, 1, 5, micro)
        attention_backward(0, 0, 6, micro)
    bias_row(8, 1)
    attention_weights(0, 0)
    finish_backward(0, 6, r.x0, r.gs.at[1], 0)
    if g.direct:
        grad_line("gqkv0", qkv_at(0), r.hq.at[0], r.aq.at[0], r.lq.at[0])
    for micro in micros[1:]:
        finish_backward(0, 6, r.x0, r.gs.at[1], micro)
    if g.direct:
        kinds = r.small[...]
        padded = jnp.concatenate([kinds, jnp.zeros((LANES - kinds.shape[0], width), F32)], axis=0)
        r.tmp[:, head_cols : head_cols + GROUP] = padded.T[:, 0:GROUP]
        out_weights(0)
        grad_line("gout0", out_at(0), r.ho.at[0], r.ao.at[0], r.lo.at[0])
        grad_line("gup", up_at, r.hu, r.au, r.lu)
        grad_relay("gbias", bias_at, r.ab, r.lb)
    results_combine()
    if g.direct:
        grad_qkv_plane(1)
        grad_plane("gout1", out_at(1), r.ao.at[1], r.mo.at[1], r.fo.at[1])
        grad_plane("gdown", down_at, r.ad, r.md, r.fd)
        grad_relay("gqkv0", qkv_at(0), r.aq.at[0], r.lq.at[0])
        grad_relay("gout0", out_at(0), r.ao.at[0], r.lo.at[0])
    for micro in micros:
        r.xs[3, own(micro), :] = (scatter_sum(7, micro) + r.xs[2, own(micro), :].astype(F32)).astype(BF16)
        gather_start(r.xs, 3, 3, micro)
    if g.direct:
        grad_relay("gup", up_at, r.au, r.lu)
    for micro in micros:
        gather_wait(r.xs, 3, 3, micro)
        gather_wait(r.gs, 0, 4, micro)
    r.sec_out[...] = r.xs[sec]
    r.sec_grad[...] = r.gs[sec]
    store("sec_out", "sec_grad")
    if g.direct:
        grad_qkv_plane(0)
        grad_plane("gout0", out_at(0), r.ao.at[0], r.mo.at[0], r.fo.at[0])
        grad_qkv_finish(1)
        grad_plane_wait("gdown", r.fd)
        for at_sec in range(g.sections):
            piece = r.fd[at_sec].astype(F32)
            unpack_wide(r.o_down.at[:, pl.ds(at_sec * hidden, hidden)], 0, piece)
        store("o_down")
        r.o_up[...] = grad_line_sum("gup", up_at, r.au)
        r.o_bup[...] = grad_line_sum("gbias", bias_at, r.ab)[0:1, 0:shard_rows]
        store("o_up", "o_bup")
        grad_plane_wait("gout1", r.fo.at[1])
        for at_sec in range(g.sections):
            unpack_out(r.o_out.at[1], 0, r.fo[1, at_sec].astype(F32), at_sec * head_cols)
        grad_qkv_finish(0)
        store("o_qkv")
        grad_plane_wait("gout0", r.fo.at[0])
        everyone = jnp.zeros((top, g.out_lanes), F32)
        for at_sec in range(g.sections):
            piece = r.fo[0, at_sec].astype(F32)
            unpack_out(r.o_out.at[0], 0, piece, at_sec * head_cols)
            everyone = everyone + piece
        r.square[...] = jnp.zeros_like(r.square)
        unpack_small(r.square, 0, everyone, 0)
        r.square[...] = r.square[...].T
        r.o_router[...] = r.square[FIRST_ROUTER : FIRST_ROUTER + g.experts, 0:cols]
        r.o_gain[...] = r.square[0:4, 0:cols]
        r.o_bias[...] = r.square[4:8, 0:cols]
        r.o_bout[...] = r.square[8:10, 0:cols]
        r.o_bdown[...] = r.square[10:11, 0:cols]
        store("o_out", "o_gain", "o_bias", "o_bout", "o_bdown", "o_router")
    else:
        r.o_small[...] = r.small[...]
        store("o_qkv", "o_out", "o_up", "o_down", "o_bup", "o_small")
    for copy in stores:
        copy.wait()
    exchanges_left()
    if g.direct:
        for offset in range(g.chips):
            do_when(near_to(offset), lambda offset=offset: out_all(offset, True))
    for share, send, arrive in left:
        wait_all(share, send, arrive, True)
    for copy, when in started:
        do_when(when, copy.wait_send)


def run_layers(g, operands):
    tokens, width, hidden, sections, chips = g.tokens, g.width, g.hidden, g.sections, g.chips
    part_rows = chips * g.quarter
    inner = operands["h_e_down"].shape[0]
    three = 3 * g.head_cols
    shape = jax.ShapeDtypeStruct
    vmem = pltpu.VMEM
    dma = pltpu.SemaphoreType.DMA
    top = g.cols - TAIL
    wide = width + width // 2
    up_rows = hidden // g.devices
    outs = dict(
        sec_out=shape((tokens, width), BF16),
        sec_grad=shape((tokens, width), BF16),
        g_eup=shape((width, inner), F32),
        g_edown=shape((inner, width), F32),
    )
    if g.direct:
        outs |= dict(
            o_qkv=shape((2, 3 * g.cols, width), F32),
            o_out=shape((2, g.cols, width), F32),
            o_up=shape((up_rows, width), F32),
            o_down=shape((g.cols, sections * hidden), F32),
            o_gain=shape((4, g.cols), F32),
            o_bias=shape((4, g.cols), F32),
            o_bout=shape((2, g.cols), F32),
            o_bdown=shape((1, g.cols), F32),
            o_router=shape((g.experts, g.cols), F32),
            o_bup=shape((1, up_rows), F32),
        )
    else:
        outs |= dict(
            o_qkv=shape((2, three, width), F32),
            o_out=shape((2, g.head_cols, width), F32),
            o_up=shape((hidden, width), F32),
            o_down=shape((width, hidden), F32),
            o_bup=shape((1, hidden), F32),
            o_small=shape((g.small, width), F32),
        )
    scratch = dict(
        xs=vmem((4, tokens, width), BF16),
        gs=vmem((4, tokens, width), BF16),
        normed=vmem((3, tokens, width), BF16),
        wide=vmem((tokens, width + LANES), BF16),
        qkv=vmem((2, 3, g.head_cols, tokens), BF16),
        probs=vmem((2, g.micro, g.heads, g.seq, g.seq), F32),
        ctx=vmem((2, g.head_cols, tokens), BF16),
        act=vmem((tokens, hidden), BF16),
        dgelu=vmem((tokens, hidden), F32),
        dpre=vmem((tokens, hidden), BF16),
        dqkv=vmem((3, g.head_cols, tokens), BF16),
        part=vmem((8, tokens, width), BF16),
        got=vmem((8, g.micro, sections - 1, g.piece, width), BF16),
        mine=vmem((tokens, width), F32),
        square=vmem((LANES, LANES), F32),
        table=vmem((g.groups, part_rows, tokens // g.groups), BF16),
        disp=vmem((g.groups, part_rows, width + LANES), BF16),
        dispc=vmem((chips, g.groups, g.quarter, width), BF16),
        rows=vmem((g.groups, g.parts, 2, part_rows, width + LANES), BF16),
        crow=vmem((g.groups, g.parts, 2, part_rows, width), BF16),
        grow=vmem((g.groups, g.parts, 2, part_rows, width), BF16),
        acte=vmem((g.groups, g.parts, 2, part_rows, inner), BF16),
        dpree=vmem((g.groups, g.parts, 2, part_rows, inner), BF16),
        both=vmem((2, g.parts, 2, part_rows, width), F32),
        small=vmem((g.small, width), F32),
        local_s=dma((len(g.loads) + len(outs),)),
    )
    g.stores = list(outs)
    for name, out in outs.items():
        scratch[name] = vmem(out.shape, out.dtype)
    for name in g.loads:
        scratch[name] = vmem(operands["h_" + name].shape, BF16)
    for which in ("d", "y"):
        scratch["keep_" + which] = vmem((g.groups, g.parts, part_rows, width), F32)
        for name in ("snd_", "rcv_"):
            scratch[name + which] = vmem((g.groups, g.parts, part_rows, width), BF16)
    scratch |= dict(
        out_d=vmem((sections - 1, g.groups, part_rows, width), BF16),
        plane_d=vmem((sections - 1, g.groups, part_rows, width), BF16),
        ret_d=vmem((g.groups, part_rows, width), BF16),
        back_d=vmem((g.groups, part_rows, width), BF16),
        ret_y=vmem((g.groups, g.parts, part_rows, width), BF16),
        back_y=vmem((chips, g.groups, g.parts, g.quarter, width), BF16),
    )
    scratch |= dict(row_s=dma((g.groups,)), row_r=dma((g.groups, max(g.parts - 1, 1))))
    scratch |= dict(scat_s=dma((1,)), gath_s=dma((1,)), scat_r=dma((8, g.micro)), gath_r=dma((8, g.micro)))
    for name, sizes in (
        ("pair", (len(g.pairs),)), ("plane", (len(g.planes),)), ("many", (len(g.manys),)),
        ("line", (len(g.lines), chips)), ("grad", (len(g.grads),)), ("pass", (len(g.grads),)),
    ):
        if sizes[0]:
            scratch |= {name + "_s": dma(sizes), name + "_r": dma(sizes)}
    if g.direct:
        del scratch["pass_s"]
    if g.direct:
        piece = (top, wide)
        out_piece = (top, g.out_lanes)
        up_piece = (up_rows, width)
        bias_piece = (2 * TAIL, LANES)
        scratch |= dict(
            pq=vmem((2, 3, *piece), BF16),
            po=vmem((2, sections, *out_piece), BF16),
            pb=vmem(bias_piece, BF16),
            rb=vmem((chips, 2, *bias_piece), BF16),
            hb=vmem((chips, *bias_piece), BF16),
            ab=vmem((chips - 1, *bias_piece), BF16),
            lb=vmem(bias_piece, BF16),
            lq=vmem((2, 3, *piece), BF16),
            lo=vmem((2, sections, *out_piece), BF16),
            lu=vmem(up_piece, BF16),
            ld=vmem((sections, *piece), BF16),
            pd=vmem((sections, *piece), BF16),
            rq=vmem((2, 2, chips, 3, *piece), BF16),
            ro=vmem((2, 2, chips, sections, *out_piece), BF16),
            ru=vmem((chips, 2, *up_piece), BF16),
            rd=vmem((2, chips, sections, *piece), BF16),
            w_qkv=vmem((2, three, width), BF16),
            w_out=vmem((2, g.head_cols, width), BF16),
            w_down=vmem((width, hidden), BF16),
            w_router=vmem((width, LANES), BF16),
            b_up=vmem((8, hidden), F32),
            prm=vmem((GROUP, width), F32),
            tmp=vmem((width, width), F32),
            hq=vmem((2, chips, 3, *piece), BF16),
            ho=vmem((2, chips, sections, *out_piece), BF16),
            hu=vmem((chips, *up_piece), BF16),
            hd=vmem((chips, sections, *piece), BF16),
            aq=vmem((2, chips - 1, 3, *piece), BF16),
            ao=vmem((2, chips - 1, sections, *out_piece), BF16),
            au=vmem((chips - 1, *up_piece), BF16),
            ad=vmem((chips - 1, sections, *piece), BF16),
            mq=vmem((2, 3, *piece), BF16),
            mo=vmem((2, sections, *out_piece), BF16),
            md=vmem((sections, *piece), BF16),
            fq=vmem((2, 3, *piece), BF16),
            fo=vmem((2, sections, *out_piece), BF16),
            fd=vmem((sections, *piece), BF16),
            wq_s=dma((3, chips + 1)),
            wq_r=dma((3, chips + 1)),
            wo_s=dma((chips,)),
            wo_r=dma((chips,)),
            gq_s=dma((2, 3)),
            gq_r=dma((2, 3)),
        )
    whole = pl.BlockSpec(memory_space=pltpu.VMEM)
    placed = pl.BlockSpec(memory_space=pl.ANY)
    apart = ["h_" + name for name in g.loads]
    names = (*operands, *("h_" + name for name in outs), *scratch)
    results = pl.pallas_call(
        functools.partial(layers_kernel, g, names),
        out_shape=tuple(outs.values()),
        in_specs=[placed if name in apart else whole for name in operands],
        out_specs=[placed] * len(outs),
        scratch_shapes=list(scratch.values()),
        compiler_params=pltpu.CompilerParams(
            collective_id=0, has_side_effects=True, vmem_limit_bytes=62 * 1024 * 1024
        ),
    )(*operands.values())
    return types.SimpleNamespace(**dict(zip(outs, results, strict=True)))


def finish_kernel(count, *refs):
    ins, outs, held = refs[:count], refs[count : 2 * count], refs[2 * count : 3 * count]
    wide, sems = refs[3 * count : 3 * count + 2], refs[-1]
    loads = [pltpu.make_async_copy(ins[i], held[i], sems.at[0, i]) for i in range(count)]
    stores = [pltpu.make_async_copy((wide[i] if i < 2 else held[i]), outs[i], sems.at[1, i]) for i in range(count)]
    for copy in loads:
        copy.start()
    for i in range(count):
        loads[i].wait()
        if i < 2:
            wide[i][...] = held[i][...].astype(F32)
        stores[i].start()
    for copy in stores:
        copy.wait()


def finish(arrays):
    count = len(arrays)
    placed = [pl.BlockSpec(memory_space=pl.ANY)] * count
    held = [pltpu.VMEM(array.shape, array.dtype) for array in arrays]
    wide = [pltpu.VMEM(array.shape, F32) for array in arrays[:2]]
    return pl.pallas_call(
        functools.partial(finish_kernel, count),
        out_shape=tuple(jax.ShapeDtypeStruct(array.shape, F32) for array in arrays),
        in_specs=placed,
        out_specs=placed,
        scratch_shapes=[*held, *wide, pltpu.SemaphoreType.DMA((2, count))],
        compiler_params=pltpu.CompilerParams(vmem_limit_bytes=62 * 1024 * 1024),
    )(*arrays)


BOTH = ("section", "dp")


def body(
    tokens, cotangent, lengths, routes, slots, norm_gain, norm_bias, attn_qkv, attn_out, attn_out_bias,
    ffn_up, ffn_up_bias, ffn_down, ffn_down_bias, router, expert_up, expert_down,
):
    sections, devices = lax.axis_size("section"), lax.axis_size("dp")
    sec = lax.axis_index("section")
    micro, _, seq, width = tokens.shape
    experts = router.shape[1]
    chips = devices // 2
    head_cols = width // sections
    hidden = ffn_up.shape[1] * devices
    cap = 2 * seq // experts
    span = micro * cap
    cols = ffn_down.shape[1]
    kinds = FIRST_ROUTER + experts
    direct = cols == 3 * TAIL and kinds <= GROUP and sections == 4 and ffn_up.shape[1] % 16 == 0
    parts = sections if span % (16 * sections) == 0 else 1
    groups = micro if cap % (16 * parts) == 0 else 1
    group_names = [str(group) for group in range(groups)]
    part_names = [str(part) for part in range(parts)]
    half_names = part_names[:2]
    g = types.SimpleNamespace(
        sections=sections, devices=devices, chips=chips, micro=micro, seq=seq, width=width, hidden=hidden, cap=cap,
        span=span, tokens=micro * seq, piece=seq // sections, heads=head_cols // HEAD_DIM,
        head_cols=head_cols, cols=cols, block=256, small=-(-kinds // 8) * 8, direct=direct, experts=experts,
        out_lanes=head_cols + 2 * GROUP + LANES, parts=parts, groups=groups, quarter=span // (parts * groups),
        loads=(["wo", "wq"] if direct else []) + ["x0", "cot"] + (["wu", "wd"] if direct else []) + ["e_up", "e_down"],
        relay=direct and chips == 4,
        my_part=(lambda section: section) if parts > 1 else (lambda section: 0),
        router_lane=FIRST_ROUTER + (LANES - 2 * GROUP if direct else 0),
        pairs=["crow" + a for a in half_names]
        + [name + a + b for name in ("rows", "d") for a in group_names for b in part_names]
        + ["y" + a + b for a in group_names for b in half_names]
        + ([
            "out0", "qkv0", "up", "bias", "down", "qkv1", "out1",
            "gqkv0", "gqkv1", "gdown", "gup", "gbias", "gout0", "gout1",
        ] if direct else []),
        lines=["out0", "qkv0", "up", "bias", "down", "qkv1", "out1"] if direct else [],
        grads=["gqkv0", "gqkv1", "gdown", "gup", "gbias", "gout0", "gout1"] if direct else [],
        manys=["crow"] + [name + b for name in ("rows", "d", "y") for b in group_names],
        planes=["crow"]
        + ["d" + b for b in group_names]
        + (["down", "out1", "gdown", "gout0", "gout1"] if direct else []),
    )

    operands = dict(
        h_x0=tokens.reshape(g.tokens, width),
        h_cot=cotangent.reshape(g.tokens, width),
        lens=lengths.T,
        routes=routes[:, 0],
        slots=slots[:, 0],
        h_e_up=expert_up[0],
        h_e_down=expert_down[0],
    )
    if direct:
        operands |= dict(
            norm_gain=norm_gain,
            norm_bias=norm_bias,
            out_bias=attn_out_bias,
            down_bias=ffn_down_bias[None],
            up_bias=ffn_up_bias[None],
            router=router.T,
            h_wq=attn_qkv.transpose(0, 2, 1),
            h_wo=attn_out.transpose(0, 2, 1),
            h_wu=ffn_up.T,
            h_wd=ffn_down.T,
        )
    else:

        def every(array, axis):
            return lax.all_gather(array, BOTH, axis=axis, tiled=True)

        def part_of(array, axis, size):
            return lax.dynamic_slice_in_dim(array, sec * size, size, axis)

        rows = [norm_gain, norm_bias, attn_out_bias, ffn_down_bias[None], router.T]
        params = every(jnp.concatenate(rows, axis=0), 1)
        params = jnp.pad(params, ((0, LANES - kinds), (0, 0)))
        b_up = lax.all_gather(ffn_up_bias, "dp", axis=0, tiled=True).astype(F32)
        full = part_of(every(attn_qkv, 2).reshape(2, width, 3, width), 3, head_cols)
        operands |= dict(
            prm=params.astype(F32),
            w_router=params.T,
            b_up=b_up[None],
            w_qkv=full.transpose(0, 2, 3, 1).reshape(2, 3 * head_cols, width),
            w_out=part_of(every(attn_out, 2), 1, head_cols),
            w_up=lax.all_gather(ffn_up, "dp", axis=1, tiled=True).T,
            w_down=part_of(every(ffn_down, 1), 0, hidden).T,
        )
    res = run_layers(g, operands)

    if direct:
        names = list(vars(res))
        done = finish([getattr(res, name) for name in names])
        res = types.SimpleNamespace(**dict(zip(names, done, strict=True)))
        grads = (
            res.o_gain, res.o_bias, res.o_qkv.transpose(0, 2, 1), res.o_out.transpose(0, 2, 1), res.o_bout,
            res.o_up.T, res.o_bup[0], res.o_down.T, res.o_bdown[0], res.o_router.T,
        )
    else:

        def embed(array, shape, axis, size):
            return lax.dynamic_update_slice_in_dim(jnp.zeros(shape, F32), array, sec * size, axis)

        def share(array, axis, over=BOTH):
            return lax.psum_scatter(array, over, scatter_dimension=axis, tiled=True)

        small = share(res.o_small[:kinds], 1)
        g_qkv = res.o_qkv.reshape(2, 3, head_cols, width).transpose(0, 3, 1, 2)
        g_qkv = embed(g_qkv, (2, width, 3, width), 3, head_cols).reshape(2, width, 3 * width)
        g_out = embed(res.o_out, (2, width, width), 1, head_cols)
        g_down = embed(res.o_down.T, (hidden * sections, width), 0, hidden)
        grads = (
            small[0:4], small[4:8], share(g_qkv, 2), share(g_out, 2), small[8:10], share(res.o_up.T, 1, "dp"),
            share(res.o_bup[0], 0, "dp"), share(g_down, 1), small[10], small[FIRST_ROUTER:].T,
        )
    out_shape = (1, micro, 1, seq, width)
    return (
        res.sec_out.reshape(out_shape).astype(F32),
        res.sec_grad.reshape(out_shape).astype(F32),
        *grads,
        res.g_eup[None],
        res.g_edown[None],
    )


def solution(mesh):
    batch = P(None, "dp", None, None)
    table = P(None, "dp", None)
    in_specs = (
        batch, batch, P(None, "dp"), table, table,
        P(None, BOTH), P(None, BOTH), P(None, None, BOTH), P(None, None, BOTH), P(None, BOTH),
        P(None, BOTH), P(BOTH), P(None, BOTH), P(BOTH), P(BOTH, None),
        P("dp", None, "section"), P("dp", "section", None),
    )
    streams = P("section", None, "dp", None, None)
    out_specs = (
        streams, streams,
        P(None, BOTH), P(None, BOTH), P(None, None, BOTH), P(None, None, BOTH), P(None, BOTH),
        P(None, BOTH), P(BOTH), P(None, BOTH), P(BOTH), P(BOTH, None),
        P("dp", None, "section"), P("dp", "section", None),
    )
    return jax.shard_map(body, mesh=mesh, in_specs=in_specs, out_specs=out_specs, check_vma=False)
```
